32 devices in a mesh: dp: 2 (over core), store: 16 (over z, y, x).
Axes of the slice: x: 2, y: 2, z: 4, core: 2. Of those that a mesh axis runs over, the one named last changes fastest.
Arguments:
- inputs: bfloat16 [4096, 768], P(('dp', 'store')), may hold values from -6 to 6
- doc_lengths: int32 [32, 2], P(('dp', 'store')), may hold values from 1 to 96, 128 in all within a row
- datastore: bfloat16 [16384, 768], P(('dp', 'store')), may hold values from -6 to 6
- kept_mask: int32 [16384], P(('dp', 'store')), may hold values from 0 to 1, as said below
- retrieved: int32 [4096, 8], P(('dp', 'store')), may hold values from 0 to 63, all different within a row; in each aligned block of 128 rows (0 to 127, 128 to 255, ...) at most 32 rows name the same one
- self_project: bfloat16 [768, 2304], replicated, may hold values from -0.21875 to 0.21875
- self_output: bfloat16 [768, 768], replicated, may hold values from -0.875 to 0.875
- cross_query: bfloat16 [768, 768], replicated, may hold values from -0.21875 to 0.21875
- cross_memory: bfloat16 [768, 1536], replicated, may hold values from -0.21875 to 0.21875
- cross_output: bfloat16 [768, 768], replicated, may hold values from -1.25 to 1.25
- expand_weight: bfloat16 [768, 3072], replicated, may hold values from -0.21875 to 0.21875
- contract_weight: bfloat16 [3072, 768], replicated, may hold values from -0.109375 to 0.109375
- biases: bfloat16 [7, 768], replicated, may hold values from -1 to 1
- expand_bias: bfloat16 [3072], replicated, may hold values from -3 to 3
- norm_gain: bfloat16 [3, 768], replicated, may hold values from 0.099609375 to 1.8984375
- norm_shift: bfloat16 [3, 768], replicated, may hold values from -3 to 3
- cotangent: bfloat16 [4096, 768], P(('dp', 'store')), may hold values from -6 to 6
Outputs:
- outputs: bfloat16 [4096, 768], P(('dp', 'store'))
- input_grad: float32 [4096, 768], P(('dp', 'store'))
- datastore_grad: float32 [16384, 768], P(('dp', 'store'))
- self_project_grad: float32 [768, 2304], P('store')
- self_output_grad: float32 [768, 768], P('store')
- cross_query_grad: float32 [768, 768], P('store')
- cross_memory_grad: float32 [768, 1536], P('store')
- cross_output_grad: float32 [768, 768], P('store')
- expand_weight_grad: float32 [768, 3072], P('store')
- contract_weight_grad: float32 [3072, 768], P('store')
- biases_grad: float32 [7, 768], P(None, 'store')
- expand_bias_grad: float32 [3072], P('store')
- norm_gain_grad: float32 [3, 768], P(None, 'store')
- norm_shift_grad: float32 [3, 768], P(None, 'store')
The draws below stay inside these ranges and needn't reach their ends.
Inputs may be any that keep to these rules, and one draw needn't show every extreme that they name: `kept_mask`: in each aligned block of 128 rows the ones form one contiguous run of half of 128 to 128 rows. `retrieved`: each row names 8 different blocks of the datastore rows of its own dp group; among the 128 rows of one device no block is named more than 32 times, and some block exactly 32 times. `doc_lengths`: each row sums to 128.
All inputs are finite; a program needn't handle non-finite values.
Results may differ from the reference program's by a relative error of at most 0.024.
Values may be sent and summed in bfloat16 or wider, within the bound.
No kernel may reach another device: no remote copies, remote signals or barrier semaphores. Data moves between devices by JAX's collectives and lax.ppermute only.
A program may use at most 192 MiB of HBM per device.

```python
import math
import jax
import jax.numpy as jnp
import numpy as np
from jax import lax

D = 768
HEADS = 12
HEAD_DIM = 64
FF = 3072
TOK_DEV = 128
TOPB = 8
BLOCK = 128
DOCS = 2
NBLK = 64
CAP = 32
ROWS = 16384
TOKENS = 4096
N_DP = 2
N_STORE = 16


def draw_kept_mask(key, part):
    block_count = ROWS // BLOCK
    first_key, second_key = jax.random.split(key)
    starts = jax.random.randint(first_key, (block_count, 1), 0, BLOCK // 2 + 1)
    extras = jax.random.randint(second_key, (block_count, 1), 0, BLOCK // 2 + 1 - starts)
    places = jnp.arange(BLOCK, dtype=jnp.int32)[None, :]
    inside = (places >= starts) & (places < starts + BLOCK // 2 + extras)
    return inside.astype(jnp.int32).reshape(ROWS)


def block_scale(stream_key, shape, cuts, smallest, largest):
    def one(dim, blocks):
        heights = jax.random.uniform(jax.random.fold_in(jax.random.fold_in(stream_key, 6), dim), (blocks,), jnp.float32, smallest / len(cuts), largest / len(cuts))
        return jnp.repeat(jnp.exp(heights), shape[dim] // blocks).reshape((-1,) + (1,) * (len(shape) - dim - 1))

    level = one(*cuts[0])
    for cut in cuts[1:]:
        level = level * one(*cut)
    return level


def length_profile(amount, total, bound, slope):
    portions = [(1 << 20) // math.isqrt(rank ** slope) + 1 for rank in range(2, amount + 1)]
    spare, given = total - bound - (amount - 1), [1] * (amount - 1)
    while spare > 0:
        candidates = [i for i in range(amount - 1) if given[i] < bound]
        pool, budget = sum([portions[i] for i in candidates]), spare
        for i in candidates:
            extra = min(bound - given[i], max(1, budget * portions[i] // pool), spare)
            given[i] = given[i] + extra
            spare = spare - extra
    return np.array([bound] + given)


def uneven(rng, number_of, total, reach, slope):
    if number_of == 2:
        one = jax.random.randint(rng, (), max(1, total - reach), min(reach, total - 1) + 1)
        return jnp.stack([one, total - one])
    sizes = jnp.asarray(length_profile(number_of, total, reach, slope), jnp.int32)
    twos = (number_of - 1) // 2
    giver, receiver = sizes[1:1 + 2 * twos:2], sizes[2:2 + 2 * twos:2]
    margin = jnp.minimum(giver - 1, reach - receiver)
    moved = jax.random.randint(jax.random.fold_in(rng, 1), (twos,), 0, 1 << 20) % (margin + 1)
    sizes = sizes.at[1:1 + 2 * twos:2].set(giver - moved).at[2:2 + 2 * twos:2].set(receiver + moved)
    return sizes[jax.random.permutation(jax.random.fold_in(rng, 2), number_of)]


def deal_out(stream_key, own, number, rows, number_of, top, limit, lean):
    order = jax.random.permutation(stream_key, number_of)
    packed, ordinary = shares(number_of, rows * top, limit, lean, True), shares(number_of, rows * top, limit, lean, False)
    places = jnp.arange(number_of)

    def named(sizes, offset_by):
        used = int((sizes > 0).sum())
        fixed = max(1, used // 4)
        passed = fixed + (places - fixed + offset_by * (used - fixed)) % max(1, number_of - fixed)
        return jnp.zeros((number_of,), jnp.int32).at[order[jnp.where(places < fixed, places, passed)]].set(jnp.asarray(sizes, jnp.int32))

    sizes = jnp.where(number % 4 == 0, named(packed, number // 4), named(ordinary, number - number // 4 - 1))
    mixed = jax.random.permutation(jax.random.fold_in(own, 3), number_of)
    giver, receiver = mixed[0:number_of // 2 * 2:2], mixed[1:number_of // 2 * 2:2]
    margin = jnp.minimum(sizes[giver] - 1, limit - sizes[receiver]) // 2
    margin = jnp.where((giver == order[0]) | (receiver == order[0]) | (sizes[receiver] == 0), 0, jnp.maximum(margin, 0))
    passed = jax.random.randint(jax.random.fold_in(own, 4), (number_of // 2,), 0, 1 << 20) % (margin + 1)
    sizes = sizes.at[giver].add(-passed).at[receiver].add(passed)
    labels = jnp.searchsorted(jnp.cumsum(sizes), jnp.arange(rows * top), side="right").astype(jnp.int32)
    grid = labels.reshape(top, rows).T
    grid = grid[jax.random.permutation(jax.random.fold_in(own, 1), rows)]
    offset_by = jax.random.randint(jax.random.fold_in(own, 2), (rows, 1), 0, top)
    return jnp.take_along_axis(grid, (jnp.arange(top)[None, :] + offset_by) % top, axis=1)


def shares(amount, total, reach, skew, full):
    portions = [(1 << 20) // math.isqrt(grade ** skew) + 1 for grade in range(1, amount + 1)]
    largest = reach if full else min(reach, max(-(-total // amount), total * portions[0] // sum(portions)))
    least = 1 if total - largest >= amount - 1 else 0
    given, rest = [largest] + [least] * (amount - 1), total - largest - least * (amount - 1)
    while rest > 0:
        candidates = [i for i in range(1, amount) if given[i] < largest] or [i for i in range(1, amount) if given[i] < reach]
        whole, budget = sum([portions[i] for i in candidates]), rest
        for i in candidates:
            more = min(reach - given[i], max(1, budget * portions[i] // whole), rest)
            given[i] = given[i] + more
            rest = rest - more
    return np.array(given)


def scatter_about(stream_key, extent, scale, bound, cuts=(), kind=jnp.bfloat16):
    result = scale * jax.random.normal(stream_key, extent, jnp.float32)
    if cuts:
        result = result * block_scale(stream_key, extent, cuts, -0.22, 0.18)
    return jnp.clip(result, -bound, bound).astype(kind)


def setup_inputs(seed: int = 0) -> dict:
    keys = jax.random.split(jax.random.key(seed), 18)
    inputs = scatter_about(keys[0], (TOKENS, D), 1.0, 6.0, ((0, 32),))
    doc_lengths = jax.vmap(lambda own: uneven(own, DOCS, TOK_DEV, 3 * TOK_DEV // 4, 2))(jax.random.split(keys[1], (N_DP * N_STORE))).reshape((N_DP * N_STORE, DOCS)).astype(jnp.int32)
    datastore = scatter_about(keys[2], (ROWS, D), 1.0, 6.0, ((0, 32),))
    kept_mask = draw_kept_mask(jax.random.fold_in(keys[17], 71), 0)
    retrieved_keys = jax.random.split(jax.random.fold_in(keys[4], 1), TOKENS // TOK_DEV)
    retrieved_turns = jax.random.permutation(jax.random.fold_in(keys[4], 3), TOKENS // TOK_DEV)
    retrieved = jax.vmap(lambda own, number: deal_out(jax.random.fold_in(keys[4], 2), own, number, TOK_DEV, NBLK, TOPB, CAP, 2))(retrieved_keys, retrieved_turns).reshape((TOKENS, TOPB))
    self_project = scatter_about(keys[5], (D, 3 * D), D ** -0.5, 0.21875)
    self_output = scatter_about(keys[6], (D, D), (D // 16) ** -0.5, 0.875)
    cross_query = scatter_about(keys[7], (D, D), D ** -0.5, 0.21875)
    cross_memory = scatter_about(keys[8], (D, 2 * D), D ** -0.5, 0.21875)
    cross_output = scatter_about(keys[9], (D, D), (D // 32) ** -0.5, 1.25)
    expand_weight = scatter_about(keys[10], (D, FF), D ** -0.5, 0.21875)
    contract_weight = scatter_about(keys[11], (FF, D), FF ** -0.5, 0.109375)
    biases = scatter_about(keys[12], (7, D), 0.2, 1.0)
    expand_bias = scatter_about(keys[13], (FF,), 0.5, 3.0)
    norm_gain = jnp.clip(1.0 + 0.18 * jax.random.normal(keys[14], (3, D), jnp.float32), 0.099609375, 1.8984375).astype(jnp.bfloat16)
    norm_shift = scatter_about(keys[15], (3, D), 0.5, 3.0)
    cotangent = scatter_about(keys[16], (TOKENS, D), 1.0, 6.0, ((0, 32),))
    return {"inputs": inputs, "doc_lengths": doc_lengths, "datastore": datastore, "kept_mask": kept_mask, "retrieved": retrieved, "self_project": self_project, "self_output": self_output, "cross_query": cross_query, "cross_memory": cross_memory, "cross_output": cross_output, "expand_weight": expand_weight, "contract_weight": contract_weight, "biases": biases, "expand_bias": expand_bias, "norm_gain": norm_gain, "norm_shift": norm_shift, "cotangent": cotangent}


@jax.custom_vjp
def low(v):
    return lax.optimization_barrier(v.astype(jnp.bfloat16)).astype(jnp.float32)

@jax.custom_vjp
def low_back(v):
    return v

def low_keep(v):
    return (low(v), None)

def low_pass(kept, grad):
    return (grad,)

def back_keep(v):
    return (v, None)

def back_low(kept, grad):
    return (low(grad),)
low.defvjp(low_keep, low_pass)
low_back.defvjp(back_keep, back_low)
EPSILON = 1e-05
MASKED = -1e+30
QUERY_SCALE = 0.125

def matmul(former, latter):
    return jnp.dot(former, latter, precision=lax.Precision.HIGHEST, preferred_element_type=jnp.float32)

def layer_norm(residual, gain_row, shift_row):
    center = residual - lax.optimization_barrier(jnp.mean(residual, axis=-1, keepdims=True))
    spread = lax.optimization_barrier(jnp.mean(center * center, axis=-1, keepdims=True))
    return center * lax.rsqrt(spread + EPSILON) * gain_row + shift_row

def doc_mask(lengths, seq_tokens):
    bounds = jnp.cumsum(lengths, axis=-1)
    places = jnp.arange(seq_tokens, dtype=jnp.int32)
    segment = lax.optimization_barrier(jnp.sum((places[:, None] >= bounds[..., None, :]).astype(jnp.int32), axis=-1))
    causal = places[:, None] >= places[None, :]
    return (segment[..., :, None] == segment[..., None, :]) & causal

def slot_numbers(picks, capacity):
    flat_ids = picks.reshape(-1).astype(jnp.int32)
    sorter = jnp.argsort(flat_ids, stable=True)
    sorted_ids = flat_ids[sorter]
    first_seen = jnp.searchsorted(sorted_ids, sorted_ids, side='left').astype(jnp.int32)
    rank_sorted = jnp.arange(flat_ids.shape[0], dtype=jnp.int32) - first_seen
    ranks = jnp.zeros_like(flat_ids).at[sorter].set(rank_sorted)
    return flat_ids * capacity + ranks

def layer_rows(tokens_step, lengths_step, picks_step, memory_group, kept_group, weights):
    self_project, self_output, cross_query, cross_memory, cross_output, expand_weight, contract_weight, biases, expand_bias, norm_gain, norm_shift = weights
    rows_total = 8 * TOK_DEV
    flat_tokens = tokens_step.reshape(rows_total, D)
    projected = matmul(flat_tokens, self_project)
    heads_all = low(low_back(jnp.concatenate([QUERY_SCALE * (projected[:, :D] + biases[0]), projected[:, D:2 * D], projected[:, 2 * D:] + biases[1]], axis=1)))
    split_heads = heads_all.reshape(8, TOK_DEV, 3, HEADS, HEAD_DIM)
    queries = split_heads[:, :, 0]
    keys_self = split_heads[:, :, 1]
    values_self = split_heads[:, :, 2]
    allowed = doc_mask(lengths_step, TOK_DEV)
    scores = low_back(jnp.einsum('rqhd,rkhd->rhqk', queries, keys_self, precision=lax.Precision.HIGHEST))
    scores = jnp.where(allowed[:, None], scores, MASKED)
    self_lse = jax.nn.logsumexp(scores, axis=-1)
    soft_low = low(jnp.exp(scores - self_lse[..., None]))
    attended = jnp.einsum('rhqk,rkhd->rqhd', soft_low, values_self, precision=lax.Precision.HIGHEST).reshape(rows_total, D)
    attended = low(low_back(attended))
    self_branch = low_back(matmul(attended, self_output) + biases[2])
    first_norm = low(layer_norm(flat_tokens + self_branch, norm_gain[0], norm_shift[0]))
    cross_queries = low(low_back(QUERY_SCALE * (matmul(first_norm, cross_query) + biases[3])))
    copies = low_back(jnp.repeat(cross_queries, TOPB, axis=0))
    slot_ids = jax.vmap(lambda picks_row: slot_numbers(picks_row, CAP))(picks_step)
    row_ids = jnp.arange(8, dtype=jnp.int32)[:, None]
    places = ((slot_ids // CAP * 8 + row_ids) * CAP + slot_ids % CAP).reshape(-1)
    slot_count = NBLK * 8 * CAP
    slot_queries = jnp.zeros((slot_count, D), jnp.float32).at[places].set(copies).reshape(NBLK, 8 * CAP, HEADS, HEAD_DIM)
    keys_memory = memory_group[:, :, :D].reshape(NBLK, BLOCK, HEADS, HEAD_DIM)
    values_memory = memory_group[:, :, D:].reshape(NBLK, BLOCK, HEADS, HEAD_DIM)
    pick_scores = low_back(jnp.einsum('bmhd,bkhd->bhmk', slot_queries, keys_memory, precision=lax.Precision.HIGHEST))
    pick_scores = jnp.where(kept_group[:, None, None, :], pick_scores, MASKED)
    pick_lse = jax.nn.logsumexp(pick_scores, axis=-1)
    pick_soft = low(jnp.exp(pick_scores - pick_lse[..., None]))
    pick_out = jnp.einsum('bhmk,bkhd->bmhd', pick_soft, values_memory, precision=lax.Precision.HIGHEST).reshape(slot_count, D)
    lse_rows = jnp.transpose(pick_lse, (0, 2, 1)).reshape(slot_count, HEADS)
    chosen_out = pick_out[places].reshape(rows_total, TOPB, HEADS, HEAD_DIM)
    chosen_lse = lse_rows[places].reshape(rows_total, TOPB, HEADS)
    cross_lse = jax.nn.logsumexp(chosen_lse, axis=1)
    mix_weights = jnp.exp(chosen_lse - cross_lse[:, None, :])
    cross_attended = jnp.einsum('tjh,tjhd->thd', mix_weights, chosen_out, precision=lax.Precision.HIGHEST).reshape(rows_total, D)
    cross_low = low(low_back(cross_attended))
    cross_branch = low_back(matmul(cross_low, cross_output) + biases[5])
    second_norm = low(layer_norm(first_norm + cross_branch, norm_gain[1], norm_shift[1]))
    expanded = low_back(matmul(second_norm, expand_weight) + expand_bias)
    activated = low(jax.nn.gelu(expanded, approximate=False))
    ffn_branch = low_back(matmul(activated, contract_weight) + biases[6])
    final_norm = layer_norm(second_norm + ffn_branch, norm_gain[2], norm_shift[2])
    return final_norm.reshape(8, TOK_DEV, D)

def forward(tokens_in, store_in, weights, doc_lengths, kept_mask, retrieved):
    cross_memory = weights[3]
    biases = weights[7]
    memory_bias = jnp.concatenate([jnp.zeros((D,), jnp.float32), biases[4]])
    memory = low(low_back(matmul(store_in, cross_memory) + memory_bias))
    memory_blocks = memory.reshape(N_DP, NBLK, BLOCK, 2 * D)
    kept_blocks = kept_mask.reshape(N_DP, NBLK, BLOCK) > 0
    step_count = N_DP * N_STORE // 8
    scanned = (tokens_in.reshape(step_count, 8, TOK_DEV, D), doc_lengths.reshape(step_count, 8, DOCS), retrieved.reshape(step_count, 8, TOK_DEV, TOPB), jnp.arange(step_count, dtype=jnp.int32))

    def step_layer(carry, scanned_step):
        tokens_step, lengths_step, picks_step, step_index = scanned_step
        group_index = step_index * 8 // N_STORE
        memory_group = lax.dynamic_index_in_dim(memory_blocks, group_index, 0, keepdims=False)
        kept_group = lax.dynamic_index_in_dim(kept_blocks, group_index, 0, keepdims=False)
        return (carry, layer_rows(tokens_step, lengths_step, picks_step, memory_group, kept_group, weights))
    unused_carry, results = lax.scan(jax.checkpoint(step_layer), jnp.zeros((), jnp.float32), scanned)
    return results.reshape(TOKENS, D)

def reference(inputs, doc_lengths, datastore, kept_mask, retrieved, self_project, self_output, cross_query, cross_memory, cross_output, expand_weight, contract_weight, biases, expand_bias, norm_gain, norm_shift, cotangent):
    weights = tuple((weight_arg.astype(jnp.float32) for weight_arg in (self_project, self_output, cross_query, cross_memory, cross_output, expand_weight, contract_weight, biases, expand_bias, norm_gain, norm_shift)))

    def whole_layer(tokens_in, store_in, *weight_list):
        return forward(tokens_in, store_in, weight_list, doc_lengths, kept_mask, retrieved)
    results, pullback = jax.vjp(whole_layer, inputs.astype(jnp.float32), datastore.astype(jnp.float32), *weights)
    gradients = pullback(cotangent.astype(jnp.float32))
    return (results.astype(jnp.bfloat16), gradients[0], gradients[1], gradients[2], gradients[3], gradients[4], gradients[5], gradients[6], gradients[7], gradients[8], gradients[9], gradients[10], gradients[11], gradients[12])
```

```python
import functools

import jax
import jax.numpy as jnp
from jax import lax
from jax.experimental import pallas as pl
from jax.experimental.pallas import tpu as pltpu
from jax.sharding import PartitionSpec as P

D = 768
HEADS = 12
HEAD_DIM = 64
TOPB = 8
BLOCK = 128
SLAB = 128
PAIRS = D // SLAB
UNIT = 384
WIDE = D + SLAB
RANK_ROWS = 16

EPSILON = 1e-05
MASKED = -1e30
QUERY_SCALE = 0.125
VMEM_LIMIT = 56 * 1024 * 1024
LOW = jnp.bfloat16
F32 = jnp.float32

_VMEM = pl.BlockSpec(memory_space=pltpu.VMEM)
_SMEM = pl.BlockSpec(memory_space=pltpu.SMEM)


def nn(a, b):
    return lax.dot_general(a, b, (((1,), (0,)), ((), ())), preferred_element_type=F32)


def nt(a, b):
    return lax.dot_general(a, b, (((1,), (1,)), ((), ())), preferred_element_type=F32)


def tn(a, b):
    return lax.dot_general(a, b, (((0,), (0,)), ((), ())), preferred_element_type=F32)


def three(v):
    high = v.astype(LOW)
    rest = v - high.astype(F32)
    mid = rest.astype(LOW)
    return high, mid, (rest - mid.astype(F32)).astype(LOW)


def lanes(shape):
    return lax.broadcasted_iota(jnp.int32, shape, len(shape) - 1)


def rows_of(shape):
    return lax.broadcasted_iota(jnp.int32, shape, len(shape) - 2)


def flag(condition):
    return jnp.where(condition, 1.0, 0.0)


def half_masks():
    first = flag(lanes((1, SLAB)) < HEAD_DIM)
    return first.astype(LOW), (1.0 - first).astype(LOW)


def two_heads(slab, first, second):
    return jnp.concatenate([slab * first, slab * second], axis=0)


def join_heads(stacked, count):
    left = lanes((count, SLAB)) < HEAD_DIM
    return jnp.where(left, stacked[:count], stacked[count:])


def norm_forward(residual, gain, shift):
    center = residual - jnp.mean(residual, axis=-1, keepdims=True)
    spread = jnp.mean(center * center, axis=-1, keepdims=True)
    scale = lax.rsqrt(spread + EPSILON)
    unit = center * scale
    return unit * gain + shift, unit, scale


def norm_backward(grad, unit, scale, gain):
    inner = grad * gain
    down = inner - jnp.mean(inner, axis=-1, keepdims=True)
    down = down - unit * jnp.mean(inner * unit, axis=-1, keepdims=True)
    return scale * down


def row_sum(v):
    return jnp.sum(v, axis=0, keepdims=True)


def call(kernel, outs, scratch=(), n_smem=0, flops=0, moved=0):
    def run(*args):
        return pl.pallas_call(
            kernel,
            out_shape=[jax.ShapeDtypeStruct(s, t) for s, t in outs],
            in_specs=[_SMEM] * n_smem + [_VMEM] * (len(args) - n_smem),
            out_specs=[_VMEM] * len(outs),
            scratch_shapes=list(scratch),
            compiler_params=pltpu.CompilerParams(vmem_limit_bytes=VMEM_LIMIT),
            cost_estimate=pl.CostEstimate(flops=flops, bytes_accessed=moved, transcendentals=0),
        )(*args)

    return run


def plane_ranks(picks_ref, me, k, tokens):
    i = rows_of((RANK_ROWS, tokens))
    group, chip, block = i // 4, (i // 2) % 2, i % 2
    apart = jnp.where(group < 2, 2 * group + chip, 2 * chip + group - 2)
    local = jnp.where(group < 2, block, 2 + block)
    plane = (me // 4) ^ k
    number = plane * 16 + ((me % 4) ^ apart) * 4 + local
    member = jnp.zeros((RANK_ROWS, tokens), F32)
    for j in range(TOPB):
        member = member + flag(picks_ref[j : j + 1, :] == number)
    earlier = flag(rows_of((tokens, tokens)) < lanes((tokens, tokens)))
    rank = nn(member.astype(LOW), earlier.astype(LOW))
    return jnp.where(member > 0.5, rank, -1.0).astype(LOW)


def self_forward_kernel(
    lengths_ref,
    place_ref,
    x_ref,
    picks_ref,
    project_ref,
    output_ref,
    query_ref,
    bias_ref,
    gain_ref,
    shift_ref,
    heads_ref,
    soft_ref,
    attended_ref,
    unit_ref,
    scale_ref,
    first_ref,
    *payload_refs,
):
    tokens = x_ref.shape[0]
    bias = bias_ref[...].astype(F32)
    x = x_ref[...]
    projected = nn(x, project_ref[...])
    heads_ref[:, :D] = (QUERY_SCALE * (projected[:, :D] + bias[0:1])).astype(LOW)
    heads_ref[:, D : 2 * D] = projected[:, D : 2 * D].astype(LOW)
    heads_ref[:, 2 * D :] = (projected[:, 2 * D :] + bias[1:2]).astype(LOW)
    place_row = lax.broadcasted_iota(jnp.int32, (2 * tokens, tokens), 0) % tokens
    place_col = lanes((2 * tokens, tokens))
    segment_row = jnp.zeros((2 * tokens, tokens), jnp.int32)
    segment_col = jnp.zeros((2 * tokens, tokens), jnp.int32)
    bound = 0
    for d in range(lengths_ref.shape[1]):
        bound = bound + lengths_ref[0, d]
        segment_row = segment_row + jnp.where(place_row >= bound, 1, 0)
        segment_col = segment_col + jnp.where(place_col >= bound, 1, 0)
    allowed = (segment_row == segment_col) & (place_row >= place_col)
    first, second = half_masks()
    for p in range(PAIRS):
        at = p * SLAB
        queries = two_heads(heads_ref[:, at : at + SLAB], first, second)
        scores = nt(queries, heads_ref[:, D + at : D + at + SLAB])
        scores = jnp.where(allowed, scores, MASKED)
        top = jnp.max(scores, axis=-1, keepdims=True)
        raised = jnp.exp(scores - top)
        soft = raised / jnp.sum(raised, axis=-1, keepdims=True)
        soft_ref[p] = soft
        mixed = nn(soft.astype(LOW), heads_ref[:, 2 * D + at : 2 * D + at + SLAB])
        attended_ref[:, at : at + SLAB] = join_heads(mixed, tokens).astype(LOW)
    residual = x.astype(F32) + nn(attended_ref[...], output_ref[...]) + bias[2:3]
    normed, unit, scale = norm_forward(
        residual, gain_ref[0:1, :].astype(F32), shift_ref[0:1, :].astype(F32)
    )
    unit_ref[...] = unit
    scale_ref[...] = scale
    low = normed.astype(LOW)
    first_ref[...] = low
    queries = (QUERY_SCALE * (nn(low, query_ref[...]) + bias[3:4])).astype(LOW)
    for k, out in enumerate(payload_refs):
        out[:tokens] = queries
        out[tokens:, tokens:] = jnp.zeros((RANK_ROWS, D - tokens), LOW)
        out[tokens:, :tokens] = plane_ranks(picks_ref, place_ref[0], k, tokens)


def memory_kernel(*refs):
    sets = (len(refs) - 2) // 6
    pieces, (weight_ref, bias_ref), outs = refs[: 2 * sets], refs[2 * sets : 2 * sets + 2], refs[2 * sets + 2 :]
    bias = bias_ref[4:5, :].astype(F32)
    lane = lanes((RANK_ROWS, SLAB))
    for s in range(sets):
        rows_ref, memory_ref, hidden_ref, side_ref = outs[4 * s : 4 * s + 4]
        for j in range(2):
            piece = pieces[2 * s + j]
            rows = piece[: 2 * BLOCK]
            rows_ref[2 * j * BLOCK : 2 * (j + 1) * BLOCK] = rows
            keys = nn(rows, weight_ref[:, :D]).astype(LOW)
            values = (nn(rows, weight_ref[:, D:]) + bias).astype(LOW)
            marks = piece[2 * BLOCK :, :SLAB]
            for l in range(2):
                at = 2 * j + l
                memory_ref[at, :, :D] = keys[l * BLOCK : (l + 1) * BLOCK]
                memory_ref[at, :, D:] = values[l * BLOCK : (l + 1) * BLOCK]
                hidden_ref[at] = (1.0 - marks[l : l + 1].astype(F32)) * MASKED
                wanted = flag((rows_of((RANK_ROWS, SLAB)) == l) & (lane == SLAB - 1))
                column = tn(marks, wanted.astype(LOW))
                place = lanes((BLOCK, SLAB))
                side = jnp.where(place == SLAB - 1, (1.0 - column) * MASKED, 0.0)
                side_ref[at] = jnp.where(place < 48, -1.0, side).astype(LOW)


def selection(ranks, capacity):
    parts = []
    wanted = rows_of((capacity, ranks.shape[1])).astype(F32)
    for b in range(ranks.shape[0]):
        parts.append(flag(ranks[b : b + 1, :] == wanted).astype(LOW))
    return jnp.concatenate(parts, axis=0)


def fill_slots(sel, rows, out_ref, k, capacity):
    got = nn(sel, rows).astype(LOW)
    for b in range(out_ref.shape[0]):
        out_ref[b, k * capacity : (k + 1) * capacity, :] = got[b * capacity : (b + 1) * capacity]


def around16(v, combine):
    for step in (16, 32, 64):
        v = combine(v, pltpu.roll(v, step, 1))
    return v


def lse_lanes(lse):
    high = lse.astype(LOW).astype(F32)
    rest = lse - high
    mid = rest.astype(LOW).astype(F32)
    low = rest - mid
    lane = lanes(lse.shape)
    packed = jnp.where(
        lane < 16, high, jnp.where(lane < 32, mid, jnp.where(lane < 48, low, 0.0))
    )
    return packed.astype(LOW)


def read_lse(packed):
    return around16(packed.astype(F32), jnp.add)


def head_spread(group):
    row = rows_of((SLAB, D))
    row = row % 16 if group else row
    return flag(row == lanes((SLAB, D)) // HEAD_DIM).astype(LOW)


def owner_forward_kernel(capacity, *refs):
    tokens_refs, memory_refs, hidden_refs = refs[0:4], refs[4:8], refs[8:12]
    slots_ref, payload_refs = refs[12], refs[13:17]
    out_scr, lse_scr, inv_scr, sel_scr, ranks_scr = refs[17:]
    sources = len(tokens_refs)
    blocks, rows = slots_ref.shape[:2]
    tokens = tokens_refs[0].shape[0] - RANK_ROWS
    first, second = half_masks()
    for k in range(sources):
        ranks_scr[...] = tokens_refs[k][tokens:, :tokens].astype(F32)
        sel = selection(ranks_scr[...], capacity)
        sel_scr[k] = sel
        fill_slots(sel, tokens_refs[k][:tokens], slots_ref, k, capacity)
    ones = jnp.ones((BLOCK, SLAB), LOW)
    lane_of = lanes((rows, SLAB))
    for s in range(4):

        def one_block(l, carry, s=s):
            i = 4 * s + l
            hidden = hidden_refs[s][l]
            tops = jnp.zeros((rows, SLAB), F32)
            totals = jnp.ones((rows, SLAB), F32)
            base = (i % 8) * 16
            slabs = [slice(p * SLAB, (p + 1) * SLAB) for p in range(PAIRS)]
            scores = [
                nt(two_heads(slots_ref[i, :, at], first, second), memory_refs[s][l, :, at])
                + hidden
                for at in slabs
            ]
            highest = [jnp.max(v, axis=-1, keepdims=True) for v in scores]
            raised = [jnp.exp(v - top).astype(LOW) for v, top in zip(scores, highest)]
            mixed = [
                nn(v, jnp.concatenate([memory_refs[s][l, :, D + at.start : D + at.stop], ones], axis=1))
                for v, at in zip(raised, slabs)
            ]
            for p, at in enumerate(slabs):
                out_scr[i, :, at] = join_heads(mixed[p][:, :SLAB], rows)
                for half in range(2):
                    here = slice(half * rows, (half + 1) * rows)
                    mine = lane_of == base + 2 * p + half
                    tops = jnp.where(mine, highest[p][here], tops)
                    totals = jnp.where(mine, mixed[p][here, SLAB:], totals)
            own = flag((lane_of >= base) & (lane_of < base + HEADS))
            lse_scr[i] = tops + jnp.log(totals)
            inv_scr[i] = own / totals
            return carry

        lax.fori_loop(0, 4, one_block, 0)
    group = 8 * capacity
    own_low = flag(
        rows_of((group, SLAB)) // capacity == lanes((group, SLAB)) // 16
    ).astype(LOW)
    spread = head_spread(True)
    for k in range(sources):
        here = slice(k * capacity, (k + 1) * capacity)

        def stacked(ref, g, here=here):
            return jnp.concatenate([ref[8 * g + b, here, :] for b in range(8)], axis=0)

        by_token, members, sels = [], [], []
        for g in range(2):
            sel = sel_scr[k, g * group : (g + 1) * group, :]
            value = sum(tn(sel, part) for part in three(stacked(lse_scr, g)))
            member = tn(sel, own_low)
            by_token.append(jnp.where(member > 0.5, value, MASKED))
            members.append(member)
            sels.append(sel)
        top = around16(jnp.maximum(*by_token), jnp.maximum)
        weights = [m * jnp.exp(v - top) for m, v in zip(members, by_token)]
        total = around16(weights[0] + weights[1], jnp.add)
        some = total > 0.5
        safe = jnp.where(some, total, 1.0)
        payload_refs[k][:, D:] = lse_lanes(jnp.where(some, top + jnp.log(safe), MASKED))
        partial = jnp.zeros((tokens, D), F32)
        for g in range(2):
            share = nn(sels[g], (weights[g] / safe).astype(LOW)) * stacked(inv_scr, g)
            value = stacked(out_scr, g) * nn(share.astype(LOW), spread)
            partial = partial + tn(sels[g], value.astype(LOW))
        payload_refs[k][:, :D] = partial.astype(LOW)


def owner_backward_kernel(capacity, *refs):
    tokens_refs, grad_refs, memory_refs, side_refs = refs[0:4], refs[4:8], refs[8:12], refs[12:16]
    slots_ref = refs[16]
    memory_grad_refs, payload_refs, bias_ref = refs[17:21], refs[21:25], refs[25]
    got_scr, query_scr, sel_scr, ranks_scr = refs[26:]
    sources = len(tokens_refs)
    blocks, rows = slots_ref.shape[:2]
    tokens = grad_refs[0].shape[0]
    first, second = half_masks()
    for k in range(sources):
        ranks_scr[...] = tokens_refs[k][tokens:, :tokens].astype(F32)
        sel = selection(ranks_scr[...], capacity)
        sel_scr[k] = sel
        fill_slots(sel, grad_refs[k][...], got_scr, k, capacity)
    lane = lanes((1, SLAB))
    last = flag(lane == SLAB - 1).astype(LOW)
    value_side = jnp.broadcast_to(
        -flag((lane >= 48) & (lane < 96)).astype(LOW), (BLOCK, SLAB)
    )

    def picked(head, base):
        inside = (lane >= base) & (lane < base + 48)
        return flag(inside & (lane % 16 == head)).astype(LOW)

    for s in range(4):

        def one_block(l, carry, s=s):
            i = 4 * s + l
            side = got_scr[i, :, D:]
            key_side = side_refs[s][l]
            slabs = [slice(p * SLAB, (p + 1) * SLAB) for p in range(PAIRS)]
            keys = [memory_refs[s][l, :, at] for at in slabs]
            queries = [two_heads(slots_ref[i, :, at], first, second) for at in slabs]
            grads = [two_heads(got_scr[i, :, at], first, second) for at in slabs]
            scores, dots = [], []
            for p in range(PAIRS):
                lse_side = jnp.concatenate(
                    [side * picked(2 * p + h, 0) + last for h in range(2)], axis=0
                )
                scores.append(
                    nt(
                        jnp.concatenate([keys[p], key_side], axis=1),
                        jnp.concatenate([queries[p], lse_side], axis=1),
                    )
                )
            for p, at in enumerate(slabs):
                delta_side = jnp.concatenate(
                    [side * picked(2 * p + h, 48) for h in range(2)], axis=0
                )
                values = memory_refs[s][l, :, D + at.start : D + at.stop]
                dots.append(
                    nt(
                        jnp.concatenate([values, value_side], axis=1),
                        jnp.concatenate([grads[p], delta_side], axis=1),
                    )
                )
            softs = [jnp.exp(v) for v in scores]
            score_grads = [(soft * v).astype(LOW) for soft, v in zip(softs, dots)]
            out = memory_grad_refs[s]
            for p, at in enumerate(slabs):
                query_scr[i, :, at] = join_heads(tn(score_grads[p], keys[p]), rows).astype(LOW)
            for p, at in enumerate(slabs):
                out[l, :, at] = nn(score_grads[p], queries[p]).astype(LOW)
            for p, at in enumerate(slabs):
                out[l, :, D + at.start : D + at.stop] = nn(softs[p].astype(LOW), grads[p]).astype(
                    LOW
                )
            return carry

        lax.fori_loop(0, 4, one_block, 0)
    for k in range(sources):
        here = slice(k * capacity, (k + 1) * capacity)
        value = jnp.concatenate([query_scr[b, here, :] for b in range(blocks)], axis=0)
        payload_refs[k][...] = tn(sel_scr[k], value).astype(LOW)
    total = jnp.zeros((1, D), F32)
    for out in memory_grad_refs:
        for l in range(4):
            total = total + row_sum(out[l, :, D:].astype(F32))
    bias_ref[...] = jnp.broadcast_to(total, (8, D))


def datastore_grad_kernel(*refs):
    weight = refs[4][...].T
    for grad, out in zip(refs[:4], refs[5:]):
        rows = jnp.concatenate([grad[l] for l in range(4)], axis=0)
        out[...] = nn(rows, weight).astype(LOW)


def middle_kernel(
    p0_ref,
    p1_ref,
    p2_ref,
    p3_ref,
    first_ref,
    cotangent_ref,
    output_ref,
    expand_ref,
    contract_ref,
    bias_ref,
    expand_bias_ref,
    gain_ref,
    shift_ref,
    out_ref,
    merged_ref,
    second_ref,
    active_ref,
    branch_grad_ref,
    expanded_grad_ref,
    cross_grad_ref,
    resid_ref,
    payload_ref,
    small_ref,
    wide_ref,
    expanded_scr,
):
    bias = bias_ref[...].astype(F32)
    gain = gain_ref[...].astype(F32)
    shift = shift_ref[...].astype(F32)
    parts = [p0_ref, p1_ref, p2_ref, p3_ref]
    lses = [read_lse(part[:, D:]) for part in parts]
    top = functools.reduce(jnp.maximum, lses)
    weights = [jnp.exp(lse - top) for lse in lses]
    total = functools.reduce(jnp.add, weights)
    overall = top + jnp.log(total)
    spread = head_spread(False)
    merged = jnp.zeros(first_ref.shape, F32)
    for part, weight in zip(parts, weights):
        share = weight / total
        high = share.astype(LOW)
        rest = (share - high.astype(F32)).astype(LOW)
        merged = merged + (nn(high, spread) + nn(rest, spread)) * part[:, :D].astype(F32)
    merged_low = merged.astype(LOW)
    merged_ref[...] = merged_low
    residual = first_ref[...].astype(F32) + nn(merged_low, output_ref[...]) + bias[5:6]
    second, unit_second, scale_second = norm_forward(residual, gain[1:2], shift[1:2])
    second_low = second.astype(LOW)
    second_ref[...] = second_low
    hidden = contract_ref.shape[0]
    for c in range(hidden // D):
        at = slice(c * D, (c + 1) * D)
        expanded = nn(second_low, expand_ref[:, at]) + expand_bias_ref[:, at].astype(F32)
        bell = 0.5 * (1.0 + lax.erf(expanded * 0.7071067811865476))
        active_ref[:, at] = (expanded * bell).astype(LOW)
        slope = bell + expanded * 0.3989422804014327 * jnp.exp(-0.5 * expanded * expanded)
        expanded_scr[:, at] = slope
    residual = second_low.astype(F32) + nn(active_ref[...], contract_ref[...]) + bias[6:7]
    final, unit_final, scale_final = norm_forward(residual, gain[2:3], shift[2:3])
    out_ref[...] = final.astype(LOW)
    cotangent = cotangent_ref[...].astype(F32)
    final_resid = norm_backward(cotangent, unit_final, scale_final, gain[2:3])
    branch_grad = final_resid.astype(LOW)
    branch_grad_ref[...] = branch_grad
    small_ref[0:1, :] = row_sum(branch_grad.astype(F32))
    small_ref[1:2, :] = row_sum(cotangent * unit_final)
    small_ref[2:3, :] = row_sum(cotangent)
    total_grad = final_resid
    for c in range(hidden // D):
        at = slice(c * D, (c + 1) * D)
        active_grad = nt(branch_grad, contract_ref[at, :])
        expanded_grad = (active_grad * expanded_scr[:, at]).astype(LOW)
        expanded_grad_ref[:, at] = expanded_grad
        wide_ref[:, at] = row_sum(expanded_grad.astype(F32))
        total_grad = total_grad + nt(expanded_grad, expand_ref[:, at])
    small_ref[4:5, :] = row_sum(total_grad * unit_second)
    small_ref[5:6, :] = row_sum(total_grad)
    second_resid = norm_backward(total_grad, unit_second, scale_second, gain[1:2])
    resid_ref[...] = second_resid
    cross_grad = second_resid.astype(LOW)
    cross_grad_ref[...] = cross_grad
    small_ref[3:4, :] = row_sum(cross_grad.astype(F32))
    small_ref[6:8, :] = jnp.zeros((2, D), F32)
    attended_grad = nt(cross_grad, output_ref[...]).astype(LOW)
    payload_ref[:, :D] = attended_grad
    product = attended_grad.astype(F32) * merged
    gather = flag(lanes((D, SLAB)) % 16 == rows_of((D, SLAB)) // HEAD_DIM).astype(LOW)
    high, mid, low = three(product)
    delta = nn(high, gather) + nn(mid, gather) + nn(low, gather)
    lane = lanes(overall.shape)
    packed = jnp.zeros(overall.shape, F32)
    for value, base in ((overall, 0), (delta, 48)):
        for i, piece in enumerate(three(value)):
            inside = (lane >= base + 16 * i) & (lane < base + 16 * i + HEADS)
            packed = jnp.where(inside, piece.astype(F32), packed)
    payload_ref[:, D:] = packed.astype(LOW)


def self_backward_kernel(
    d0_ref,
    d1_ref,
    d2_ref,
    d3_ref,
    resid_ref,
    unit_ref,
    scale_ref,
    heads_ref,
    soft_ref,
    query_ref,
    output_ref,
    project_ref,
    gain_ref,
    pre_grad_ref,
    branch_grad_ref,
    project_grad_ref,
    input_grad_ref,
    small_ref,
    attended_scr,
):
    tokens = resid_ref.shape[0]
    query_sum = functools.reduce(
        jnp.add, [d[...].astype(F32) for d in (d0_ref, d1_ref, d2_ref, d3_ref)]
    ).astype(LOW)
    pre_grad = (query_sum.astype(F32) * QUERY_SCALE).astype(LOW)
    pre_grad_ref[...] = pre_grad
    total = resid_ref[...] + nt(pre_grad, query_ref[...])
    unit = unit_ref[...]
    first_resid = norm_backward(total, unit, scale_ref[...], gain_ref[0:1, :].astype(F32))
    branch_grad = first_resid.astype(LOW)
    branch_grad_ref[...] = branch_grad
    attended_scr[...] = nt(branch_grad, output_ref[...]).astype(LOW)
    first, second = half_masks()
    for p in range(PAIRS):
        at = p * SLAB
        grads = two_heads(attended_scr[:, at : at + SLAB], first, second)
        queries = two_heads(heads_ref[:, at : at + SLAB], first, second)
        keys = heads_ref[:, D + at : D + at + SLAB]
        dots = nt(grads, heads_ref[:, 2 * D + at : 2 * D + at + SLAB])
        soft = soft_ref[p]
        score_grad = (soft * (dots - jnp.sum(soft * dots, axis=-1, keepdims=True))).astype(LOW)
        query_grad = join_heads(nn(score_grad, keys), tokens).astype(LOW)
        project_grad_ref[:, at : at + SLAB] = (query_grad.astype(F32) * QUERY_SCALE).astype(LOW)
        project_grad_ref[:, D + at : D + at + SLAB] = tn(score_grad, queries).astype(LOW)
        project_grad_ref[:, 2 * D + at : 2 * D + at + SLAB] = tn(soft.astype(LOW), grads).astype(
            LOW
        )
    input_grad_ref[...] = first_resid + nt(project_grad_ref[...], project_ref[...])
    small_ref[0:1, :] = row_sum(project_grad_ref[:, :D].astype(F32))
    small_ref[1:2, :] = row_sum(project_grad_ref[:, 2 * D :].astype(F32))
    small_ref[2:3, :] = row_sum(branch_grad.astype(F32))
    small_ref[3:4, :] = row_sum(pre_grad.astype(F32))
    small_ref[4:5, :] = row_sum(total * unit)
    small_ref[5:6, :] = row_sum(total)
    small_ref[6:8, :] = jnp.zeros((2, D), F32)


def weight_grad_kernel(plan, count, packed, place_ref, *refs):
    kept_ref, sent_ref = refs[-2:]
    me, core = place_ref[0], place_ref[1]
    at_ref = 0
    for number, rows, columns, at in plan:
        pairs = [refs[at_ref + 2 * i : at_ref + 2 * i + 2] for i in range(number)]
        at_ref += 2 * number
        block = rows // count
        half = columns // 2
        for m in range(rows // D):
            xs = [x_ref[:, m * D : (m + 1) * D].T for x_ref, _ in pairs]
            for c in range(half // UNIT):
                for mine, out in ((core, kept_ref), (1 - core, sent_ref)):
                    start = pl.multiple_of(mine * half + c * UNIT, SLAB)
                    part = sum(
                        nn(x, g_ref[:, pl.ds(start, UNIT)]) for x, (_, g_ref) in zip(xs, pairs)
                    ).astype(LOW)
                    for k in range(D // block):
                        to = me ^ (m * (D // block) + k)
                        low = at + c * block
                        out[to, low : low + block, :] = part[k * block : (k + 1) * block]
    if packed is not None:
        small_ref = refs[at_ref]
        for r in range(count):
            kept_ref[me ^ r, packed : packed + RANK_ROWS, :] = small_ref[r, core]
            sent_ref[me ^ r, packed : packed + RANK_ROWS, :] = small_ref[r, 1 - core]


def swap(v, bits):
    count = lax.axis_size("store")
    return lax.ppermute(v, "store", [(i, i ^ bits) for i in range(count)])


def swap_core(v):
    return lax.ppermute(v, "dp", [(0, 1), (1, 0)])


def after(v, *earlier):
    return lax.optimization_barrier((v, *earlier))[0]


def sum_kernel(w_ref, c1_ref, c2_ref, c3_ref, out_ref):
    total = w_ref[...].astype(F32)
    for come in (c1_ref, c2_ref, c3_ref):
        total = total + come[...].astype(F32)
    out_ref[...] = total.astype(LOW)


def spread_kernel(plan, count, packed, place_ref, own_ref, other_ref, *outs):
    core = place_ref[1]
    for (rows, columns, at), out in zip(plan, outs):
        block = rows // count
        half = columns // 2
        for c in range(half // UNIT):
            low = at + c * block
            for value, mine in ((own_ref, core), (other_ref, 1 - core)):
                start = pl.multiple_of(mine * half + c * UNIT, SLAB)
                out[:, pl.ds(start, UNIT)] = value[low : low + block].astype(F32)
    if packed is not None:
        outs[-1][core] = own_ref[packed : packed + RANK_ROWS].astype(F32)
        outs[-1][1 - core] = other_ref[packed : packed + RANK_ROWS].astype(F32)


class WeightSums:
    def __init__(self, place, count):
        self.place, self.count = place, count
        self.groups = ([], [])
        self.plan, self.packed = [], None
        self.rows = [0, 0]

    def add(self, group, products, small=None):
        plan, at = [], 0
        for pairs in products:
            rows, columns = pairs[0][0].shape[1], pairs[0][1].shape[1]
            plan.append((len(pairs), rows, columns, at))
            self.plan.append((group, rows, columns, self.rows[group] + at))
            at += rows // self.count * (columns // 2 // UNIT)
        args = [v for pairs in products for pair in pairs for v in pair]
        packed = None
        if small is not None:
            packed = at
            self.packed = (group, self.rows[group] + at)
            at += RANK_ROWS
            args.append(small)
        self.rows[group] += at
        shape = (self.count, at, UNIT)
        flops = sum(2 * x.size * g.shape[1] for pairs in products for x, g in pairs)
        kept, sent = call(
            functools.partial(weight_grad_kernel, tuple(plan), self.count, packed),
            [(shape, LOW), (shape, LOW)],
            n_smem=1,
            flops=flops,
            moved=4 * at * self.count * UNIT,
        )(self.place, *args)
        self.groups[group].append((kept, swap_core(sent)))

    def both(self, group, cut):
        parts = [
            cut(kept.reshape(4, 2, 2, *kept.shape[1:]))
            + cut(come.reshape(4, 2, 2, *come.shape[1:]))
            for kept, come in self.groups[group]
        ]
        return jnp.concatenate(parts, axis=2) if len(parts) > 1 else parts[0]

    def start(self):
        self.sent = (self.both(0, lambda v: v[:, :, 1]), self.both(1, lambda v: v[:, 1]))
        self.kept = (self.both(0, lambda v: v[:, :, 0]), self.both(1, lambda v: v[:, 0]))
        return self.sent

    def first(self):
        come = (swap(self.sent[0], 1), swap(self.sent[1], 2))
        self.sent = tuple(k[:, 1] + c[:, 1] for k, c in zip(self.kept, come))
        self.kept = tuple(k[:, 0] + c[:, 0] for k, c in zip(self.kept, come))
        return self.sent

    def second(self):
        come = (swap(self.sent[0], 2), swap(self.sent[1], 1))
        self.w = jnp.concatenate([k + c for k, c in zip(self.kept, come)], axis=1)
        return self.w

    def third(self):
        come = [swap(self.w[k], 4 * k) for k in (1, 2, 3)]
        (self.own,) = call(sum_kernel, [(come[0].shape, LOW)])(self.w[0], *come)
        return self.own

    def finish(self):
        other = swap_core(self.own)
        shift = (0, self.rows[0])
        plan = tuple((rows, columns, shift[g] + at) for g, rows, columns, at in self.plan)
        shapes = [((rows // self.count, columns), F32) for rows, columns, _ in plan]
        packed = None
        if self.packed is not None:
            packed = shift[self.packed[0]] + self.packed[1]
            shapes.append(((2, RANK_ROWS, UNIT), F32))
        return call(
            functools.partial(spread_kernel, plan, self.count, packed), shapes, n_smem=1
        )(self.place, self.own, other)


def local_tree(
    inputs,
    doc_lengths,
    datastore,
    kept_mask,
    retrieved,
    self_project,
    self_output,
    cross_query,
    cross_memory,
    cross_output,
    expand_weight,
    contract_weight,
    biases,
    expand_bias,
    norm_gain,
    norm_shift,
    cotangent,
):
    tokens = inputs.shape[0]
    count = lax.axis_size("store")
    local_blocks = datastore.shape[0] // BLOCK
    all_blocks = local_blocks * count
    capacity = 2 * tokens * TOPB // all_blocks
    plane_blocks = 4 * local_blocks
    rows_in = 4 * capacity
    hidden = expand_weight.shape[1]
    me = lax.axis_index("store").astype(jnp.int32)
    core = lax.axis_index("dp").astype(jnp.int32)
    place = jnp.stack([me, core])

    marks = kept_mask.reshape(2, 2, BLOCK).astype(LOW)
    marks = jnp.pad(marks, ((0, 0), (0, RANK_ROWS - 2), (0, D - BLOCK)))
    halves = datastore.reshape(2, 2 * BLOCK, D)
    a0, b0 = (jnp.concatenate([halves[h], marks[h]]) for h in range(2))
    a1, b1 = swap(a0, 1), swap(b0, 2)
    ay = swap(jnp.stack([a0, a1]), 2)
    bx = swap(jnp.stack([b0, b1]), 1)

    heads_all, soft_self, attended, unit_first, scale_first, first_low, *queries = call(
        self_forward_kernel,
        [
            ((tokens, 3 * D), LOW),
            ((PAIRS, 2 * tokens, tokens), F32),
            ((tokens, D), LOW),
            ((tokens, D), F32),
            ((tokens, 1), F32),
            ((tokens, D), LOW),
        ]
        + [((tokens + RANK_ROWS, D), LOW)] * 4,
        n_smem=2,
        flops=2 * tokens * D * D * 5,
        moved=10 * D * D,
    )(
        doc_lengths,
        place,
        inputs,
        retrieved.T,
        self_project,
        self_output,
        cross_query,
        biases,
        norm_gain,
        norm_shift,
    )
    queries = [queries[0]] + [swap(queries[k], 4 * k) for k in (1, 2, 3)]

    one_set = [
        ((4 * BLOCK, D), LOW),
        ((4, BLOCK, 2 * D), LOW),
        ((4, 1, BLOCK), F32),
        ((4, BLOCK, SLAB), LOW),
    ]
    memory_call = call(
        memory_kernel,
        one_set * 2,
        flops=2 * 8 * BLOCK * D * 2 * D,
        moved=8 * BLOCK * D * 8,
    )
    near = memory_call(a0, a1, b0, b1, cross_memory, biases)
    far = memory_call(ay[0], ay[1], bx[0], bx[1], cross_memory, biases)
    sets = [near[:4], far[:4], near[4:], far[4:]]
    stored, memory, hidden_rows, key_side = zip(*sets)

    slots, *payloads = call(
        functools.partial(owner_forward_kernel, capacity),
        [((plane_blocks, rows_in, D), LOW)] + [((tokens, WIDE), LOW)] * 4,
        scratch=[
            pltpu.VMEM((plane_blocks, rows_in, D), F32),
            pltpu.VMEM((plane_blocks, rows_in, SLAB), F32),
            pltpu.VMEM((plane_blocks, rows_in, SLAB), F32),
            pltpu.VMEM((4, plane_blocks * capacity, tokens), LOW),
            pltpu.VMEM((RANK_ROWS, tokens), F32),
        ],
        flops=8 * rows_in * plane_blocks * BLOCK * D,
        moved=2 * plane_blocks * BLOCK * 4 * D,
    )(*queries, *memory, *hidden_rows)
    parts = [payloads[0]] + [swap(payloads[k], 4 * k) for k in (1, 2, 3)]

    (
        outputs,
        merged_low,
        second_low,
        active_low,
        branch_grad,
        expanded_grad,
        cross_grad,
        second_resid,
        payload,
        small_middle,
        wide_bias,
    ) = call(
        middle_kernel,
        [
            ((tokens, D), LOW),
            ((tokens, D), LOW),
            ((tokens, D), LOW),
            ((tokens, hidden), LOW),
            ((tokens, D), LOW),
            ((tokens, hidden), LOW),
            ((tokens, D), LOW),
            ((tokens, D), F32),
            ((tokens, WIDE), LOW),
            ((8, D), F32),
            ((1, hidden), F32),
        ],
        scratch=[pltpu.VMEM((tokens, hidden), F32)],
        flops=2 * tokens * D * (4 * hidden + 2 * D),
        moved=2 * D * (2 * hidden + D),
    )(
        *parts,
        first_low,
        cotangent,
        cross_output,
        expand_weight,
        contract_weight,
        biases,
        expand_bias.reshape(1, hidden),
        norm_gain,
        norm_shift,
    )
    grads = [payload] + [swap(payload, 4 * k) for k in (1, 2, 3)]

    early = WeightSums(place, count)
    early.add(0, [[(active_low, branch_grad)], [(merged_low, cross_grad)]])
    early.add(1, [[(second_low, expanded_grad)]])
    early_start = early.start()
    slots = after(slots, *early_start)

    out = call(
        functools.partial(owner_backward_kernel, capacity),
        [((4, BLOCK, 2 * D), LOW)] * 4 + [((tokens, D), LOW)] * 4 + [((8, D), F32)],
        scratch=[
            pltpu.VMEM((plane_blocks, rows_in, WIDE), LOW),
            pltpu.VMEM((plane_blocks, rows_in, D), LOW),
            pltpu.VMEM((4, plane_blocks * capacity, tokens), LOW),
            pltpu.VMEM((RANK_ROWS, tokens), F32),
        ],
        flops=20 * rows_in * plane_blocks * BLOCK * D,
        moved=2 * plane_blocks * BLOCK * 8 * D,
    )(*queries, *grads, *memory, *key_side, slots)
    memory_grads, query_grads, value_bias_grad = out[:4], out[4:8], out[8]
    parts = [query_grads[0]] + [swap(query_grads[k], 4 * k) for k in (1, 2, 3)]

    late = WeightSums(place, count)
    late.add(
        1,
        [
            [
                (rows, grad.reshape(4 * BLOCK, 2 * D))
                for rows, grad in zip(stored, memory_grads)
            ]
        ],
    )
    early_first = early.first()
    plane_grads = call(
        datastore_grad_kernel,
        [((4 * BLOCK, D), LOW)] * 4,
        flops=2 * plane_blocks * BLOCK * D * 2 * D,
        moved=plane_blocks * BLOCK * D * 6,
    )(*memory_grads, after(cross_memory, *early_first))
    early_second = early.second()
    near_a, far_a, near_b, far_b = plane_grads
    a = (near_a + swap(far_a, 2)).reshape(2, 2 * BLOCK, D)
    b = (near_b + swap(far_b, 1)).reshape(2, 2 * BLOCK, D)
    datastore_grad = jnp.concatenate(
        [
            a[0].astype(F32) + swap(a[1], 1).astype(F32),
            b[0].astype(F32) + swap(b[1], 2).astype(F32),
        ]
    )

    second_resid = after(second_resid, early_second, far_a, far_b)
    pre_grad, self_branch_grad, project_grad, input_grad, small_self = call(
        self_backward_kernel,
        [
            ((tokens, D), LOW),
            ((tokens, D), LOW),
            ((tokens, 3 * D), LOW),
            ((tokens, D), F32),
            ((8, D), F32),
        ],
        scratch=[pltpu.VMEM((tokens, D), LOW)],
        flops=2 * tokens * D * D * 5,
        moved=10 * D * D,
    )(
        *parts,
        second_resid,
        unit_first,
        scale_first,
        heads_all,
        soft_self,
        cross_query,
        self_output,
        self_project,
        norm_gain,
    )
    narrow = jnp.concatenate(
        [
            small_self[0:4],
            value_bias_grad[0:1],
            small_middle[3:4],
            small_middle[0:1],
            small_self[4:5],
            small_middle[4:5],
            small_middle[1:2],
            small_self[5:6],
            small_middle[5:6],
            small_middle[2:3],
        ]
    )
    share = D // count
    narrow = jnp.swapaxes(narrow.reshape(13, count, share), 0, 1)
    small = jnp.concatenate([narrow, wide_bias.reshape(count, hidden // D, share)], axis=1)
    small = jnp.pad(small, ((0, 0), (0, 7), (0, 0))).reshape(count, 3, UNIT).astype(LOW)
    small = jnp.stack(
        [
            jnp.pad(small[:, :2], ((0, 0), (0, RANK_ROWS - 2), (0, 0))),
            jnp.pad(small[:, 2:], ((0, 0), (0, RANK_ROWS - 1), (0, 0))),
        ],
        axis=1,
    )
    early.third()
    contract_weight_grad, cross_output_grad, expand_weight_grad = early.finish()
    late.add(0, [[(inputs, project_grad)]], small)
    late.add(1, [[(attended, self_branch_grad)], [(first_low, pre_grad)]])
    late.start()
    late.first()
    late.second()
    late.third()
    (
        cross_memory_grad,
        self_project_grad,
        self_output_grad,
        cross_query_grad,
        small,
    ) = late.finish()
    small = jnp.concatenate([small[0, :2], small[1, :1]])
    small = small.reshape(24, share)
    return (
        outputs,
        input_grad,
        datastore_grad,
        self_project_grad,
        self_output_grad,
        cross_query_grad,
        cross_memory_grad,
        cross_output_grad,
        expand_weight_grad,
        contract_weight_grad,
        small[:7],
        small[13:17].reshape(hidden // count),
        small[7:10],
        small[10:13],
    )


def layer_norm(residual, gain_row, shift_row):
    center = residual - jnp.mean(residual, axis=-1, keepdims=True)
    spread = jnp.mean(center * center, axis=-1, keepdims=True)
    return center * lax.rsqrt(spread + EPSILON) * gain_row + shift_row


def doc_mask(lengths, seq_tokens):
    upto = jnp.tri(lengths.shape[-1], dtype=jnp.int32)
    bounds = jnp.sum(lengths[..., None, :] * upto, axis=-1)
    places = jnp.arange(seq_tokens, dtype=jnp.int32)
    segment = jnp.sum((places[:, None] >= bounds[..., None, :]).astype(jnp.int32), axis=-1)
    causal = places[:, None] >= places[None, :]
    return (segment[..., :, None] == segment[..., None, :]) & causal


def slot_numbers(picks, capacity):
    flat_ids = picks.reshape(-1)
    sorter = jnp.argsort(flat_ids, stable=True)
    sorted_ids = flat_ids[sorter]
    first_seen = jnp.searchsorted(sorted_ids, sorted_ids, side="left")
    rank_sorted = jnp.arange(flat_ids.shape[0], dtype=jnp.int32) - first_seen
    ranks = jnp.zeros_like(flat_ids).at[sorter].set(rank_sorted)
    return flat_ids * capacity + ranks


def place_rows(rows, slot_ids, total_slots, store_count, local_blocks, capacity):
    placed = jnp.zeros((total_slots, rows.shape[1]), rows.dtype).at[slot_ids].set(rows)
    return placed.reshape(store_count, local_blocks, capacity, rows.shape[1])


def local_slots(
    inputs,
    doc_lengths,
    datastore,
    kept_mask,
    retrieved,
    self_project,
    self_output,
    cross_query,
    cross_memory,
    cross_output,
    expand_weight,
    contract_weight,
    biases,
    expand_bias,
    norm_gain,
    norm_shift,
    cotangent,
):
    tok_count = inputs.shape[0]
    store_count = lax.axis_size("store")
    local_blocks = datastore.shape[0] // BLOCK
    all_blocks = local_blocks * store_count
    capacity = 2 * tok_count * TOPB // all_blocks
    rows_in = store_count * capacity
    total_slots = all_blocks * capacity
    gain_rows = norm_gain.astype(jnp.float32)
    shift_rows = norm_shift.astype(jnp.float32)
    bias_rows = biases.astype(jnp.float32)
    projected = jnp.dot(inputs, self_project, preferred_element_type=jnp.float32)
    heads_all = jnp.concatenate(
        [
            QUERY_SCALE * (projected[:, :D] + bias_rows[0]),
            projected[:, D : 2 * D],
            projected[:, 2 * D :] + bias_rows[1],
        ],
        axis=1,
    ).astype(jnp.bfloat16)
    queries = heads_all[:, :D].reshape(tok_count, HEADS, HEAD_DIM)
    keys_self = heads_all[:, D : 2 * D].reshape(tok_count, HEADS, HEAD_DIM)
    values_self = heads_all[:, 2 * D :].reshape(tok_count, HEADS, HEAD_DIM)
    allowed = doc_mask(doc_lengths[0], tok_count)

    def self_scores():
        raw_scores = jnp.einsum(
            "qhd,khd->hqk", queries, keys_self, preferred_element_type=jnp.float32
        )
        return jnp.where(allowed[None], raw_scores, MASKED)

    scores = self_scores()
    self_lse = jax.nn.logsumexp(scores, axis=-1)
    soft_low = jnp.exp(scores - self_lse[..., None]).astype(jnp.bfloat16)
    attended = (
        jnp.einsum("hqk,khd->qhd", soft_low, values_self, preferred_element_type=jnp.float32)
        .reshape(tok_count, D)
        .astype(jnp.bfloat16)
    )
    self_branch = jnp.dot(attended, self_output, preferred_element_type=jnp.float32) + bias_rows[2]
    first_norm, first_back = jax.vjp(
        layer_norm, inputs.astype(jnp.float32) + self_branch, gain_rows[0], shift_rows[0]
    )
    first_low = first_norm.astype(jnp.bfloat16)
    cross_queries = (
        QUERY_SCALE
        * (jnp.dot(first_low, cross_query, preferred_element_type=jnp.float32) + bias_rows[3])
    ).astype(jnp.bfloat16)
    slot_ids = slot_numbers(retrieved, capacity)
    send_buffer = place_rows(
        jnp.repeat(cross_queries, TOPB, axis=0),
        slot_ids,
        total_slots,
        store_count,
        local_blocks,
        capacity,
    )
    arrived = lax.all_to_all(send_buffer, "store", split_axis=0, concat_axis=2, tiled=True)
    owner_queries = arrived[0].reshape(local_blocks, rows_in, HEADS, HEAD_DIM)
    memory_bias = jnp.concatenate([jnp.zeros((D,), jnp.float32), bias_rows[4]])
    memory_low = (
        jnp.dot(datastore, cross_memory, preferred_element_type=jnp.float32) + memory_bias
    ).astype(jnp.bfloat16)
    memory_blocks = memory_low.reshape(local_blocks, BLOCK, 2 * D)
    store_keys = memory_blocks[:, :, :D].reshape(local_blocks, BLOCK, HEADS, HEAD_DIM)
    store_values = memory_blocks[:, :, D:].reshape(local_blocks, BLOCK, HEADS, HEAD_DIM)
    kept_rows = kept_mask.reshape(local_blocks, BLOCK) > 0

    def block_scores(query_blocks):
        raw_scores = jnp.einsum(
            "bmhd,bkhd->bhmk", query_blocks, store_keys, preferred_element_type=jnp.float32
        )
        return jnp.where(kept_rows[:, None, None, :], raw_scores, MASKED)

    owner_scores = block_scores(owner_queries)
    owner_lse = jax.nn.logsumexp(owner_scores, axis=-1)
    owner_soft = jnp.exp(owner_scores - owner_lse[..., None]).astype(jnp.bfloat16)
    partial_value = jnp.einsum(
        "bhmk,bkhd->bmhd", owner_soft, store_values, preferred_element_type=jnp.float32
    ).reshape(local_blocks, rows_in, D)
    partial_lse = jnp.transpose(owner_lse, (0, 2, 1))
    returned, returned_lse = (
        lax.all_to_all(partial_value[None], "store", split_axis=2, concat_axis=0, tiled=True),
        lax.all_to_all(partial_lse[None], "store", split_axis=2, concat_axis=0, tiled=True),
    )
    picked = returned.reshape(total_slots, D)[slot_ids].reshape(tok_count, TOPB, HEADS, HEAD_DIM)
    picked_lse = returned_lse.reshape(total_slots, HEADS)[slot_ids].reshape(tok_count, TOPB, HEADS)
    overall = jax.nn.logsumexp(picked_lse, axis=1)
    mix_weights = jnp.exp(picked_lse - overall[:, None, :])
    merged = jnp.einsum(
        "tjh,tjhd->thd", mix_weights, picked, precision=lax.Precision.HIGHEST
    ).reshape(tok_count, D)
    merged_low = merged.astype(jnp.bfloat16)
    cross_branch = (
        jnp.dot(merged_low, cross_output, preferred_element_type=jnp.float32) + bias_rows[5]
    )
    second_norm, second_back = jax.vjp(
        layer_norm, first_low.astype(jnp.float32) + cross_branch, gain_rows[1], shift_rows[1]
    )
    second_low = second_norm.astype(jnp.bfloat16)
    expanded = jnp.dot(
        second_low, expand_weight, preferred_element_type=jnp.float32
    ) + expand_bias.astype(jnp.float32)
    activated, gelu_back = jax.vjp(
        lambda pre_act: jax.nn.gelu(pre_act, approximate=False), expanded
    )
    activated_low = activated.astype(jnp.bfloat16)
    ffn_branch = (
        jnp.dot(activated_low, contract_weight, preferred_element_type=jnp.float32) + bias_rows[6]
    )
    final_norm, final_back = jax.vjp(
        layer_norm, second_low.astype(jnp.float32) + ffn_branch, gain_rows[2], shift_rows[2]
    )
    outputs = final_norm.astype(jnp.bfloat16)
    final_resid, final_gain, final_shift = final_back(cotangent.astype(jnp.float32))
    ffn_branch_grad = final_resid.astype(jnp.bfloat16)
    contract_weight_grad = jnp.dot(
        activated_low.T, ffn_branch_grad, preferred_element_type=jnp.float32
    )
    activated_grad = jnp.dot(ffn_branch_grad, contract_weight.T, preferred_element_type=jnp.float32)
    (expanded_raw,) = gelu_back(activated_grad)
    expanded_grad = expanded_raw.astype(jnp.bfloat16)
    expand_weight_grad = jnp.dot(second_low.T, expanded_grad, preferred_element_type=jnp.float32)
    expand_bias_grad = jnp.sum(expanded_grad.astype(jnp.float32), axis=0)
    second_total = final_resid + jnp.dot(
        expanded_grad, expand_weight.T, preferred_element_type=jnp.float32
    )
    second_resid, second_gain, second_shift = second_back(second_total)
    cross_branch_grad = second_resid.astype(jnp.bfloat16)
    cross_output_grad = jnp.dot(merged_low.T, cross_branch_grad, preferred_element_type=jnp.float32)
    attended_grad = jnp.dot(
        cross_branch_grad, cross_output.T, preferred_element_type=jnp.float32
    ).astype(jnp.bfloat16)
    delta_rows = jnp.sum(
        attended_grad.reshape(tok_count, HEADS, HEAD_DIM).astype(jnp.float32)
        * merged.reshape(tok_count, HEADS, HEAD_DIM),
        axis=-1,
    )
    grad_buffer = place_rows(
        jnp.repeat(attended_grad, TOPB, axis=0),
        slot_ids,
        total_slots,
        store_count,
        local_blocks,
        capacity,
    )
    overall_buffer = place_rows(
        jnp.repeat(overall, TOPB, axis=0),
        slot_ids,
        total_slots,
        store_count,
        local_blocks,
        capacity,
    )
    delta_buffer = place_rows(
        jnp.repeat(delta_rows, TOPB, axis=0),
        slot_ids,
        total_slots,
        store_count,
        local_blocks,
        capacity,
    )
    arrived_grad = lax.all_to_all(grad_buffer, "store", split_axis=0, concat_axis=2, tiled=True)
    arrived_overall, arrived_delta = (
        lax.all_to_all(overall_buffer, "store", split_axis=0, concat_axis=2, tiled=True),
        lax.all_to_all(delta_buffer, "store", split_axis=0, concat_axis=2, tiled=True),
    )
    owner_grad = arrived_grad[0].reshape(local_blocks, rows_in, HEADS, HEAD_DIM)
    overall_heads = jnp.transpose(arrived_overall[0], (0, 2, 1))
    delta_heads = jnp.transpose(arrived_delta[0], (0, 2, 1))
    soft_again = jnp.exp(block_scores(owner_queries) - owner_lse[..., None])
    soft_again_low = soft_again.astype(jnp.bfloat16).astype(jnp.float32)
    weight_mix = jnp.exp(owner_lse - overall_heads)
    value_dots = jnp.einsum(
        "bmhd,bkhd->bhmk", owner_grad, store_values, preferred_element_type=jnp.float32
    )
    exact_sum = jnp.sum(soft_again * value_dots, axis=-1, keepdims=True)
    rounded_sum = jnp.sum(soft_again_low * value_dots, axis=-1, keepdims=True)
    score_grad = (
        weight_mix[..., None]
        * soft_again
        * (value_dots - exact_sum + rounded_sum - delta_heads[..., None])
    ).astype(jnp.bfloat16)
    query_grad = (
        jnp.einsum("bhmk,bkhd->bmhd", score_grad, store_keys, preferred_element_type=jnp.float32)
        .astype(jnp.bfloat16)
        .reshape(local_blocks, rows_in, D)
    )
    key_grad = jnp.einsum(
        "bhmk,bmhd->bkhd", score_grad, owner_queries, preferred_element_type=jnp.float32
    )
    weighted_soft = weight_mix[..., None] * soft_again_low
    value_grad = jnp.einsum(
        "bhmk,bmhd->bkhd",
        weighted_soft,
        owner_grad.astype(jnp.float32),
        precision=lax.Precision.HIGHEST,
    )
    row_count = local_blocks * BLOCK
    memory_grad = jnp.concatenate(
        [key_grad.reshape(row_count, D), value_grad.reshape(row_count, D)], axis=1
    ).astype(jnp.bfloat16)
    cross_memory_grad = jnp.dot(datastore.T, memory_grad, preferred_element_type=jnp.float32)
    value_bias_grad = jnp.sum(memory_grad[:, D:].astype(jnp.float32), axis=0)
    datastore_grad = jnp.dot(memory_grad, cross_memory.T, preferred_element_type=jnp.float32)
    returned_grad = lax.all_to_all(
        query_grad[None], "store", split_axis=2, concat_axis=0, tiled=True
    )
    per_pick = returned_grad.reshape(total_slots, D)[slot_ids].reshape(tok_count, TOPB, D)
    query_sum = jnp.sum(per_pick.astype(jnp.float32), axis=1).astype(jnp.bfloat16)
    cross_pre_grad = (query_sum.astype(jnp.float32) * QUERY_SCALE).astype(jnp.bfloat16)
    cross_query_grad = jnp.dot(first_low.T, cross_pre_grad, preferred_element_type=jnp.float32)
    first_total = second_resid + jnp.dot(
        cross_pre_grad, cross_query.T, preferred_element_type=jnp.float32
    )
    first_resid, first_gain, first_shift = first_back(first_total)
    self_branch_grad = first_resid.astype(jnp.bfloat16)
    self_output_grad = jnp.dot(attended.T, self_branch_grad, preferred_element_type=jnp.float32)
    self_attended_grad = (
        jnp.dot(self_branch_grad, self_output.T, preferred_element_type=jnp.float32)
        .astype(jnp.bfloat16)
        .reshape(tok_count, HEADS, HEAD_DIM)
    )
    soft_self = jnp.exp(self_scores() - self_lse[..., None])
    soft_dots = jnp.einsum(
        "qhd,khd->hqk", self_attended_grad, values_self, preferred_element_type=jnp.float32
    )
    self_score_grad = (
        soft_self * (soft_dots - jnp.sum(soft_self * soft_dots, axis=-1, keepdims=True))
    ).astype(jnp.bfloat16)
    query_self_grad = jnp.einsum(
        "hqk,khd->qhd", self_score_grad, keys_self, preferred_element_type=jnp.float32
    ).reshape(tok_count, D)
    key_self_grad = jnp.einsum(
        "hqk,qhd->khd", self_score_grad, queries, preferred_element_type=jnp.float32
    ).reshape(tok_count, D)
    value_self_grad = jnp.einsum(
        "hqk,qhd->khd", soft_low, self_attended_grad, preferred_element_type=jnp.float32
    ).reshape(tok_count, D)
    heads_grad = jnp.concatenate([query_self_grad, key_self_grad, value_self_grad], axis=1).astype(
        jnp.bfloat16
    )
    project_grad = jnp.concatenate(
        [
            (heads_grad[:, :D].astype(jnp.float32) * QUERY_SCALE).astype(jnp.bfloat16),
            heads_grad[:, D:],
        ],
        axis=1,
    )
    self_project_grad = jnp.dot(inputs.T, project_grad, preferred_element_type=jnp.float32)
    input_grad = first_resid + jnp.dot(
        project_grad, self_project.T, preferred_element_type=jnp.float32
    )
    biases_grad = jnp.stack(
        [
            jnp.sum(project_grad[:, :D].astype(jnp.float32), axis=0),
            jnp.sum(project_grad[:, 2 * D :].astype(jnp.float32), axis=0),
            jnp.sum(self_branch_grad.astype(jnp.float32), axis=0),
            jnp.sum(cross_pre_grad.astype(jnp.float32), axis=0),
            value_bias_grad,
            jnp.sum(cross_branch_grad.astype(jnp.float32), axis=0),
            jnp.sum(ffn_branch_grad.astype(jnp.float32), axis=0),
        ]
    )
    gain_grad = jnp.stack([first_gain, second_gain, final_gain])
    shift_grad = jnp.stack([first_shift, second_shift, final_shift])
    shared = (
        lax.psum_scatter(self_project_grad, "store", scatter_dimension=0, tiled=True),
        lax.psum_scatter(self_output_grad, "store", scatter_dimension=0, tiled=True),
        lax.psum_scatter(cross_query_grad, "store", scatter_dimension=0, tiled=True),
        lax.psum_scatter(cross_memory_grad, "store", scatter_dimension=0, tiled=True),
        lax.psum_scatter(cross_output_grad, "store", scatter_dimension=0, tiled=True),
        lax.psum_scatter(expand_weight_grad, "store", scatter_dimension=0, tiled=True),
        lax.psum_scatter(contract_weight_grad, "store", scatter_dimension=0, tiled=True),
        lax.psum_scatter(biases_grad, "store", scatter_dimension=1, tiled=True),
        lax.psum_scatter(expand_bias_grad, "store", scatter_dimension=0, tiled=True),
        lax.psum_scatter(gain_grad, "store", scatter_dimension=1, tiled=True),
        lax.psum_scatter(shift_grad, "store", scatter_dimension=1, tiled=True),
    )
    reduced = (
        lax.psum(shared[0].astype(jnp.bfloat16), "dp").astype(jnp.float32),
        lax.psum(shared[1].astype(jnp.bfloat16), "dp").astype(jnp.float32),
        lax.psum(shared[2].astype(jnp.bfloat16), "dp").astype(jnp.float32),
        lax.psum(shared[3].astype(jnp.bfloat16), "dp").astype(jnp.float32),
        lax.psum(shared[4].astype(jnp.bfloat16), "dp").astype(jnp.float32),
        lax.psum(shared[5].astype(jnp.bfloat16), "dp").astype(jnp.float32),
        lax.psum(shared[6].astype(jnp.bfloat16), "dp").astype(jnp.float32),
        lax.psum(shared[7].astype(jnp.bfloat16), "dp").astype(jnp.float32),
        lax.psum(shared[8].astype(jnp.bfloat16), "dp").astype(jnp.float32),
        lax.psum(shared[9].astype(jnp.bfloat16), "dp").astype(jnp.float32),
        lax.psum(shared[10].astype(jnp.bfloat16), "dp").astype(jnp.float32),
    )
    return (
        outputs,
        input_grad,
        datastore_grad,
        reduced[0],
        reduced[1],
        reduced[2],
        reduced[3],
        reduced[4],
        reduced[5],
        reduced[6],
        reduced[7],
        reduced[8],
        reduced[9],
        reduced[10],
    )


def solution(mesh):
    placed = (
        P(("dp", "store"), None),
        P(("dp", "store"), None),
        P(("dp", "store"), None),
        P(("dp", "store")),
        P(("dp", "store"), None),
        P(),
        P(),
        P(),
        P(),
        P(),
        P(),
        P(),
        P(),
        P(),
        P(),
        P(),
        P(("dp", "store"), None),
    )
    return jax.shard_map(
        local_tree if mesh.shape["store"] == 16 else local_slots,
        mesh=mesh,
        in_specs=placed,
        out_specs=(
            P(("dp", "store"), None),
            P(("dp", "store"), None),
            P(("dp", "store"), None),
            P("store", None),
            P("store", None),
            P("store", None),
            P("store", None),
            P("store", None),
            P("store", None),
            P("store", None),
            P(None, "store"),
            P("store"),
            P(None, "store"),
            P(None, "store"),
        ),
        check_vma=False,
    )
```

```python
import functools

import jax
import jax.numpy as jnp
from jax import lax
from jax.experimental import pallas as pl
from jax.experimental.pallas import tpu as pltpu
from jax.sharding import PartitionSpec as P

D = 768
HEADS = 12
HEAD_DIM = 64
TOPB = 8
BLOCK = 128
SLAB = 128
PAIRS = D // SLAB
UNIT = 384
WIDE = D + SLAB
RANK_ROWS = 16

EPSILON = 1e-05
MASKED = -1e30
QUERY_SCALE = 0.125
VMEM_LIMIT = 56 * 1024 * 1024
SMALL_LIMIT = 20 * 1024 * 1024
LONG = 30_000_000_000
MICROSECOND = 50_000_000
LOW = jnp.bfloat16
F32 = jnp.float32

_VMEM = pl.BlockSpec(memory_space=pltpu.VMEM)
_SMEM = pl.BlockSpec(memory_space=pltpu.SMEM)
_ANY = pl.BlockSpec(memory_space=pl.ANY)


def nn(a, b):
    return lax.dot_general(a, b, (((1,), (0,)), ((), ())), preferred_element_type=F32)


def nt(a, b):
    return lax.dot_general(a, b, (((1,), (1,)), ((), ())), preferred_element_type=F32)


def tn(a, b):
    return lax.dot_general(a, b, (((0,), (0,)), ((), ())), preferred_element_type=F32)


def three(v):
    high = v.astype(LOW)
    rest = v - high.astype(F32)
    mid = rest.astype(LOW)
    return high, mid, (rest - mid.astype(F32)).astype(LOW)


def lanes(shape):
    return lax.broadcasted_iota(jnp.int32, shape, len(shape) - 1)


def rows_of(shape):
    return lax.broadcasted_iota(jnp.int32, shape, len(shape) - 2)


def flag(condition):
    return jnp.where(condition, 1.0, 0.0)


def half_masks():
    first = flag(lanes((1, SLAB)) < HEAD_DIM)
    return first.astype(LOW), (1.0 - first).astype(LOW)


def two_heads(slab, first, second):
    return jnp.concatenate([slab * first, slab * second], axis=0)


def join_heads(stacked, count):
    left = lanes((count, SLAB)) < HEAD_DIM
    return jnp.where(left, stacked[:count], stacked[count:])


def norm_forward(residual, gain, shift):
    center = residual - jnp.mean(residual, axis=-1, keepdims=True)
    spread = jnp.mean(center * center, axis=-1, keepdims=True)
    scale = lax.rsqrt(spread + EPSILON)
    unit = center * scale
    return unit * gain + shift, unit, scale


def norm_backward(grad, unit, scale, gain):
    inner = grad * gain
    down = inner - jnp.mean(inner, axis=-1, keepdims=True)
    down = down - unit * jnp.mean(inner * unit, axis=-1, keepdims=True)
    return scale * down


def row_sum(v):
    return jnp.sum(v, axis=0, keepdims=True)


def call(
    kernel,
    outs,
    scratch=(),
    n_smem=0,
    far_in=(),
    far_out=(),
    earlier=(),
    aliases=None,
    flops=0,
    limit=VMEM_LIMIT,
):
    def run(*args):
        count = len(args)

        def body(*refs):
            kernel(*refs[:count], *refs[count + len(earlier) :])

        specs = [_ANY if i in far_in else _VMEM for i in range(n_smem, count)]
        return pl.pallas_call(
            body,
            out_shape=[jax.ShapeDtypeStruct(s, t) for s, t in outs],
            in_specs=[_SMEM] * n_smem + specs + [_ANY] * len(earlier),
            out_specs=[_ANY if i in far_out else _VMEM for i in range(len(outs))],
            scratch_shapes=list(scratch),
            input_output_aliases=aliases or {},
            compiler_params=pltpu.CompilerParams(vmem_limit_bytes=limit),
            cost_estimate=pl.CostEstimate(flops=flops, bytes_accessed=0, transcendentals=0),
        )(*args, *earlier)

    return run


def copies(pairs, sems):
    return [pltpu.make_async_copy(a, b, sems.at[i]) for i, (a, b) in enumerate(pairs)]


def after(v, *earlier):
    return call(
        lambda *refs: None,
        [(v.shape, v.dtype)],
        far_in=(0,),
        far_out=(0,),
        earlier=earlier,
        aliases={0: 0},
        limit=1024 * 1024,
    )(v)[0]


def start_all(items):
    for item in items:
        item.start()


def wait_all(items):
    for item in items:
        item.wait()


def plane_ranks(picks_ref, me, k, tokens):
    i = rows_of((RANK_ROWS, tokens))
    group, chip, block = i // 4, (i // 2) % 2, i % 2
    apart = jnp.where(group < 2, 2 * group + chip, 2 * chip + group - 2)
    local = jnp.where(group < 2, block, 2 + block)
    plane = (me // 4) ^ k
    number = plane * 16 + ((me % 4) ^ apart) * 4 + local
    member = jnp.zeros((RANK_ROWS, tokens), F32)
    for j in range(TOPB):
        member = member + flag(picks_ref[j : j + 1, :] == number)
    earlier = flag(rows_of((tokens, tokens)) < lanes((tokens, tokens)))
    rank = nn(member.astype(LOW), earlier.astype(LOW))
    return jnp.where(member > 0.5, rank, -1.0).astype(LOW)


def self_forward_kernel(
    lengths_ref,
    place_ref,
    x_ref,
    picks_ref,
    project_ref,
    output_ref,
    query_ref,
    bias_ref,
    gain_ref,
    shift_ref,
    heads_ref,
    soft_ref,
    attended_ref,
    unit_ref,
    scale_ref,
    first_ref,
    *rest,
):
    payload_refs, (project_scr, output_scr, query_scr, sems) = rest[:4], rest[4:]
    thirds = [slice(i * D, (i + 1) * D) for i in range(3)]
    fetch = copies(
        [(project_ref.at[:, at], project_scr.at[:, at]) for at in thirds]
        + [(output_ref, output_scr), (query_ref, query_scr)],
        sems,
    )
    start_all(fetch)
    tokens = x_ref.shape[0]
    bias = bias_ref[...].astype(F32)
    x = x_ref[...]
    for i, at in enumerate(thirds):
        fetch[i].wait()
        part = nn(x, project_scr[:, at])
        if i == 0:
            part = QUERY_SCALE * (part + bias[0:1])
        if i == 2:
            part = part + bias[1:2]
        heads_ref[:, at] = part.astype(LOW)
    place_row = lax.broadcasted_iota(jnp.int32, (2 * tokens, tokens), 0) % tokens
    place_col = lanes((2 * tokens, tokens))
    segment_row = jnp.zeros((2 * tokens, tokens), jnp.int32)
    segment_col = jnp.zeros((2 * tokens, tokens), jnp.int32)
    bound = 0
    for d in range(lengths_ref.shape[1]):
        bound = bound + lengths_ref[0, d]
        segment_row = segment_row + jnp.where(place_row >= bound, 1, 0)
        segment_col = segment_col + jnp.where(place_col >= bound, 1, 0)
    allowed = (segment_row == segment_col) & (place_row >= place_col)
    first, second = half_masks()
    for p in range(PAIRS):
        at = p * SLAB
        queries = two_heads(heads_ref[:, at : at + SLAB], first, second)
        scores = nt(queries, heads_ref[:, D + at : D + at + SLAB])
        scores = jnp.where(allowed, scores, MASKED)
        top = jnp.max(scores, axis=-1, keepdims=True)
        raised = jnp.exp(scores - top)
        soft = raised / jnp.sum(raised, axis=-1, keepdims=True)
        soft_ref[p] = soft
        mixed = nn(soft.astype(LOW), heads_ref[:, 2 * D + at : 2 * D + at + SLAB])
        attended_ref[:, at : at + SLAB] = join_heads(mixed, tokens).astype(LOW)
    fetch[3].wait()
    residual = x.astype(F32) + nn(attended_ref[...], output_scr[...]) + bias[2:3]
    normed, unit, scale = norm_forward(
        residual, gain_ref[0:1, :].astype(F32), shift_ref[0:1, :].astype(F32)
    )
    unit_ref[...] = unit
    scale_ref[...] = scale
    low = normed.astype(LOW)
    first_ref[...] = low
    fetch[4].wait()
    queries = (QUERY_SCALE * (nn(low, query_scr[...]) + bias[3:4])).astype(LOW)
    for k, out in enumerate(payload_refs):
        out[:tokens] = queries
        out[tokens:, tokens:] = jnp.zeros((RANK_ROWS, D - tokens), LOW)
        out[tokens:, :tokens] = plane_ranks(picks_ref, place_ref[0], k, tokens)


def memory_kernel(*refs):
    sets = (len(refs) - 2) // 6
    pieces, (weight_ref, bias_ref), outs = refs[: 2 * sets], refs[2 * sets : 2 * sets + 2], refs[2 * sets + 2 :]
    bias = bias_ref[4:5, :].astype(F32)
    lane = lanes((RANK_ROWS, SLAB))
    for s in range(sets):
        rows_ref, memory_ref, hidden_ref, side_ref = outs[4 * s : 4 * s + 4]
        for j in range(2):
            piece = pieces[2 * s + j]
            rows = piece[: 2 * BLOCK]
            rows_ref[2 * j * BLOCK : 2 * (j + 1) * BLOCK] = rows
            keys = nn(rows, weight_ref[:, :D]).astype(LOW)
            values = (nn(rows, weight_ref[:, D:]) + bias).astype(LOW)
            marks = piece[2 * BLOCK :, :SLAB]
            for l in range(2):
                at = 2 * j + l
                memory_ref[at, :, :D] = keys[l * BLOCK : (l + 1) * BLOCK]
                memory_ref[at, :, D:] = values[l * BLOCK : (l + 1) * BLOCK]
                hidden_ref[at] = (1.0 - marks[l : l + 1].astype(F32)) * MASKED
                wanted = flag((rows_of((RANK_ROWS, SLAB)) == l) & (lane == SLAB - 1))
                column = tn(marks, wanted.astype(LOW))
                place = lanes((BLOCK, SLAB))
                side = jnp.where(place == SLAB - 1, (1.0 - column) * MASKED, 0.0)
                side_ref[at] = jnp.where(place < 48, -1.0, side).astype(LOW)


def selection(ranks, capacity):
    parts = []
    wanted = rows_of((capacity, ranks.shape[1])).astype(F32)
    for b in range(ranks.shape[0]):
        parts.append(flag(ranks[b : b + 1, :] == wanted).astype(LOW))
    return jnp.concatenate(parts, axis=0)


def fill_slots(sel, rows, out_ref, k, capacity):
    got = nn(sel, rows).astype(LOW)
    for b in range(out_ref.shape[0]):
        out_ref[b, k * capacity : (k + 1) * capacity, :] = got[b * capacity : (b + 1) * capacity]


def around16(v, combine):
    for step in (16, 32, 64):
        v = combine(v, pltpu.roll(v, step, 1))
    return v


def lse_lanes(lse):
    high = lse.astype(LOW).astype(F32)
    rest = lse - high
    mid = rest.astype(LOW).astype(F32)
    low = rest - mid
    lane = lanes(lse.shape)
    packed = jnp.where(
        lane < 16, high, jnp.where(lane < 32, mid, jnp.where(lane < 48, low, 0.0))
    )
    return packed.astype(LOW)


def read_lse(packed):
    return around16(packed.astype(F32), jnp.add)


def head_spread(group):
    row = rows_of((SLAB, D))
    row = row % 16 if group else row
    return flag(row == lanes((SLAB, D)) // HEAD_DIM).astype(LOW)


def owner_forward_kernel(capacity, *refs):
    tokens_refs, memory_refs, hidden_refs = refs[0:4], refs[4:8], refs[8:12]
    far_slots_ref, payload_refs = refs[12], refs[13:17]
    out_scr, lse_scr, inv_scr, sel_scr, ranks_scr, slots_ref, memory_scr, sems, slots_sem = refs[17:]
    fetch = copies([(ref, memory_scr.at[s]) for s, ref in enumerate(memory_refs)], sems)
    start_all(fetch)
    sources = len(tokens_refs)
    blocks, rows = slots_ref.shape[:2]
    tokens = tokens_refs[0].shape[0] - RANK_ROWS
    first, second = half_masks()
    for k in range(sources):
        ranks_scr[...] = tokens_refs[k][tokens:, :tokens].astype(F32)
        sel = selection(ranks_scr[...], capacity)
        sel_scr[k] = sel
        fill_slots(sel, tokens_refs[k][:tokens], slots_ref, k, capacity)
    (keep,) = copies([(slots_ref, far_slots_ref)], slots_sem)
    keep.start()
    ones = jnp.ones((BLOCK, SLAB), LOW)
    lane_of = lanes((rows, SLAB))
    for s in range(4):
        fetch[s].wait()

        def one_block(l, carry, s=s):
            i = 4 * s + l
            hidden = hidden_refs[s][l]
            tops = jnp.zeros((rows, SLAB), F32)
            totals = jnp.ones((rows, SLAB), F32)
            base = (i % 8) * 16
            slabs = [slice(p * SLAB, (p + 1) * SLAB) for p in range(PAIRS)]
            scores = [
                nt(two_heads(slots_ref[i, :, at], first, second), memory_scr[s, l, :, at])
                + hidden
                for at in slabs
            ]
            highest = [jnp.max(v, axis=-1, keepdims=True) for v in scores]
            raised = [jnp.exp(v - top).astype(LOW) for v, top in zip(scores, highest)]
            mixed = [
                nn(v, jnp.concatenate([memory_scr[s, l, :, D + at.start : D + at.stop], ones], axis=1))
                for v, at in zip(raised, slabs)
            ]
            for p, at in enumerate(slabs):
                out_scr[i, :, at] = join_heads(mixed[p][:, :SLAB], rows)
                for half in range(2):
                    here = slice(half * rows, (half + 1) * rows)
                    mine = lane_of == base + 2 * p + half
                    tops = jnp.where(mine, highest[p][here], tops)
                    totals = jnp.where(mine, mixed[p][here, SLAB:], totals)
            own = flag((lane_of >= base) & (lane_of < base + HEADS))
            lse_scr[i] = tops + jnp.log(totals)
            inv_scr[i] = own / totals
            return carry

        lax.fori_loop(0, 4, one_block, 0)
    group = 8 * capacity
    own_low = flag(
        rows_of((group, SLAB)) // capacity == lanes((group, SLAB)) // 16
    ).astype(LOW)
    spread = head_spread(True)
    for k in range(sources):
        here = slice(k * capacity, (k + 1) * capacity)

        def stacked(ref, g, here=here):
            return jnp.concatenate([ref[8 * g + b, here, :] for b in range(8)], axis=0)

        by_token, members, sels = [], [], []
        for g in range(2):
            sel = sel_scr[k, g * group : (g + 1) * group, :]
            value = sum(tn(sel, part) for part in three(stacked(lse_scr, g)))
            member = tn(sel, own_low)
            by_token.append(jnp.where(member > 0.5, value, MASKED))
            members.append(member)
            sels.append(sel)
        top = around16(jnp.maximum(*by_token), jnp.maximum)
        weights = [m * jnp.exp(v - top) for m, v in zip(members, by_token)]
        total = around16(weights[0] + weights[1], jnp.add)
        some = total > 0.5
        safe = jnp.where(some, total, 1.0)
        payload_refs[k][:, D:] = lse_lanes(jnp.where(some, top + jnp.log(safe), MASKED))
        partial = jnp.zeros((tokens, D), F32)
        for g in range(2):
            share = nn(sels[g], (weights[g] / safe).astype(LOW)) * stacked(inv_scr, g)
            value = stacked(out_scr, g) * nn(share.astype(LOW), spread)
            partial = partial + tn(sels[g], value.astype(LOW))
        payload_refs[k][:, :D] = partial.astype(LOW)
    keep.wait()


def owner_backward_kernel(capacity, *refs):
    tokens_refs, grad_refs, memory_refs, side_refs = refs[0:4], refs[4:8], refs[8:12], refs[12:16]
    far_slots_ref = refs[16]
    far_grad_refs, payload_refs, bias_ref = refs[17:21], refs[21:25], refs[25]
    got_scr, query_scr, sel_scr, ranks_scr, slots_ref, memory_scr, grad_scr, sems, out_sems = refs[26:]
    fetch = copies(
        [(far_slots_ref, slots_ref)] + [(ref, memory_scr.at[s]) for s, ref in enumerate(memory_refs)],
        sems,
    )
    start_all(fetch)
    keep = copies([(grad_scr.at[s], ref) for s, ref in enumerate(far_grad_refs)], out_sems)
    sources = len(tokens_refs)
    blocks, rows = slots_ref.shape[:2]
    tokens = grad_refs[0].shape[0]
    first, second = half_masks()
    for k in range(sources):
        ranks_scr[...] = tokens_refs[k][tokens:, :tokens].astype(F32)
        sel = selection(ranks_scr[...], capacity)
        sel_scr[k] = sel
        fill_slots(sel, grad_refs[k][...], got_scr, k, capacity)
    lane = lanes((1, SLAB))
    last = flag(lane == SLAB - 1).astype(LOW)
    value_side = jnp.broadcast_to(
        -flag((lane >= 48) & (lane < 96)).astype(LOW), (BLOCK, SLAB)
    )

    def picked(head, base):
        inside = (lane >= base) & (lane < base + 48)
        return flag(inside & (lane % 16 == head)).astype(LOW)

    fetch[0].wait()
    for s in range(4):
        fetch[1 + s].wait()

        def one_block(l, carry, s=s):
            i = 4 * s + l
            side = got_scr[i, :, D:]
            key_side = side_refs[s][l]
            slabs = [slice(p * SLAB, (p + 1) * SLAB) for p in range(PAIRS)]
            keys = [memory_scr[s, l, :, at] for at in slabs]
            queries = [two_heads(slots_ref[i, :, at], first, second) for at in slabs]
            grads = [two_heads(got_scr[i, :, at], first, second) for at in slabs]
            scores, dots = [], []
            for p in range(PAIRS):
                lse_side = jnp.concatenate(
                    [side * picked(2 * p + h, 0) + last for h in range(2)], axis=0
                )
                scores.append(
                    nt(
                        jnp.concatenate([keys[p], key_side], axis=1),
                        jnp.concatenate([queries[p], lse_side], axis=1),
                    )
                )
            for p, at in enumerate(slabs):
                delta_side = jnp.concatenate(
                    [side * picked(2 * p + h, 48) for h in range(2)], axis=0
                )
                values = memory_scr[s, l, :, D + at.start : D + at.stop]
                dots.append(
                    nt(
                        jnp.concatenate([values, value_side], axis=1),
                        jnp.concatenate([grads[p], delta_side], axis=1),
                    )
                )
            softs = [jnp.exp(v) for v in scores]
            score_grads = [(soft * v).astype(LOW) for soft, v in zip(softs, dots)]
            out = grad_scr.at[s]
            for p, at in enumerate(slabs):
                query_scr[i, :, at] = join_heads(tn(score_grads[p], keys[p]), rows).astype(LOW)
            for p, at in enumerate(slabs):
                out[l, :, at] = nn(score_grads[p], queries[p]).astype(LOW)
            for p, at in enumerate(slabs):
                out[l, :, D + at.start : D + at.stop] = nn(softs[p].astype(LOW), grads[p]).astype(
                    LOW
                )
            return carry

        lax.fori_loop(0, 4, one_block, 0)
        keep[s].start()
    for k in range(sources):
        here = slice(k * capacity, (k + 1) * capacity)
        value = jnp.concatenate([query_scr[b, here, :] for b in range(blocks)], axis=0)
        payload_refs[k][...] = tn(sel_scr[k], value).astype(LOW)
    total = jnp.zeros((1, D), F32)
    for s in range(4):
        for l in range(4):
            total = total + row_sum(grad_scr[s, l, :, D:].astype(F32))
    bias_ref[...] = jnp.broadcast_to(total, (8, D))
    wait_all(keep)


def memory_backward_kernel(count, place_ref, weight_ref, *refs):
    far_grads, far_rows = refs[:4], refs[4:8]
    outs, far_outs = refs[8:14], refs[14:16]
    kept_ref, sent_ref, grad_scr, rows_scr, sum_scr, sems, out_sems = refs[16:]
    fetch = [
        copies([(far_grads[s], grad_scr.at[s]), (far_rows[s], rows_scr.at[s])], sems.at[s])
        for s in range(4)
    ]
    for items in fetch:
        start_all(items)
    me, core = place_ref[0], place_ref[1]
    weight = weight_ref[...].T
    near_a0, near_a1, far_a, near_b0, near_b1, far_b = outs
    groups = ((near_a0, near_a1), (far_a,), (near_b0, near_b1), (far_b,))
    for s in range(4):
        wait_all(fetch[s])
        value = nn(grad_scr[s], weight).astype(LOW)
        size = value.shape[0] // len(groups[s])
        for i, out in enumerate(groups[s]):
            out[...] = value[i * size : (i + 1) * size]
        rows = rows_scr[s].T
        for h in range(2):
            part = nn(rows, grad_scr[s, :, h * D : (h + 1) * D])
            sum_scr[h] = part if s == 0 else sum_scr[h] + part
    block = D // count
    for h in range(2):

        def store(out, h=h):
            total = sum_scr[h].astype(LOW)
            for k in range(count):
                for u in range(D // UNIT):
                    out[me ^ k, u * block : (u + 1) * block, :] = total[
                        k * block : (k + 1) * block, u * UNIT : (u + 1) * UNIT
                    ]

        pl.when(core == h)(functools.partial(store, kept_ref))
        pl.when(core != h)(functools.partial(store, sent_ref))
    size = 2 * block
    keep = copies(
        [(near, far.at[:, :size, :]) for near, far in zip((kept_ref, sent_ref), far_outs)],
        out_sems,
    )
    start_all(keep)
    wait_all(keep)


def middle_kernel(
    p0_ref,
    p1_ref,
    p2_ref,
    p3_ref,
    first_ref,
    cotangent_ref,
    output_ref,
    expand_ref,
    contract_ref,
    bias_ref,
    expand_bias_ref,
    gain_ref,
    shift_ref,
    out_ref,
    merged_ref,
    second_ref,
    active_ref,
    branch_grad_ref,
    expanded_grad_ref,
    cross_grad_ref,
    resid_ref,
    payload_ref,
    small_ref,
    wide_ref,
    expanded_scr,
    output_scr,
    expand_scr,
    contract_scr,
    sems,
):
    fetch = copies(
        [(output_ref, output_scr), (expand_ref, expand_scr), (contract_ref, contract_scr)], sems
    )
    start_all(fetch)
    bias = bias_ref[...].astype(F32)
    gain = gain_ref[...].astype(F32)
    shift = shift_ref[...].astype(F32)
    parts = [p0_ref, p1_ref, p2_ref, p3_ref]
    lses = [read_lse(part[:, D:]) for part in parts]
    top = functools.reduce(jnp.maximum, lses)
    weights = [jnp.exp(lse - top) for lse in lses]
    total = functools.reduce(jnp.add, weights)
    overall = top + jnp.log(total)
    spread = head_spread(False)
    merged = jnp.zeros(first_ref.shape, F32)
    for part, weight in zip(parts, weights):
        share = weight / total
        high = share.astype(LOW)
        rest = (share - high.astype(F32)).astype(LOW)
        merged = merged + (nn(high, spread) + nn(rest, spread)) * part[:, :D].astype(F32)
    merged_low = merged.astype(LOW)
    merged_ref[...] = merged_low
    fetch[0].wait()
    residual = first_ref[...].astype(F32) + nn(merged_low, output_scr[...]) + bias[5:6]
    second, unit_second, scale_second = norm_forward(residual, gain[1:2], shift[1:2])
    second_low = second.astype(LOW)
    second_ref[...] = second_low
    hidden = contract_scr.shape[0]
    fetch[1].wait()
    for c in range(hidden // D):
        at = slice(c * D, (c + 1) * D)
        expanded = nn(second_low, expand_scr[:, at]) + expand_bias_ref[:, at].astype(F32)
        bell = 0.5 * (1.0 + lax.erf(expanded * 0.7071067811865476))
        active_ref[:, at] = (expanded * bell).astype(LOW)
        slope = bell + expanded * 0.3989422804014327 * jnp.exp(-0.5 * expanded * expanded)
        expanded_scr[:, at] = slope
    fetch[2].wait()
    residual = second_low.astype(F32) + nn(active_ref[...], contract_scr[...]) + bias[6:7]
    final, unit_final, scale_final = norm_forward(residual, gain[2:3], shift[2:3])
    out_ref[...] = final.astype(LOW)
    cotangent = cotangent_ref[...].astype(F32)
    final_resid = norm_backward(cotangent, unit_final, scale_final, gain[2:3])
    branch_grad = final_resid.astype(LOW)
    branch_grad_ref[...] = branch_grad
    small_ref[0:1, :] = row_sum(branch_grad.astype(F32))
    small_ref[1:2, :] = row_sum(cotangent * unit_final)
    small_ref[2:3, :] = row_sum(cotangent)
    total_grad = final_resid
    for c in range(hidden // D):
        at = slice(c * D, (c + 1) * D)
        active_grad = nt(branch_grad, contract_scr[at, :])
        expanded_grad = (active_grad * expanded_scr[:, at]).astype(LOW)
        expanded_grad_ref[:, at] = expanded_grad
        wide_ref[:, at] = row_sum(expanded_grad.astype(F32))
        total_grad = total_grad + nt(expanded_grad, expand_scr[:, at])
    small_ref[4:5, :] = row_sum(total_grad * unit_second)
    small_ref[5:6, :] = row_sum(total_grad)
    second_resid = norm_backward(total_grad, unit_second, scale_second, gain[1:2])
    resid_ref[...] = second_resid
    cross_grad = second_resid.astype(LOW)
    cross_grad_ref[...] = cross_grad
    small_ref[3:4, :] = row_sum(cross_grad.astype(F32))
    small_ref[6:8, :] = jnp.zeros((2, D), F32)
    attended_grad = nt(cross_grad, output_scr[...]).astype(LOW)
    payload_ref[:, :D] = attended_grad
    product = attended_grad.astype(F32) * merged
    gather = flag(lanes((D, SLAB)) % 16 == rows_of((D, SLAB)) // HEAD_DIM).astype(LOW)
    high, mid, low = three(product)
    delta = nn(high, gather) + nn(mid, gather) + nn(low, gather)
    lane = lanes(overall.shape)
    packed = jnp.zeros(overall.shape, F32)
    for value, base in ((overall, 0), (delta, 48)):
        for i, piece in enumerate(three(value)):
            inside = (lane >= base + 16 * i) & (lane < base + 16 * i + HEADS)
            packed = jnp.where(inside, piece.astype(F32), packed)
    payload_ref[:, D:] = packed.astype(LOW)


def self_backward_kernel(
    d0_ref,
    d1_ref,
    d2_ref,
    d3_ref,
    resid_ref,
    unit_ref,
    scale_ref,
    heads_ref,
    soft_ref,
    query_ref,
    output_ref,
    project_ref,
    gain_ref,
    pre_grad_ref,
    branch_grad_ref,
    project_grad_ref,
    input_grad_ref,
    small_ref,
    attended_scr,
    query_scr,
    output_scr,
    heads_scr,
    soft_scr,
    project_scr,
    sems,
):
    fetch = copies(
        [
            (query_ref, query_scr),
            (output_ref, output_scr),
            (heads_ref, heads_scr),
            (soft_ref, soft_scr),
            (project_ref, project_scr),
        ],
        sems,
    )
    start_all(fetch)
    tokens = resid_ref.shape[0]
    query_sum = functools.reduce(
        jnp.add, [d[...].astype(F32) for d in (d0_ref, d1_ref, d2_ref, d3_ref)]
    ).astype(LOW)
    pre_grad = (query_sum.astype(F32) * QUERY_SCALE).astype(LOW)
    pre_grad_ref[...] = pre_grad
    fetch[0].wait()
    total = resid_ref[...] + nt(pre_grad, query_scr[...])
    unit = unit_ref[...]
    first_resid = norm_backward(total, unit, scale_ref[...], gain_ref[0:1, :].astype(F32))
    branch_grad = first_resid.astype(LOW)
    branch_grad_ref[...] = branch_grad
    fetch[1].wait()
    attended_scr[...] = nt(branch_grad, output_scr[...]).astype(LOW)
    fetch[2].wait()
    fetch[3].wait()
    first, second = half_masks()
    for p in range(PAIRS):
        at = p * SLAB
        grads = two_heads(attended_scr[:, at : at + SLAB], first, second)
        queries = two_heads(heads_scr[:, at : at + SLAB], first, second)
        keys = heads_scr[:, D + at : D + at + SLAB]
        dots = nt(grads, heads_scr[:, 2 * D + at : 2 * D + at + SLAB])
        soft = soft_scr[p]
        score_grad = (soft * (dots - jnp.sum(soft * dots, axis=-1, keepdims=True))).astype(LOW)
        query_grad = join_heads(nn(score_grad, keys), tokens).astype(LOW)
        project_grad_ref[:, at : at + SLAB] = (query_grad.astype(F32) * QUERY_SCALE).astype(LOW)
        project_grad_ref[:, D + at : D + at + SLAB] = tn(score_grad, queries).astype(LOW)
        project_grad_ref[:, 2 * D + at : 2 * D + at + SLAB] = tn(soft.astype(LOW), grads).astype(
            LOW
        )
    fetch[4].wait()
    input_grad_ref[...] = first_resid + nt(project_grad_ref[...], project_scr[...])
    small_ref[0:1, :] = row_sum(project_grad_ref[:, :D].astype(F32))
    small_ref[1:2, :] = row_sum(project_grad_ref[:, 2 * D :].astype(F32))
    small_ref[2:3, :] = row_sum(branch_grad.astype(F32))
    small_ref[3:4, :] = row_sum(pre_grad.astype(F32))
    small_ref[4:5, :] = row_sum(total * unit)
    small_ref[5:6, :] = row_sum(total)
    small_ref[6:8, :] = jnp.zeros((2, D), F32)


def weight_grad_kernel(plan, count, packed, n_args, place_ref, *refs):
    far_refs, (kept_ref, sent_ref, sems) = refs[-5:-3], refs[-3:]
    me, core = place_ref[0], place_ref[1]
    at_ref = 0
    base = plan[0][3]
    going = []

    def send(at, size):
        for near, far in zip((kept_ref, sent_ref), far_refs):
            item = pltpu.make_async_copy(
                near.at[:, pl.ds(at - base, size), :], far.at[:, pl.ds(at, size), :], sems.at[len(going)]
            )
            item.start()
            going.append(item)

    for number, rows, columns, at in plan:
        pairs = [refs[at_ref + 2 * i : at_ref + 2 * i + 2] for i in range(number)]
        at_ref += 2 * number
        block = rows // count
        half = columns // 2
        for m in range(rows // D):
            xs = [x_ref[:, m * D : (m + 1) * D].T for x_ref, _ in pairs]
            for c in range(0, half, D):
                wide = min(D, half - c)
                for mine, out in ((core, kept_ref), (1 - core, sent_ref)):
                    start = pl.multiple_of(mine * half + c, SLAB)
                    part = sum(
                        nn(x, g_ref[:, pl.ds(start, wide)]) for x, (_, g_ref) in zip(xs, pairs)
                    ).astype(LOW)
                    for u in range(wide // UNIT):
                        low = at - base + (c // UNIT + u) * block
                        for k in range(D // block):
                            to = me ^ (m * (D // block) + k)
                            out[to, low : low + block, :] = part[
                                k * block : (k + 1) * block, u * UNIT : (u + 1) * UNIT
                            ]
        send(at, half // UNIT * block)
    if packed is not None:
        small_ref = refs[at_ref]
        for r in range(count):
            low = packed - base
            kept_ref[me ^ r, low : low + RANK_ROWS, :] = small_ref[r, core]
            sent_ref[me ^ r, low : low + RANK_ROWS, :] = small_ref[r, 1 - core]
        send(packed, RANK_ROWS)
    wait_all(going)


def total_of(*refs):
    return functools.reduce(jnp.add, [ref[...].astype(F32) for ref in refs])


def split_kernel(x, kept_ref, come_ref, *refs):
    far = () if x else refs[:2]
    outs, refs = refs[len(far) : 2 * len(far) + 2 if far else 2], refs[2 * len(far) + 2 if far else 2 :]
    number = 3 if far else 2
    ins, results, in_sems, out_sems = refs[: 2 * number], refs[2 * number : -2], refs[-2], refs[-1]
    half = kept_ref.shape[3] // 2
    fetch, keep = [], []
    for z in range(4):
        pairs = []
        for i, ref in enumerate((kept_ref, come_ref)):
            pairs.append((ref.at[z, :, x, :half], ins[i].at[z]))
            pairs.append((ref.at[z, x, :, half:], ins[number + i].at[z]))
        for i, ref in enumerate(far):
            pairs.append((ref.at[z], ins[number * i + 2].at[z]))
        fetch.append(copies(pairs, in_sems.at[z]))
        start_all(fetch[z])
    for z in range(4):
        wait_all(fetch[z])
        pairs = []
        for g in range(2):
            total = total_of(*[ref.at[z] for ref in ins[number * g : number * (g + 1)]]).astype(LOW)
            if far:
                for i in range(2):
                    results[2 * g + i][z] = total[i]
                    pairs.append((results[2 * g + i].at[z], outs[2 * g + i].at[z]))
            else:
                results[g][z] = total
                pairs.append((results[g].at[z], outs[g].at[z]))
        keep.append(copies(pairs, out_sems.at[z]))
        start_all(keep[z])
    for items in keep:
        wait_all(items)


def join_kernel(a_keep, a_come, b_keep, b_come, *outs):
    rows = a_keep.shape[1]
    a = total_of(a_keep, a_come).astype(LOW)
    b = total_of(b_keep, b_come).astype(LOW)
    for z in range(4):
        out = outs[z] if len(outs) == 4 else outs[z // 2].at[z % 2]
        out[:rows] = a[z]
        out[rows:] = b[z]


def pair_kernel(keep, come, out_keep, out_send):
    total = total_of(keep, come).astype(LOW)
    out_keep[...] = total[0]
    out_send[...] = total[1]


def sum_kernel(*refs):
    refs[-1][...] = total_of(*refs[:-1]).astype(LOW)


def spread_kernel(plan, count, packed, place_ref, own_ref, other_ref, *outs):
    core = place_ref[1]
    for (rows, columns, at), out in zip(plan, outs):
        block = rows // count
        half = columns // 2
        for c in range(half // UNIT):
            low = at + c * block
            for value, mine in ((own_ref, core), (other_ref, 1 - core)):
                start = pl.multiple_of(mine * half + c * UNIT, SLAB)
                out[:, pl.ds(start, UNIT)] = value[low : low + block].astype(F32)
    if packed is not None:
        outs[-1][core] = own_ref[packed : packed + RANK_ROWS].astype(F32)
        outs[-1][1 - core] = other_ref[packed : packed + RANK_ROWS].astype(F32)


def swap(v, bits):
    count = lax.axis_size("store")
    return lax.ppermute(v, "store", [(i, i ^ bits) for i in range(count)])


def swap_core(v):
    return lax.ppermute(v, "dp", [(0, 1), (1, 0)])


class WeightSums:
    def __init__(self, place, count, rows):
        self.place, self.count, self.rows = place, count, rows
        self.plan, self.packed, self.at = [], None, 0
        self.buffers = ()

    def add(self, products, small=None, earlier=(), flops=0):
        plan, base, packed = [], self.at, None
        for pairs in products:
            rows, columns = pairs[0][0].shape[1], pairs[0][1].shape[1]
            plan.append((len(pairs), rows, columns, self.at))
            self.plan.append((rows, columns, self.at))
            self.at += rows // self.count * (columns // 2 // UNIT)
        args = [v for pairs in products for pair in pairs for v in pair]
        if small is not None:
            packed = self.packed = self.at
            self.at += RANK_ROWS
            args.append(small)
        n_args = 1 + len(args)
        shape = (self.count, self.rows, UNIT)
        near = (self.count, self.at - base, UNIT)
        sends = 2 * (len(products) + (small is not None))

        def kernel(*refs):
            refs = refs[:n_args] + refs[n_args + len(self.buffers) :]
            weight_grad_kernel(tuple(plan), self.count, packed, n_args, *refs)

        self.buffers = call(
            kernel,
            [(shape, LOW), (shape, LOW)],
            scratch=[
                pltpu.VMEM(near, LOW),
                pltpu.VMEM(near, LOW),
                pltpu.SemaphoreType.DMA((sends,)),
            ],
            n_smem=1,
            far_in=(n_args, n_args + 1),
            far_out=(0, 1),
            aliases={n_args + i: i for i in range(len(self.buffers))},
            earlier=earlier,
            flops=flops,
        )(self.place, *args, *self.buffers)
        return self.buffers

    def split(self, x, far=(), earlier=()):
        half = (4, 2, self.rows // 2, UNIT)
        outs = [half[:1] + half[2:]] * 4 if far else [half] * 2
        number = 3 if far else 2
        args = [v.reshape(4, 2, 2, self.rows, UNIT) for v in (self.kept, self.come)] + list(far)
        return call(
            functools.partial(split_kernel, x),
            [(shape, LOW) for shape in outs],
            scratch=[pltpu.VMEM(half, LOW)] * (2 * number)
            + [pltpu.VMEM(shape, LOW) for shape in outs]
            + [pltpu.SemaphoreType.DMA((4, 2 * number)), pltpu.SemaphoreType.DMA((4, len(outs)))],
            far_in=range(len(args)),
            far_out=range(len(outs)),
            earlier=earlier,
            limit=SMALL_LIMIT,
        )(*args)

    def start(self, *earlier):
        self.kept, sent = self.buffers
        self.come = swap_core(after(sent, *earlier) if earlier else sent)
        self.sent = self.split(1)
        return self.sent

    def first(self, *earlier):
        come = (swap(self.sent[0], 1), swap(self.sent[1], 2))
        a_keep, a_send, b_keep, b_send = self.split(0, come, earlier)
        self.kept, self.sent = (a_keep, b_keep), (a_send, b_send)
        return self.sent

    def second(self, outs, *earlier):
        come = (swap(self.sent[0], 2), swap(self.sent[1], 1))
        shape = (self.rows, UNIT) if outs == 4 else (2, self.rows, UNIT)
        self.w = call(join_kernel, [(shape, LOW)] * outs, earlier=earlier)(
            self.kept[0], come[0], self.kept[1], come[1]
        )
        return self.w

    def third(self, *earlier):
        come = [swap(self.w[k], 4 * k) for k in (1, 2, 3)]
        (self.own,) = call(sum_kernel, [(come[0].shape, LOW)], earlier=earlier)(self.w[0], *come)
        return self.own

    def third_far(self, *earlier):
        shape = self.w[0].shape[1:]
        self.w = call(pair_kernel, [(shape, LOW)] * 2, earlier=earlier)(
            self.w[0], swap(self.w[1], 8)
        )
        return self.w

    def third_near(self, *earlier):
        (self.own,) = call(sum_kernel, [(self.w[0].shape, LOW)], earlier=earlier)(
            self.w[0], swap(self.w[1], 4)
        )
        return self.own

    def finish(self):
        other = swap_core(self.own)
        shapes = [((rows // self.count, columns), F32) for rows, columns, _ in self.plan]
        if self.packed is not None:
            shapes.append(((2, RANK_ROWS, UNIT), F32))
        return call(
            functools.partial(spread_kernel, tuple(self.plan), self.count, self.packed),
            shapes,
            n_smem=1,
        )(self.place, self.own, other)


def local_tree(
    inputs,
    doc_lengths,
    datastore,
    kept_mask,
    retrieved,
    self_project,
    self_output,
    cross_query,
    cross_memory,
    cross_output,
    expand_weight,
    contract_weight,
    biases,
    expand_bias,
    norm_gain,
    norm_shift,
    cotangent,
):
    tokens = inputs.shape[0]
    count = lax.axis_size("store")
    local_blocks = datastore.shape[0] // BLOCK
    all_blocks = local_blocks * count
    capacity = 2 * tokens * TOPB // all_blocks
    plane_blocks = 4 * local_blocks
    rows_in = 4 * capacity
    hidden = expand_weight.shape[1]
    me = lax.axis_index("store").astype(jnp.int32)
    core = lax.axis_index("dp").astype(jnp.int32)
    place = jnp.stack([me, core])

    marks = kept_mask.reshape(2, 2, BLOCK).astype(LOW)
    marks = jnp.pad(marks, ((0, 0), (0, RANK_ROWS - 2), (0, D - BLOCK)))
    halves = datastore.reshape(2, 2 * BLOCK, D)
    a0, b0 = (jnp.concatenate([halves[h], marks[h]]) for h in range(2))
    a1, b1 = swap(a0, 1), swap(b0, 2)
    heads_all, soft_self, attended, unit_first, scale_first, first_low, *queries = call(
        self_forward_kernel,
        [
            ((tokens, 3 * D), LOW),
            ((PAIRS, 2 * tokens, tokens), F32),
            ((tokens, D), LOW),
            ((tokens, D), F32),
            ((tokens, 1), F32),
            ((tokens, D), LOW),
        ]
        + [((tokens + RANK_ROWS, D), LOW)] * 4,
        scratch=[
            pltpu.VMEM((D, 3 * D), LOW),
            pltpu.VMEM((D, D), LOW),
            pltpu.VMEM((D, D), LOW),
            pltpu.SemaphoreType.DMA((5,)),
        ],
        n_smem=2,
        far_in=(4, 5, 6),
        flops=8 * MICROSECOND,
    )(
        doc_lengths,
        place,
        inputs,
        retrieved.T,
        self_project,
        self_output,
        cross_query,
        biases,
        norm_gain,
        norm_shift,
    )
    ay = swap(after(jnp.stack([a0, a1]), first_low), 2)
    bx = swap(after(jnp.stack([b0, b1]), first_low), 1)
    queries = [queries[0]] + [swap(queries[k], 4 * k) for k in (1, 2, 3)]

    one_set = [
        ((4 * BLOCK, D), LOW),
        ((4, BLOCK, 2 * D), LOW),
        ((4, 1, BLOCK), F32),
        ((4, BLOCK, SLAB), LOW),
    ]
    memory_call = call(
        memory_kernel,
        one_set * 2,
    )
    near = memory_call(a0, a1, b0, b1, cross_memory, biases)
    far = memory_call(ay[0], ay[1], bx[0], bx[1], cross_memory, biases)
    sets = [near[:4], far[:4], near[4:], far[4:]]
    stored, memory, hidden_rows, key_side = zip(*sets)

    slots, *payloads = call(
        functools.partial(owner_forward_kernel, capacity),
        [((plane_blocks, rows_in, D), LOW)] + [((tokens, WIDE), LOW)] * 4,
        scratch=[
            pltpu.VMEM((plane_blocks, rows_in, D), F32),
            pltpu.VMEM((plane_blocks, rows_in, SLAB), F32),
            pltpu.VMEM((plane_blocks, rows_in, SLAB), F32),
            pltpu.VMEM((4, plane_blocks * capacity, tokens), LOW),
            pltpu.VMEM((RANK_ROWS, tokens), F32),
            pltpu.VMEM((plane_blocks, rows_in, D), LOW),
            pltpu.VMEM((4, 4, BLOCK, 2 * D), LOW),
            pltpu.SemaphoreType.DMA((4,)),
            pltpu.SemaphoreType.DMA((1,)),
        ],
        far_in=(4, 5, 6, 7),
        far_out=(0,),
        flops=20 * MICROSECOND,
    )(*queries, *memory, *hidden_rows)
    parts = [payloads[0]] + [swap(payloads[k], 4 * k) for k in (1, 2, 3)]

    (
        outputs,
        merged_low,
        second_low,
        active_low,
        branch_grad,
        expanded_grad,
        cross_grad,
        second_resid,
        payload,
        small_middle,
        wide_bias,
    ) = call(
        middle_kernel,
        [
            ((tokens, D), LOW),
            ((tokens, D), LOW),
            ((tokens, D), LOW),
            ((tokens, hidden), LOW),
            ((tokens, D), LOW),
            ((tokens, hidden), LOW),
            ((tokens, D), LOW),
            ((tokens, D), F32),
            ((tokens, WIDE), LOW),
            ((8, D), F32),
            ((1, hidden), F32),
        ],
        scratch=[
            pltpu.VMEM((tokens, hidden), F32),
            pltpu.VMEM((D, D), LOW),
            pltpu.VMEM((D, hidden), LOW),
            pltpu.VMEM((hidden, D), LOW),
            pltpu.SemaphoreType.DMA((3,)),
        ],
        far_in=(6, 7, 8),
        flops=12 * MICROSECOND,
    )(
        *parts,
        first_low,
        cotangent,
        cross_output,
        expand_weight,
        contract_weight,
        biases,
        expand_bias.reshape(1, hidden),
        norm_gain,
        norm_shift,
    )
    grads = [payload] + [swap(payload, 4 * k) for k in (1, 2, 3)]

    early = WeightSums(place, count, 432)
    early.add(
        [[(active_low, branch_grad)], [(merged_low, cross_grad)], [(second_low, expanded_grad)]],
        flops=8 * MICROSECOND,
    )
    early_start = early.start()

    out = call(
        functools.partial(owner_backward_kernel, capacity),
        [((4, BLOCK, 2 * D), LOW)] * 4 + [((tokens, D), LOW)] * 4 + [((8, D), F32)],
        scratch=[
            pltpu.VMEM((plane_blocks, rows_in, WIDE), LOW),
            pltpu.VMEM((plane_blocks, rows_in, D), LOW),
            pltpu.VMEM((4, plane_blocks * capacity, tokens), LOW),
            pltpu.VMEM((RANK_ROWS, tokens), F32),
            pltpu.VMEM((plane_blocks, rows_in, D), LOW),
            pltpu.VMEM((4, 4, BLOCK, 2 * D), LOW),
            pltpu.VMEM((4, 4, BLOCK, 2 * D), LOW),
            pltpu.SemaphoreType.DMA((5,)),
            pltpu.SemaphoreType.DMA((4,)),
        ],
        far_in=(8, 9, 10, 11, 16),
        far_out=(0, 1, 2, 3),
        earlier=early_start,
        flops=LONG,
    )(*queries, *grads, *memory, *key_side, slots)
    memory_grads, query_grads, value_bias_grad = out[:4], out[4:8], out[8]
    parts = [query_grads[0]] + [swap(query_grads[k], 4 * k) for k in (1, 2, 3)]

    early_first = early.first(memory_grads[0])
    late = WeightSums(place, count, 352)
    near_a0, near_a1, far_a, near_b0, near_b1, far_b, *late.buffers = call(
        functools.partial(memory_backward_kernel, count),
        [((2 * BLOCK, D), LOW), ((2 * BLOCK, D), LOW), ((4 * BLOCK, D), LOW)] * 2
        + [((count, late.rows, UNIT), LOW)] * 2,
        scratch=[
            pltpu.VMEM((count, 2 * D // count, UNIT), LOW),
            pltpu.VMEM((count, 2 * D // count, UNIT), LOW),
            pltpu.VMEM((4, 4 * BLOCK, 2 * D), LOW),
            pltpu.VMEM((4, 4 * BLOCK, D), LOW),
            pltpu.VMEM((2, D, D), F32),
            pltpu.SemaphoreType.DMA((4, 2)),
            pltpu.SemaphoreType.DMA((2,)),
        ],
        n_smem=1,
        far_in=range(2, 10),
        far_out=(6, 7),
        earlier=early_first,
        flops=10 * MICROSECOND,
    )(place, cross_memory, *[v.reshape(4 * BLOCK, 2 * D) for v in memory_grads], *stored)
    late.plan, late.at = [(D, 2 * D, 0)], 2 * D // count
    early_second = early.second(2)
    come_a, come_b = swap(far_a, 2), swap(far_b, 1)

    pre_grad, self_branch_grad, project_grad, input_grad, small_self = call(
        self_backward_kernel,
        [
            ((tokens, D), LOW),
            ((tokens, D), LOW),
            ((tokens, 3 * D), LOW),
            ((tokens, D), F32),
            ((8, D), F32),
        ],
        scratch=[
            pltpu.VMEM((tokens, D), LOW),
            pltpu.VMEM((D, D), LOW),
            pltpu.VMEM((D, D), LOW),
            pltpu.VMEM((tokens, 3 * D), LOW),
            pltpu.VMEM((PAIRS, 2 * tokens, tokens), F32),
            pltpu.VMEM((D, 3 * D), LOW),
            pltpu.SemaphoreType.DMA((5,)),
        ],
        far_in=(7, 8, 9, 10, 11),
        earlier=(early_second[0], late.buffers[0]),
        flops=8 * MICROSECOND,
    )(
        *parts,
        second_resid,
        unit_first,
        scale_first,
        heads_all,
        soft_self,
        cross_query,
        self_output,
        self_project,
        norm_gain,
    )
    narrow = jnp.concatenate(
        [
            small_self[0:4],
            value_bias_grad[0:1],
            small_middle[3:4],
            small_middle[0:1],
            small_self[4:5],
            small_middle[4:5],
            small_middle[1:2],
            small_self[5:6],
            small_middle[5:6],
            small_middle[2:3],
        ]
    )
    share = D // count
    narrow = jnp.swapaxes(narrow.reshape(13, count, share), 0, 1)
    small = jnp.concatenate([narrow, wide_bias.reshape(count, hidden // D, share)], axis=1)
    small = jnp.pad(small, ((0, 0), (0, 7), (0, 0))).reshape(count, 3, UNIT).astype(LOW)
    small = jnp.stack(
        [
            jnp.pad(small[:, :2], ((0, 0), (0, RANK_ROWS - 2), (0, 0))),
            jnp.pad(small[:, 2:], ((0, 0), (0, RANK_ROWS - 1), (0, 0))),
        ],
        axis=1,
    )
    late.add(
        [[(attended, self_branch_grad)], [(first_low, pre_grad)], [(inputs, project_grad)]],
        small,
        flops=6 * MICROSECOND,
    )
    near_two = 2 * BLOCK
    send_a = near_a1 + come_a[near_two:]
    send_b = near_b1 + come_b[near_two:]
    late.start(send_a, send_b)
    late_first = late.first()
    early.third_far(late_first[0])
    early_near = early.third_near()
    contract_weight_grad, cross_output_grad, expand_weight_grad = early.finish()
    late.second(4, early_near)
    last_a, last_b = swap(send_a, 1), swap(send_b, 2)
    datastore_grad = jnp.concatenate(
        [
            near.astype(F32) + come[:near_two].astype(F32) + last.astype(F32)
            for near, come, last in ((near_a0, come_a, last_a), (near_b0, come_b, last_b))
        ]
    )
    late.third(datastore_grad, contract_weight_grad)
    (
        cross_memory_grad,
        self_output_grad,
        cross_query_grad,
        self_project_grad,
        small,
    ) = late.finish()
    small = jnp.concatenate([small[0, :2], small[1, :1]])
    small = small.reshape(24, share)
    return (
        outputs,
        input_grad,
        datastore_grad,
        self_project_grad,
        self_output_grad,
        cross_query_grad,
        cross_memory_grad,
        cross_output_grad,
        expand_weight_grad,
        contract_weight_grad,
        small[:7],
        small[13:17].reshape(hidden // count),
        small[7:10],
        small[10:13],
    )


def layer_norm(residual, gain_row, shift_row):
    center = residual - jnp.mean(residual, axis=-1, keepdims=True)
    spread = jnp.mean(center * center, axis=-1, keepdims=True)
    return center * lax.rsqrt(spread + EPSILON) * gain_row + shift_row


def doc_mask(lengths, seq_tokens):
    upto = jnp.tri(lengths.shape[-1], dtype=jnp.int32)
    bounds = jnp.sum(lengths[..., None, :] * upto, axis=-1)
    places = jnp.arange(seq_tokens, dtype=jnp.int32)
    segment = jnp.sum((places[:, None] >= bounds[..., None, :]).astype(jnp.int32), axis=-1)
    causal = places[:, None] >= places[None, :]
    return (segment[..., :, None] == segment[..., None, :]) & causal


def slot_numbers(picks, capacity):
    flat_ids = picks.reshape(-1)
    sorter = jnp.argsort(flat_ids, stable=True)
    sorted_ids = flat_ids[sorter]
    first_seen = jnp.searchsorted(sorted_ids, sorted_ids, side="left")
    rank_sorted = jnp.arange(flat_ids.shape[0], dtype=jnp.int32) - first_seen
    ranks = jnp.zeros_like(flat_ids).at[sorter].set(rank_sorted)
    return flat_ids * capacity + ranks


def place_rows(rows, slot_ids, total_slots, store_count, local_blocks, capacity):
    placed = jnp.zeros((total_slots, rows.shape[1]), rows.dtype).at[slot_ids].set(rows)
    return placed.reshape(store_count, local_blocks, capacity, rows.shape[1])


def local_slots(
    inputs,
    doc_lengths,
    datastore,
    kept_mask,
    retrieved,
    self_project,
    self_output,
    cross_query,
    cross_memory,
    cross_output,
    expand_weight,
    contract_weight,
    biases,
    expand_bias,
    norm_gain,
    norm_shift,
    cotangent,
):
    tok_count = inputs.shape[0]
    store_count = lax.axis_size("store")
    local_blocks = datastore.shape[0] // BLOCK
    all_blocks = local_blocks * store_count
    capacity = 2 * tok_count * TOPB // all_blocks
    rows_in = store_count * capacity
    total_slots = all_blocks * capacity
    gain_rows = norm_gain.astype(jnp.float32)
    shift_rows = norm_shift.astype(jnp.float32)
    bias_rows = biases.astype(jnp.float32)
    projected = jnp.dot(inputs, self_project, preferred_element_type=jnp.float32)
    heads_all = jnp.concatenate(
        [
            QUERY_SCALE * (projected[:, :D] + bias_rows[0]),
            projected[:, D : 2 * D],
            projected[:, 2 * D :] + bias_rows[1],
        ],
        axis=1,
    ).astype(jnp.bfloat16)
    queries = heads_all[:, :D].reshape(tok_count, HEADS, HEAD_DIM)
    keys_self = heads_all[:, D : 2 * D].reshape(tok_count, HEADS, HEAD_DIM)
    values_self = heads_all[:, 2 * D :].reshape(tok_count, HEADS, HEAD_DIM)
    allowed = doc_mask(doc_lengths[0], tok_count)

    def self_scores():
        raw_scores = jnp.einsum(
            "qhd,khd->hqk", queries, keys_self, preferred_element_type=jnp.float32
        )
        return jnp.where(allowed[None], raw_scores, MASKED)

    scores = self_scores()
    self_lse = jax.nn.logsumexp(scores, axis=-1)
    soft_low = jnp.exp(scores - self_lse[..., None]).astype(jnp.bfloat16)
    attended = (
        jnp.einsum("hqk,khd->qhd", soft_low, values_self, preferred_element_type=jnp.float32)
        .reshape(tok_count, D)
        .astype(jnp.bfloat16)
    )
    self_branch = jnp.dot(attended, self_output, preferred_element_type=jnp.float32) + bias_rows[2]
    first_norm, first_back = jax.vjp(
        layer_norm, inputs.astype(jnp.float32) + self_branch, gain_rows[0], shift_rows[0]
    )
    first_low = first_norm.astype(jnp.bfloat16)
    cross_queries = (
        QUERY_SCALE
        * (jnp.dot(first_low, cross_query, preferred_element_type=jnp.float32) + bias_rows[3])
    ).astype(jnp.bfloat16)
    slot_ids = slot_numbers(retrieved, capacity)
    send_buffer = place_rows(
        jnp.repeat(cross_queries, TOPB, axis=0),
        slot_ids,
        total_slots,
        store_count,
        local_blocks,
        capacity,
    )
    arrived = lax.all_to_all(send_buffer, "store", split_axis=0, concat_axis=2, tiled=True)
    owner_queries = arrived[0].reshape(local_blocks, rows_in, HEADS, HEAD_DIM)
    memory_bias = jnp.concatenate([jnp.zeros((D,), jnp.float32), bias_rows[4]])
    memory_low = (
        jnp.dot(datastore, cross_memory, preferred_element_type=jnp.float32) + memory_bias
    ).astype(jnp.bfloat16)
    memory_blocks = memory_low.reshape(local_blocks, BLOCK, 2 * D)
    store_keys = memory_blocks[:, :, :D].reshape(local_blocks, BLOCK, HEADS, HEAD_DIM)
    store_values = memory_blocks[:, :, D:].reshape(local_blocks, BLOCK, HEADS, HEAD_DIM)
    kept_rows = kept_mask.reshape(local_blocks, BLOCK) > 0

    def block_scores(query_blocks):
        raw_scores = jnp.einsum(
            "bmhd,bkhd->bhmk", query_blocks, store_keys, preferred_element_type=jnp.float32
        )
        return jnp.where(kept_rows[:, None, None, :], raw_scores, MASKED)

    owner_scores = block_scores(owner_queries)
    owner_lse = jax.nn.logsumexp(owner_scores, axis=-1)
    owner_soft = jnp.exp(owner_scores - owner_lse[..., None]).astype(jnp.bfloat16)
    partial_value = jnp.einsum(
        "bhmk,bkhd->bmhd", owner_soft, store_values, preferred_element_type=jnp.float32
    ).reshape(local_blocks, rows_in, D)
    partial_lse = jnp.transpose(owner_lse, (0, 2, 1))
    returned, returned_lse = (
        lax.all_to_all(partial_value[None], "store", split_axis=2, concat_axis=0, tiled=True),
        lax.all_to_all(partial_lse[None], "store", split_axis=2, concat_axis=0, tiled=True),
    )
    picked = returned.reshape(total_slots, D)[slot_ids].reshape(tok_count, TOPB, HEADS, HEAD_DIM)
    picked_lse = returned_lse.reshape(total_slots, HEADS)[slot_ids].reshape(tok_count, TOPB, HEADS)
    overall = jax.nn.logsumexp(picked_lse, axis=1)
    mix_weights = jnp.exp(picked_lse - overall[:, None, :])
    merged = jnp.einsum(
        "tjh,tjhd->thd", mix_weights, picked, precision=lax.Precision.HIGHEST
    ).reshape(tok_count, D)
    merged_low = merged.astype(jnp.bfloat16)
    cross_branch = (
        jnp.dot(merged_low, cross_output, preferred_element_type=jnp.float32) + bias_rows[5]
    )
    second_norm, second_back = jax.vjp(
        layer_norm, first_low.astype(jnp.float32) + cross_branch, gain_rows[1], shift_rows[1]
    )
    second_low = second_norm.astype(jnp.bfloat16)
    expanded = jnp.dot(
        second_low, expand_weight, preferred_element_type=jnp.float32
    ) + expand_bias.astype(jnp.float32)
    activated, gelu_back = jax.vjp(
        lambda pre_act: jax.nn.gelu(pre_act, approximate=False), expanded
    )
    activated_low = activated.astype(jnp.bfloat16)
    ffn_branch = (
        jnp.dot(activated_low, contract_weight, preferred_element_type=jnp.float32) + bias_rows[6]
    )
    final_norm, final_back = jax.vjp(
        layer_norm, second_low.astype(jnp.float32) + ffn_branch, gain_rows[2], shift_rows[2]
    )
    outputs = final_norm.astype(jnp.bfloat16)
    final_resid, final_gain, final_shift = final_back(cotangent.astype(jnp.float32))
    ffn_branch_grad = final_resid.astype(jnp.bfloat16)
    contract_weight_grad = jnp.dot(
        activated_low.T, ffn_branch_grad, preferred_element_type=jnp.float32
    )
    activated_grad = jnp.dot(ffn_branch_grad, contract_weight.T, preferred_element_type=jnp.float32)
    (expanded_raw,) = gelu_back(activated_grad)
    expanded_grad = expanded_raw.astype(jnp.bfloat16)
    expand_weight_grad = jnp.dot(second_low.T, expanded_grad, preferred_element_type=jnp.float32)
    expand_bias_grad = jnp.sum(expanded_grad.astype(jnp.float32), axis=0)
    second_total = final_resid + jnp.dot(
        expanded_grad, expand_weight.T, preferred_element_type=jnp.float32
    )
    second_resid, second_gain, second_shift = second_back(second_total)
    cross_branch_grad = second_resid.astype(jnp.bfloat16)
    cross_output_grad = jnp.dot(merged_low.T, cross_branch_grad, preferred_element_type=jnp.float32)
    attended_grad = jnp.dot(
        cross_branch_grad, cross_output.T, preferred_element_type=jnp.float32
    ).astype(jnp.bfloat16)
    delta_rows = jnp.sum(
        attended_grad.reshape(tok_count, HEADS, HEAD_DIM).astype(jnp.float32)
        * merged.reshape(tok_count, HEADS, HEAD_DIM),
        axis=-1,
    )
    grad_buffer = place_rows(
        jnp.repeat(attended_grad, TOPB, axis=0),
        slot_ids,
        total_slots,
        store_count,
        local_blocks,
        capacity,
    )
    overall_buffer = place_rows(
        jnp.repeat(overall, TOPB, axis=0),
        slot_ids,
        total_slots,
        store_count,
        local_blocks,
        capacity,
    )
    delta_buffer = place_rows(
        jnp.repeat(delta_rows, TOPB, axis=0),
        slot_ids,
        total_slots,
        store_count,
        local_blocks,
        capacity,
    )
    arrived_grad = lax.all_to_all(grad_buffer, "store", split_axis=0, concat_axis=2, tiled=True)
    arrived_overall, arrived_delta = (
        lax.all_to_all(overall_buffer, "store", split_axis=0, concat_axis=2, tiled=True),
        lax.all_to_all(delta_buffer, "store", split_axis=0, concat_axis=2, tiled=True),
    )
    owner_grad = arrived_grad[0].reshape(local_blocks, rows_in, HEADS, HEAD_DIM)
    overall_heads = jnp.transpose(arrived_overall[0], (0, 2, 1))
    delta_heads = jnp.transpose(arrived_delta[0], (0, 2, 1))
    soft_again = jnp.exp(block_scores(owner_queries) - owner_lse[..., None])
    soft_again_low = soft_again.astype(jnp.bfloat16).astype(jnp.float32)
    weight_mix = jnp.exp(owner_lse - overall_heads)
    value_dots = jnp.einsum(
        "bmhd,bkhd->bhmk", owner_grad, store_values, preferred_element_type=jnp.float32
    )
    exact_sum = jnp.sum(soft_again * value_dots, axis=-1, keepdims=True)
    rounded_sum = jnp.sum(soft_again_low * value_dots, axis=-1, keepdims=True)
    score_grad = (
        weight_mix[..., None]
        * soft_again
        * (value_dots - exact_sum + rounded_sum - delta_heads[..., None])
    ).astype(jnp.bfloat16)
    query_grad = (
        jnp.einsum("bhmk,bkhd->bmhd", score_grad, store_keys, preferred_element_type=jnp.float32)
        .astype(jnp.bfloat16)
        .reshape(local_blocks, rows_in, D)
    )
    key_grad = jnp.einsum(
        "bhmk,bmhd->bkhd", score_grad, owner_queries, preferred_element_type=jnp.float32
    )
    weighted_soft = weight_mix[..., None] * soft_again_low
    value_grad = jnp.einsum(
        "bhmk,bmhd->bkhd",
        weighted_soft,
        owner_grad.astype(jnp.float32),
        precision=lax.Precision.HIGHEST,
    )
    row_count = local_blocks * BLOCK
    memory_grad = jnp.concatenate(
        [key_grad.reshape(row_count, D), value_grad.reshape(row_count, D)], axis=1
    ).astype(jnp.bfloat16)
    cross_memory_grad = jnp.dot(datastore.T, memory_grad, preferred_element_type=jnp.float32)
    value_bias_grad = jnp.sum(memory_grad[:, D:].astype(jnp.float32), axis=0)
    datastore_grad = jnp.dot(memory_grad, cross_memory.T, preferred_element_type=jnp.float32)
    returned_grad = lax.all_to_all(
        query_grad[None], "store", split_axis=2, concat_axis=0, tiled=True
    )
    per_pick = returned_grad.reshape(total_slots, D)[slot_ids].reshape(tok_count, TOPB, D)
    query_sum = jnp.sum(per_pick.astype(jnp.float32), axis=1).astype(jnp.bfloat16)
    cross_pre_grad = (query_sum.astype(jnp.float32) * QUERY_SCALE).astype(jnp.bfloat16)
    cross_query_grad = jnp.dot(first_low.T, cross_pre_grad, preferred_element_type=jnp.float32)
    first_total = second_resid + jnp.dot(
        cross_pre_grad, cross_query.T, preferred_element_type=jnp.float32
    )
    first_resid, first_gain, first_shift = first_back(first_total)
    self_branch_grad = first_resid.astype(jnp.bfloat16)
    self_output_grad = jnp.dot(attended.T, self_branch_grad, preferred_element_type=jnp.float32)
    self_attended_grad = (
        jnp.dot(self_branch_grad, self_output.T, preferred_element_type=jnp.float32)
        .astype(jnp.bfloat16)
        .reshape(tok_count, HEADS, HEAD_DIM)
    )
    soft_self = jnp.exp(self_scores() - self_lse[..., None])
    soft_dots = jnp.einsum(
        "qhd,khd->hqk", self_attended_grad, values_self, preferred_element_type=jnp.float32
    )
    self_score_grad = (
        soft_self * (soft_dots - jnp.sum(soft_self * soft_dots, axis=-1, keepdims=True))
    ).astype(jnp.bfloat16)
    query_self_grad = jnp.einsum(
        "hqk,khd->qhd", self_score_grad, keys_self, preferred_element_type=jnp.float32
    ).reshape(tok_count, D)
    key_self_grad = jnp.einsum(
        "hqk,qhd->khd", self_score_grad, queries, preferred_element_type=jnp.float32
    ).reshape(tok_count, D)
    value_self_grad = jnp.einsum(
        "hqk,qhd->khd", soft_low, self_attended_grad, preferred_element_type=jnp.float32
    ).reshape(tok_count, D)
    heads_grad = jnp.concatenate([query_self_grad, key_self_grad, value_self_grad], axis=1).astype(
        jnp.bfloat16
    )
    project_grad = jnp.concatenate(
        [
            (heads_grad[:, :D].astype(jnp.float32) * QUERY_SCALE).astype(jnp.bfloat16),
            heads_grad[:, D:],
        ],
        axis=1,
    )
    self_project_grad = jnp.dot(inputs.T, project_grad, preferred_element_type=jnp.float32)
    input_grad = first_resid + jnp.dot(
        project_grad, self_project.T, preferred_element_type=jnp.float32
    )
    biases_grad = jnp.stack(
        [
            jnp.sum(project_grad[:, :D].astype(jnp.float32), axis=0),
            jnp.sum(project_grad[:, 2 * D :].astype(jnp.float32), axis=0),
            jnp.sum(self_branch_grad.astype(jnp.float32), axis=0),
            jnp.sum(cross_pre_grad.astype(jnp.float32), axis=0),
            value_bias_grad,
            jnp.sum(cross_branch_grad.astype(jnp.float32), axis=0),
            jnp.sum(ffn_branch_grad.astype(jnp.float32), axis=0),
        ]
    )
    gain_grad = jnp.stack([first_gain, second_gain, final_gain])
    shift_grad = jnp.stack([first_shift, second_shift, final_shift])
    shared = (
        lax.psum_scatter(self_project_grad, "store", scatter_dimension=0, tiled=True),
        lax.psum_scatter(self_output_grad, "store", scatter_dimension=0, tiled=True),
        lax.psum_scatter(cross_query_grad, "store", scatter_dimension=0, tiled=True),
        lax.psum_scatter(cross_memory_grad, "store", scatter_dimension=0, tiled=True),
        lax.psum_scatter(cross_output_grad, "store", scatter_dimension=0, tiled=True),
        lax.psum_scatter(expand_weight_grad, "store", scatter_dimension=0, tiled=True),
        lax.psum_scatter(contract_weight_grad, "store", scatter_dimension=0, tiled=True),
        lax.psum_scatter(biases_grad, "store", scatter_dimension=1, tiled=True),
        lax.psum_scatter(expand_bias_grad, "store", scatter_dimension=0, tiled=True),
        lax.psum_scatter(gain_grad, "store", scatter_dimension=1, tiled=True),
        lax.psum_scatter(shift_grad, "store", scatter_dimension=1, tiled=True),
    )
    reduced = (
        lax.psum(shared[0].astype(jnp.bfloat16), "dp").astype(jnp.float32),
        lax.psum(shared[1].astype(jnp.bfloat16), "dp").astype(jnp.float32),
        lax.psum(shared[2].astype(jnp.bfloat16), "dp").astype(jnp.float32),
        lax.psum(shared[3].astype(jnp.bfloat16), "dp").astype(jnp.float32),
        lax.psum(shared[4].astype(jnp.bfloat16), "dp").astype(jnp.float32),
        lax.psum(shared[5].astype(jnp.bfloat16), "dp").astype(jnp.float32),
        lax.psum(shared[6].astype(jnp.bfloat16), "dp").astype(jnp.float32),
        lax.psum(shared[7].astype(jnp.bfloat16), "dp").astype(jnp.float32),
        lax.psum(shared[8].astype(jnp.bfloat16), "dp").astype(jnp.float32),
        lax.psum(shared[9].astype(jnp.bfloat16), "dp").astype(jnp.float32),
        lax.psum(shared[10].astype(jnp.bfloat16), "dp").astype(jnp.float32),
    )
    return (
        outputs,
        input_grad,
        datastore_grad,
        reduced[0],
        reduced[1],
        reduced[2],
        reduced[3],
        reduced[4],
        reduced[5],
        reduced[6],
        reduced[7],
        reduced[8],
        reduced[9],
        reduced[10],
    )


def solution(mesh):
    placed = (
        P(("dp", "store"), None),
        P(("dp", "store"), None),
        P(("dp", "store"), None),
        P(("dp", "store")),
        P(("dp", "store"), None),
        P(),
        P(),
        P(),
        P(),
        P(),
        P(),
        P(),
        P(),
        P(),
        P(),
        P(),
        P(("dp", "store"), None),
    )
    return jax.shard_map(
        local_tree if mesh.shape["store"] == 16 else local_slots,
        mesh=mesh,
        in_specs=placed,
        out_specs=(
            P(("dp", "store"), None),
            P(("dp", "store"), None),
            P(("dp", "store"), None),
            P("store", None),
            P("store", None),
            P("store", None),
            P("store", None),
            P("store", None),
            P("store", None),
            P("store", None),
            P(None, "store"),
            P("store"),
            P(None, "store"),
            P(None, "store"),
        ),
        check_vma=False,
    )
```

```python
import functools

import jax
import jax.numpy as jnp
from jax import lax
from jax.experimental import pallas as pl
from jax.experimental.pallas import tpu as pltpu
from jax.sharding import PartitionSpec as P

D = 768
HEADS = 12
HEAD_DIM = 64
TOPB = 8
BLOCK = 128
SLAB = 128
PAIRS = D // SLAB
UNIT = 384
WIDE = D + SLAB
RANK_ROWS = 16

EPSILON = 1e-05
MASKED = -1e30
QUERY_SCALE = 0.125
VMEM_LIMIT = 32 * 1024 * 1024
SMALL_LIMIT = 20 * 1024 * 1024
LONG = 30_000_000_000
MICROSECOND = 50_000_000
LOW = jnp.bfloat16
F32 = jnp.float32

_VMEM = pl.BlockSpec(memory_space=pltpu.VMEM)
_SMEM = pl.BlockSpec(memory_space=pltpu.SMEM)
_ANY = pl.BlockSpec(memory_space=pl.ANY)


def nn(a, b):
    return lax.dot_general(a, b, (((1,), (0,)), ((), ())), preferred_element_type=F32)


def nt(a, b):
    return lax.dot_general(a, b, (((1,), (1,)), ((), ())), preferred_element_type=F32)


def tn(a, b):
    return lax.dot_general(a, b, (((0,), (0,)), ((), ())), preferred_element_type=F32)


def three(v):
    high = v.astype(LOW)
    rest = v - high.astype(F32)
    mid = rest.astype(LOW)
    return high, mid, (rest - mid.astype(F32)).astype(LOW)


def lanes(shape):
    return lax.broadcasted_iota(jnp.int32, shape, len(shape) - 1)


def rows_of(shape):
    return lax.broadcasted_iota(jnp.int32, shape, len(shape) - 2)


def flag(condition):
    return jnp.where(condition, 1.0, 0.0)


def half_masks():
    first = flag(lanes((1, SLAB)) < HEAD_DIM)
    return first.astype(LOW), (1.0 - first).astype(LOW)


def two_heads(slab, first, second):
    return jnp.concatenate([slab * first, slab * second], axis=0)


def join_heads(stacked, count):
    left = lanes((count, SLAB)) < HEAD_DIM
    return jnp.where(left, stacked[:count], stacked[count:])


def norm_forward(residual, gain, shift):
    center = residual - jnp.mean(residual, axis=-1, keepdims=True)
    spread = jnp.mean(center * center, axis=-1, keepdims=True)
    scale = lax.rsqrt(spread + EPSILON)
    unit = center * scale
    return unit * gain + shift, unit, scale


def norm_backward(grad, unit, scale, gain):
    inner = grad * gain
    down = inner - jnp.mean(inner, axis=-1, keepdims=True)
    down = down - unit * jnp.mean(inner * unit, axis=-1, keepdims=True)
    return scale * down


def row_sum(v):
    return jnp.sum(v, axis=0, keepdims=True)


def call(
    kernel,
    outs,
    scratch=(),
    n_smem=0,
    far_in=(),
    far_out=(),
    earlier=(),
    aliases=None,
    flops=0,
    limit=VMEM_LIMIT,
):
    def run(*args):
        count = len(args)

        def body(*refs):
            kernel(*refs[:count], *refs[count + len(earlier) :])

        specs = [_ANY if i in far_in else _VMEM for i in range(n_smem, count)]
        return pl.pallas_call(
            body,
            out_shape=[jax.ShapeDtypeStruct(s, t) for s, t in outs],
            in_specs=[_SMEM] * n_smem + specs + [_ANY] * len(earlier),
            out_specs=[_ANY if i in far_out else _VMEM for i in range(len(outs))],
            scratch_shapes=list(scratch),
            input_output_aliases=aliases or {},
            compiler_params=pltpu.CompilerParams(vmem_limit_bytes=limit),
            cost_estimate=pl.CostEstimate(flops=flops, bytes_accessed=0, transcendentals=0),
        )(*args, *earlier)

    return run


def copies(pairs, sems):
    return [pltpu.make_async_copy(a, b, sems.at[i]) for i, (a, b) in enumerate(pairs)]


def after(v, *earlier):
    return call(
        lambda *refs: None,
        [(v.shape, v.dtype)],
        far_in=(0,),
        far_out=(0,),
        earlier=earlier,
        aliases={0: 0},
        limit=1024 * 1024,
    )(v)[0]


def start_all(items):
    for item in items:
        item.start()


def wait_all(items):
    for item in items:
        item.wait()


def plane_ranks(picks_ref, me, k, tokens):
    i = rows_of((RANK_ROWS, tokens))
    group, chip, block = i // 4, (i // 2) % 2, i % 2
    apart = jnp.where(group < 2, 2 * group + chip, 2 * chip + group - 2)
    local = jnp.where(group < 2, block, 2 + block)
    plane = (me // 4) ^ k
    number = plane * 16 + ((me % 4) ^ apart) * 4 + local
    member = jnp.zeros((RANK_ROWS, tokens), F32)
    for j in range(TOPB):
        member = member + flag(picks_ref[j : j + 1, :] == number)
    earlier = flag(rows_of((tokens, tokens)) < lanes((tokens, tokens)))
    rank = nn(member.astype(LOW), earlier.astype(LOW))
    return jnp.where(member > 0.5, rank, -1.0).astype(LOW)


def self_forward_kernel(
    lengths_ref,
    place_ref,
    x_ref,
    picks_ref,
    project_ref,
    output_ref,
    query_ref,
    bias_ref,
    gain_ref,
    shift_ref,
    heads_ref,
    soft_ref,
    attended_ref,
    unit_ref,
    scale_ref,
    first_ref,
    *rest,
):
    payload_refs, (project_scr, output_scr, query_scr, sems) = rest[:4], rest[4:]
    thirds = [slice(i * D, (i + 1) * D) for i in range(3)]
    fetch = copies(
        [(project_ref.at[:, at], project_scr.at[:, at]) for at in thirds]
        + [(output_ref, output_scr), (query_ref, query_scr)],
        sems,
    )
    start_all(fetch)
    tokens = x_ref.shape[0]
    bias = bias_ref[...].astype(F32)
    x = x_ref[...]
    for i, at in enumerate(thirds):
        fetch[i].wait()
        part = nn(x, project_scr[:, at])
        if i == 0:
            part = QUERY_SCALE * (part + bias[0:1])
        if i == 2:
            part = part + bias[1:2]
        heads_ref[:, at] = part.astype(LOW)
    place_row = lax.broadcasted_iota(jnp.int32, (2 * tokens, tokens), 0) % tokens
    place_col = lanes((2 * tokens, tokens))
    segment_row = jnp.zeros((2 * tokens, tokens), jnp.int32)
    segment_col = jnp.zeros((2 * tokens, tokens), jnp.int32)
    bound = 0
    for d in range(lengths_ref.shape[1]):
        bound = bound + lengths_ref[0, d]
        segment_row = segment_row + jnp.where(place_row >= bound, 1, 0)
        segment_col = segment_col + jnp.where(place_col >= bound, 1, 0)
    allowed = (segment_row == segment_col) & (place_row >= place_col)
    first, second = half_masks()
    for p in range(PAIRS):
        at = p * SLAB
        queries = two_heads(heads_ref[:, at : at + SLAB], first, second)
        scores = nt(queries, heads_ref[:, D + at : D + at + SLAB])
        scores = jnp.where(allowed, scores, MASKED)
        top = jnp.max(scores, axis=-1, keepdims=True)
        raised = jnp.exp(scores - top)
        soft = raised / jnp.sum(raised, axis=-1, keepdims=True)
        soft_ref[p] = soft
        mixed = nn(soft.astype(LOW), heads_ref[:, 2 * D + at : 2 * D + at + SLAB])
        attended_ref[:, at : at + SLAB] = join_heads(mixed, tokens).astype(LOW)
    fetch[3].wait()
    residual = x.astype(F32) + nn(attended_ref[...], output_scr[...]) + bias[2:3]
    normed, unit, scale = norm_forward(
        residual, gain_ref[0:1, :].astype(F32), shift_ref[0:1, :].astype(F32)
    )
    unit_ref[...] = unit
    scale_ref[...] = scale
    low = normed.astype(LOW)
    first_ref[...] = low
    fetch[4].wait()
    queries = (QUERY_SCALE * (nn(low, query_scr[...]) + bias[3:4])).astype(LOW)
    for k, out in enumerate(payload_refs):
        out[:tokens] = queries
        out[tokens:, tokens:] = jnp.zeros((RANK_ROWS, D - tokens), LOW)
        out[tokens:, :tokens] = plane_ranks(picks_ref, place_ref[0], k, tokens)


def memory_kernel(*refs):
    sets = (len(refs) - 2) // 6
    pieces, (weight_ref, bias_ref), outs = refs[: 2 * sets], refs[2 * sets : 2 * sets + 2], refs[2 * sets + 2 :]
    bias = bias_ref[4:5, :].astype(F32)
    lane = lanes((RANK_ROWS, SLAB))
    for s in range(sets):
        rows_ref, memory_ref, hidden_ref, side_ref = outs[4 * s : 4 * s + 4]
        for j in range(2):
            piece = pieces[2 * s + j]
            rows = piece[: 2 * BLOCK]
            rows_ref[2 * j * BLOCK : 2 * (j + 1) * BLOCK] = rows
            keys = nn(rows, weight_ref[:, :D]).astype(LOW)
            values = (nn(rows, weight_ref[:, D:]) + bias).astype(LOW)
            marks = piece[2 * BLOCK :, :SLAB]
            for l in range(2):
                at = 2 * j + l
                memory_ref[at, :, :D] = keys[l * BLOCK : (l + 1) * BLOCK]
                memory_ref[at, :, D:] = values[l * BLOCK : (l + 1) * BLOCK]
                hidden_ref[at] = (1.0 - marks[l : l + 1].astype(F32)) * MASKED
                wanted = flag((rows_of((RANK_ROWS, SLAB)) == l) & (lane == SLAB - 1))
                column = tn(marks, wanted.astype(LOW))
                place = lanes((BLOCK, SLAB))
                side = jnp.where(place == SLAB - 1, (1.0 - column) * MASKED, 0.0)
                side_ref[at] = jnp.where(place < 48, -1.0, side).astype(LOW)


def selection(ranks, capacity):
    parts = []
    wanted = rows_of((capacity, ranks.shape[1])).astype(F32)
    for b in range(ranks.shape[0]):
        parts.append(flag(ranks[b : b + 1, :] == wanted).astype(LOW))
    return jnp.concatenate(parts, axis=0)


def fill_slots(sel, rows, out_ref, k, capacity):
    got = nn(sel, rows).astype(LOW)
    for b in range(out_ref.shape[0]):
        out_ref[b, k * capacity : (k + 1) * capacity, :] = got[b * capacity : (b + 1) * capacity]


def around16(v, combine):
    for step in (16, 32, 64):
        v = combine(v, pltpu.roll(v, step, 1))
    return v


def lse_lanes(lse):
    high = lse.astype(LOW).astype(F32)
    rest = lse - high
    mid = rest.astype(LOW).astype(F32)
    low = rest - mid
    lane = lanes(lse.shape)
    packed = jnp.where(
        lane < 16, high, jnp.where(lane < 32, mid, jnp.where(lane < 48, low, 0.0))
    )
    return packed.astype(LOW)


def read_lse(packed):
    return around16(packed.astype(F32), jnp.add)


def head_spread(group):
    row = rows_of((SLAB, D))
    row = row % 16 if group else row
    return flag(row == lanes((SLAB, D)) // HEAD_DIM).astype(LOW)


def owner_forward_kernel(capacity, *refs):
    tokens_refs, memory_refs, hidden_refs = refs[0:4], refs[4:8], refs[8:12]
    far_slots_ref, payload_refs = refs[12], refs[13:17]
    out_scr, lse_scr, inv_scr, sel_scr, ranks_scr, slots_ref, memory_scr, sems, slots_sem = refs[17:]
    fetch = copies([(ref, memory_scr.at[s]) for s, ref in enumerate(memory_refs)], sems)
    start_all(fetch)
    sources = len(tokens_refs)
    blocks, rows = slots_ref.shape[:2]
    tokens = tokens_refs[0].shape[0] - RANK_ROWS
    first, second = half_masks()
    for k in range(sources):
        ranks_scr[...] = tokens_refs[k][tokens:, :tokens].astype(F32)
        sel = selection(ranks_scr[...], capacity)
        sel_scr[k] = sel
        fill_slots(sel, tokens_refs[k][:tokens], slots_ref, k, capacity)
    (keep,) = copies([(slots_ref, far_slots_ref)], slots_sem)
    keep.start()
    ones = jnp.ones((BLOCK, SLAB), LOW)
    lane_of = lanes((rows, SLAB))
    for s in range(4):
        fetch[s].wait()

        def one_block(l, carry, s=s):
            i = 4 * s + l
            hidden = hidden_refs[s][l]
            tops = jnp.zeros((rows, SLAB), F32)
            totals = jnp.ones((rows, SLAB), F32)
            base = (i % 8) * 16
            slabs = [slice(p * SLAB, (p + 1) * SLAB) for p in range(PAIRS)]
            scores = [
                nt(two_heads(slots_ref[i, :, at], first, second), memory_scr[s, l, :, at])
                + hidden
                for at in slabs
            ]
            highest = [jnp.max(v, axis=-1, keepdims=True) for v in scores]
            raised = [jnp.exp(v - top).astype(LOW) for v, top in zip(scores, highest)]
            mixed = [
                nn(v, jnp.concatenate([memory_scr[s, l, :, D + at.start : D + at.stop], ones], axis=1))
                for v, at in zip(raised, slabs)
            ]
            for p, at in enumerate(slabs):
                out_scr[i, :, at] = join_heads(mixed[p][:, :SLAB], rows)
                for half in range(2):
                    here = slice(half * rows, (half + 1) * rows)
                    mine = lane_of == base + 2 * p + half
                    tops = jnp.where(mine, highest[p][here], tops)
                    totals = jnp.where(mine, mixed[p][here, SLAB:], totals)
            own = flag((lane_of >= base) & (lane_of < base + HEADS))
            lse_scr[i] = tops + jnp.log(totals)
            inv_scr[i] = own / totals
            return carry

        lax.fori_loop(0, 4, one_block, 0)
    group = 8 * capacity
    own_low = flag(
        rows_of((group, SLAB)) // capacity == lanes((group, SLAB)) // 16
    ).astype(LOW)
    spread = head_spread(True)
    for k in range(sources):
        here = slice(k * capacity, (k + 1) * capacity)

        def stacked(ref, g, here=here):
            return jnp.concatenate([ref[8 * g + b, here, :] for b in range(8)], axis=0)

        by_token, members, sels = [], [], []
        for g in range(2):
            sel = sel_scr[k, g * group : (g + 1) * group, :]
            value = sum(tn(sel, part) for part in three(stacked(lse_scr, g)))
            member = tn(sel, own_low)
            by_token.append(jnp.where(member > 0.5, value, MASKED))
            members.append(member)
            sels.append(sel)
        top = around16(jnp.maximum(*by_token), jnp.maximum)
        weights = [m * jnp.exp(v - top) for m, v in zip(members, by_token)]
        total = around16(weights[0] + weights[1], jnp.add)
        some = total > 0.5
        safe = jnp.where(some, total, 1.0)
        payload_refs[k][:, D:] = lse_lanes(jnp.where(some, top + jnp.log(safe), MASKED))
        partial = jnp.zeros((tokens, D), F32)
        for g in range(2):
            share = nn(sels[g], (weights[g] / safe).astype(LOW)) * stacked(inv_scr, g)
            value = stacked(out_scr, g) * nn(share.astype(LOW), spread)
            partial = partial + tn(sels[g], value.astype(LOW))
        payload_refs[k][:, :D] = partial.astype(LOW)
    keep.wait()


def owner_backward_kernel(capacity, *refs):
    tokens_refs, grad_refs, memory_refs, side_refs = refs[0:4], refs[4:8], refs[8:12], refs[12:16]
    far_slots_ref = refs[16]
    far_grad_refs, payload_refs, bias_ref = refs[17:21], refs[21:25], refs[25]
    got_scr, query_scr, sel_scr, ranks_scr, slots_ref, memory_scr, grad_scr, sems, out_sems = refs[26:]
    fetch = copies(
        [(far_slots_ref, slots_ref)] + [(ref, memory_scr.at[s]) for s, ref in enumerate(memory_refs)],
        sems,
    )
    start_all(fetch)
    keep = copies([(grad_scr.at[s], ref) for s, ref in enumerate(far_grad_refs)], out_sems)
    sources = len(tokens_refs)
    blocks, rows = slots_ref.shape[:2]
    tokens = grad_refs[0].shape[0]
    first, second = half_masks()
    for k in range(sources):
        ranks_scr[...] = tokens_refs[k][tokens:, :tokens].astype(F32)
        sel = selection(ranks_scr[...], capacity)
        sel_scr[k] = sel
        fill_slots(sel, grad_refs[k][...], got_scr, k, capacity)
    lane = lanes((1, SLAB))
    last = flag(lane == SLAB - 1).astype(LOW)
    value_side = jnp.broadcast_to(
        -flag((lane >= 48) & (lane < 96)).astype(LOW), (BLOCK, SLAB)
    )

    def picked(head, base):
        inside = (lane >= base) & (lane < base + 48)
        return flag(inside & (lane % 16 == head)).astype(LOW)

    fetch[0].wait()
    for s in range(4):
        fetch[1 + s].wait()

        def one_block(l, carry, s=s):
            i = 4 * s + l
            side = got_scr[i, :, D:]
            key_side = side_refs[s][l]
            slabs = [slice(p * SLAB, (p + 1) * SLAB) for p in range(PAIRS)]
            keys = [memory_scr[s, l, :, at] for at in slabs]
            queries = [two_heads(slots_ref[i, :, at], first, second) for at in slabs]
            grads = [two_heads(got_scr[i, :, at], first, second) for at in slabs]
            scores, dots = [], []
            for p in range(PAIRS):
                lse_side = jnp.concatenate(
                    [side * picked(2 * p + h, 0) + last for h in range(2)], axis=0
                )
                scores.append(
                    nt(
                        jnp.concatenate([keys[p], key_side], axis=1),
                        jnp.concatenate([queries[p], lse_side], axis=1),
                    )
                )
            for p, at in enumerate(slabs):
                delta_side = jnp.concatenate(
                    [side * picked(2 * p + h, 48) for h in range(2)], axis=0
                )
                values = memory_scr[s, l, :, D + at.start : D + at.stop]
                dots.append(
                    nt(
                        jnp.concatenate([values, value_side], axis=1),
                        jnp.concatenate([grads[p], delta_side], axis=1),
                    )
                )
            softs = [jnp.exp(v) for v in scores]
            score_grads = [(soft * v).astype(LOW) for soft, v in zip(softs, dots)]
            out = grad_scr.at[s]
            for p, at in enumerate(slabs):
                query_scr[i, :, at] = join_heads(tn(score_grads[p], keys[p]), rows).astype(LOW)
            for p, at in enumerate(slabs):
                out[l, :, at] = nn(score_grads[p], queries[p]).astype(LOW)
            for p, at in enumerate(slabs):
                out[l, :, D + at.start : D + at.stop] = nn(softs[p].astype(LOW), grads[p]).astype(
                    LOW
                )
            return carry

        lax.fori_loop(0, 4, one_block, 0)
        keep[s].start()
    for k in range(sources):
        here = slice(k * capacity, (k + 1) * capacity)
        value = jnp.concatenate([query_scr[b, here, :] for b in range(blocks)], axis=0)
        payload_refs[k][...] = tn(sel_scr[k], value).astype(LOW)
    total = jnp.zeros((1, D), F32)
    for s in range(4):
        for l in range(4):
            total = total + row_sum(grad_scr[s, l, :, D:].astype(F32))
    bias_ref[...] = jnp.broadcast_to(total, (8, D))
    wait_all(keep)


def memory_weight_kernel(count, place_ref, *refs):
    far_grads, far_rows, far_outs = refs[:4], refs[4:8], refs[8:10]
    kept_ref, sent_ref, grad_scr, rows_scr, sum_scr, sems, out_sems = refs[10:]
    fetch = [
        copies([(far_grads[s], grad_scr.at[s]), (far_rows[s], rows_scr.at[s])], sems.at[s])
        for s in range(4)
    ]
    for items in fetch:
        start_all(items)
    me, core = place_ref[0], place_ref[1]
    for s in range(4):
        wait_all(fetch[s])
        rows = rows_scr[s].T
        for h in range(2):
            part = nn(rows, grad_scr[s, :, h * D : (h + 1) * D])
            sum_scr[h] = part if s == 0 else sum_scr[h] + part
    block = D // count
    for h in range(2):

        def store(out, h=h):
            total = sum_scr[h].astype(LOW)
            for k in range(count):
                for u in range(D // UNIT):
                    out[me ^ k, u * block : (u + 1) * block, :] = total[
                        k * block : (k + 1) * block, u * UNIT : (u + 1) * UNIT
                    ]

        pl.when(core == h)(functools.partial(store, kept_ref))
        pl.when(core != h)(functools.partial(store, sent_ref))
    size = 2 * block
    keep = copies(
        [(near, far.at[:, :size, :]) for near, far in zip((kept_ref, sent_ref), far_outs)],
        out_sems,
    )
    start_all(keep)
    wait_all(keep)


def datastore_grad_kernel(weight_ref, *refs):
    far_grads, outs, (grad_scr, sems) = refs[:4], refs[4:10], refs[10:]
    fetch = copies([(ref, grad_scr.at[s]) for s, ref in enumerate(far_grads)], sems)
    start_all(fetch)
    weight = weight_ref[...].T
    near_a0, near_a1, far_a, near_b0, near_b1, far_b = outs
    groups = ((near_a0, near_a1), (far_a,), (near_b0, near_b1), (far_b,))
    for s in range(4):
        fetch[s].wait()
        value = nn(grad_scr[s], weight).astype(LOW)
        size = value.shape[0] // len(groups[s])
        for i, out in enumerate(groups[s]):
            out[...] = value[i * size : (i + 1) * size]


def middle_kernel(
    p0_ref,
    p1_ref,
    p2_ref,
    p3_ref,
    first_ref,
    cotangent_ref,
    output_ref,
    expand_ref,
    contract_ref,
    bias_ref,
    expand_bias_ref,
    gain_ref,
    shift_ref,
    out_ref,
    merged_ref,
    second_ref,
    active_ref,
    branch_grad_ref,
    expanded_grad_ref,
    cross_grad_ref,
    resid_ref,
    payload_ref,
    small_ref,
    wide_ref,
    expanded_scr,
    output_scr,
    expand_scr,
    contract_scr,
    sems,
):
    fetch = copies(
        [(output_ref, output_scr), (expand_ref, expand_scr), (contract_ref, contract_scr)], sems
    )
    start_all(fetch)
    bias = bias_ref[...].astype(F32)
    gain = gain_ref[...].astype(F32)
    shift = shift_ref[...].astype(F32)
    parts = [p0_ref, p1_ref, p2_ref, p3_ref]
    lses = [read_lse(part[:, D:]) for part in parts]
    top = functools.reduce(jnp.maximum, lses)
    weights = [jnp.exp(lse - top) for lse in lses]
    total = functools.reduce(jnp.add, weights)
    overall = top + jnp.log(total)
    spread = head_spread(False)
    merged = jnp.zeros(first_ref.shape, F32)
    for part, weight in zip(parts, weights):
        share = weight / total
        high = share.astype(LOW)
        rest = (share - high.astype(F32)).astype(LOW)
        merged = merged + (nn(high, spread) + nn(rest, spread)) * part[:, :D].astype(F32)
    merged_low = merged.astype(LOW)
    merged_ref[...] = merged_low
    fetch[0].wait()
    residual = first_ref[...].astype(F32) + nn(merged_low, output_scr[...]) + bias[5:6]
    second, unit_second, scale_second = norm_forward(residual, gain[1:2], shift[1:2])
    second_low = second.astype(LOW)
    second_ref[...] = second_low
    hidden = contract_scr.shape[0]
    fetch[1].wait()
    for c in range(hidden // D):
        at = slice(c * D, (c + 1) * D)
        expanded = nn(second_low, expand_scr[:, at]) + expand_bias_ref[:, at].astype(F32)
        bell = 0.5 * (1.0 + lax.erf(expanded * 0.7071067811865476))
        active_ref[:, at] = (expanded * bell).astype(LOW)
        slope = bell + expanded * 0.3989422804014327 * jnp.exp(-0.5 * expanded * expanded)
        expanded_scr[:, at] = slope
    fetch[2].wait()
    residual = second_low.astype(F32) + nn(active_ref[...], contract_scr[...]) + bias[6:7]
    final, unit_final, scale_final = norm_forward(residual, gain[2:3], shift[2:3])
    out_ref[...] = final.astype(LOW)
    cotangent = cotangent_ref[...].astype(F32)
    final_resid = norm_backward(cotangent, unit_final, scale_final, gain[2:3])
    branch_grad = final_resid.astype(LOW)
    branch_grad_ref[...] = branch_grad
    small_ref[0:1, :] = row_sum(branch_grad.astype(F32))
    small_ref[1:2, :] = row_sum(cotangent * unit_final)
    small_ref[2:3, :] = row_sum(cotangent)
    total_grad = final_resid
    for c in range(hidden // D):
        at = slice(c * D, (c + 1) * D)
        active_grad = nt(branch_grad, contract_scr[at, :])
        expanded_grad = (active_grad * expanded_scr[:, at]).astype(LOW)
        expanded_grad_ref[:, at] = expanded_grad
        wide_ref[:, at] = row_sum(expanded_grad.astype(F32))
        total_grad = total_grad + nt(expanded_grad, expand_scr[:, at])
    small_ref[4:5, :] = row_sum(total_grad * unit_second)
    small_ref[5:6, :] = row_sum(total_grad)
    second_resid = norm_backward(total_grad, unit_second, scale_second, gain[1:2])
    resid_ref[...] = second_resid
    cross_grad = second_resid.astype(LOW)
    cross_grad_ref[...] = cross_grad
    small_ref[3:4, :] = row_sum(cross_grad.astype(F32))
    small_ref[6:8, :] = jnp.zeros((2, D), F32)
    attended_grad = nt(cross_grad, output_scr[...]).astype(LOW)
    payload_ref[:, :D] = attended_grad
    product = attended_grad.astype(F32) * merged
    gather = flag(lanes((D, SLAB)) % 16 == rows_of((D, SLAB)) // HEAD_DIM).astype(LOW)
    high, mid, low = three(product)
    delta = nn(high, gather) + nn(mid, gather) + nn(low, gather)
    lane = lanes(overall.shape)
    packed = jnp.zeros(overall.shape, F32)
    for value, base in ((overall, 0), (delta, 48)):
        for i, piece in enumerate(three(value)):
            inside = (lane >= base + 16 * i) & (lane < base + 16 * i + HEADS)
            packed = jnp.where(inside, piece.astype(F32), packed)
    payload_ref[:, D:] = packed.astype(LOW)


def self_backward_kernel(
    d0_ref,
    d1_ref,
    d2_ref,
    d3_ref,
    resid_ref,
    unit_ref,
    scale_ref,
    heads_ref,
    soft_ref,
    query_ref,
    output_ref,
    project_ref,
    gain_ref,
    pre_grad_ref,
    branch_grad_ref,
    project_grad_ref,
    input_grad_ref,
    small_ref,
    attended_scr,
    query_scr,
    output_scr,
    heads_scr,
    soft_scr,
    project_scr,
    sems,
):
    fetch = copies(
        [
            (query_ref, query_scr),
            (output_ref, output_scr),
            (heads_ref, heads_scr),
            (soft_ref, soft_scr),
            (project_ref, project_scr),
        ],
        sems,
    )
    start_all(fetch)
    tokens = resid_ref.shape[0]
    query_sum = functools.reduce(
        jnp.add, [d[...].astype(F32) for d in (d0_ref, d1_ref, d2_ref, d3_ref)]
    ).astype(LOW)
    pre_grad = (query_sum.astype(F32) * QUERY_SCALE).astype(LOW)
    pre_grad_ref[...] = pre_grad
    fetch[0].wait()
    total = resid_ref[...] + nt(pre_grad, query_scr[...])
    unit = unit_ref[...]
    first_resid = norm_backward(total, unit, scale_ref[...], gain_ref[0:1, :].astype(F32))
    branch_grad = first_resid.astype(LOW)
    branch_grad_ref[...] = branch_grad
    fetch[1].wait()
    attended_scr[...] = nt(branch_grad, output_scr[...]).astype(LOW)
    fetch[2].wait()
    fetch[3].wait()
    first, second = half_masks()
    for p in range(PAIRS):
        at = p * SLAB
        grads = two_heads(attended_scr[:, at : at + SLAB], first, second)
        queries = two_heads(heads_scr[:, at : at + SLAB], first, second)
        keys = heads_scr[:, D + at : D + at + SLAB]
        dots = nt(grads, heads_scr[:, 2 * D + at : 2 * D + at + SLAB])
        soft = soft_scr[p]
        score_grad = (soft * (dots - jnp.sum(soft * dots, axis=-1, keepdims=True))).astype(LOW)
        query_grad = join_heads(nn(score_grad, keys), tokens).astype(LOW)
        project_grad_ref[:, at : at + SLAB] = (query_grad.astype(F32) * QUERY_SCALE).astype(LOW)
        project_grad_ref[:, D + at : D + at + SLAB] = tn(score_grad, queries).astype(LOW)
        project_grad_ref[:, 2 * D + at : 2 * D + at + SLAB] = tn(soft.astype(LOW), grads).astype(
            LOW
        )
    fetch[4].wait()
    input_grad_ref[...] = first_resid + nt(project_grad_ref[...], project_scr[...])
    small_ref[0:1, :] = row_sum(project_grad_ref[:, :D].astype(F32))
    small_ref[1:2, :] = row_sum(project_grad_ref[:, 2 * D :].astype(F32))
    small_ref[2:3, :] = row_sum(branch_grad.astype(F32))
    small_ref[3:4, :] = row_sum(pre_grad.astype(F32))
    small_ref[4:5, :] = row_sum(total * unit)
    small_ref[5:6, :] = row_sum(total)
    small_ref[6:8, :] = jnp.zeros((2, D), F32)


def weight_grad_kernel(plan, count, packed, n_args, place_ref, *refs):
    far_refs, (kept_ref, sent_ref, sems) = refs[-5:-3], refs[-3:]
    me, core = place_ref[0], place_ref[1]
    at_ref = 0
    base = plan[0][3]
    going = []

    def send(at, size):
        for near, far in zip((kept_ref, sent_ref), far_refs):
            item = pltpu.make_async_copy(
                near.at[:, pl.ds(at - base, size), :], far.at[:, pl.ds(at, size), :], sems.at[len(going)]
            )
            item.start()
            going.append(item)

    for number, rows, columns, at in plan:
        pairs = [refs[at_ref + 2 * i : at_ref + 2 * i + 2] for i in range(number)]
        at_ref += 2 * number
        block = rows // count
        half = columns // 2
        for m in range(rows // D):
            xs = [x_ref[:, m * D : (m + 1) * D].T for x_ref, _ in pairs]
            for c in range(0, half, D):
                wide = min(D, half - c)
                for mine, out in ((core, kept_ref), (1 - core, sent_ref)):
                    start = pl.multiple_of(mine * half + c, SLAB)
                    part = sum(
                        nn(x, g_ref[:, pl.ds(start, wide)]) for x, (_, g_ref) in zip(xs, pairs)
                    ).astype(LOW)
                    for u in range(wide // UNIT):
                        low = at - base + (c // UNIT + u) * block
                        for k in range(D // block):
                            to = me ^ (m * (D // block) + k)
                            out[to, low : low + block, :] = part[
                                k * block : (k + 1) * block, u * UNIT : (u + 1) * UNIT
                            ]
        send(at, half // UNIT * block)
    if packed is not None:
        low = packed - base
        pack_small(refs[at_ref : at_ref + 4], kept_ref, sent_ref, low, me, core, count)
        send(packed, RANK_ROWS)
    wait_all(going)


def pack_small(small_refs, kept_ref, sent_ref, low, me, core, count):
    own, middle, value_bias, wide = small_refs
    order = [own[0:4], value_bias[0:1], middle[3:4], middle[0:1], own[4:5], middle[4:5]]
    order += [middle[1:2], own[5:6], middle[5:6], middle[2:3], jnp.zeros((3, D), F32)]
    narrow = jnp.concatenate(order, axis=0)
    share = D // count
    broad = wide.shape[1] // count
    for r in range(count):
        first = narrow[:, r * share : (r + 1) * share]
        first = jnp.concatenate([first, jnp.zeros((RANK_ROWS, UNIT - share), F32)], axis=1)
        second = wide[:, r * broad : (r + 1) * broad]
        second = jnp.concatenate([second, jnp.zeros((1, UNIT - broad), F32)], axis=1)
        second = jnp.broadcast_to(second, (RANK_ROWS, UNIT))
        here = slice(low, low + RANK_ROWS)
        kept_ref[me ^ r, here, :] = jnp.where(core == 0, first, second).astype(LOW)
        sent_ref[me ^ r, here, :] = jnp.where(core == 0, second, first).astype(LOW)


def total_of(*refs):
    return functools.reduce(jnp.add, [ref[...].astype(F32) for ref in refs])


def split_kernel(x, kept_ref, come_ref, *refs):
    far, outs = ((), refs) if x else (refs[:2], refs[2:])
    half = kept_ref.shape[3] // 2
    for z in range(4):
        for g in range(2):
            at = (z, slice(None), x, slice(0, half)) if g == 0 else (z, x, slice(None), slice(half, 2 * half))
            total = kept_ref[at].astype(F32) + come_ref[at].astype(F32)
            if far:
                total = total + far[g][z].astype(F32)
                for i in range(2):
                    outs[2 * g + i][z] = total[i].astype(LOW)
            else:
                outs[g][z] = total.astype(LOW)


def join_kernel(a_keep, a_come, b_keep, b_come, *outs):
    rows = a_keep.shape[1]
    for z, out in enumerate(outs):
        out[:rows] = total_of(a_keep.at[z], a_come.at[z]).astype(LOW)
        out[rows:] = total_of(b_keep.at[z], b_come.at[z]).astype(LOW)


def sum_kernel(*refs):
    refs[-1][...] = total_of(*refs[:-1]).astype(LOW)


def spread_kernel(plan, count, packed, place_ref, own_ref, other_ref, *outs):
    core = place_ref[1]
    for (rows, columns, at), out in zip(plan, outs):
        block = rows // count
        half = columns // 2
        for c in range(half // UNIT):
            low = at + c * block
            for value, mine in ((own_ref, core), (other_ref, 1 - core)):
                start = pl.multiple_of(mine * half + c * UNIT, SLAB)
                out[:, pl.ds(start, UNIT)] = value[low : low + block].astype(F32)
    if packed is not None:
        here = slice(packed, packed + RANK_ROWS)
        own, other = own_ref[here].astype(F32), other_ref[here].astype(F32)
        narrow, wide = jnp.where(core == 0, own, other), jnp.where(core == 0, other, own)
        biases_ref, wide_ref, gain_ref, shift_ref = outs[len(plan) :]
        share = biases_ref.shape[1]
        biases_ref[...] = narrow[0:7, :share]
        gain_ref[...] = narrow[7:10, :share]
        shift_ref[...] = narrow[10:13, :share]
        wide_ref[...] = wide[0:1, : wide_ref.shape[1]]


def swap(v, bits):
    count = lax.axis_size("store")
    return lax.ppermute(v, "store", [(i, i ^ bits) for i in range(count)])


def swap_core(v):
    return lax.ppermute(v, "dp", [(0, 1), (1, 0)])


class WeightSums:
    def __init__(self, place, count, rows):
        self.place, self.count, self.rows = place, count, rows
        self.plan, self.packed, self.at = [], None, 0
        self.buffers = ()

    def add(self, products, small=None, earlier=(), flops=0):
        plan, base, packed = [], self.at, None
        for pairs in products:
            rows, columns = pairs[0][0].shape[1], pairs[0][1].shape[1]
            plan.append((len(pairs), rows, columns, self.at))
            self.plan.append((rows, columns, self.at))
            self.at += rows // self.count * (columns // 2 // UNIT)
        args = [v for pairs in products for pair in pairs for v in pair]
        if small is not None:
            packed = self.packed = self.at
            self.at += RANK_ROWS
            args.extend(small)
        n_args = 1 + len(args)
        shape = (self.count, self.rows, UNIT)
        near = (self.count, self.at - base, UNIT)
        sends = 2 * (len(products) + (small is not None))

        def kernel(*refs):
            refs = refs[:n_args] + refs[n_args + len(self.buffers) :]
            weight_grad_kernel(tuple(plan), self.count, packed, n_args, *refs)

        self.buffers = call(
            kernel,
            [(shape, LOW), (shape, LOW)],
            scratch=[
                pltpu.VMEM(near, LOW),
                pltpu.VMEM(near, LOW),
                pltpu.SemaphoreType.DMA((sends,)),
            ],
            n_smem=1,
            far_in=(n_args, n_args + 1),
            far_out=(0, 1),
            aliases={n_args + i: i for i in range(len(self.buffers))},
            earlier=earlier,
            flops=flops,
        )(self.place, *args, *self.buffers)
        return self.buffers

    def split(self, x, far=(), earlier=()):
        half = (4, 2, self.rows // 2, UNIT)
        outs = [half[:1] + half[2:]] * 4 if far else [half] * 2
        args = [v.reshape(4, 2, 2, self.rows, UNIT) for v in (self.kept, self.come)] + list(far)
        return call(
            functools.partial(split_kernel, x),
            [(shape, LOW) for shape in outs],
            earlier=earlier,
            limit=SMALL_LIMIT,
        )(*args)

    def start(self, earlier=()):
        self.kept, sent = self.buffers
        self.come = swap_core(sent)
        self.sent = self.split(1, earlier=earlier)
        return self.sent

    def first(self, *earlier):
        come = (swap(self.sent[0], 1), swap(self.sent[1], 2))
        a_keep, a_send, b_keep, b_send = self.split(0, come, earlier)
        self.kept, self.sent = (a_keep, b_keep), (a_send, b_send)
        return self.sent

    def second(self, *earlier):
        come = (swap(self.sent[0], 2), swap(self.sent[1], 1))
        self.w = call(
            join_kernel, [((self.rows, UNIT), LOW)] * 4, earlier=earlier, limit=SMALL_LIMIT
        )(self.kept[0], come[0], self.kept[1], come[1])
        return self.w

    def third(self, *earlier):
        come = [swap(self.w[k], 4 * k) for k in (1, 2, 3)]
        (self.own,) = call(
            sum_kernel, [(come[0].shape, LOW)], earlier=earlier, limit=SMALL_LIMIT
        )(self.w[0], *come)
        return self.own

    def finish(self, small=()):
        other = swap_core(self.own)
        shapes = [((rows // self.count, columns), F32) for rows, columns, _ in self.plan]
        shapes += [(shape, F32) for shape in small]
        return call(
            functools.partial(spread_kernel, tuple(self.plan), self.count, self.packed),
            shapes,
            n_smem=1,
            limit=SMALL_LIMIT,
        )(self.place, self.own, other)


def local_tree(
    inputs,
    doc_lengths,
    datastore,
    kept_mask,
    retrieved,
    self_project,
    self_output,
    cross_query,
    cross_memory,
    cross_output,
    expand_weight,
    contract_weight,
    biases,
    expand_bias,
    norm_gain,
    norm_shift,
    cotangent,
):
    tokens = inputs.shape[0]
    count = lax.axis_size("store")
    local_blocks = datastore.shape[0] // BLOCK
    all_blocks = local_blocks * count
    capacity = 2 * tokens * TOPB // all_blocks
    plane_blocks = 4 * local_blocks
    rows_in = 4 * capacity
    hidden = expand_weight.shape[1]
    me = lax.axis_index("store").astype(jnp.int32)
    core = lax.axis_index("dp").astype(jnp.int32)
    place = jnp.stack([me, core])

    marks = kept_mask.reshape(2, 2, BLOCK).astype(LOW)
    marks = jnp.pad(marks, ((0, 0), (0, RANK_ROWS - 2), (0, D - BLOCK)))
    halves = datastore.reshape(2, 2 * BLOCK, D)
    a0, b0 = (jnp.concatenate([halves[h], marks[h]]) for h in range(2))
    a1, b1 = swap(a0, 1), swap(b0, 2)
    heads_all, soft_self, attended, unit_first, scale_first, first_low, *queries = call(
        self_forward_kernel,
        [
            ((tokens, 3 * D), LOW),
            ((PAIRS, 2 * tokens, tokens), F32),
            ((tokens, D), LOW),
            ((tokens, D), F32),
            ((tokens, 1), F32),
            ((tokens, D), LOW),
        ]
        + [((tokens + RANK_ROWS, D), LOW)] * 4,
        scratch=[
            pltpu.VMEM((D, 3 * D), LOW),
            pltpu.VMEM((D, D), LOW),
            pltpu.VMEM((D, D), LOW),
            pltpu.SemaphoreType.DMA((5,)),
        ],
        n_smem=2,
        far_in=(4, 5, 6),
        flops=8 * MICROSECOND,
    )(
        doc_lengths,
        place,
        inputs,
        retrieved.T,
        self_project,
        self_output,
        cross_query,
        biases,
        norm_gain,
        norm_shift,
    )
    ay = swap(after(jnp.stack([a0, a1]), first_low), 2)
    bx = swap(after(jnp.stack([b0, b1]), first_low), 1)
    queries = [queries[0]] + [swap(queries[k], 4 * k) for k in (1, 2, 3)]

    one_set = [
        ((4 * BLOCK, D), LOW),
        ((4, BLOCK, 2 * D), LOW),
        ((4, 1, BLOCK), F32),
        ((4, BLOCK, SLAB), LOW),
    ]
    memory_call = call(
        memory_kernel,
        one_set * 2,
    )
    near = memory_call(a0, a1, b0, b1, cross_memory, biases)
    far = memory_call(ay[0], ay[1], bx[0], bx[1], cross_memory, biases)
    sets = [near[:4], far[:4], near[4:], far[4:]]
    stored, memory, hidden_rows, key_side = zip(*sets)

    slots, *payloads = call(
        functools.partial(owner_forward_kernel, capacity),
        [((plane_blocks, rows_in, D), LOW)] + [((tokens, WIDE), LOW)] * 4,
        scratch=[
            pltpu.VMEM((plane_blocks, rows_in, D), F32),
            pltpu.VMEM((plane_blocks, rows_in, SLAB), F32),
            pltpu.VMEM((plane_blocks, rows_in, SLAB), F32),
            pltpu.VMEM((4, plane_blocks * capacity, tokens), LOW),
            pltpu.VMEM((RANK_ROWS, tokens), F32),
            pltpu.VMEM((plane_blocks, rows_in, D), LOW),
            pltpu.VMEM((4, 4, BLOCK, 2 * D), LOW),
            pltpu.SemaphoreType.DMA((4,)),
            pltpu.SemaphoreType.DMA((1,)),
        ],
        far_in=(4, 5, 6, 7),
        far_out=(0,),
        flops=20 * MICROSECOND,
    )(*queries, *memory, *hidden_rows)
    parts = [payloads[0]] + [swap(payloads[k], 4 * k) for k in (1, 2, 3)]

    (
        outputs,
        merged_low,
        second_low,
        active_low,
        branch_grad,
        expanded_grad,
        cross_grad,
        second_resid,
        payload,
        small_middle,
        wide_bias,
    ) = call(
        middle_kernel,
        [
            ((tokens, D), LOW),
            ((tokens, D), LOW),
            ((tokens, D), LOW),
            ((tokens, hidden), LOW),
            ((tokens, D), LOW),
            ((tokens, hidden), LOW),
            ((tokens, D), LOW),
            ((tokens, D), F32),
            ((tokens, WIDE), LOW),
            ((8, D), F32),
            ((1, hidden), F32),
        ],
        scratch=[
            pltpu.VMEM((tokens, hidden), F32),
            pltpu.VMEM((D, D), LOW),
            pltpu.VMEM((D, hidden), LOW),
            pltpu.VMEM((hidden, D), LOW),
            pltpu.SemaphoreType.DMA((3,)),
        ],
        far_in=(6, 7, 8),
        flops=12 * MICROSECOND,
    )(
        *parts,
        first_low,
        cotangent,
        cross_output,
        expand_weight,
        contract_weight,
        biases,
        expand_bias.reshape(1, hidden),
        norm_gain,
        norm_shift,
    )
    grads = [payload] + [swap(payload, 4 * k) for k in (1, 2, 3)]

    early = WeightSums(place, count, 432)
    early.add(
        [[(active_low, branch_grad)], [(merged_low, cross_grad)], [(second_low, expanded_grad)]],
        flops=8 * MICROSECOND,
    )
    early_start = early.start()

    out = call(
        functools.partial(owner_backward_kernel, capacity),
        [((4, BLOCK, 2 * D), LOW)] * 4 + [((tokens, D), LOW)] * 4 + [((8, D), F32)],
        scratch=[
            pltpu.VMEM((plane_blocks, rows_in, WIDE), LOW),
            pltpu.VMEM((plane_blocks, rows_in, D), LOW),
            pltpu.VMEM((4, plane_blocks * capacity, tokens), LOW),
            pltpu.VMEM((RANK_ROWS, tokens), F32),
            pltpu.VMEM((plane_blocks, rows_in, D), LOW),
            pltpu.VMEM((4, 4, BLOCK, 2 * D), LOW),
            pltpu.VMEM((4, 4, BLOCK, 2 * D), LOW),
            pltpu.SemaphoreType.DMA((5,)),
            pltpu.SemaphoreType.DMA((4,)),
        ],
        far_in=(8, 9, 10, 11, 16),
        far_out=(0, 1, 2, 3),
        earlier=early_start,
        flops=LONG,
    )(*queries, *grads, *memory, *key_side, slots)
    memory_grads, query_grads, value_bias_grad = out[:4], out[4:8], out[8]
    parts = [query_grads[0]] + [swap(query_grads[k], 4 * k) for k in (1, 2, 3)]

    early_first = early.first(memory_grads[0])
    late = WeightSums(place, count, 352)
    flat_grads = [v.reshape(4 * BLOCK, 2 * D) for v in memory_grads]
    late.buffers = call(
        functools.partial(memory_weight_kernel, count),
        [((count, late.rows, UNIT), LOW)] * 2,
        scratch=[
            pltpu.VMEM((count, 2 * D // count, UNIT), LOW),
            pltpu.VMEM((count, 2 * D // count, UNIT), LOW),
            pltpu.VMEM((4, 4 * BLOCK, 2 * D), LOW),
            pltpu.VMEM((4, 4 * BLOCK, D), LOW),
            pltpu.VMEM((2, D, D), F32),
            pltpu.SemaphoreType.DMA((4, 2)),
            pltpu.SemaphoreType.DMA((2,)),
        ],
        n_smem=1,
        far_in=range(1, 9),
        far_out=(0, 1),
        earlier=early_first,
        flops=MICROSECOND // 10,
    )(place, *flat_grads, *stored)
    late.plan, late.at = [(D, 2 * D, 0)], 2 * D // count

    pre_grad, self_branch_grad, project_grad, input_grad, small_self = call(
        self_backward_kernel,
        [
            ((tokens, D), LOW),
            ((tokens, D), LOW),
            ((tokens, 3 * D), LOW),
            ((tokens, D), F32),
            ((8, D), F32),
        ],
        scratch=[
            pltpu.VMEM((tokens, D), LOW),
            pltpu.VMEM((D, D), LOW),
            pltpu.VMEM((D, D), LOW),
            pltpu.VMEM((tokens, 3 * D), LOW),
            pltpu.VMEM((PAIRS, 2 * tokens, tokens), F32),
            pltpu.VMEM((D, 3 * D), LOW),
            pltpu.SemaphoreType.DMA((5,)),
        ],
        far_in=(7, 8, 9, 10, 11),
        earlier=(late.buffers[0],),
        flops=LONG // 3,
    )(
        *parts,
        second_resid,
        unit_first,
        scale_first,
        heads_all,
        soft_self,
        cross_query,
        self_output,
        self_project,
        norm_gain,
    )
    early_second = early.second()
    late.add(
        [[(attended, self_branch_grad)], [(first_low, pre_grad)], [(inputs, project_grad)]],
        (small_self, small_middle, value_bias_grad, wide_bias),
        earlier=(early_second[0],),
        flops=MICROSECOND // 10,
    )
    near_a0, near_a1, far_a, near_b0, near_b1, far_b = call(
        datastore_grad_kernel,
        [((2 * BLOCK, D), LOW), ((2 * BLOCK, D), LOW), ((4 * BLOCK, D), LOW)] * 2,
        scratch=[pltpu.VMEM((4, 4 * BLOCK, 2 * D), LOW), pltpu.SemaphoreType.DMA((4,))],
        far_in=range(1, 5),
        earlier=(late.buffers[0],),
        flops=MICROSECOND // 10,
    )(cross_memory, *flat_grads)
    late.start(earlier=(far_a,))
    late_first = late.first()
    early.third(late_first[0])
    contract_weight_grad, cross_output_grad, expand_weight_grad = early.finish()
    late.second(contract_weight_grad)
    near_two = 2 * BLOCK
    far_a, far_b = (after(v, late.w[0]) for v in (far_a, far_b))
    come_a, come_b = swap(far_a, 2), swap(far_b, 1)
    send_a = near_a1 + come_a[near_two:]
    send_b = near_b1 + come_b[near_two:]
    last_a, last_b = swap(send_a, 1), swap(send_b, 2)
    datastore_grad = jnp.concatenate(
        [
            near.astype(F32) + come[:near_two].astype(F32) + last.astype(F32)
            for near, come, last in ((near_a0, come_a, last_a), (near_b0, come_b, last_b))
        ]
    )
    late.third(come_a, come_b)
    share = D // count
    (
        cross_memory_grad,
        self_output_grad,
        cross_query_grad,
        self_project_grad,
        biases_grad,
        wide_grad,
        gain_grad,
        shift_grad,
    ) = late.finish([(7, share), (1, hidden // count), (3, share), (3, share)])
    return (
        outputs,
        input_grad,
        datastore_grad,
        self_project_grad,
        self_output_grad,
        cross_query_grad,
        cross_memory_grad,
        cross_output_grad,
        expand_weight_grad,
        contract_weight_grad,
        biases_grad,
        wide_grad.reshape(hidden // count),
        gain_grad,
        shift_grad,
    )


def layer_norm(residual, gain_row, shift_row):
    center = residual - jnp.mean(residual, axis=-1, keepdims=True)
    spread = jnp.mean(center * center, axis=-1, keepdims=True)
    return center * lax.rsqrt(spread + EPSILON) * gain_row + shift_row


def doc_mask(lengths, seq_tokens):
    upto = jnp.tri(lengths.shape[-1], dtype=jnp.int32)
    bounds = jnp.sum(lengths[..., None, :] * upto, axis=-1)
    places = jnp.arange(seq_tokens, dtype=jnp.int32)
    segment = jnp.sum((places[:, None] >= bounds[..., None, :]).astype(jnp.int32), axis=-1)
    causal = places[:, None] >= places[None, :]
    return (segment[..., :, None] == segment[..., None, :]) & causal


def slot_numbers(picks, capacity):
    flat_ids = picks.reshape(-1)
    sorter = jnp.argsort(flat_ids, stable=True)
    sorted_ids = flat_ids[sorter]
    first_seen = jnp.searchsorted(sorted_ids, sorted_ids, side="left")
    rank_sorted = jnp.arange(flat_ids.shape[0], dtype=jnp.int32) - first_seen
    ranks = jnp.zeros_like(flat_ids).at[sorter].set(rank_sorted)
    return flat_ids * capacity + ranks


def place_rows(rows, slot_ids, total_slots, store_count, local_blocks, capacity):
    placed = jnp.zeros((total_slots, rows.shape[1]), rows.dtype).at[slot_ids].set(rows)
    return placed.reshape(store_count, local_blocks, capacity, rows.shape[1])


def local_slots(
    inputs,
    doc_lengths,
    datastore,
    kept_mask,
    retrieved,
    self_project,
    self_output,
    cross_query,
    cross_memory,
    cross_output,
    expand_weight,
    contract_weight,
    biases,
    expand_bias,
    norm_gain,
    norm_shift,
    cotangent,
):
    tok_count = inputs.shape[0]
    store_count = lax.axis_size("store")
    local_blocks = datastore.shape[0] // BLOCK
    all_blocks = local_blocks * store_count
    capacity = 2 * tok_count * TOPB // all_blocks
    rows_in = store_count * capacity
    total_slots = all_blocks * capacity
    gain_rows = norm_gain.astype(jnp.float32)
    shift_rows = norm_shift.astype(jnp.float32)
    bias_rows = biases.astype(jnp.float32)
    projected = jnp.dot(inputs, self_project, preferred_element_type=jnp.float32)
    heads_all = jnp.concatenate(
        [
            QUERY_SCALE * (projected[:, :D] + bias_rows[0]),
            projected[:, D : 2 * D],
            projected[:, 2 * D :] + bias_rows[1],
        ],
        axis=1,
    ).astype(jnp.bfloat16)
    queries = heads_all[:, :D].reshape(tok_count, HEADS, HEAD_DIM)
    keys_self = heads_all[:, D : 2 * D].reshape(tok_count, HEADS, HEAD_DIM)
    values_self = heads_all[:, 2 * D :].reshape(tok_count, HEADS, HEAD_DIM)
    allowed = doc_mask(doc_lengths[0], tok_count)

    def self_scores():
        raw_scores = jnp.einsum(
            "qhd,khd->hqk", queries, keys_self, preferred_element_type=jnp.float32
        )
        return jnp.where(allowed[None], raw_scores, MASKED)

    scores = self_scores()
    self_lse = jax.nn.logsumexp(scores, axis=-1)
    soft_low = jnp.exp(scores - self_lse[..., None]).astype(jnp.bfloat16)
    attended = (
        jnp.einsum("hqk,khd->qhd", soft_low, values_self, preferred_element_type=jnp.float32)
        .reshape(tok_count, D)
        .astype(jnp.bfloat16)
    )
    self_branch = jnp.dot(attended, self_output, preferred_element_type=jnp.float32) + bias_rows[2]
    first_norm, first_back = jax.vjp(
        layer_norm, inputs.astype(jnp.float32) + self_branch, gain_rows[0], shift_rows[0]
    )
    first_low = first_norm.astype(jnp.bfloat16)
    cross_queries = (
        QUERY_SCALE
        * (jnp.dot(first_low, cross_query, preferred_element_type=jnp.float32) + bias_rows[3])
    ).astype(jnp.bfloat16)
    slot_ids = slot_numbers(retrieved, capacity)
    send_buffer = place_rows(
        jnp.repeat(cross_queries, TOPB, axis=0),
        slot_ids,
        total_slots,
        store_count,
        local_blocks,
        capacity,
    )
    arrived = lax.all_to_all(send_buffer, "store", split_axis=0, concat_axis=2, tiled=True)
    owner_queries = arrived[0].reshape(local_blocks, rows_in, HEADS, HEAD_DIM)
    memory_bias = jnp.concatenate([jnp.zeros((D,), jnp.float32), bias_rows[4]])
    memory_low = (
        jnp.dot(datastore, cross_memory, preferred_element_type=jnp.float32) + memory_bias
    ).astype(jnp.bfloat16)
    memory_blocks = memory_low.reshape(local_blocks, BLOCK, 2 * D)
    store_keys = memory_blocks[:, :, :D].reshape(local_blocks, BLOCK, HEADS, HEAD_DIM)
    store_values = memory_blocks[:, :, D:].reshape(local_blocks, BLOCK, HEADS, HEAD_DIM)
    kept_rows = kept_mask.reshape(local_blocks, BLOCK) > 0

    def block_scores(query_blocks):
        raw_scores = jnp.einsum(
            "bmhd,bkhd->bhmk", query_blocks, store_keys, preferred_element_type=jnp.float32
        )
        return jnp.where(kept_rows[:, None, None, :], raw_scores, MASKED)

    owner_scores = block_scores(owner_queries)
    owner_lse = jax.nn.logsumexp(owner_scores, axis=-1)
    owner_soft = jnp.exp(owner_scores - owner_lse[..., None]).astype(jnp.bfloat16)
    partial_value = jnp.einsum(
        "bhmk,bkhd->bmhd", owner_soft, store_values, preferred_element_type=jnp.float32
    ).reshape(local_blocks, rows_in, D)
    partial_lse = jnp.transpose(owner_lse, (0, 2, 1))
    returned, returned_lse = (
        lax.all_to_all(partial_value[None], "store", split_axis=2, concat_axis=0, tiled=True),
        lax.all_to_all(partial_lse[None], "store", split_axis=2, concat_axis=0, tiled=True),
    )
    picked = returned.reshape(total_slots, D)[slot_ids].reshape(tok_count, TOPB, HEADS, HEAD_DIM)
    picked_lse = returned_lse.reshape(total_slots, HEADS)[slot_ids].reshape(tok_count, TOPB, HEADS)
    overall = jax.nn.logsumexp(picked_lse, axis=1)
    mix_weights = jnp.exp(picked_lse - overall[:, None, :])
    merged = jnp.einsum(
        "tjh,tjhd->thd", mix_weights, picked, precision=lax.Precision.HIGHEST
    ).reshape(tok_count, D)
    merged_low = merged.astype(jnp.bfloat16)
    cross_branch = (
        jnp.dot(merged_low, cross_output, preferred_element_type=jnp.float32) + bias_rows[5]
    )
    second_norm, second_back = jax.vjp(
        layer_norm, first_low.astype(jnp.float32) + cross_branch, gain_rows[1], shift_rows[1]
    )
    second_low = second_norm.astype(jnp.bfloat16)
    expanded = jnp.dot(
        second_low, expand_weight, preferred_element_type=jnp.float32
    ) + expand_bias.astype(jnp.float32)
    activated, gelu_back = jax.vjp(
        lambda pre_act: jax.nn.gelu(pre_act, approximate=False), expanded
    )
    activated_low = activated.astype(jnp.bfloat16)
    ffn_branch = (
        jnp.dot(activated_low, contract_weight, preferred_element_type=jnp.float32) + bias_rows[6]
    )
    final_norm, final_back = jax.vjp(
        layer_norm, second_low.astype(jnp.float32) + ffn_branch, gain_rows[2], shift_rows[2]
    )
    outputs = final_norm.astype(jnp.bfloat16)
    final_resid, final_gain, final_shift = final_back(cotangent.astype(jnp.float32))
    ffn_branch_grad = final_resid.astype(jnp.bfloat16)
    contract_weight_grad = jnp.dot(
        activated_low.T, ffn_branch_grad, preferred_element_type=jnp.float32
    )
    activated_grad = jnp.dot(ffn_branch_grad, contract_weight.T, preferred_element_type=jnp.float32)
    (expanded_raw,) = gelu_back(activated_grad)
    expanded_grad = expanded_raw.astype(jnp.bfloat16)
    expand_weight_grad = jnp.dot(second_low.T, expanded_grad, preferred_element_type=jnp.float32)
    expand_bias_grad = jnp.sum(expanded_grad.astype(jnp.float32), axis=0)
    second_total = final_resid + jnp.dot(
        expanded_grad, expand_weight.T, preferred_element_type=jnp.float32
    )
    second_resid, second_gain, second_shift = second_back(second_total)
    cross_branch_grad = second_resid.astype(jnp.bfloat16)
    cross_output_grad = jnp.dot(merged_low.T, cross_branch_grad, preferred_element_type=jnp.float32)
    attended_grad = jnp.dot(
        cross_branch_grad, cross_output.T, preferred_element_type=jnp.float32
    ).astype(jnp.bfloat16)
    delta_rows = jnp.sum(
        attended_grad.reshape(tok_count, HEADS, HEAD_DIM).astype(jnp.float32)
        * merged.reshape(tok_count, HEADS, HEAD_DIM),
        axis=-1,
    )
    grad_buffer = place_rows(
        jnp.repeat(attended_grad, TOPB, axis=0),
        slot_ids,
        total_slots,
        store_count,
        local_blocks,
        capacity,
    )
    overall_buffer = place_rows(
        jnp.repeat(overall, TOPB, axis=0),
        slot_ids,
        total_slots,
        store_count,
        local_blocks,
        capacity,
    )
    delta_buffer = place_rows(
        jnp.repeat(delta_rows, TOPB, axis=0),
        slot_ids,
        total_slots,
        store_count,
        local_blocks,
        capacity,
    )
    arrived_grad = lax.all_to_all(grad_buffer, "store", split_axis=0, concat_axis=2, tiled=True)
    arrived_overall, arrived_delta = (
        lax.all_to_all(overall_buffer, "store", split_axis=0, concat_axis=2, tiled=True),
        lax.all_to_all(delta_buffer, "store", split_axis=0, concat_axis=2, tiled=True),
    )
    owner_grad = arrived_grad[0].reshape(local_blocks, rows_in, HEADS, HEAD_DIM)
    overall_heads = jnp.transpose(arrived_overall[0], (0, 2, 1))
    delta_heads = jnp.transpose(arrived_delta[0], (0, 2, 1))
    soft_again = jnp.exp(block_scores(owner_queries) - owner_lse[..., None])
    soft_again_low = soft_again.astype(jnp.bfloat16).astype(jnp.float32)
    weight_mix = jnp.exp(owner_lse - overall_heads)
    value_dots = jnp.einsum(
        "bmhd,bkhd->bhmk", owner_grad, store_values, preferred_element_type=jnp.float32
    )
    exact_sum = jnp.sum(soft_again * value_dots, axis=-1, keepdims=True)
    rounded_sum = jnp.sum(soft_again_low * value_dots, axis=-1, keepdims=True)
    score_grad = (
        weight_mix[..., None]
        * soft_again
        * (value_dots - exact_sum + rounded_sum - delta_heads[..., None])
    ).astype(jnp.bfloat16)
    query_grad = (
        jnp.einsum("bhmk,bkhd->bmhd", score_grad, store_keys, preferred_element_type=jnp.float32)
        .astype(jnp.bfloat16)
        .reshape(local_blocks, rows_in, D)
    )
    key_grad = jnp.einsum(
        "bhmk,bmhd->bkhd", score_grad, owner_queries, preferred_element_type=jnp.float32
    )
    weighted_soft = weight_mix[..., None] * soft_again_low
    value_grad = jnp.einsum(
        "bhmk,bmhd->bkhd",
        weighted_soft,
        owner_grad.astype(jnp.float32),
        precision=lax.Precision.HIGHEST,
    )
    row_count = local_blocks * BLOCK
    memory_grad = jnp.concatenate(
        [key_grad.reshape(row_count, D), value_grad.reshape(row_count, D)], axis=1
    ).astype(jnp.bfloat16)
    cross_memory_grad = jnp.dot(datastore.T, memory_grad, preferred_element_type=jnp.float32)
    value_bias_grad = jnp.sum(memory_grad[:, D:].astype(jnp.float32), axis=0)
    datastore_grad = jnp.dot(memory_grad, cross_memory.T, preferred_element_type=jnp.float32)
    returned_grad = lax.all_to_all(
        query_grad[None], "store", split_axis=2, concat_axis=0, tiled=True
    )
    per_pick = returned_grad.reshape(total_slots, D)[slot_ids].reshape(tok_count, TOPB, D)
    query_sum = jnp.sum(per_pick.astype(jnp.float32), axis=1).astype(jnp.bfloat16)
    cross_pre_grad = (query_sum.astype(jnp.float32) * QUERY_SCALE).astype(jnp.bfloat16)
    cross_query_grad = jnp.dot(first_low.T, cross_pre_grad, preferred_element_type=jnp.float32)
    first_total = second_resid + jnp.dot(
        cross_pre_grad, cross_query.T, preferred_element_type=jnp.float32
    )
    first_resid, first_gain, first_shift = first_back(first_total)
    self_branch_grad = first_resid.astype(jnp.bfloat16)
    self_output_grad = jnp.dot(attended.T, self_branch_grad, preferred_element_type=jnp.float32)
    self_attended_grad = (
        jnp.dot(self_branch_grad, self_output.T, preferred_element_type=jnp.float32)
        .astype(jnp.bfloat16)
        .reshape(tok_count, HEADS, HEAD_DIM)
    )
    soft_self = jnp.exp(self_scores() - self_lse[..., None])
    soft_dots = jnp.einsum(
        "qhd,khd->hqk", self_attended_grad, values_self, preferred_element_type=jnp.float32
    )
    self_score_grad = (
        soft_self * (soft_dots - jnp.sum(soft_self * soft_dots, axis=-1, keepdims=True))
    ).astype(jnp.bfloat16)
    query_self_grad = jnp.einsum(
        "hqk,khd->qhd", self_score_grad, keys_self, preferred_element_type=jnp.float32
    ).reshape(tok_count, D)
    key_self_grad = jnp.einsum(
        "hqk,qhd->khd", self_score_grad, queries, preferred_element_type=jnp.float32
    ).reshape(tok_count, D)
    value_self_grad = jnp.einsum(
        "hqk,qhd->khd", soft_low, self_attended_grad, preferred_element_type=jnp.float32
    ).reshape(tok_count, D)
    heads_grad = jnp.concatenate([query_self_grad, key_self_grad, value_self_grad], axis=1).astype(
        jnp.bfloat16
    )
    project_grad = jnp.concatenate(
        [
            (heads_grad[:, :D].astype(jnp.float32) * QUERY_SCALE).astype(jnp.bfloat16),
            heads_grad[:, D:],
        ],
        axis=1,
    )
    self_project_grad = jnp.dot(inputs.T, project_grad, preferred_element_type=jnp.float32)
    input_grad = first_resid + jnp.dot(
        project_grad, self_project.T, preferred_element_type=jnp.float32
    )
    biases_grad = jnp.stack(
        [
            jnp.sum(project_grad[:, :D].astype(jnp.float32), axis=0),
            jnp.sum(project_grad[:, 2 * D :].astype(jnp.float32), axis=0),
            jnp.sum(self_branch_grad.astype(jnp.float32), axis=0),
            jnp.sum(cross_pre_grad.astype(jnp.float32), axis=0),
            value_bias_grad,
            jnp.sum(cross_branch_grad.astype(jnp.float32), axis=0),
            jnp.sum(ffn_branch_grad.astype(jnp.float32), axis=0),
        ]
    )
    gain_grad = jnp.stack([first_gain, second_gain, final_gain])
    shift_grad = jnp.stack([first_shift, second_shift, final_shift])
    shared = (
        lax.psum_scatter(self_project_grad, "store", scatter_dimension=0, tiled=True),
        lax.psum_scatter(self_output_grad, "store", scatter_dimension=0, tiled=True),
        lax.psum_scatter(cross_query_grad, "store", scatter_dimension=0, tiled=True),
        lax.psum_scatter(cross_memory_grad, "store", scatter_dimension=0, tiled=True),
        lax.psum_scatter(cross_output_grad, "store", scatter_dimension=0, tiled=True),
        lax.psum_scatter(expand_weight_grad, "store", scatter_dimension=0, tiled=True),
        lax.psum_scatter(contract_weight_grad, "store", scatter_dimension=0, tiled=True),
        lax.psum_scatter(biases_grad, "store", scatter_dimension=1, tiled=True),
        lax.psum_scatter(expand_bias_grad, "store", scatter_dimension=0, tiled=True),
        lax.psum_scatter(gain_grad, "store", scatter_dimension=1, tiled=True),
        lax.psum_scatter(shift_grad, "store", scatter_dimension=1, tiled=True),
    )
    reduced = (
        lax.psum(shared[0].astype(jnp.bfloat16), "dp").astype(jnp.float32),
        lax.psum(shared[1].astype(jnp.bfloat16), "dp").astype(jnp.float32),
        lax.psum(shared[2].astype(jnp.bfloat16), "dp").astype(jnp.float32),
        lax.psum(shared[3].astype(jnp.bfloat16), "dp").astype(jnp.float32),
        lax.psum(shared[4].astype(jnp.bfloat16), "dp").astype(jnp.float32),
        lax.psum(shared[5].astype(jnp.bfloat16), "dp").astype(jnp.float32),
        lax.psum(shared[6].astype(jnp.bfloat16), "dp").astype(jnp.float32),
        lax.psum(shared[7].astype(jnp.bfloat16), "dp").astype(jnp.float32),
        lax.psum(shared[8].astype(jnp.bfloat16), "dp").astype(jnp.float32),
        lax.psum(shared[9].astype(jnp.bfloat16), "dp").astype(jnp.float32),
        lax.psum(shared[10].astype(jnp.bfloat16), "dp").astype(jnp.float32),
    )
    return (
        outputs,
        input_grad,
        datastore_grad,
        reduced[0],
        reduced[1],
        reduced[2],
        reduced[3],
        reduced[4],
        reduced[5],
        reduced[6],
        reduced[7],
        reduced[8],
        reduced[9],
        reduced[10],
    )


def solution(mesh):
    placed = (
        P(("dp", "store"), None),
        P(("dp", "store"), None),
        P(("dp", "store"), None),
        P(("dp", "store")),
        P(("dp", "store"), None),
        P(),
        P(),
        P(),
        P(),
        P(),
        P(),
        P(),
        P(),
        P(),
        P(),
        P(),
        P(("dp", "store"), None),
    )
    return jax.shard_map(
        local_tree if mesh.shape["store"] == 16 else local_slots,
        mesh=mesh,
        in_specs=placed,
        out_specs=(
            P(("dp", "store"), None),
            P(("dp", "store"), None),
            P(("dp", "store"), None),
            P("store", None),
            P("store", None),
            P("store", None),
            P("store", None),
            P("store", None),
            P("store", None),
            P("store", None),
            P(None, "store"),
            P("store"),
            P(None, "store"),
            P(None, "store"),
        ),
        check_vma=False,
    )
```

```python
import functools

import jax
import jax.numpy as jnp
from jax import lax
from jax.experimental import pallas as pl
from jax.experimental.pallas import tpu as pltpu
from jax.sharding import PartitionSpec as P

D = 768
HEADS = 12
HEAD_DIM = 64
TOPB = 8
BLOCK = 128
SLAB = 128
PAIRS = D // SLAB
UNIT = 384
WIDE = D + SLAB
RANK_ROWS = 16

EPSILON = 1e-05
MASKED = -1e30
QUERY_SCALE = 0.125
VMEM_LIMIT = 20 * 1024 * 1024
SMALL_LIMIT = 20 * 1024 * 1024
LONG = 30_000_000_000
MICROSECOND = 50_000_000
LOW = jnp.bfloat16
F32 = jnp.float32

_VMEM = pl.BlockSpec(memory_space=pltpu.VMEM)
_SMEM = pl.BlockSpec(memory_space=pltpu.SMEM)
_ANY = pl.BlockSpec(memory_space=pl.ANY)


def nn(a, b):
    return lax.dot_general(a, b, (((1,), (0,)), ((), ())), preferred_element_type=F32)


def nt(a, b):
    return lax.dot_general(a, b, (((1,), (1,)), ((), ())), preferred_element_type=F32)


def tn(a, b):
    return lax.dot_general(a, b, (((0,), (0,)), ((), ())), preferred_element_type=F32)


def three(v):
    high = v.astype(LOW)
    rest = v - high.astype(F32)
    mid = rest.astype(LOW)
    return high, mid, (rest - mid.astype(F32)).astype(LOW)


def lanes(shape):
    return lax.broadcasted_iota(jnp.int32, shape, len(shape) - 1)


def rows_of(shape):
    return lax.broadcasted_iota(jnp.int32, shape, len(shape) - 2)


def flag(condition):
    return jnp.where(condition, 1.0, 0.0)


def half_masks():
    first = flag(lanes((1, SLAB)) < HEAD_DIM)
    return first.astype(LOW), (1.0 - first).astype(LOW)


def two_heads(slab, first, second):
    return jnp.concatenate([slab * first, slab * second], axis=0)


def join_heads(stacked, count):
    left = lanes((count, SLAB)) < HEAD_DIM
    return jnp.where(left, stacked[:count], stacked[count:])


def norm_forward(residual, gain, shift):
    center = residual - jnp.mean(residual, axis=-1, keepdims=True)
    spread = jnp.mean(center * center, axis=-1, keepdims=True)
    scale = lax.rsqrt(spread + EPSILON)
    unit = center * scale
    return unit * gain + shift, unit, scale


def norm_backward(grad, unit, scale, gain):
    inner = grad * gain
    down = inner - jnp.mean(inner, axis=-1, keepdims=True)
    down = down - unit * jnp.mean(inner * unit, axis=-1, keepdims=True)
    return scale * down


def row_sum(v):
    return jnp.sum(v, axis=0, keepdims=True)


def call(
    kernel,
    outs,
    scratch=(),
    n_smem=0,
    far_in=(),
    far_out=(),
    earlier=(),
    aliases=None,
    flops=0,
    limit=VMEM_LIMIT,
):
    def run(*args):
        count = len(args)

        def body(*refs):
            kernel(*refs[:count], *refs[count + len(earlier) :])

        args = [
            pltpu.with_memory_space_constraint(v, pltpu.HBM) if i in far_in and not aliases else v
            for i, v in enumerate(args)
        ]
        specs = [_ANY if i in far_in else _VMEM for i in range(n_smem, count)]
        return pl.pallas_call(
            body,
            out_shape=[jax.ShapeDtypeStruct(s, t) for s, t in outs],
            in_specs=[_SMEM] * n_smem + specs + [_ANY] * len(earlier),
            out_specs=[_ANY if i in far_out else _VMEM for i in range(len(outs))],
            scratch_shapes=list(scratch),
            input_output_aliases=aliases or {},
            compiler_params=pltpu.CompilerParams(vmem_limit_bytes=limit),
            cost_estimate=pl.CostEstimate(flops=flops, bytes_accessed=0, transcendentals=0),
        )(*args, *earlier)

    return run


def copies(pairs, sems):
    return [pltpu.make_async_copy(a, b, sems.at[i]) for i, (a, b) in enumerate(pairs)]


def after(v, *earlier):
    return call(
        lambda *refs: None,
        [(v.shape, v.dtype)],
        far_in=(0,),
        far_out=(0,),
        earlier=earlier,
        aliases={0: 0},
        limit=1024 * 1024,
    )(v)[0]


def start_all(items):
    for item in items:
        item.start()


def wait_all(items):
    for item in items:
        item.wait()


def plane_ranks(picks_ref, me, k, tokens):
    i = rows_of((RANK_ROWS, tokens))
    group, chip, block = i // 4, (i // 2) % 2, i % 2
    apart = jnp.where(group < 2, 2 * group + chip, 2 * chip + group - 2)
    local = jnp.where(group < 2, block, 2 + block)
    plane = (me // 4) ^ k
    number = plane * 16 + ((me % 4) ^ apart) * 4 + local
    member = jnp.zeros((RANK_ROWS, tokens), F32)
    for j in range(TOPB):
        member = member + flag(picks_ref[j : j + 1, :] == number)
    earlier = flag(rows_of((tokens, tokens)) < lanes((tokens, tokens)))
    rank = nn(member.astype(LOW), earlier.astype(LOW))
    return jnp.where(member > 0.5, rank, -1.0).astype(LOW)


def self_forward_kernel(
    lengths_ref,
    place_ref,
    x_ref,
    picks_ref,
    project_ref,
    output_ref,
    query_ref,
    bias_ref,
    gain_ref,
    shift_ref,
    heads_ref,
    soft_ref,
    attended_ref,
    unit_ref,
    scale_ref,
    first_ref,
    *rest,
):
    payload_refs, (project_scr, output_scr, query_scr, sems) = rest[:4], rest[4:]
    thirds = [slice(i * D, (i + 1) * D) for i in range(3)]
    fetch = copies(
        [(project_ref.at[:, at], project_scr.at[:, at]) for at in thirds]
        + [(output_ref, output_scr), (query_ref, query_scr)],
        sems,
    )
    start_all(fetch)
    tokens = x_ref.shape[0]
    bias = bias_ref[...].astype(F32)
    x = x_ref[...]
    for i, at in enumerate(thirds):
        fetch[i].wait()
        part = nn(x, project_scr[:, at])
        if i == 0:
            part = QUERY_SCALE * (part + bias[0:1])
        if i == 2:
            part = part + bias[1:2]
        heads_ref[:, at] = part.astype(LOW)
    place_row = lax.broadcasted_iota(jnp.int32, (2 * tokens, tokens), 0) % tokens
    place_col = lanes((2 * tokens, tokens))
    segment_row = jnp.zeros((2 * tokens, tokens), jnp.int32)
    segment_col = jnp.zeros((2 * tokens, tokens), jnp.int32)
    bound = 0
    for d in range(lengths_ref.shape[1]):
        bound = bound + lengths_ref[0, d]
        segment_row = segment_row + jnp.where(place_row >= bound, 1, 0)
        segment_col = segment_col + jnp.where(place_col >= bound, 1, 0)
    allowed = (segment_row == segment_col) & (place_row >= place_col)
    first, second = half_masks()
    for p in range(PAIRS):
        at = p * SLAB
        queries = two_heads(heads_ref[:, at : at + SLAB], first, second)
        scores = nt(queries, heads_ref[:, D + at : D + at + SLAB])
        scores = jnp.where(allowed, scores, MASKED)
        top = jnp.max(scores, axis=-1, keepdims=True)
        raised = jnp.exp(scores - top)
        soft = raised / jnp.sum(raised, axis=-1, keepdims=True)
        soft_ref[p] = soft
        mixed = nn(soft.astype(LOW), heads_ref[:, 2 * D + at : 2 * D + at + SLAB])
        attended_ref[:, at : at + SLAB] = join_heads(mixed, tokens).astype(LOW)
    fetch[3].wait()
    residual = x.astype(F32) + nn(attended_ref[...], output_scr[...]) + bias[2:3]
    normed, unit, scale = norm_forward(
        residual, gain_ref[0:1, :].astype(F32), shift_ref[0:1, :].astype(F32)
    )
    unit_ref[...] = unit
    scale_ref[...] = scale
    low = normed.astype(LOW)
    first_ref[...] = low
    fetch[4].wait()
    queries = (QUERY_SCALE * (nn(low, query_scr[...]) + bias[3:4])).astype(LOW)
    for k, out in enumerate(payload_refs):
        out[:tokens] = queries
        out[tokens:, tokens:] = jnp.zeros((RANK_ROWS, D - tokens), LOW)
        out[tokens:, :tokens] = plane_ranks(picks_ref, place_ref[0], k, tokens)


def memory_kernel(*refs):
    sets = (len(refs) - 2) // 6
    pieces, (weight_ref, bias_ref), outs = refs[: 2 * sets], refs[2 * sets : 2 * sets + 2], refs[2 * sets + 2 :]
    bias = bias_ref[4:5, :].astype(F32)
    lane = lanes((RANK_ROWS, SLAB))
    for s in range(sets):
        rows_ref, memory_ref, hidden_ref, side_ref = outs[4 * s : 4 * s + 4]
        for j in range(2):
            piece = pieces[2 * s + j]
            rows = piece[: 2 * BLOCK]
            rows_ref[2 * j * BLOCK : 2 * (j + 1) * BLOCK] = rows
            keys = nn(rows, weight_ref[:, :D]).astype(LOW)
            values = (nn(rows, weight_ref[:, D:]) + bias).astype(LOW)
            marks = piece[2 * BLOCK :, :SLAB]
            for l in range(2):
                at = 2 * j + l
                memory_ref[at, :, :D] = keys[l * BLOCK : (l + 1) * BLOCK]
                memory_ref[at, :, D:] = values[l * BLOCK : (l + 1) * BLOCK]
                hidden_ref[at] = (1.0 - marks[l : l + 1].astype(F32)) * MASKED
                wanted = flag((rows_of((RANK_ROWS, SLAB)) == l) & (lane == SLAB - 1))
                column = tn(marks, wanted.astype(LOW))
                place = lanes((BLOCK, SLAB))
                side = jnp.where(place == SLAB - 1, (1.0 - column) * MASKED, 0.0)
                side_ref[at] = jnp.where(place < 48, -1.0, side).astype(LOW)


def selection(ranks, capacity):
    parts = []
    wanted = rows_of((capacity, ranks.shape[1])).astype(F32)
    for b in range(ranks.shape[0]):
        parts.append(flag(ranks[b : b + 1, :] == wanted).astype(LOW))
    return jnp.concatenate(parts, axis=0)


def fill_slots(sel, rows, out_ref, k, capacity):
    got = nn(sel, rows).astype(LOW)
    for b in range(out_ref.shape[0]):
        out_ref[b, k * capacity : (k + 1) * capacity, :] = got[b * capacity : (b + 1) * capacity]


def around16(v, combine):
    for step in (16, 32, 64):
        v = combine(v, pltpu.roll(v, step, 1))
    return v


def lse_lanes(lse):
    high = lse.astype(LOW).astype(F32)
    rest = lse - high
    mid = rest.astype(LOW).astype(F32)
    low = rest - mid
    lane = lanes(lse.shape)
    packed = jnp.where(
        lane < 16, high, jnp.where(lane < 32, mid, jnp.where(lane < 48, low, 0.0))
    )
    return packed.astype(LOW)


def read_lse(packed):
    return around16(packed.astype(F32), jnp.add)


def head_spread(group):
    row = rows_of((SLAB, D))
    row = row % 16 if group else row
    return flag(row == lanes((SLAB, D)) // HEAD_DIM).astype(LOW)


def owner_forward_kernel(capacity, *refs):
    tokens_refs, memory_refs, hidden_refs = refs[0:4], refs[4:8], refs[8:12]
    slots_ref, payload_refs = refs[12], refs[13:17]
    out_scr, lse_scr, inv_scr, sel_scr, ranks_scr = refs[17:]
    sources = len(tokens_refs)
    blocks, rows = slots_ref.shape[:2]
    tokens = tokens_refs[0].shape[0] - RANK_ROWS
    first, second = half_masks()
    for k in range(sources):
        ranks_scr[...] = tokens_refs[k][tokens:, :tokens].astype(F32)
        sel = selection(ranks_scr[...], capacity)
        sel_scr[k] = sel
        fill_slots(sel, tokens_refs[k][:tokens], slots_ref, k, capacity)
    ones = jnp.ones((BLOCK, SLAB), LOW)
    lane_of = lanes((rows, SLAB))
    for s in range(4):

        def one_block(l, carry, s=s):
            i = 4 * s + l
            hidden = hidden_refs[s][l]
            tops = jnp.zeros((rows, SLAB), F32)
            totals = jnp.ones((rows, SLAB), F32)
            base = (i % 8) * 16
            slabs = [slice(p * SLAB, (p + 1) * SLAB) for p in range(PAIRS)]
            scores = [
                nt(two_heads(slots_ref[i, :, at], first, second), memory_refs[s][l, :, at])
                + hidden
                for at in slabs
            ]
            highest = [jnp.max(v, axis=-1, keepdims=True) for v in scores]
            raised = [jnp.exp(v - top).astype(LOW) for v, top in zip(scores, highest)]
            mixed = [
                nn(v, jnp.concatenate([memory_refs[s][l, :, D + at.start : D + at.stop], ones], axis=1))
                for v, at in zip(raised, slabs)
            ]
            for p, at in enumerate(slabs):
                out_scr[i, :, at] = join_heads(mixed[p][:, :SLAB], rows)
                for half in range(2):
                    here = slice(half * rows, (half + 1) * rows)
                    mine = lane_of == base + 2 * p + half
                    tops = jnp.where(mine, highest[p][here], tops)
                    totals = jnp.where(mine, mixed[p][here, SLAB:], totals)
            own = flag((lane_of >= base) & (lane_of < base + HEADS))
            lse_scr[i] = tops + jnp.log(totals)
            inv_scr[i] = own / totals
            return carry

        lax.fori_loop(0, 4, one_block, 0)
    group = 8 * capacity
    own_low = flag(
        rows_of((group, SLAB)) // capacity == lanes((group, SLAB)) // 16
    ).astype(LOW)
    spread = head_spread(True)
    for k in range(sources):
        here = slice(k * capacity, (k + 1) * capacity)

        def stacked(ref, g, here=here):
            return jnp.concatenate([ref[8 * g + b, here, :] for b in range(8)], axis=0)

        by_token, members, sels = [], [], []
        for g in range(2):
            sel = sel_scr[k, g * group : (g + 1) * group, :]
            value = sum(tn(sel, part) for part in three(stacked(lse_scr, g)))
            member = tn(sel, own_low)
            by_token.append(jnp.where(member > 0.5, value, MASKED))
            members.append(member)
            sels.append(sel)
        top = around16(jnp.maximum(*by_token), jnp.maximum)
        weights = [m * jnp.exp(v - top) for m, v in zip(members, by_token)]
        total = around16(weights[0] + weights[1], jnp.add)
        some = total > 0.5
        safe = jnp.where(some, total, 1.0)
        payload_refs[k][:, D:] = lse_lanes(jnp.where(some, top + jnp.log(safe), MASKED))
        partial = jnp.zeros((tokens, D), F32)
        for g in range(2):
            share = nn(sels[g], (weights[g] / safe).astype(LOW)) * stacked(inv_scr, g)
            value = stacked(out_scr, g) * nn(share.astype(LOW), spread)
            partial = partial + tn(sels[g], value.astype(LOW))
        payload_refs[k][:, :D] = partial.astype(LOW)


def owner_backward_kernel(capacity, *refs):
    tokens_refs, grad_refs, memory_refs, side_refs = refs[0:4], refs[4:8], refs[8:12], refs[12:16]
    slots_ref = refs[16]
    grad_outs, payload_refs, bias_ref = refs[17:21], refs[21:25], refs[25]
    got_scr, query_scr, sel_scr, ranks_scr = refs[26:]
    sources = len(tokens_refs)
    blocks, rows = slots_ref.shape[:2]
    tokens = grad_refs[0].shape[0]
    first, second = half_masks()
    for k in range(sources):
        ranks_scr[...] = tokens_refs[k][tokens:, :tokens].astype(F32)
        sel = selection(ranks_scr[...], capacity)
        sel_scr[k] = sel
        fill_slots(sel, grad_refs[k][...], got_scr, k, capacity)
    lane = lanes((1, SLAB))
    last = flag(lane == SLAB - 1).astype(LOW)
    value_side = jnp.broadcast_to(
        -flag((lane >= 48) & (lane < 96)).astype(LOW), (BLOCK, SLAB)
    )

    def picked(head, base):
        inside = (lane >= base) & (lane < base + 48)
        return flag(inside & (lane % 16 == head)).astype(LOW)

    for s in range(4):

        def one_block(l, carry, s=s):
            i = 4 * s + l
            side = got_scr[i, :, D:]
            key_side = side_refs[s][l]
            slabs = [slice(p * SLAB, (p + 1) * SLAB) for p in range(PAIRS)]
            keys = [memory_refs[s][l, :, at] for at in slabs]
            queries = [two_heads(slots_ref[i, :, at], first, second) for at in slabs]
            grads = [two_heads(got_scr[i, :, at], first, second) for at in slabs]
            scores, dots = [], []
            for p in range(PAIRS):
                lse_side = jnp.concatenate(
                    [side * picked(2 * p + h, 0) + last for h in range(2)], axis=0
                )
                scores.append(
                    nt(
                        jnp.concatenate([keys[p], key_side], axis=1),
                        jnp.concatenate([queries[p], lse_side], axis=1),
                    )
                )
            for p, at in enumerate(slabs):
                delta_side = jnp.concatenate(
                    [side * picked(2 * p + h, 48) for h in range(2)], axis=0
                )
                values = memory_refs[s][l, :, D + at.start : D + at.stop]
                dots.append(
                    nt(
                        jnp.concatenate([values, value_side], axis=1),
                        jnp.concatenate([grads[p], delta_side], axis=1),
                    )
                )
            softs = [jnp.exp(v) for v in scores]
            score_grads = [(soft * v).astype(LOW) for soft, v in zip(softs, dots)]
            out = grad_outs[s]
            for p, at in enumerate(slabs):
                query_scr[i, :, at] = join_heads(tn(score_grads[p], keys[p]), rows).astype(LOW)
            for p, at in enumerate(slabs):
                out[l, :, at] = nn(score_grads[p], queries[p]).astype(LOW)
            for p, at in enumerate(slabs):
                out[l, :, D + at.start : D + at.stop] = nn(softs[p].astype(LOW), grads[p]).astype(
                    LOW
                )
            return carry

        lax.fori_loop(0, 4, one_block, 0)
    for k in range(sources):
        here = slice(k * capacity, (k + 1) * capacity)
        value = jnp.concatenate([query_scr[b, here, :] for b in range(blocks)], axis=0)
        payload_refs[k][...] = tn(sel_scr[k], value).astype(LOW)
    total = jnp.zeros((1, D), F32)
    for s in range(4):
        for l in range(4):
            total = total + row_sum(grad_outs[s][l, :, D:].astype(F32))
    bias_ref[...] = jnp.broadcast_to(total, (8, D))


def memory_weight_kernel(count, place_ref, *refs):
    grads, rows_refs, (kept_ref, sent_ref, sum_scr) = refs[:4], refs[4:8], refs[8:]
    me, core = place_ref[0], place_ref[1]
    for s in range(4):
        rows = rows_refs[s][...].T
        for h in range(2):
            part = nn(rows, grads[s][:, h * D : (h + 1) * D])
            sum_scr[h] = part if s == 0 else sum_scr[h] + part
    block = D // count
    for h in range(2):

        def store(out, h=h):
            total = sum_scr[h].astype(LOW)
            for k in range(count):
                for u in range(D // UNIT):
                    out[me ^ k, u * block : (u + 1) * block, :] = total[
                        k * block : (k + 1) * block, u * UNIT : (u + 1) * UNIT
                    ]

        pl.when(core == h)(functools.partial(store, kept_ref))
        pl.when(core != h)(functools.partial(store, sent_ref))


def datastore_grad_kernel(weight_ref, *refs):
    grads, outs = refs[:4], refs[4:10]
    weight = weight_ref[...].T
    near_a0, near_a1, far_a, near_b0, near_b1, far_b = outs
    groups = ((near_a0, near_a1), (far_a,), (near_b0, near_b1), (far_b,))
    for s in range(4):
        value = nn(grads[s][...], weight).astype(LOW)
        size = value.shape[0] // len(groups[s])
        for i, out in enumerate(groups[s]):
            out[...] = value[i * size : (i + 1) * size]


def middle_kernel(
    p0_ref,
    p1_ref,
    p2_ref,
    p3_ref,
    first_ref,
    cotangent_ref,
    output_ref,
    expand_ref,
    contract_ref,
    bias_ref,
    expand_bias_ref,
    gain_ref,
    shift_ref,
    out_ref,
    merged_ref,
    second_ref,
    active_ref,
    branch_grad_ref,
    expanded_grad_ref,
    cross_grad_ref,
    resid_ref,
    payload_ref,
    small_ref,
    wide_ref,
    expanded_scr,
    output_scr,
    expand_scr,
    contract_scr,
    sems,
):
    fetch = copies(
        [(output_ref, output_scr), (expand_ref, expand_scr), (contract_ref, contract_scr)], sems
    )
    start_all(fetch)
    bias = bias_ref[...].astype(F32)
    gain = gain_ref[...].astype(F32)
    shift = shift_ref[...].astype(F32)
    parts = [p0_ref, p1_ref, p2_ref, p3_ref]
    lses = [read_lse(part[:, D:]) for part in parts]
    top = functools.reduce(jnp.maximum, lses)
    weights = [jnp.exp(lse - top) for lse in lses]
    total = functools.reduce(jnp.add, weights)
    overall = top + jnp.log(total)
    spread = head_spread(False)
    merged = jnp.zeros(first_ref.shape, F32)
    for part, weight in zip(parts, weights):
        share = weight / total
        high = share.astype(LOW)
        rest = (share - high.astype(F32)).astype(LOW)
        merged = merged + (nn(high, spread) + nn(rest, spread)) * part[:, :D].astype(F32)
    merged_low = merged.astype(LOW)
    merged_ref[...] = merged_low
    fetch[0].wait()
    residual = first_ref[...].astype(F32) + nn(merged_low, output_scr[...]) + bias[5:6]
    second, unit_second, scale_second = norm_forward(residual, gain[1:2], shift[1:2])
    second_low = second.astype(LOW)
    second_ref[...] = second_low
    hidden = contract_scr.shape[0]
    fetch[1].wait()
    for c in range(hidden // D):
        at = slice(c * D, (c + 1) * D)
        expanded = nn(second_low, expand_scr[:, at]) + expand_bias_ref[:, at].astype(F32)
        bell = 0.5 * (1.0 + lax.erf(expanded * 0.7071067811865476))
        active_ref[:, at] = (expanded * bell).astype(LOW)
        slope = bell + expanded * 0.3989422804014327 * jnp.exp(-0.5 * expanded * expanded)
        expanded_scr[:, at] = slope
    fetch[2].wait()
    residual = second_low.astype(F32) + nn(active_ref[...], contract_scr[...]) + bias[6:7]
    final, unit_final, scale_final = norm_forward(residual, gain[2:3], shift[2:3])
    out_ref[...] = final.astype(LOW)
    cotangent = cotangent_ref[...].astype(F32)
    final_resid = norm_backward(cotangent, unit_final, scale_final, gain[2:3])
    branch_grad = final_resid.astype(LOW)
    branch_grad_ref[...] = branch_grad
    small_ref[0:1, :] = row_sum(branch_grad.astype(F32))
    small_ref[1:2, :] = row_sum(cotangent * unit_final)
    small_ref[2:3, :] = row_sum(cotangent)
    total_grad = final_resid
    for c in range(hidden // D):
        at = slice(c * D, (c + 1) * D)
        active_grad = nt(branch_grad, contract_scr[at, :])
        expanded_grad = (active_grad * expanded_scr[:, at]).astype(LOW)
        expanded_grad_ref[:, at] = expanded_grad
        wide_ref[:, at] = row_sum(expanded_grad.astype(F32))
        total_grad = total_grad + nt(expanded_grad, expand_scr[:, at])
    small_ref[4:5, :] = row_sum(total_grad * unit_second)
    small_ref[5:6, :] = row_sum(total_grad)
    second_resid = norm_backward(total_grad, unit_second, scale_second, gain[1:2])
    resid_ref[...] = second_resid
    cross_grad = second_resid.astype(LOW)
    cross_grad_ref[...] = cross_grad
    small_ref[3:4, :] = row_sum(cross_grad.astype(F32))
    small_ref[6:8, :] = jnp.zeros((2, D), F32)
    attended_grad = nt(cross_grad, output_scr[...]).astype(LOW)
    payload_ref[:, :D] = attended_grad
    product = attended_grad.astype(F32) * merged
    gather = flag(lanes((D, SLAB)) % 16 == rows_of((D, SLAB)) // HEAD_DIM).astype(LOW)
    high, mid, low = three(product)
    delta = nn(high, gather) + nn(mid, gather) + nn(low, gather)
    lane = lanes(overall.shape)
    packed = jnp.zeros(overall.shape, F32)
    for value, base in ((overall, 0), (delta, 48)):
        for i, piece in enumerate(three(value)):
            inside = (lane >= base + 16 * i) & (lane < base + 16 * i + HEADS)
            packed = jnp.where(inside, piece.astype(F32), packed)
    payload_ref[:, D:] = packed.astype(LOW)


def self_backward_kernel(
    d0_ref,
    d1_ref,
    d2_ref,
    d3_ref,
    resid_ref,
    unit_ref,
    scale_ref,
    heads_ref,
    soft_ref,
    query_ref,
    output_ref,
    project_ref,
    gain_ref,
    pre_grad_ref,
    branch_grad_ref,
    project_grad_ref,
    input_grad_ref,
    small_ref,
    attended_scr,
    query_scr,
    output_scr,
    heads_scr,
    soft_scr,
    project_scr,
    sems,
):
    fetch = copies(
        [
            (query_ref, query_scr),
            (output_ref, output_scr),
            (heads_ref, heads_scr),
            (soft_ref, soft_scr),
            (project_ref, project_scr),
        ],
        sems,
    )
    start_all(fetch)
    tokens = resid_ref.shape[0]
    query_sum = functools.reduce(
        jnp.add, [d[...].astype(F32) for d in (d0_ref, d1_ref, d2_ref, d3_ref)]
    ).astype(LOW)
    pre_grad = (query_sum.astype(F32) * QUERY_SCALE).astype(LOW)
    pre_grad_ref[...] = pre_grad
    fetch[0].wait()
    total = resid_ref[...] + nt(pre_grad, query_scr[...])
    unit = unit_ref[...]
    first_resid = norm_backward(total, unit, scale_ref[...], gain_ref[0:1, :].astype(F32))
    branch_grad = first_resid.astype(LOW)
    branch_grad_ref[...] = branch_grad
    fetch[1].wait()
    attended_scr[...] = nt(branch_grad, output_scr[...]).astype(LOW)
    fetch[2].wait()
    fetch[3].wait()
    first, second = half_masks()
    for p in range(PAIRS):
        at = p * SLAB
        grads = two_heads(attended_scr[:, at : at + SLAB], first, second)
        queries = two_heads(heads_scr[:, at : at + SLAB], first, second)
        keys = heads_scr[:, D + at : D + at + SLAB]
        dots = nt(grads, heads_scr[:, 2 * D + at : 2 * D + at + SLAB])
        soft = soft_scr[p]
        score_grad = (soft * (dots - jnp.sum(soft * dots, axis=-1, keepdims=True))).astype(LOW)
        query_grad = join_heads(nn(score_grad, keys), tokens).astype(LOW)
        project_grad_ref[:, at : at + SLAB] = (query_grad.astype(F32) * QUERY_SCALE).astype(LOW)
        project_grad_ref[:, D + at : D + at + SLAB] = tn(score_grad, queries).astype(LOW)
        project_grad_ref[:, 2 * D + at : 2 * D + at + SLAB] = tn(soft.astype(LOW), grads).astype(
            LOW
        )
    fetch[4].wait()
    input_grad_ref[...] = first_resid + nt(project_grad_ref[...], project_scr[...])
    small_ref[0:1, :] = row_sum(project_grad_ref[:, :D].astype(F32))
    small_ref[1:2, :] = row_sum(project_grad_ref[:, 2 * D :].astype(F32))
    small_ref[2:3, :] = row_sum(branch_grad.astype(F32))
    small_ref[3:4, :] = row_sum(pre_grad.astype(F32))
    small_ref[4:5, :] = row_sum(total * unit)
    small_ref[5:6, :] = row_sum(total)
    small_ref[6:8, :] = jnp.zeros((2, D), F32)


def weight_grad_kernel(plan, count, packed, held, place_ref, *refs):
    kept_ref, sent_ref = refs[-2:]
    me, core = place_ref[0], place_ref[1]
    at_ref = 0
    for number, rows, columns, at in plan:
        pairs = [refs[at_ref + 2 * i : at_ref + 2 * i + 2] for i in range(number)]
        at_ref += 2 * number
        block = rows // count
        half = columns // 2
        for m in range(rows // D):
            xs = [x_ref[:, m * D : (m + 1) * D].T for x_ref, _ in pairs]
            for c in range(0, half, D):
                wide = min(D, half - c)
                for mine, out in ((core, kept_ref), (1 - core, sent_ref)):
                    start = pl.multiple_of(mine * half + c, SLAB)
                    part = sum(
                        nn(x, g_ref[:, pl.ds(start, wide)]) for x, (_, g_ref) in zip(xs, pairs)
                    ).astype(LOW)
                    for u in range(wide // UNIT):
                        low = at + (c // UNIT + u) * block
                        for k in range(D // block):
                            to = me ^ (m * (D // block) + k)
                            out[to, low : low + block, :] = part[
                                k * block : (k + 1) * block, u * UNIT : (u + 1) * UNIT
                            ]
    if packed is not None:
        pack_small(refs[at_ref : at_ref + 4], kept_ref, sent_ref, packed, me, core, count)
        at_ref += 4
    if held:
        for ref, out in zip(refs[at_ref : at_ref + 2], (kept_ref, sent_ref)):
            out[:, :held, :] = ref[...]


def pack_small(small_refs, kept_ref, sent_ref, low, me, core, count):
    own, middle, value_bias, wide = small_refs
    order = [own[0:4], value_bias[0:1], middle[3:4], middle[0:1], own[4:5], middle[4:5]]
    order += [middle[1:2], own[5:6], middle[5:6], middle[2:3], jnp.zeros((3, D), F32)]
    narrow = jnp.concatenate(order, axis=0)
    share = D // count
    broad = wide.shape[1] // count
    for r in range(count):
        first = narrow[:, r * share : (r + 1) * share]
        first = jnp.concatenate([first, jnp.zeros((RANK_ROWS, UNIT - share), F32)], axis=1)
        second = wide[:, r * broad : (r + 1) * broad]
        second = jnp.concatenate([second, jnp.zeros((1, UNIT - broad), F32)], axis=1)
        second = jnp.broadcast_to(second, (RANK_ROWS, UNIT))
        here = slice(low, low + RANK_ROWS)
        kept_ref[me ^ r, here, :] = jnp.where(core == 0, first, second).astype(LOW)
        sent_ref[me ^ r, here, :] = jnp.where(core == 0, second, first).astype(LOW)


def total_of(*refs):
    return functools.reduce(jnp.add, [ref[...].astype(F32) for ref in refs])


def split_kernel(x, kept_ref, come_ref, *refs):
    far, outs = ((), refs) if x else (refs[:2], refs[2:])
    half = kept_ref.shape[3] // 2
    for z in range(4):
        for g in range(2):
            at = (z, slice(None), x, slice(0, half)) if g == 0 else (z, x, slice(None), slice(half, 2 * half))
            total = kept_ref[at].astype(F32) + come_ref[at].astype(F32)
            if far:
                total = total + far[g][z].astype(F32)
                for i in range(2):
                    outs[2 * g + i][z] = total[i].astype(LOW)
            else:
                outs[g][z] = total.astype(LOW)


def join_kernel(a_keep, a_come, b_keep, b_come, *outs):
    rows = a_keep.shape[1]
    for z, out in enumerate(outs):
        out[:rows] = total_of(a_keep.at[z], a_come.at[z]).astype(LOW)
        out[rows:] = total_of(b_keep.at[z], b_come.at[z]).astype(LOW)


def sum_kernel(*refs):
    refs[-1][...] = total_of(*refs[:-1]).astype(LOW)


def spread_kernel(plan, count, packed, place_ref, own_ref, other_ref, *outs):
    core = place_ref[1]
    for (rows, columns, at), out in zip(plan, outs):
        block = rows // count
        half = columns // 2
        for c in range(half // UNIT):
            low = at + c * block
            for value, mine in ((own_ref, core), (other_ref, 1 - core)):
                start = pl.multiple_of(mine * half + c * UNIT, SLAB)
                out[:, pl.ds(start, UNIT)] = value[low : low + block].astype(F32)
    if packed is not None:
        here = slice(packed, packed + RANK_ROWS)
        own, other = own_ref[here].astype(F32), other_ref[here].astype(F32)
        narrow, wide = jnp.where(core == 0, own, other), jnp.where(core == 0, other, own)
        biases_ref, wide_ref, gain_ref, shift_ref = outs[len(plan) :]
        share = biases_ref.shape[1]
        biases_ref[...] = narrow[0:7, :share]
        gain_ref[...] = narrow[7:10, :share]
        shift_ref[...] = narrow[10:13, :share]
        wide_ref[...] = wide[0:1, : wide_ref.shape[1]]


def swap(v, bits):
    count = lax.axis_size("store")
    return lax.ppermute(v, "store", [(i, i ^ bits) for i in range(count)])


def swap_core(v):
    return lax.ppermute(v, "dp", [(0, 1), (1, 0)])


class WeightSums:
    def __init__(self, place, count, rows):
        self.place, self.count, self.rows = place, count, rows
        self.plan, self.packed, self.at = [], None, 0
        self.buffers = ()

    def add(self, products, small=None, earlier=(), flops=0):
        plan, base, packed = [], self.at, None
        for pairs in products:
            rows, columns = pairs[0][0].shape[1], pairs[0][1].shape[1]
            plan.append((len(pairs), rows, columns, self.at))
            self.plan.append((rows, columns, self.at))
            self.at += rows // self.count * (columns // 2 // UNIT)
        args = [v for pairs in products for pair in pairs for v in pair]
        if small is not None:
            packed = self.packed = self.at
            self.at += RANK_ROWS
            args.extend(small)
        shape = (self.count, self.rows, UNIT)
        self.buffers = call(
            functools.partial(weight_grad_kernel, tuple(plan), self.count, packed, base),
            [(shape, LOW), (shape, LOW)],
            n_smem=1,
            earlier=earlier,
            flops=flops,
        )(self.place, *args, *self.buffers)
        return self.buffers

    def split(self, x, far=(), earlier=()):
        half = (4, 2, self.rows // 2, UNIT)
        outs = [half[:1] + half[2:]] * 4 if far else [half] * 2
        args = [v.reshape(4, 2, 2, self.rows, UNIT) for v in (self.kept, self.come)] + list(far)
        return call(
            functools.partial(split_kernel, x),
            [(shape, LOW) for shape in outs],
            earlier=earlier,
            limit=SMALL_LIMIT,
        )(*args)

    def start(self, earlier=()):
        self.kept, sent = self.buffers
        self.come = swap_core(sent)
        self.sent = self.split(1, earlier=earlier)
        return self.sent

    def first(self, *earlier):
        come = (swap(self.sent[0], 1), swap(self.sent[1], 2))
        a_keep, a_send, b_keep, b_send = self.split(0, come, earlier)
        self.kept, self.sent = (a_keep, b_keep), (a_send, b_send)
        return self.sent

    def second(self, *earlier):
        come = (swap(self.sent[0], 2), swap(self.sent[1], 1))
        self.w = call(
            join_kernel, [((self.rows, UNIT), LOW)] * 4, earlier=earlier, limit=SMALL_LIMIT
        )(self.kept[0], come[0], self.kept[1], come[1])
        return self.w

    def third(self, *earlier):
        come = [swap(self.w[k], 4 * k) for k in (1, 2, 3)]
        (self.own,) = call(
            sum_kernel, [(come[0].shape, LOW)], earlier=earlier, limit=SMALL_LIMIT
        )(self.w[0], *come)
        return self.own

    def finish(self, small=()):
        other = swap_core(self.own)
        shapes = [((rows // self.count, columns), F32) for rows, columns, _ in self.plan]
        shapes += [(shape, F32) for shape in small]
        return call(
            functools.partial(spread_kernel, tuple(self.plan), self.count, self.packed),
            shapes,
            n_smem=1,
            limit=SMALL_LIMIT,
        )(self.place, self.own, other)


def local_tree(
    inputs,
    doc_lengths,
    datastore,
    kept_mask,
    retrieved,
    self_project,
    self_output,
    cross_query,
    cross_memory,
    cross_output,
    expand_weight,
    contract_weight,
    biases,
    expand_bias,
    norm_gain,
    norm_shift,
    cotangent,
):
    tokens = inputs.shape[0]
    count = lax.axis_size("store")
    local_blocks = datastore.shape[0] // BLOCK
    all_blocks = local_blocks * count
    capacity = 2 * tokens * TOPB // all_blocks
    plane_blocks = 4 * local_blocks
    rows_in = 4 * capacity
    hidden = expand_weight.shape[1]
    me = lax.axis_index("store").astype(jnp.int32)
    core = lax.axis_index("dp").astype(jnp.int32)
    place = jnp.stack([me, core])

    marks = kept_mask.reshape(2, 2, BLOCK).astype(LOW)
    marks = jnp.pad(marks, ((0, 0), (0, RANK_ROWS - 2), (0, D - BLOCK)))
    halves = datastore.reshape(2, 2 * BLOCK, D)
    a0, b0 = (jnp.concatenate([halves[h], marks[h]]) for h in range(2))
    a1, b1 = swap(a0, 1), swap(b0, 2)
    heads_all, soft_self, attended, unit_first, scale_first, first_low, *queries = call(
        self_forward_kernel,
        [
            ((tokens, 3 * D), LOW),
            ((PAIRS, 2 * tokens, tokens), F32),
            ((tokens, D), LOW),
            ((tokens, D), F32),
            ((tokens, 1), F32),
            ((tokens, D), LOW),
        ]
        + [((tokens + RANK_ROWS, D), LOW)] * 4,
        scratch=[
            pltpu.VMEM((D, 3 * D), LOW),
            pltpu.VMEM((D, D), LOW),
            pltpu.VMEM((D, D), LOW),
            pltpu.SemaphoreType.DMA((5,)),
        ],
        n_smem=2,
        far_in=(4, 5, 6),
        flops=8 * MICROSECOND,
    )(
        doc_lengths,
        place,
        inputs,
        retrieved.T,
        self_project,
        self_output,
        cross_query,
        biases,
        norm_gain,
        norm_shift,
    )
    ay = swap(after(jnp.stack([a0, a1]), first_low), 2)
    bx = swap(after(jnp.stack([b0, b1]), first_low), 1)
    queries = [queries[0]] + [swap(queries[k], 4 * k) for k in (1, 2, 3)]

    one_set = [
        ((4 * BLOCK, D), LOW),
        ((4, BLOCK, 2 * D), LOW),
        ((4, 1, BLOCK), F32),
        ((4, BLOCK, SLAB), LOW),
    ]
    memory_call = call(
        memory_kernel,
        one_set * 2,
    )
    near = memory_call(a0, a1, b0, b1, cross_memory, biases)
    far = memory_call(ay[0], ay[1], bx[0], bx[1], cross_memory, biases)
    sets = [near[:4], far[:4], near[4:], far[4:]]
    stored, memory, hidden_rows, key_side = zip(*sets)

    slots, *payloads = call(
        functools.partial(owner_forward_kernel, capacity),
        [((plane_blocks, rows_in, D), LOW)] + [((tokens, WIDE), LOW)] * 4,
        scratch=[
            pltpu.VMEM((plane_blocks, rows_in, D), F32),
            pltpu.VMEM((plane_blocks, rows_in, SLAB), F32),
            pltpu.VMEM((plane_blocks, rows_in, SLAB), F32),
            pltpu.VMEM((4, plane_blocks * capacity, tokens), LOW),
            pltpu.VMEM((RANK_ROWS, tokens), F32),
        ],
        flops=20 * MICROSECOND,
    )(*queries, *memory, *hidden_rows)
    parts = [payloads[0]] + [swap(payloads[k], 4 * k) for k in (1, 2, 3)]

    (
        outputs,
        merged_low,
        second_low,
        active_low,
        branch_grad,
        expanded_grad,
        cross_grad,
        second_resid,
        payload,
        small_middle,
        wide_bias,
    ) = call(
        middle_kernel,
        [
            ((tokens, D), LOW),
            ((tokens, D), LOW),
            ((tokens, D), LOW),
            ((tokens, hidden), LOW),
            ((tokens, D), LOW),
            ((tokens, hidden), LOW),
            ((tokens, D), LOW),
            ((tokens, D), F32),
            ((tokens, WIDE), LOW),
            ((8, D), F32),
            ((1, hidden), F32),
        ],
        scratch=[
            pltpu.VMEM((tokens, hidden), F32),
            pltpu.VMEM((D, D), LOW),
            pltpu.VMEM((D, hidden), LOW),
            pltpu.VMEM((hidden, D), LOW),
            pltpu.SemaphoreType.DMA((3,)),
        ],
        far_in=(6, 7, 8),
        flops=12 * MICROSECOND,
    )(
        *parts,
        first_low,
        cotangent,
        cross_output,
        expand_weight,
        contract_weight,
        biases,
        expand_bias.reshape(1, hidden),
        norm_gain,
        norm_shift,
    )
    grads = [payload] + [swap(payload, 4 * k) for k in (1, 2, 3)]

    early = WeightSums(place, count, 432)
    early.add(
        [[(active_low, branch_grad)], [(merged_low, cross_grad)], [(second_low, expanded_grad)]],
        flops=8 * MICROSECOND,
    )
    early_start = early.start()

    out = call(
        functools.partial(owner_backward_kernel, capacity),
        [((4, BLOCK, 2 * D), LOW)] * 4 + [((tokens, D), LOW)] * 4 + [((8, D), F32)],
        scratch=[
            pltpu.VMEM((plane_blocks, rows_in, WIDE), LOW),
            pltpu.VMEM((plane_blocks, rows_in, D), LOW),
            pltpu.VMEM((4, plane_blocks * capacity, tokens), LOW),
            pltpu.VMEM((RANK_ROWS, tokens), F32),
        ],
        earlier=early_start,
        flops=LONG,
    )(*queries, *grads, *memory, *key_side, slots)
    memory_grads, query_grads, value_bias_grad = out[:4], out[4:8], out[8]
    parts = [query_grads[0]] + [swap(query_grads[k], 4 * k) for k in (1, 2, 3)]

    early_first = early.first(memory_grads[0])
    late = WeightSums(place, count, 352)
    flat_grads = [v.reshape(4 * BLOCK, 2 * D) for v in memory_grads]
    late.buffers = call(
        functools.partial(memory_weight_kernel, count),
        [((count, 2 * D // count, UNIT), LOW)] * 2,
        scratch=[pltpu.VMEM((2, D, D), F32)],
        n_smem=1,
        earlier=early_first,
        flops=MICROSECOND // 10,
    )(place, *flat_grads, *stored)
    late.plan, late.at = [(D, 2 * D, 0)], 2 * D // count

    pre_grad, self_branch_grad, project_grad, input_grad, small_self = call(
        self_backward_kernel,
        [
            ((tokens, D), LOW),
            ((tokens, D), LOW),
            ((tokens, 3 * D), LOW),
            ((tokens, D), F32),
            ((8, D), F32),
        ],
        scratch=[
            pltpu.VMEM((tokens, D), LOW),
            pltpu.VMEM((D, D), LOW),
            pltpu.VMEM((D, D), LOW),
            pltpu.VMEM((tokens, 3 * D), LOW),
            pltpu.VMEM((PAIRS, 2 * tokens, tokens), F32),
            pltpu.VMEM((D, 3 * D), LOW),
            pltpu.SemaphoreType.DMA((5,)),
        ],
        far_in=(7, 8, 9, 10, 11),
        earlier=(late.buffers[0],),
        flops=LONG // 3,
    )(
        *parts,
        second_resid,
        unit_first,
        scale_first,
        heads_all,
        soft_self,
        cross_query,
        self_output,
        self_project,
        norm_gain,
    )
    early_second = early.second()
    late.add(
        [[(attended, self_branch_grad)], [(first_low, pre_grad)], [(inputs, project_grad)]],
        (small_self, small_middle, value_bias_grad, wide_bias),
        earlier=(early_second[0],),
        flops=MICROSECOND // 10,
    )
    near_a0, near_a1, far_a, near_b0, near_b1, far_b = call(
        datastore_grad_kernel,
        [((2 * BLOCK, D), LOW), ((2 * BLOCK, D), LOW), ((4 * BLOCK, D), LOW)] * 2,
        earlier=(late.buffers[0],),
        flops=MICROSECOND // 10,
    )(cross_memory, *flat_grads)
    late.start(earlier=(far_a,))
    late_first = late.first()
    early.third(late_first[0])
    contract_weight_grad, cross_output_grad, expand_weight_grad = early.finish()
    late.second(contract_weight_grad)
    near_two = 2 * BLOCK
    far_a, far_b = (after(v, late.w[0]) for v in (far_a, far_b))
    come_a, come_b = swap(far_a, 2), swap(far_b, 1)
    send_a = near_a1 + come_a[near_two:]
    send_b = near_b1 + come_b[near_two:]
    last_a, last_b = swap(send_a, 1), swap(send_b, 2)
    datastore_grad = jnp.concatenate(
        [
            near.astype(F32) + come[:near_two].astype(F32) + last.astype(F32)
            for near, come, last in ((near_a0, come_a, last_a), (near_b0, come_b, last_b))
        ]
    )
    late.third(come_a, come_b)
    share = D // count
    (
        cross_memory_grad,
        self_output_grad,
        cross_query_grad,
        self_project_grad,
        biases_grad,
        wide_grad,
        gain_grad,
        shift_grad,
    ) = late.finish([(7, share), (1, hidden // count), (3, share), (3, share)])
    return (
        outputs,
        input_grad,
        datastore_grad,
        self_project_grad,
        self_output_grad,
        cross_query_grad,
        cross_memory_grad,
        cross_output_grad,
        expand_weight_grad,
        contract_weight_grad,
        biases_grad,
        wide_grad.reshape(hidden // count),
        gain_grad,
        shift_grad,
    )


def layer_norm(residual, gain_row, shift_row):
    center = residual - jnp.mean(residual, axis=-1, keepdims=True)
    spread = jnp.mean(center * center, axis=-1, keepdims=True)
    return center * lax.rsqrt(spread + EPSILON) * gain_row + shift_row


def doc_mask(lengths, seq_tokens):
    upto = jnp.tri(lengths.shape[-1], dtype=jnp.int32)
    bounds = jnp.sum(lengths[..., None, :] * upto, axis=-1)
    places = jnp.arange(seq_tokens, dtype=jnp.int32)
    segment = jnp.sum((places[:, None] >= bounds[..., None, :]).astype(jnp.int32), axis=-1)
    causal = places[:, None] >= places[None, :]
    return (segment[..., :, None] == segment[..., None, :]) & causal


def slot_numbers(picks, capacity):
    flat_ids = picks.reshape(-1)
    sorter = jnp.argsort(flat_ids, stable=True)
    sorted_ids = flat_ids[sorter]
    first_seen = jnp.searchsorted(sorted_ids, sorted_ids, side="left")
    rank_sorted = jnp.arange(flat_ids.shape[0], dtype=jnp.int32) - first_seen
    ranks = jnp.zeros_like(flat_ids).at[sorter].set(rank_sorted)
    return flat_ids * capacity + ranks


def place_rows(rows, slot_ids, total_slots, store_count, local_blocks, capacity):
    placed = jnp.zeros((total_slots, rows.shape[1]), rows.dtype).at[slot_ids].set(rows)
    return placed.reshape(store_count, local_blocks, capacity, rows.shape[1])


def local_slots(
    inputs,
    doc_lengths,
    datastore,
    kept_mask,
    retrieved,
    self_project,
    self_output,
    cross_query,
    cross_memory,
    cross_output,
    expand_weight,
    contract_weight,
    biases,
    expand_bias,
    norm_gain,
    norm_shift,
    cotangent,
):
    tok_count = inputs.shape[0]
    store_count = lax.axis_size("store")
    local_blocks = datastore.shape[0] // BLOCK
    all_blocks = local_blocks * store_count
    capacity = 2 * tok_count * TOPB // all_blocks
    rows_in = store_count * capacity
    total_slots = all_blocks * capacity
    gain_rows = norm_gain.astype(jnp.float32)
    shift_rows = norm_shift.astype(jnp.float32)
    bias_rows = biases.astype(jnp.float32)
    projected = jnp.dot(inputs, self_project, preferred_element_type=jnp.float32)
    heads_all = jnp.concatenate(
        [
            QUERY_SCALE * (projected[:, :D] + bias_rows[0]),
            projected[:, D : 2 * D],
            projected[:, 2 * D :] + bias_rows[1],
        ],
        axis=1,
    ).astype(jnp.bfloat16)
    queries = heads_all[:, :D].reshape(tok_count, HEADS, HEAD_DIM)
    keys_self = heads_all[:, D : 2 * D].reshape(tok_count, HEADS, HEAD_DIM)
    values_self = heads_all[:, 2 * D :].reshape(tok_count, HEADS, HEAD_DIM)
    allowed = doc_mask(doc_lengths[0], tok_count)

    def self_scores():
        raw_scores = jnp.einsum(
            "qhd,khd->hqk", queries, keys_self, preferred_element_type=jnp.float32
        )
        return jnp.where(allowed[None], raw_scores, MASKED)

    scores = self_scores()
    self_lse = jax.nn.logsumexp(scores, axis=-1)
    soft_low = jnp.exp(scores - self_lse[..., None]).astype(jnp.bfloat16)
    attended = (
        jnp.einsum("hqk,khd->qhd", soft_low, values_self, preferred_element_type=jnp.float32)
        .reshape(tok_count, D)
        .astype(jnp.bfloat16)
    )
    self_branch = jnp.dot(attended, self_output, preferred_element_type=jnp.float32) + bias_rows[2]
    first_norm, first_back = jax.vjp(
        layer_norm, inputs.astype(jnp.float32) + self_branch, gain_rows[0], shift_rows[0]
    )
    first_low = first_norm.astype(jnp.bfloat16)
    cross_queries = (
        QUERY_SCALE
        * (jnp.dot(first_low, cross_query, preferred_element_type=jnp.float32) + bias_rows[3])
    ).astype(jnp.bfloat16)
    slot_ids = slot_numbers(retrieved, capacity)
    send_buffer = place_rows(
        jnp.repeat(cross_queries, TOPB, axis=0),
        slot_ids,
        total_slots,
        store_count,
        local_blocks,
        capacity,
    )
    arrived = lax.all_to_all(send_buffer, "store", split_axis=0, concat_axis=2, tiled=True)
    owner_queries = arrived[0].reshape(local_blocks, rows_in, HEADS, HEAD_DIM)
    memory_bias = jnp.concatenate([jnp.zeros((D,), jnp.float32), bias_rows[4]])
    memory_low = (
        jnp.dot(datastore, cross_memory, preferred_element_type=jnp.float32) + memory_bias
    ).astype(jnp.bfloat16)
    memory_blocks = memory_low.reshape(local_blocks, BLOCK, 2 * D)
    store_keys = memory_blocks[:, :, :D].reshape(local_blocks, BLOCK, HEADS, HEAD_DIM)
    store_values = memory_blocks[:, :, D:].reshape(local_blocks, BLOCK, HEADS, HEAD_DIM)
    kept_rows = kept_mask.reshape(local_blocks, BLOCK) > 0

    def block_scores(query_blocks):
        raw_scores = jnp.einsum(
            "bmhd,bkhd->bhmk", query_blocks, store_keys, preferred_element_type=jnp.float32
        )
        return jnp.where(kept_rows[:, None, None, :], raw_scores, MASKED)

    owner_scores = block_scores(owner_queries)
    owner_lse = jax.nn.logsumexp(owner_scores, axis=-1)
    owner_soft = jnp.exp(owner_scores - owner_lse[..., None]).astype(jnp.bfloat16)
    partial_value = jnp.einsum(
        "bhmk,bkhd->bmhd", owner_soft, store_values, preferred_element_type=jnp.float32
    ).reshape(local_blocks, rows_in, D)
    partial_lse = jnp.transpose(owner_lse, (0, 2, 1))
    returned, returned_lse = (
        lax.all_to_all(partial_value[None], "store", split_axis=2, concat_axis=0, tiled=True),
        lax.all_to_all(partial_lse[None], "store", split_axis=2, concat_axis=0, tiled=True),
    )
    picked = returned.reshape(total_slots, D)[slot_ids].reshape(tok_count, TOPB, HEADS, HEAD_DIM)
    picked_lse = returned_lse.reshape(total_slots, HEADS)[slot_ids].reshape(tok_count, TOPB, HEADS)
    overall = jax.nn.logsumexp(picked_lse, axis=1)
    mix_weights = jnp.exp(picked_lse - overall[:, None, :])
    merged = jnp.einsum(
        "tjh,tjhd->thd", mix_weights, picked, precision=lax.Precision.HIGHEST
    ).reshape(tok_count, D)
    merged_low = merged.astype(jnp.bfloat16)
    cross_branch = (
        jnp.dot(merged_low, cross_output, preferred_element_type=jnp.float32) + bias_rows[5]
    )
    second_norm, second_back = jax.vjp(
        layer_norm, first_low.astype(jnp.float32) + cross_branch, gain_rows[1], shift_rows[1]
    )
    second_low = second_norm.astype(jnp.bfloat16)
    expanded = jnp.dot(
        second_low, expand_weight, preferred_element_type=jnp.float32
    ) + expand_bias.astype(jnp.float32)
    activated, gelu_back = jax.vjp(
        lambda pre_act: jax.nn.gelu(pre_act, approximate=False), expanded
    )
    activated_low = activated.astype(jnp.bfloat16)
    ffn_branch = (
        jnp.dot(activated_low, contract_weight, preferred_element_type=jnp.float32) + bias_rows[6]
    )
    final_norm, final_back = jax.vjp(
        layer_norm, second_low.astype(jnp.float32) + ffn_branch, gain_rows[2], shift_rows[2]
    )
    outputs = final_norm.astype(jnp.bfloat16)
    final_resid, final_gain, final_shift = final_back(cotangent.astype(jnp.float32))
    ffn_branch_grad = final_resid.astype(jnp.bfloat16)
    contract_weight_grad = jnp.dot(
        activated_low.T, ffn_branch_grad, preferred_element_type=jnp.float32
    )
    activated_grad = jnp.dot(ffn_branch_grad, contract_weight.T, preferred_element_type=jnp.float32)
    (expanded_raw,) = gelu_back(activated_grad)
    expanded_grad = expanded_raw.astype(jnp.bfloat16)
    expand_weight_grad = jnp.dot(second_low.T, expanded_grad, preferred_element_type=jnp.float32)
    expand_bias_grad = jnp.sum(expanded_grad.astype(jnp.float32), axis=0)
    second_total = final_resid + jnp.dot(
        expanded_grad, expand_weight.T, preferred_element_type=jnp.float32
    )
    second_resid, second_gain, second_shift = second_back(second_total)
    cross_branch_grad = second_resid.astype(jnp.bfloat16)
    cross_output_grad = jnp.dot(merged_low.T, cross_branch_grad, preferred_element_type=jnp.float32)
    attended_grad = jnp.dot(
        cross_branch_grad, cross_output.T, preferred_element_type=jnp.float32
    ).astype(jnp.bfloat16)
    delta_rows = jnp.sum(
        attended_grad.reshape(tok_count, HEADS, HEAD_DIM).astype(jnp.float32)
        * merged.reshape(tok_count, HEADS, HEAD_DIM),
        axis=-1,
    )
    grad_buffer = place_rows(
        jnp.repeat(attended_grad, TOPB, axis=0),
        slot_ids,
        total_slots,
        store_count,
        local_blocks,
        capacity,
    )
    overall_buffer = place_rows(
        jnp.repeat(overall, TOPB, axis=0),
        slot_ids,
        total_slots,
        store_count,
        local_blocks,
        capacity,
    )
    delta_buffer = place_rows(
        jnp.repeat(delta_rows, TOPB, axis=0),
        slot_ids,
        total_slots,
        store_count,
        local_blocks,
        capacity,
    )
    arrived_grad = lax.all_to_all(grad_buffer, "store", split_axis=0, concat_axis=2, tiled=True)
    arrived_overall, arrived_delta = (
        lax.all_to_all(overall_buffer, "store", split_axis=0, concat_axis=2, tiled=True),
        lax.all_to_all(delta_buffer, "store", split_axis=0, concat_axis=2, tiled=True),
    )
    owner_grad = arrived_grad[0].reshape(local_blocks, rows_in, HEADS, HEAD_DIM)
    overall_heads = jnp.transpose(arrived_overall[0], (0, 2, 1))
    delta_heads = jnp.transpose(arrived_delta[0], (0, 2, 1))
    soft_again = jnp.exp(block_scores(owner_queries) - owner_lse[..., None])
    soft_again_low = soft_again.astype(jnp.bfloat16).astype(jnp.float32)
    weight_mix = jnp.exp(owner_lse - overall_heads)
    value_dots = jnp.einsum(
        "bmhd,bkhd->bhmk", owner_grad, store_values, preferred_element_type=jnp.float32
    )
    exact_sum = jnp.sum(soft_again * value_dots, axis=-1, keepdims=True)
    rounded_sum = jnp.sum(soft_again_low * value_dots, axis=-1, keepdims=True)
    score_grad = (
        weight_mix[..., None]
        * soft_again
        * (value_dots - exact_sum + rounded_sum - delta_heads[..., None])
    ).astype(jnp.bfloat16)
    query_grad = (
        jnp.einsum("bhmk,bkhd->bmhd", score_grad, store_keys, preferred_element_type=jnp.float32)
        .astype(jnp.bfloat16)
        .reshape(local_blocks, rows_in, D)
    )
    key_grad = jnp.einsum(
        "bhmk,bmhd->bkhd", score_grad, owner_queries, preferred_element_type=jnp.float32
    )
    weighted_soft = weight_mix[..., None] * soft_again_low
    value_grad = jnp.einsum(
        "bhmk,bmhd->bkhd",
        weighted_soft,
        owner_grad.astype(jnp.float32),
        precision=lax.Precision.HIGHEST,
    )
    row_count = local_blocks * BLOCK
    memory_grad = jnp.concatenate(
        [key_grad.reshape(row_count, D), value_grad.reshape(row_count, D)], axis=1
    ).astype(jnp.bfloat16)
    cross_memory_grad = jnp.dot(datastore.T, memory_grad, preferred_element_type=jnp.float32)
    value_bias_grad = jnp.sum(memory_grad[:, D:].astype(jnp.float32), axis=0)
    datastore_grad = jnp.dot(memory_grad, cross_memory.T, preferred_element_type=jnp.float32)
    returned_grad = lax.all_to_all(
        query_grad[None], "store", split_axis=2, concat_axis=0, tiled=True
    )
    per_pick = returned_grad.reshape(total_slots, D)[slot_ids].reshape(tok_count, TOPB, D)
    query_sum = jnp.sum(per_pick.astype(jnp.float32), axis=1).astype(jnp.bfloat16)
    cross_pre_grad = (query_sum.astype(jnp.float32) * QUERY_SCALE).astype(jnp.bfloat16)
    cross_query_grad = jnp.dot(first_low.T, cross_pre_grad, preferred_element_type=jnp.float32)
    first_total = second_resid + jnp.dot(
        cross_pre_grad, cross_query.T, preferred_element_type=jnp.float32
    )
    first_resid, first_gain, first_shift = first_back(first_total)
    self_branch_grad = first_resid.astype(jnp.bfloat16)
    self_output_grad = jnp.dot(attended.T, self_branch_grad, preferred_element_type=jnp.float32)
    self_attended_grad = (
        jnp.dot(self_branch_grad, self_output.T, preferred_element_type=jnp.float32)
        .astype(jnp.bfloat16)
        .reshape(tok_count, HEADS, HEAD_DIM)
    )
    soft_self = jnp.exp(self_scores() - self_lse[..., None])
    soft_dots = jnp.einsum(
        "qhd,khd->hqk", self_attended_grad, values_self, preferred_element_type=jnp.float32
    )
    self_score_grad = (
        soft_self * (soft_dots - jnp.sum(soft_self * soft_dots, axis=-1, keepdims=True))
    ).astype(jnp.bfloat16)
    query_self_grad = jnp.einsum(
        "hqk,khd->qhd", self_score_grad, keys_self, preferred_element_type=jnp.float32
    ).reshape(tok_count, D)
    key_self_grad = jnp.einsum(
        "hqk,qhd->khd", self_score_grad, queries, preferred_element_type=jnp.float32
    ).reshape(tok_count, D)
    value_self_grad = jnp.einsum(
        "hqk,qhd->khd", soft_low, self_attended_grad, preferred_element_type=jnp.float32
    ).reshape(tok_count, D)
    heads_grad = jnp.concatenate([query_self_grad, key_self_grad, value_self_grad], axis=1).astype(
        jnp.bfloat16
    )
    project_grad = jnp.concatenate(
        [
            (heads_grad[:, :D].astype(jnp.float32) * QUERY_SCALE).astype(jnp.bfloat16),
            heads_grad[:, D:],
        ],
        axis=1,
    )
    self_project_grad = jnp.dot(inputs.T, project_grad, preferred_element_type=jnp.float32)
    input_grad = first_resid + jnp.dot(
        project_grad, self_project.T, preferred_element_type=jnp.float32
    )
    biases_grad = jnp.stack(
        [
            jnp.sum(project_grad[:, :D].astype(jnp.float32), axis=0),
            jnp.sum(project_grad[:, 2 * D :].astype(jnp.float32), axis=0),
            jnp.sum(self_branch_grad.astype(jnp.float32), axis=0),
            jnp.sum(cross_pre_grad.astype(jnp.float32), axis=0),
            value_bias_grad,
            jnp.sum(cross_branch_grad.astype(jnp.float32), axis=0),
            jnp.sum(ffn_branch_grad.astype(jnp.float32), axis=0),
        ]
    )
    gain_grad = jnp.stack([first_gain, second_gain, final_gain])
    shift_grad = jnp.stack([first_shift, second_shift, final_shift])
    shared = (
        lax.psum_scatter(self_project_grad, "store", scatter_dimension=0, tiled=True),
        lax.psum_scatter(self_output_grad, "store", scatter_dimension=0, tiled=True),
        lax.psum_scatter(cross_query_grad, "store", scatter_dimension=0, tiled=True),
        lax.psum_scatter(cross_memory_grad, "store", scatter_dimension=0, tiled=True),
        lax.psum_scatter(cross_output_grad, "store", scatter_dimension=0, tiled=True),
        lax.psum_scatter(expand_weight_grad, "store", scatter_dimension=0, tiled=True),
        lax.psum_scatter(contract_weight_grad, "store", scatter_dimension=0, tiled=True),
        lax.psum_scatter(biases_grad, "store", scatter_dimension=1, tiled=True),
        lax.psum_scatter(expand_bias_grad, "store", scatter_dimension=0, tiled=True),
        lax.psum_scatter(gain_grad, "store", scatter_dimension=1, tiled=True),
        lax.psum_scatter(shift_grad, "store", scatter_dimension=1, tiled=True),
    )
    reduced = (
        lax.psum(shared[0].astype(jnp.bfloat16), "dp").astype(jnp.float32),
        lax.psum(shared[1].astype(jnp.bfloat16), "dp").astype(jnp.float32),
        lax.psum(shared[2].astype(jnp.bfloat16), "dp").astype(jnp.float32),
        lax.psum(shared[3].astype(jnp.bfloat16), "dp").astype(jnp.float32),
        lax.psum(shared[4].astype(jnp.bfloat16), "dp").astype(jnp.float32),
        lax.psum(shared[5].astype(jnp.bfloat16), "dp").astype(jnp.float32),
        lax.psum(shared[6].astype(jnp.bfloat16), "dp").astype(jnp.float32),
        lax.psum(shared[7].astype(jnp.bfloat16), "dp").astype(jnp.float32),
        lax.psum(shared[8].astype(jnp.bfloat16), "dp").astype(jnp.float32),
        lax.psum(shared[9].astype(jnp.bfloat16), "dp").astype(jnp.float32),
        lax.psum(shared[10].astype(jnp.bfloat16), "dp").astype(jnp.float32),
    )
    return (
        outputs,
        input_grad,
        datastore_grad,
        reduced[0],
        reduced[1],
        reduced[2],
        reduced[3],
        reduced[4],
        reduced[5],
        reduced[6],
        reduced[7],
        reduced[8],
        reduced[9],
        reduced[10],
    )


def solution(mesh):
    placed = (
        P(("dp", "store"), None),
        P(("dp", "store"), None),
        P(("dp", "store"), None),
        P(("dp", "store")),
        P(("dp", "store"), None),
        P(),
        P(),
        P(),
        P(),
        P(),
        P(),
        P(),
        P(),
        P(),
        P(),
        P(),
        P(("dp", "store"), None),
    )
    return jax.shard_map(
        local_tree if mesh.shape["store"] == 16 else local_slots,
        mesh=mesh,
        in_specs=placed,
        out_specs=(
            P(("dp", "store"), None),
            P(("dp", "store"), None),
            P(("dp", "store"), None),
            P("store", None),
            P("store", None),
            P("store", None),
            P("store", None),
            P("store", None),
            P("store", None),
            P("store", None),
            P(None, "store"),
            P("store"),
            P(None, "store"),
            P(None, "store"),
        ),
        check_vma=False,
    )
```

```python
import functools

import jax
import jax.numpy as jnp
from jax import lax
from jax.experimental import pallas as pl
from jax.experimental.pallas import tpu as pltpu
from jax.sharding import PartitionSpec as P

D = 768
HEADS = 12
HEAD_DIM = 64
TOPB = 8
BLOCK = 128
SLAB = 128
PAIRS = D // SLAB
UNIT = 384
WIDE = D + SLAB
RANK_ROWS = 16

EPSILON = 1e-05
MASKED = -1e30
QUERY_SCALE = 0.125
VMEM_LIMIT = 16 * 1024 * 1024
SMALL_LIMIT = 16 * 1024 * 1024
LONG = 30_000_000_000
UNROLL = 4
MICROSECOND = 50_000_000
LOW = jnp.bfloat16
F32 = jnp.float32

_VMEM = pl.BlockSpec(memory_space=pltpu.VMEM)
_SMEM = pl.BlockSpec(memory_space=pltpu.SMEM)
_ANY = pl.BlockSpec(memory_space=pl.ANY)


def nn(a, b):
    return lax.dot_general(a, b, (((1,), (0,)), ((), ())), preferred_element_type=F32)


def nt(a, b):
    return lax.dot_general(a, b, (((1,), (1,)), ((), ())), preferred_element_type=F32)


def tn(a, b):
    return lax.dot_general(a, b, (((0,), (0,)), ((), ())), preferred_element_type=F32)


def three(v):
    high = v.astype(LOW)
    rest = v - high.astype(F32)
    mid = rest.astype(LOW)
    return high, mid, (rest - mid.astype(F32)).astype(LOW)


def lanes(shape):
    return lax.broadcasted_iota(jnp.int32, shape, len(shape) - 1)


def rows_of(shape):
    return lax.broadcasted_iota(jnp.int32, shape, len(shape) - 2)


def flag(condition):
    return jnp.where(condition, 1.0, 0.0)


def half_masks():
    first = flag(lanes((1, SLAB)) < HEAD_DIM)
    return first.astype(LOW), (1.0 - first).astype(LOW)


def two_heads(slab, first, second):
    return jnp.concatenate([slab * first, slab * second], axis=0)


def join_heads(stacked, count):
    left = lanes((count, SLAB)) < HEAD_DIM
    return jnp.where(left, stacked[:count], stacked[count:])


def norm_forward(residual, gain, shift):
    center = residual - jnp.mean(residual, axis=-1, keepdims=True)
    spread = jnp.mean(center * center, axis=-1, keepdims=True)
    scale = lax.rsqrt(spread + EPSILON)
    unit = center * scale
    return unit * gain + shift, unit, scale


def norm_backward(grad, unit, scale, gain):
    inner = grad * gain
    down = inner - jnp.mean(inner, axis=-1, keepdims=True)
    down = down - unit * jnp.mean(inner * unit, axis=-1, keepdims=True)
    return scale * down


def row_sum(v):
    return jnp.sum(v, axis=0, keepdims=True)


def call(
    kernel,
    outs,
    scratch=(),
    n_smem=0,
    far_in=(),
    far_out=(),
    earlier=(),
    aliases=None,
    flops=0,
    limit=VMEM_LIMIT,
):
    def run(*args):
        count = len(args)

        def body(*refs):
            kernel(*refs[:count], *refs[count + len(earlier) :])

        args = [
            pltpu.with_memory_space_constraint(v, pltpu.HBM) if i in far_in and not aliases else v
            for i, v in enumerate(args)
        ]
        specs = [_ANY if i in far_in else _VMEM for i in range(n_smem, count)]
        return pl.pallas_call(
            body,
            out_shape=[jax.ShapeDtypeStruct(s, t) for s, t in outs],
            in_specs=[_SMEM] * n_smem + specs + [_ANY] * len(earlier),
            out_specs=[_ANY if i in far_out else _VMEM for i in range(len(outs))],
            scratch_shapes=list(scratch),
            input_output_aliases=aliases or {},
            compiler_params=pltpu.CompilerParams(vmem_limit_bytes=limit),
            cost_estimate=pl.CostEstimate(flops=flops, bytes_accessed=0, transcendentals=0),
        )(*args, *earlier)

    return run


def copies(pairs, sems):
    return [pltpu.make_async_copy(a, b, sems.at[i]) for i, (a, b) in enumerate(pairs)]


def after(v, *earlier):
    return call(
        lambda *refs: None,
        [(v.shape, v.dtype)],
        far_in=(0,),
        far_out=(0,),
        earlier=earlier,
        aliases={0: 0},
        limit=1024 * 1024,
    )(v)[0]


def start_all(items):
    for item in items:
        item.start()


def wait_all(items):
    for item in items:
        item.wait()


def plane_ranks(picks_ref, me, k, tokens):
    i = rows_of((RANK_ROWS, tokens))
    group, chip, block = i // 4, (i // 2) % 2, i % 2
    apart = jnp.where(group < 2, 2 * group + chip, 2 * chip + group - 2)
    local = jnp.where(group < 2, block, 2 + block)
    plane = (me // 4) ^ k
    number = plane * 16 + ((me % 4) ^ apart) * 4 + local
    member = jnp.zeros((RANK_ROWS, tokens), F32)
    for j in range(TOPB):
        member = member + flag(picks_ref[j : j + 1, :] == number)
    earlier = flag(rows_of((tokens, tokens)) < lanes((tokens, tokens)))
    rank = nn(member.astype(LOW), earlier.astype(LOW))
    return jnp.where(member > 0.5, rank, -1.0).astype(LOW)


def self_forward_kernel(
    lengths_ref,
    place_ref,
    x_ref,
    picks_ref,
    project_ref,
    output_ref,
    query_ref,
    bias_ref,
    gain_ref,
    shift_ref,
    heads_ref,
    soft_ref,
    attended_ref,
    unit_ref,
    scale_ref,
    first_ref,
    *rest,
):
    payload_refs, (project_scr, output_scr, query_scr, sems) = rest[:4], rest[4:]
    thirds = [slice(i * D, (i + 1) * D) for i in range(3)]
    fetch = copies(
        [(project_ref.at[:, at], project_scr.at[:, at]) for at in thirds]
        + [(output_ref, output_scr), (query_ref, query_scr)],
        sems,
    )
    start_all(fetch)
    tokens = x_ref.shape[0]
    bias = bias_ref[...].astype(F32)
    x = x_ref[...]
    for i, at in enumerate(thirds):
        fetch[i].wait()
        part = nn(x, project_scr[:, at])
        if i == 0:
            part = QUERY_SCALE * (part + bias[0:1])
        if i == 2:
            part = part + bias[1:2]
        heads_ref[:, at] = part.astype(LOW)
    place_row = lax.broadcasted_iota(jnp.int32, (2 * tokens, tokens), 0) % tokens
    place_col = lanes((2 * tokens, tokens))
    segment_row = jnp.zeros((2 * tokens, tokens), jnp.int32)
    segment_col = jnp.zeros((2 * tokens, tokens), jnp.int32)
    bound = 0
    for d in range(lengths_ref.shape[1]):
        bound = bound + lengths_ref[0, d]
        segment_row = segment_row + jnp.where(place_row >= bound, 1, 0)
        segment_col = segment_col + jnp.where(place_col >= bound, 1, 0)
    allowed = (segment_row == segment_col) & (place_row >= place_col)
    first, second = half_masks()
    for p in range(PAIRS):
        at = p * SLAB
        queries = two_heads(heads_ref[:, at : at + SLAB], first, second)
        scores = nt(queries, heads_ref[:, D + at : D + at + SLAB])
        scores = jnp.where(allowed, scores, MASKED)
        top = jnp.max(scores, axis=-1, keepdims=True)
        raised = jnp.exp(scores - top)
        soft = raised / jnp.sum(raised, axis=-1, keepdims=True)
        soft_ref[p] = soft
        mixed = nn(soft.astype(LOW), heads_ref[:, 2 * D + at : 2 * D + at + SLAB])
        attended_ref[:, at : at + SLAB] = join_heads(mixed, tokens).astype(LOW)
    fetch[3].wait()
    residual = x.astype(F32) + nn(attended_ref[...], output_scr[...]) + bias[2:3]
    normed, unit, scale = norm_forward(
        residual, gain_ref[0:1, :].astype(F32), shift_ref[0:1, :].astype(F32)
    )
    unit_ref[...] = unit
    scale_ref[...] = scale
    low = normed.astype(LOW)
    first_ref[...] = low
    fetch[4].wait()
    queries = (QUERY_SCALE * (nn(low, query_scr[...]) + bias[3:4])).astype(LOW)
    for k, out in enumerate(payload_refs):
        out[:tokens] = queries
        out[tokens:, tokens:] = jnp.zeros((RANK_ROWS, D - tokens), LOW)
        out[tokens:, :tokens] = plane_ranks(picks_ref, place_ref[0], k, tokens)


def piece_kernel(rows_ref, kept_ref, a_ref, b_ref):
    for h, out in enumerate((a_ref, b_ref)):
        out[: 2 * BLOCK] = rows_ref[2 * h * BLOCK : 2 * (h + 1) * BLOCK]
        marks = kept_ref[2 * h : 2 * h + 2, :].astype(F32)
        marks = jnp.concatenate([marks, jnp.zeros((RANK_ROWS - 2, BLOCK), F32)], axis=0)
        out[2 * BLOCK :, :BLOCK] = marks.astype(LOW)
        out[2 * BLOCK :, BLOCK:] = jnp.zeros((RANK_ROWS, D - BLOCK), LOW)


def pair_kernel(first_ref, second_ref, out_ref):
    out_ref[0] = first_ref[...]
    out_ref[1] = second_ref[...]


def memory_kernel(*refs):
    if len(refs) == 16:
        pieces = [ref.at[j] for ref in refs[:2] for j in range(2)]
        (weight_ref, bias_ref), given, outs = refs[2:4], refs[4:12], refs[12:]
    else:
        pieces, (weight_ref, bias_ref), given, outs = refs[:4], refs[4:6], (), refs[6:]
    bias = bias_ref[4:5, :].astype(F32)
    lane = lanes((RANK_ROWS, SLAB))
    place = lanes((BLOCK, SLAB))
    for s in range(2):
        if given:
            near, here = 8 * s, 8 * s + 4
            rows_ref, memory_ref, hidden_ref, side_ref = outs
            rows_ref[near * BLOCK : (near + 4) * BLOCK] = given[4 * s][...]
            for out, ref in zip(outs[1:], given[4 * s + 1 : 4 * s + 4]):
                out[near : near + 4] = ref[...]
        else:
            here = 0
            rows_ref, memory_ref, hidden_ref, side_ref = outs[4 * s : 4 * s + 4]
        for j in range(2):
            piece = pieces[2 * s + j]
            rows = piece[: 2 * BLOCK]
            first = here + 2 * j
            rows_ref[first * BLOCK : (first + 2) * BLOCK] = rows
            keys = nn(rows, weight_ref[:, :D]).astype(LOW)
            values = (nn(rows, weight_ref[:, D:]) + bias).astype(LOW)
            marks = piece[2 * BLOCK :, :SLAB]
            for l in range(2):
                at = first + l
                memory_ref[at, :, :D] = keys[l * BLOCK : (l + 1) * BLOCK]
                memory_ref[at, :, D:] = values[l * BLOCK : (l + 1) * BLOCK]
                hidden_ref[at] = (1.0 - marks[l : l + 1].astype(F32)) * MASKED
                wanted = flag((rows_of((RANK_ROWS, SLAB)) == l) & (lane == SLAB - 1))
                column = tn(marks, wanted.astype(LOW))
                side = jnp.where(place == SLAB - 1, (1.0 - column) * MASKED, 0.0)
                side_ref[at] = jnp.where(place < 48, -1.0, side).astype(LOW)


def selection(ranks, capacity):
    parts = []
    wanted = rows_of((capacity, ranks.shape[1])).astype(F32)
    for b in range(ranks.shape[0]):
        parts.append(flag(ranks[b : b + 1, :] == wanted).astype(LOW))
    return jnp.concatenate(parts, axis=0)


def fill_slots(sel, rows, out_ref, k, capacity):
    got = nn(sel, rows).astype(LOW)
    for b in range(out_ref.shape[0]):
        out_ref[b, k * capacity : (k + 1) * capacity, :] = got[b * capacity : (b + 1) * capacity]


def around16(v, combine):
    for step in (16, 32, 64):
        v = combine(v, pltpu.roll(v, step, 1))
    return v


def lse_lanes(lse):
    high = lse.astype(LOW).astype(F32)
    rest = lse - high
    mid = rest.astype(LOW).astype(F32)
    low = rest - mid
    lane = lanes(lse.shape)
    packed = jnp.where(
        lane < 16, high, jnp.where(lane < 32, mid, jnp.where(lane < 48, low, 0.0))
    )
    return packed.astype(LOW)


def read_lse(packed):
    return around16(packed.astype(F32), jnp.add)


def head_spread(group):
    row = rows_of((SLAB, D))
    row = row % 16 if group else row
    return flag(row == lanes((SLAB, D)) // HEAD_DIM).astype(LOW)


def owner_forward_kernel(capacity, *refs):
    tokens_refs, memory_ref, hidden_ref = refs[0:4], refs[4], refs[5]
    slots_ref, payload_refs = refs[6], refs[7:11]
    out_scr, lse_scr, inv_scr, sel_scr, ranks_scr = refs[11:]
    sources = len(tokens_refs)
    blocks, rows = slots_ref.shape[:2]
    tokens = tokens_refs[0].shape[0] - RANK_ROWS
    first, second = half_masks()
    for k in range(sources):
        ranks_scr[...] = tokens_refs[k][tokens:, :tokens].astype(F32)
        sel = selection(ranks_scr[...], capacity)
        sel_scr[k] = sel
        fill_slots(sel, tokens_refs[k][:tokens], slots_ref, k, capacity)
    ones = jnp.ones((BLOCK, SLAB), LOW)
    lane_of = lanes((rows, SLAB))
    def one_block(i, carry):
        hidden = hidden_ref[i]
        tops = jnp.zeros((rows, SLAB), F32)
        totals = jnp.ones((rows, SLAB), F32)
        base = (i % 8) * 16
        slabs = [slice(p * SLAB, (p + 1) * SLAB) for p in range(PAIRS)]
        scores = [
            nt(two_heads(slots_ref[i, :, at], first, second), memory_ref[i, :, at])
            + hidden
            for at in slabs
        ]
        highest = [jnp.max(v, axis=-1, keepdims=True) for v in scores]
        raised = [jnp.exp(v - top).astype(LOW) for v, top in zip(scores, highest)]
        mixed = [
            nn(v, jnp.concatenate([memory_ref[i, :, D + at.start : D + at.stop], ones], axis=1))
            for v, at in zip(raised, slabs)
        ]
        for p, at in enumerate(slabs):
            out_scr[i, :, at] = join_heads(mixed[p][:, :SLAB], rows)
            for half in range(2):
                here = slice(half * rows, (half + 1) * rows)
                mine = lane_of == base + 2 * p + half
                tops = jnp.where(mine, highest[p][here], tops)
                totals = jnp.where(mine, mixed[p][here, SLAB:], totals)
        own = flag((lane_of >= base) & (lane_of < base + HEADS))
        lse_scr[i] = tops + jnp.log(totals)
        inv_scr[i] = own / totals
        return carry

    lax.fori_loop(0, blocks, one_block, 0, unroll=UNROLL)
    group = 8 * capacity
    own_low = flag(
        rows_of((group, SLAB)) // capacity == lanes((group, SLAB)) // 16
    ).astype(LOW)
    spread = head_spread(True)
    for k in range(sources):
        here = slice(k * capacity, (k + 1) * capacity)

        def stacked(ref, g, here=here):
            return jnp.concatenate([ref[8 * g + b, here, :] for b in range(8)], axis=0)

        by_token, members, sels = [], [], []
        for g in range(2):
            sel = sel_scr[k, g * group : (g + 1) * group, :]
            value = sum(tn(sel, part) for part in three(stacked(lse_scr, g)))
            member = tn(sel, own_low)
            by_token.append(jnp.where(member > 0.5, value, MASKED))
            members.append(member)
            sels.append(sel)
        top = around16(jnp.maximum(*by_token), jnp.maximum)
        weights = [m * jnp.exp(v - top) for m, v in zip(members, by_token)]
        total = around16(weights[0] + weights[1], jnp.add)
        some = total > 0.5
        safe = jnp.where(some, total, 1.0)
        payload_refs[k][:, D:] = lse_lanes(jnp.where(some, top + jnp.log(safe), MASKED))
        partial = jnp.zeros((tokens, D), F32)
        for g in range(2):
            share = nn(sels[g], (weights[g] / safe).astype(LOW)) * stacked(inv_scr, g)
            value = stacked(out_scr, g) * nn(share.astype(LOW), spread)
            partial = partial + tn(sels[g], value.astype(LOW))
        payload_refs[k][:, :D] = partial.astype(LOW)


def owner_backward_kernel(capacity, *refs):
    tokens_refs, grad_refs, memory_ref, side_ref, slots_ref = refs[0:4], refs[4:8], *refs[8:11]
    out, payload_refs, bias_ref = refs[11], refs[12:16], refs[16]
    got_scr, query_scr, sel_scr, ranks_scr = refs[17:]
    sources = len(tokens_refs)
    blocks, rows = slots_ref.shape[:2]
    tokens = grad_refs[0].shape[0]
    first, second = half_masks()
    for k in range(sources):
        ranks_scr[...] = tokens_refs[k][tokens:, :tokens].astype(F32)
        sel = selection(ranks_scr[...], capacity)
        sel_scr[k] = sel
        fill_slots(sel, grad_refs[k][...], got_scr, k, capacity)
    lane = lanes((1, SLAB))
    last = flag(lane == SLAB - 1).astype(LOW)
    value_side = jnp.broadcast_to(
        -flag((lane >= 48) & (lane < 96)).astype(LOW), (BLOCK, SLAB)
    )

    def picked(head, base):
        inside = (lane >= base) & (lane < base + 48)
        return flag(inside & (lane % 16 == head)).astype(LOW)

    def one_block(i, carry):
        side = got_scr[i, :, D:]
        key_side = side_ref[i]
        slabs = [slice(p * SLAB, (p + 1) * SLAB) for p in range(PAIRS)]
        keys = [memory_ref[i, :, at] for at in slabs]
        queries = [two_heads(slots_ref[i, :, at], first, second) for at in slabs]
        grads = [two_heads(got_scr[i, :, at], first, second) for at in slabs]
        scores, dots = [], []
        for p in range(PAIRS):
            lse_side = jnp.concatenate(
                [side * picked(2 * p + h, 0) + last for h in range(2)], axis=0
            )
            scores.append(
                nt(
                    jnp.concatenate([keys[p], key_side], axis=1),
                    jnp.concatenate([queries[p], lse_side], axis=1),
                )
            )
        for p, at in enumerate(slabs):
            delta_side = jnp.concatenate(
                [side * picked(2 * p + h, 48) for h in range(2)], axis=0
            )
            values = memory_ref[i, :, D + at.start : D + at.stop]
            dots.append(
                nt(
                    jnp.concatenate([values, value_side], axis=1),
                    jnp.concatenate([grads[p], delta_side], axis=1),
                )
            )
        softs = [jnp.exp(v) for v in scores]
        score_grads = [(soft * v).astype(LOW) for soft, v in zip(softs, dots)]
        for p, at in enumerate(slabs):
            query_scr[i, :, at] = join_heads(tn(score_grads[p], keys[p]), rows).astype(LOW)
        for p, at in enumerate(slabs):
            out[i, :, at] = nn(score_grads[p], queries[p]).astype(LOW)
        for p, at in enumerate(slabs):
            out[i, :, D + at.start : D + at.stop] = nn(softs[p].astype(LOW), grads[p]).astype(
                LOW
            )
        return carry

    lax.fori_loop(0, blocks, one_block, 0, unroll=UNROLL)
    for k in range(sources):
        here = slice(k * capacity, (k + 1) * capacity)
        value = jnp.concatenate([query_scr[b, here, :] for b in range(blocks)], axis=0)
        payload_refs[k][...] = tn(sel_scr[k], value).astype(LOW)
    total = lax.fori_loop(
        0,
        blocks,
        lambda i, v: v + row_sum(out[i, :, D:].astype(F32)),
        jnp.zeros((1, D), F32),
    )
    bias_ref[...] = jnp.broadcast_to(total, (8, D))


def memory_weight_kernel(count, place_ref, *refs):
    grad_ref, rows_ref, kept_ref, sent_ref, sum_scr = refs
    me, core = place_ref[0], place_ref[1]
    size = 4 * BLOCK
    sum_scr[...] = jnp.zeros(sum_scr.shape, F32)

    def one_set(s, carry):
        at = pl.ds(pl.multiple_of(s * size, size), size)
        rows = rows_ref[at, :].T
        for h in range(2):
            sum_scr[h] = sum_scr[h] + nn(rows, grad_ref[at, h * D : (h + 1) * D])
        return carry

    lax.fori_loop(0, rows_ref.shape[0] // size, one_set, 0)
    block = D // count
    for h in range(2):

        def store(out, h=h):
            total = sum_scr[h].astype(LOW)
            for k in range(count):
                for u in range(D // UNIT):
                    out[me ^ k, u * block : (u + 1) * block, :] = total[
                        k * block : (k + 1) * block, u * UNIT : (u + 1) * UNIT
                    ]

        pl.when(core == h)(functools.partial(store, kept_ref))
        pl.when(core != h)(functools.partial(store, sent_ref))


def datastore_grad_kernel(weight_ref, *refs):
    grad_ref, outs = refs[0], refs[1:7]
    weight = weight_ref[...].T
    near_a0, near_a1, far_a, near_b0, near_b1, far_b = outs
    groups = ((near_a0, near_a1), (far_a,), (near_b0, near_b1), (far_b,))
    for s in range(4):
        value = nn(grad_ref[4 * s * BLOCK : 4 * (s + 1) * BLOCK], weight).astype(LOW)
        size = value.shape[0] // len(groups[s])
        for i, out in enumerate(groups[s]):
            out[...] = value[i * size : (i + 1) * size]


def datastore_step_kernel(*refs):
    ins, sends, keeps = refs[:6], refs[6:8], refs[8:10]
    size = 2 * BLOCK
    for g in range(2):
        stay, go, come = ins[3 * g : 3 * g + 3]
        keeps[g][...] = stay[...].astype(F32) + come[:size].astype(F32)
        sends[g][...] = (go[...].astype(F32) + come[size:].astype(F32)).astype(LOW)


def datastore_sum_kernel(keep_a, come_a, keep_b, come_b, out_ref):
    size = keep_a.shape[0]
    out_ref[:size] = keep_a[...] + come_a[...].astype(F32)
    out_ref[size:] = keep_b[...] + come_b[...].astype(F32)


def middle_kernel(
    p0_ref,
    p1_ref,
    p2_ref,
    p3_ref,
    first_ref,
    cotangent_ref,
    output_ref,
    expand_ref,
    contract_ref,
    bias_ref,
    expand_bias_ref,
    gain_ref,
    shift_ref,
    out_ref,
    merged_ref,
    second_ref,
    active_ref,
    branch_grad_ref,
    expanded_grad_ref,
    cross_grad_ref,
    resid_ref,
    payload_ref,
    small_ref,
    wide_ref,
    expanded_scr,
    output_scr,
    expand_scr,
    contract_scr,
    sems,
):
    fetch = copies(
        [(output_ref, output_scr), (expand_ref, expand_scr), (contract_ref, contract_scr)], sems
    )
    start_all(fetch)
    bias = bias_ref[...].astype(F32)
    gain = gain_ref[...].astype(F32)
    shift = shift_ref[...].astype(F32)
    parts = [p0_ref, p1_ref, p2_ref, p3_ref]
    lses = [read_lse(part[:, D:]) for part in parts]
    top = functools.reduce(jnp.maximum, lses)
    weights = [jnp.exp(lse - top) for lse in lses]
    total = functools.reduce(jnp.add, weights)
    overall = top + jnp.log(total)
    spread = head_spread(False)
    merged = jnp.zeros(first_ref.shape, F32)
    for part, weight in zip(parts, weights):
        share = weight / total
        high = share.astype(LOW)
        rest = (share - high.astype(F32)).astype(LOW)
        merged = merged + (nn(high, spread) + nn(rest, spread)) * part[:, :D].astype(F32)
    merged_low = merged.astype(LOW)
    merged_ref[...] = merged_low
    fetch[0].wait()
    residual = first_ref[...].astype(F32) + nn(merged_low, output_scr[...]) + bias[5:6]
    second, unit_second, scale_second = norm_forward(residual, gain[1:2], shift[1:2])
    second_low = second.astype(LOW)
    second_ref[...] = second_low
    hidden = contract_scr.shape[0]
    fetch[1].wait()
    for c in range(hidden // D):
        at = slice(c * D, (c + 1) * D)
        expanded = nn(second_low, expand_scr[:, at]) + expand_bias_ref[:, at].astype(F32)
        bell = 0.5 * (1.0 + lax.erf(expanded * 0.7071067811865476))
        active_ref[:, at] = (expanded * bell).astype(LOW)
        slope = bell + expanded * 0.3989422804014327 * jnp.exp(-0.5 * expanded * expanded)
        expanded_scr[:, at] = slope
    fetch[2].wait()
    residual = second_low.astype(F32) + nn(active_ref[...], contract_scr[...]) + bias[6:7]
    final, unit_final, scale_final = norm_forward(residual, gain[2:3], shift[2:3])
    out_ref[...] = final.astype(LOW)
    cotangent = cotangent_ref[...].astype(F32)
    final_resid = norm_backward(cotangent, unit_final, scale_final, gain[2:3])
    branch_grad = final_resid.astype(LOW)
    branch_grad_ref[...] = branch_grad
    small_ref[0:1, :] = row_sum(branch_grad.astype(F32))
    small_ref[1:2, :] = row_sum(cotangent * unit_final)
    small_ref[2:3, :] = row_sum(cotangent)
    total_grad = final_resid
    for c in range(hidden // D):
        at = slice(c * D, (c + 1) * D)
        active_grad = nt(branch_grad, contract_scr[at, :])
        expanded_grad = (active_grad * expanded_scr[:, at]).astype(LOW)
        expanded_grad_ref[:, at] = expanded_grad
        wide_ref[:, at] = row_sum(expanded_grad.astype(F32))
        total_grad = total_grad + nt(expanded_grad, expand_scr[:, at])
    small_ref[4:5, :] = row_sum(total_grad * unit_second)
    small_ref[5:6, :] = row_sum(total_grad)
    second_resid = norm_backward(total_grad, unit_second, scale_second, gain[1:2])
    resid_ref[...] = second_resid
    cross_grad = second_resid.astype(LOW)
    cross_grad_ref[...] = cross_grad
    small_ref[3:4, :] = row_sum(cross_grad.astype(F32))
    small_ref[6:8, :] = jnp.zeros((2, D), F32)
    attended_grad = nt(cross_grad, output_scr[...]).astype(LOW)
    payload_ref[:, :D] = attended_grad
    product = attended_grad.astype(F32) * merged
    gather = flag(lanes((D, SLAB)) % 16 == rows_of((D, SLAB)) // HEAD_DIM).astype(LOW)
    high, mid, low = three(product)
    delta = nn(high, gather) + nn(mid, gather) + nn(low, gather)
    lane = lanes(overall.shape)
    packed = jnp.zeros(overall.shape, F32)
    for value, base in ((overall, 0), (delta, 48)):
        for i, piece in enumerate(three(value)):
            inside = (lane >= base + 16 * i) & (lane < base + 16 * i + HEADS)
            packed = jnp.where(inside, piece.astype(F32), packed)
    payload_ref[:, D:] = packed.astype(LOW)


def self_backward_kernel(
    d0_ref,
    d1_ref,
    d2_ref,
    d3_ref,
    resid_ref,
    unit_ref,
    scale_ref,
    heads_ref,
    soft_ref,
    query_ref,
    output_ref,
    project_ref,
    gain_ref,
    pre_grad_ref,
    branch_grad_ref,
    project_grad_ref,
    input_grad_ref,
    small_ref,
    attended_scr,
    query_scr,
    output_scr,
    heads_scr,
    soft_scr,
    project_scr,
    sems,
):
    fetch = copies(
        [
            (query_ref, query_scr),
            (output_ref, output_scr),
            (heads_ref, heads_scr),
            (soft_ref, soft_scr),
            (project_ref, project_scr),
        ],
        sems,
    )
    start_all(fetch)
    tokens = resid_ref.shape[0]
    query_sum = functools.reduce(
        jnp.add, [d[...].astype(F32) for d in (d0_ref, d1_ref, d2_ref, d3_ref)]
    ).astype(LOW)
    pre_grad = (query_sum.astype(F32) * QUERY_SCALE).astype(LOW)
    pre_grad_ref[...] = pre_grad
    fetch[0].wait()
    total = resid_ref[...] + nt(pre_grad, query_scr[...])
    unit = unit_ref[...]
    first_resid = norm_backward(total, unit, scale_ref[...], gain_ref[0:1, :].astype(F32))
    branch_grad = first_resid.astype(LOW)
    branch_grad_ref[...] = branch_grad
    fetch[1].wait()
    attended_scr[...] = nt(branch_grad, output_scr[...]).astype(LOW)
    fetch[2].wait()
    fetch[3].wait()
    first, second = half_masks()
    for p in range(PAIRS):
        at = p * SLAB
        grads = two_heads(attended_scr[:, at : at + SLAB], first, second)
        queries = two_heads(heads_scr[:, at : at + SLAB], first, second)
        keys = heads_scr[:, D + at : D + at + SLAB]
        dots = nt(grads, heads_scr[:, 2 * D + at : 2 * D + at + SLAB])
        soft = soft_scr[p]
        score_grad = (soft * (dots - jnp.sum(soft * dots, axis=-1, keepdims=True))).astype(LOW)
        query_grad = join_heads(nn(score_grad, keys), tokens).astype(LOW)
        project_grad_ref[:, at : at + SLAB] = (query_grad.astype(F32) * QUERY_SCALE).astype(LOW)
        project_grad_ref[:, D + at : D + at + SLAB] = tn(score_grad, queries).astype(LOW)
        project_grad_ref[:, 2 * D + at : 2 * D + at + SLAB] = tn(soft.astype(LOW), grads).astype(
            LOW
        )
    fetch[4].wait()
    input_grad_ref[...] = first_resid + nt(project_grad_ref[...], project_scr[...])
    small_ref[0:1, :] = row_sum(project_grad_ref[:, :D].astype(F32))
    small_ref[1:2, :] = row_sum(project_grad_ref[:, 2 * D :].astype(F32))
    small_ref[2:3, :] = row_sum(branch_grad.astype(F32))
    small_ref[3:4, :] = row_sum(pre_grad.astype(F32))
    small_ref[4:5, :] = row_sum(total * unit)
    small_ref[5:6, :] = row_sum(total)
    small_ref[6:8, :] = jnp.zeros((2, D), F32)


def weight_grad_kernel(plan, count, packed, held, place_ref, *refs):
    kept_ref, sent_ref = refs[-2:]
    me, core = place_ref[0], place_ref[1]
    at_ref = 0
    for number, rows, columns, at in plan:
        pairs = [refs[at_ref + 2 * i : at_ref + 2 * i + 2] for i in range(number)]
        at_ref += 2 * number
        block = rows // count
        half = columns // 2
        steps = [(c, min(D, half - c)) for c in range(0, half, D)]

        def unit(m, c, wide, block=block, half=half, at=at, pairs=pairs):
            xs = [x_ref[:, pl.ds(pl.multiple_of(m * D, SLAB), D)].T for x_ref, _ in pairs]
            for mine, out in ((core, kept_ref), (1 - core, sent_ref)):
                start = pl.multiple_of(mine * half + c, SLAB)
                part = sum(nn(x, g_ref[:, pl.ds(start, wide)]) for x, (_, g_ref) in zip(xs, pairs))
                part = part.astype(LOW)
                for u in range(wide // UNIT):
                    low = pl.multiple_of(at + (c // UNIT + u) * block, 16)
                    for k in range(D // block):
                        to = me ^ (m * (D // block) + k)
                        out[to, pl.ds(low, block), :] = part[
                            k * block : (k + 1) * block, u * UNIT : (u + 1) * UNIT
                        ]

        if rows > D:
            for c, wide in steps:

                def by_rows(m, carry, c=c, wide=wide, unit=unit):
                    unit(m, c, wide)
                    return carry

                lax.fori_loop(0, rows // D, by_rows, 0)
        elif half % D == 0 and half > D:

            def by_columns(c, carry, unit=unit):
                unit(0, c * D, D)
                return carry

            lax.fori_loop(0, half // D, by_columns, 0)
        else:
            for c, wide in steps:
                unit(0, c, wide)
    if packed is not None:
        pack_small(refs[at_ref : at_ref + 4], kept_ref, sent_ref, packed, me, core, count)
        at_ref += 4
    if held:
        for ref, out in zip(refs[at_ref : at_ref + 2], (kept_ref, sent_ref)):
            out[:, :held, :] = ref[...]


def pack_small(small_refs, kept_ref, sent_ref, low, me, core, count):
    own, middle, value_bias, wide = small_refs
    order = [own[0:4], value_bias[0:1], middle[3:4], middle[0:1], own[4:5], middle[4:5]]
    order += [middle[1:2], own[5:6], middle[5:6], middle[2:3], jnp.zeros((3, D), F32)]
    narrow = jnp.concatenate(order, axis=0)
    share = D // count
    broad = wide.shape[1] // count
    for r in range(count):
        first = narrow[:, r * share : (r + 1) * share]
        first = jnp.concatenate([first, jnp.zeros((RANK_ROWS, UNIT - share), F32)], axis=1)
        second = wide[:, r * broad : (r + 1) * broad]
        second = jnp.concatenate([second, jnp.zeros((1, UNIT - broad), F32)], axis=1)
        second = jnp.broadcast_to(second, (RANK_ROWS, UNIT))
        here = slice(low, low + RANK_ROWS)
        kept_ref[me ^ r, here, :] = jnp.where(core == 0, first, second).astype(LOW)
        sent_ref[me ^ r, here, :] = jnp.where(core == 0, second, first).astype(LOW)


def total_of(*refs):
    return functools.reduce(jnp.add, [ref[...].astype(F32) for ref in refs])


def split_kernel(x, kept_ref, come_ref, *refs):
    far, outs = ((), refs) if x else (refs[:2], refs[2:])
    half = kept_ref.shape[3] // 2
    for z in range(4):
        for g in range(2):
            at = (z, slice(None), x, slice(0, half)) if g == 0 else (z, x, slice(None), slice(half, 2 * half))
            total = kept_ref[at].astype(F32) + come_ref[at].astype(F32)
            if far:
                total = total + far[g][z].astype(F32)
                for i in range(2):
                    outs[2 * g + i][z] = total[i].astype(LOW)
            else:
                outs[g][z] = total.astype(LOW)


def join_kernel(a_keep, a_come, b_keep, b_come, *outs):
    rows = a_keep.shape[1]
    for z, out in enumerate(outs):
        out[:rows] = total_of(a_keep.at[z], a_come.at[z]).astype(LOW)
        out[rows:] = total_of(b_keep.at[z], b_come.at[z]).astype(LOW)


def sum_kernel(*refs):
    refs[-1][...] = total_of(*refs[:-1]).astype(LOW)


def spread_kernel(plan, count, packed, place_ref, own_ref, other_ref, *outs):
    core = place_ref[1]
    for (rows, columns, at), out in zip(plan, outs):
        block = rows // count
        half = columns // 2
        for c in range(half // UNIT):
            low = at + c * block
            for value, mine in ((own_ref, core), (other_ref, 1 - core)):
                start = pl.multiple_of(mine * half + c * UNIT, SLAB)
                out[:, pl.ds(start, UNIT)] = value[low : low + block].astype(F32)
    if packed is not None:
        here = slice(packed, packed + RANK_ROWS)
        own, other = own_ref[here].astype(F32), other_ref[here].astype(F32)
        narrow, wide = jnp.where(core == 0, own, other), jnp.where(core == 0, other, own)
        biases_ref, wide_ref, gain_ref, shift_ref = outs[len(plan) :]
        share = biases_ref.shape[1]
        biases_ref[...] = narrow[0:7, :share]
        gain_ref[...] = narrow[7:10, :share]
        shift_ref[...] = narrow[10:13, :share]
        wide_ref[...] = wide[0:1, : wide_ref.shape[1]]


def swap(v, bits):
    count = lax.axis_size("store")
    return lax.ppermute(v, "store", [(i, i ^ bits) for i in range(count)])


def swap_core(v):
    return lax.ppermute(v, "dp", [(0, 1), (1, 0)])


class WeightSums:
    def __init__(self, place, count, rows):
        self.place, self.count, self.rows = place, count, rows
        self.plan, self.packed, self.at = [], None, 0
        self.buffers = ()

    def add(self, products, small=None, earlier=(), flops=0):
        plan, base, packed = [], self.at, None
        for pairs in products:
            rows, columns = pairs[0][0].shape[1], pairs[0][1].shape[1]
            plan.append((len(pairs), rows, columns, self.at))
            self.plan.append((rows, columns, self.at))
            self.at += rows // self.count * (columns // 2 // UNIT)
        args = [v for pairs in products for pair in pairs for v in pair]
        if small is not None:
            packed = self.packed = self.at
            self.at += RANK_ROWS
            args.extend(small)
        shape = (self.count, self.rows, UNIT)
        self.buffers = call(
            functools.partial(weight_grad_kernel, tuple(plan), self.count, packed, base),
            [(shape, LOW), (shape, LOW)],
            n_smem=1,
            earlier=earlier,
            flops=flops,
        )(self.place, *args, *self.buffers)
        return self.buffers

    def split(self, x, far=(), earlier=()):
        half = (4, 2, self.rows // 2, UNIT)
        outs = [half[:1] + half[2:]] * 4 if far else [half] * 2
        args = [v.reshape(4, 2, 2, self.rows, UNIT) for v in (self.kept, self.come)] + list(far)
        return call(
            functools.partial(split_kernel, x),
            [(shape, LOW) for shape in outs],
            earlier=earlier,
            limit=SMALL_LIMIT,
        )(*args)

    def start(self, earlier=()):
        self.kept, sent = self.buffers
        self.come = swap_core(sent)
        self.sent = self.split(1, earlier=earlier)
        return self.sent

    def first(self, *earlier):
        come = (swap(self.sent[0], 1), swap(self.sent[1], 2))
        a_keep, a_send, b_keep, b_send = self.split(0, come, earlier)
        self.kept, self.sent = (a_keep, b_keep), (a_send, b_send)
        return self.sent

    def second(self, *earlier):
        come = (swap(self.sent[0], 2), swap(self.sent[1], 1))
        self.w = call(
            join_kernel, [((self.rows, UNIT), LOW)] * 4, earlier=earlier, limit=SMALL_LIMIT
        )(self.kept[0], come[0], self.kept[1], come[1])
        return self.w

    def third(self, *earlier):
        come = [swap(self.w[k], 4 * k) for k in (1, 2, 3)]
        (self.own,) = call(
            sum_kernel, [(come[0].shape, LOW)], earlier=earlier, limit=SMALL_LIMIT
        )(self.w[0], *come)
        return self.own

    def finish(self, small=()):
        other = swap_core(self.own)
        shapes = [((rows // self.count, columns), F32) for rows, columns, _ in self.plan]
        shapes += [(shape, F32) for shape in small]
        return call(
            functools.partial(spread_kernel, tuple(self.plan), self.count, self.packed),
            shapes,
            n_smem=1,
            limit=SMALL_LIMIT,
        )(self.place, self.own, other)


def local_tree(
    inputs,
    doc_lengths,
    datastore,
    kept_mask,
    retrieved,
    self_project,
    self_output,
    cross_query,
    cross_memory,
    cross_output,
    expand_weight,
    contract_weight,
    biases,
    expand_bias,
    norm_gain,
    norm_shift,
    cotangent,
):
    tokens = inputs.shape[0]
    count = lax.axis_size("store")
    local_blocks = datastore.shape[0] // BLOCK
    all_blocks = local_blocks * count
    capacity = 2 * tokens * TOPB // all_blocks
    plane_blocks = 4 * local_blocks
    rows_in = 4 * capacity
    hidden = expand_weight.shape[1]
    me = lax.axis_index("store").astype(jnp.int32)
    core = lax.axis_index("dp").astype(jnp.int32)
    place = jnp.stack([me, core])

    piece = ((2 * BLOCK + RANK_ROWS, D), LOW)
    a0, b0 = call(piece_kernel, [piece] * 2)(datastore, kept_mask.reshape(local_blocks, BLOCK))
    a1, b1 = swap(a0, 1), swap(b0, 2)
    heads_all, soft_self, attended, unit_first, scale_first, first_low, *queries = call(
        self_forward_kernel,
        [
            ((tokens, 3 * D), LOW),
            ((PAIRS, 2 * tokens, tokens), F32),
            ((tokens, D), LOW),
            ((tokens, D), F32),
            ((tokens, 1), F32),
            ((tokens, D), LOW),
        ]
        + [((tokens + RANK_ROWS, D), LOW)] * 4,
        scratch=[
            pltpu.VMEM((D, 3 * D), LOW),
            pltpu.VMEM((D, D), LOW),
            pltpu.VMEM((D, D), LOW),
            pltpu.SemaphoreType.DMA((5,)),
        ],
        n_smem=2,
        far_in=(4, 5, 6),
        flops=8 * MICROSECOND,
    )(
        doc_lengths,
        place,
        inputs,
        retrieved.T,
        self_project,
        self_output,
        cross_query,
        biases,
        norm_gain,
        norm_shift,
    )
    pair = call(pair_kernel, [((2, *piece[0]), LOW)], earlier=(first_low,))
    ay, bx = swap(pair(a0, a1)[0], 2), swap(pair(b0, b1)[0], 1)
    queries = [queries[0]] + [swap(queries[k], 4 * k) for k in (1, 2, 3)]

    def of_blocks(blocks):
        return [
            ((blocks * BLOCK, D), LOW),
            ((blocks, BLOCK, 2 * D), LOW),
            ((blocks, 1, BLOCK), F32),
            ((blocks, BLOCK, SLAB), LOW),
        ]

    near = call(memory_kernel, of_blocks(4) * 2)(a0, a1, b0, b1, cross_memory, biases)
    stored, memory, hidden_rows, key_side = call(memory_kernel, of_blocks(plane_blocks))(
        ay, bx, cross_memory, biases, *near
    )

    slots, *payloads = call(
        functools.partial(owner_forward_kernel, capacity),
        [((plane_blocks, rows_in, D), LOW)] + [((tokens, WIDE), LOW)] * 4,
        scratch=[
            pltpu.VMEM((plane_blocks, rows_in, D), F32),
            pltpu.VMEM((plane_blocks, rows_in, SLAB), F32),
            pltpu.VMEM((plane_blocks, rows_in, SLAB), F32),
            pltpu.VMEM((4, plane_blocks * capacity, tokens), LOW),
            pltpu.VMEM((RANK_ROWS, tokens), F32),
        ],
        flops=20 * MICROSECOND,
    )(*queries, memory, hidden_rows)
    parts = [payloads[0]] + [swap(payloads[k], 4 * k) for k in (1, 2, 3)]

    (
        outputs,
        merged_low,
        second_low,
        active_low,
        branch_grad,
        expanded_grad,
        cross_grad,
        second_resid,
        payload,
        small_middle,
        wide_bias,
    ) = call(
        middle_kernel,
        [
            ((tokens, D), LOW),
            ((tokens, D), LOW),
            ((tokens, D), LOW),
            ((tokens, hidden), LOW),
            ((tokens, D), LOW),
            ((tokens, hidden), LOW),
            ((tokens, D), LOW),
            ((tokens, D), F32),
            ((tokens, WIDE), LOW),
            ((8, D), F32),
            ((1, hidden), F32),
        ],
        scratch=[
            pltpu.VMEM((tokens, hidden), F32),
            pltpu.VMEM((D, D), LOW),
            pltpu.VMEM((D, hidden), LOW),
            pltpu.VMEM((hidden, D), LOW),
            pltpu.SemaphoreType.DMA((3,)),
        ],
        far_in=(6, 7, 8),
        flops=12 * MICROSECOND,
    )(
        *parts,
        first_low,
        cotangent,
        cross_output,
        expand_weight,
        contract_weight,
        biases,
        expand_bias.reshape(1, hidden),
        norm_gain,
        norm_shift,
    )
    grads = [payload] + [swap(payload, 4 * k) for k in (1, 2, 3)]

    early = WeightSums(place, count, 432)
    early.add(
        [[(active_low, branch_grad)], [(merged_low, cross_grad)], [(second_low, expanded_grad)]],
        flops=8 * MICROSECOND,
    )
    early_start = early.start()

    out = call(
        functools.partial(owner_backward_kernel, capacity),
        [((plane_blocks, BLOCK, 2 * D), LOW)] + [((tokens, D), LOW)] * 4 + [((8, D), F32)],
        scratch=[
            pltpu.VMEM((plane_blocks, rows_in, WIDE), LOW),
            pltpu.VMEM((plane_blocks, rows_in, D), LOW),
            pltpu.VMEM((4, plane_blocks * capacity, tokens), LOW),
            pltpu.VMEM((RANK_ROWS, tokens), F32),
        ],
        earlier=early_start,
        flops=LONG,
    )(*queries, *grads, memory, key_side, slots)
    memory_grad, query_grads, value_bias_grad = out[0], out[1:5], out[5]
    parts = [query_grads[0]] + [swap(query_grads[k], 4 * k) for k in (1, 2, 3)]

    early_first = early.first(memory_grad)
    late = WeightSums(place, count, 352)
    flat_grad = memory_grad.reshape(plane_blocks * BLOCK, 2 * D)
    late.buffers = call(
        functools.partial(memory_weight_kernel, count),
        [((count, 2 * D // count, UNIT), LOW)] * 2,
        scratch=[pltpu.VMEM((2, D, D), F32)],
        n_smem=1,
        earlier=early_first,
        flops=MICROSECOND // 10,
    )(place, flat_grad, stored)
    late.plan, late.at = [(D, 2 * D, 0)], 2 * D // count

    pre_grad, self_branch_grad, project_grad, input_grad, small_self = call(
        self_backward_kernel,
        [
            ((tokens, D), LOW),
            ((tokens, D), LOW),
            ((tokens, 3 * D), LOW),
            ((tokens, D), F32),
            ((8, D), F32),
        ],
        scratch=[
            pltpu.VMEM((tokens, D), LOW),
            pltpu.VMEM((D, D), LOW),
            pltpu.VMEM((D, D), LOW),
            pltpu.VMEM((tokens, 3 * D), LOW),
            pltpu.VMEM((PAIRS, 2 * tokens, tokens), F32),
            pltpu.VMEM((D, 3 * D), LOW),
            pltpu.SemaphoreType.DMA((5,)),
        ],
        far_in=(7, 8, 9, 10, 11),
        earlier=(late.buffers[0],),
        flops=LONG // 3,
    )(
        *parts,
        second_resid,
        unit_first,
        scale_first,
        heads_all,
        soft_self,
        cross_query,
        self_output,
        self_project,
        norm_gain,
    )
    early_second = early.second()
    late.add(
        [[(attended, self_branch_grad)], [(first_low, pre_grad)], [(inputs, project_grad)]],
        (small_self, small_middle, value_bias_grad, wide_bias),
        earlier=(early_second[0],),
        flops=MICROSECOND // 10,
    )
    near_a0, near_a1, far_a, near_b0, near_b1, far_b = call(
        datastore_grad_kernel,
        [((2 * BLOCK, D), LOW), ((2 * BLOCK, D), LOW), ((4 * BLOCK, D), LOW)] * 2,
        earlier=(late.buffers[0],),
        flops=MICROSECOND // 10,
    )(cross_memory, flat_grad)
    late.start(earlier=(far_a,))
    late_first = late.first()
    early.third(late_first[0])
    contract_weight_grad, cross_output_grad, expand_weight_grad = early.finish()
    late.second(contract_weight_grad)
    far_a, far_b = (after(v, late.w[0]) for v in (far_a, far_b))
    come_a, come_b = swap(far_a, 2), swap(far_b, 1)
    quarter = (2 * BLOCK, D)
    send_a, send_b, keep_a, keep_b = call(
        datastore_step_kernel, [(quarter, LOW)] * 2 + [(quarter, F32)] * 2, limit=SMALL_LIMIT
    )(near_a0, near_a1, come_a, near_b0, near_b1, come_b)
    (datastore_grad,) = call(
        datastore_sum_kernel, [((4 * BLOCK, D), F32)], limit=SMALL_LIMIT
    )(keep_a, swap(send_a, 1), keep_b, swap(send_b, 2))
    late.third(send_a)
    share = D // count
    (
        cross_memory_grad,
        self_output_grad,
        cross_query_grad,
        self_project_grad,
        biases_grad,
        wide_grad,
        gain_grad,
        shift_grad,
    ) = late.finish([(7, share), (1, hidden // count), (3, share), (3, share)])
    return (
        outputs,
        input_grad,
        datastore_grad,
        self_project_grad,
        self_output_grad,
        cross_query_grad,
        cross_memory_grad,
        cross_output_grad,
        expand_weight_grad,
        contract_weight_grad,
        biases_grad,
        wide_grad.reshape(hidden // count),
        gain_grad,
        shift_grad,
    )


def layer_norm(residual, gain_row, shift_row):
    center = residual - jnp.mean(residual, axis=-1, keepdims=True)
    spread = jnp.mean(center * center, axis=-1, keepdims=True)
    return center * lax.rsqrt(spread + EPSILON) * gain_row + shift_row


def doc_mask(lengths, seq_tokens):
    upto = jnp.tri(lengths.shape[-1], dtype=jnp.int32)
    bounds = jnp.sum(lengths[..., None, :] * upto, axis=-1)
    places = jnp.arange(seq_tokens, dtype=jnp.int32)
    segment = jnp.sum((places[:, None] >= bounds[..., None, :]).astype(jnp.int32), axis=-1)
    causal = places[:, None] >= places[None, :]
    return (segment[..., :, None] == segment[..., None, :]) & causal


def slot_numbers(picks, capacity):
    flat_ids = picks.reshape(-1)
    sorter = jnp.argsort(flat_ids, stable=True)
    sorted_ids = flat_ids[sorter]
    first_seen = jnp.searchsorted(sorted_ids, sorted_ids, side="left")
    rank_sorted = jnp.arange(flat_ids.shape[0], dtype=jnp.int32) - first_seen
    ranks = jnp.zeros_like(flat_ids).at[sorter].set(rank_sorted)
    return flat_ids * capacity + ranks


def place_rows(rows, slot_ids, total_slots, store_count, local_blocks, capacity):
    placed = jnp.zeros((total_slots, rows.shape[1]), rows.dtype).at[slot_ids].set(rows)
    return placed.reshape(store_count, local_blocks, capacity, rows.shape[1])


def local_slots(
    inputs,
    doc_lengths,
    datastore,
    kept_mask,
    retrieved,
    self_project,
    self_output,
    cross_query,
    cross_memory,
    cross_output,
    expand_weight,
    contract_weight,
    biases,
    expand_bias,
    norm_gain,
    norm_shift,
    cotangent,
):
    tok_count = inputs.shape[0]
    store_count = lax.axis_size("store")
    local_blocks = datastore.shape[0] // BLOCK
    all_blocks = local_blocks * store_count
    capacity = 2 * tok_count * TOPB // all_blocks
    rows_in = store_count * capacity
    total_slots = all_blocks * capacity
    gain_rows = norm_gain.astype(jnp.float32)
    shift_rows = norm_shift.astype(jnp.float32)
    bias_rows = biases.astype(jnp.float32)
    projected = jnp.dot(inputs, self_project, preferred_element_type=jnp.float32)
    heads_all = jnp.concatenate(
        [
            QUERY_SCALE * (projected[:, :D] + bias_rows[0]),
            projected[:, D : 2 * D],
            projected[:, 2 * D :] + bias_rows[1],
        ],
        axis=1,
    ).astype(jnp.bfloat16)
    queries = heads_all[:, :D].reshape(tok_count, HEADS, HEAD_DIM)
    keys_self = heads_all[:, D : 2 * D].reshape(tok_count, HEADS, HEAD_DIM)
    values_self = heads_all[:, 2 * D :].reshape(tok_count, HEADS, HEAD_DIM)
    allowed = doc_mask(doc_lengths[0], tok_count)

    def self_scores():
        raw_scores = jnp.einsum(
            "qhd,khd->hqk", queries, keys_self, preferred_element_type=jnp.float32
        )
        return jnp.where(allowed[None], raw_scores, MASKED)

    scores = self_scores()
    self_lse = jax.nn.logsumexp(scores, axis=-1)
    soft_low = jnp.exp(scores - self_lse[..., None]).astype(jnp.bfloat16)
    attended = (
        jnp.einsum("hqk,khd->qhd", soft_low, values_self, preferred_element_type=jnp.float32)
        .reshape(tok_count, D)
        .astype(jnp.bfloat16)
    )
    self_branch = jnp.dot(attended, self_output, preferred_element_type=jnp.float32) + bias_rows[2]
    first_norm, first_back = jax.vjp(
        layer_norm, inputs.astype(jnp.float32) + self_branch, gain_rows[0], shift_rows[0]
    )
    first_low = first_norm.astype(jnp.bfloat16)
    cross_queries = (
        QUERY_SCALE
        * (jnp.dot(first_low, cross_query, preferred_element_type=jnp.float32) + bias_rows[3])
    ).astype(jnp.bfloat16)
    slot_ids = slot_numbers(retrieved, capacity)
    send_buffer = place_rows(
        jnp.repeat(cross_queries, TOPB, axis=0),
        slot_ids,
        total_slots,
        store_count,
        local_blocks,
        capacity,
    )
    arrived = lax.all_to_all(send_buffer, "store", split_axis=0, concat_axis=2, tiled=True)
    owner_queries = arrived[0].reshape(local_blocks, rows_in, HEADS, HEAD_DIM)
    memory_bias = jnp.concatenate([jnp.zeros((D,), jnp.float32), bias_rows[4]])
    memory_low = (
        jnp.dot(datastore, cross_memory, preferred_element_type=jnp.float32) + memory_bias
    ).astype(jnp.bfloat16)
    memory_blocks = memory_low.reshape(local_blocks, BLOCK, 2 * D)
    store_keys = memory_blocks[:, :, :D].reshape(local_blocks, BLOCK, HEADS, HEAD_DIM)
    store_values = memory_blocks[:, :, D:].reshape(local_blocks, BLOCK, HEADS, HEAD_DIM)
    kept_rows = kept_mask.reshape(local_blocks, BLOCK) > 0

    def block_scores(query_blocks):
        raw_scores = jnp.einsum(
            "bmhd,bkhd->bhmk", query_blocks, store_keys, preferred_element_type=jnp.float32
        )
        return jnp.where(kept_rows[:, None, None, :], raw_scores, MASKED)

    owner_scores = block_scores(owner_queries)
    owner_lse = jax.nn.logsumexp(owner_scores, axis=-1)
    owner_soft = jnp.exp(owner_scores - owner_lse[..., None]).astype(jnp.bfloat16)
    partial_value = jnp.einsum(
        "bhmk,bkhd->bmhd", owner_soft, store_values, preferred_element_type=jnp.float32
    ).reshape(local_blocks, rows_in, D)
    partial_lse = jnp.transpose(owner_lse, (0, 2, 1))
    returned, returned_lse = (
        lax.all_to_all(partial_value[None], "store", split_axis=2, concat_axis=0, tiled=True),
        lax.all_to_all(partial_lse[None], "store", split_axis=2, concat_axis=0, tiled=True),
    )
    picked = returned.reshape(total_slots, D)[slot_ids].reshape(tok_count, TOPB, HEADS, HEAD_DIM)
    picked_lse = returned_lse.reshape(total_slots, HEADS)[slot_ids].reshape(tok_count, TOPB, HEADS)
    overall = jax.nn.logsumexp(picked_lse, axis=1)
    mix_weights = jnp.exp(picked_lse - overall[:, None, :])
    merged = jnp.einsum(
        "tjh,tjhd->thd", mix_weights, picked, precision=lax.Precision.HIGHEST
    ).reshape(tok_count, D)
    merged_low = merged.astype(jnp.bfloat16)
    cross_branch = (
        jnp.dot(merged_low, cross_output, preferred_element_type=jnp.float32) + bias_rows[5]
    )
    second_norm, second_back = jax.vjp(
        layer_norm, first_low.astype(jnp.float32) + cross_branch, gain_rows[1], shift_rows[1]
    )
    second_low = second_norm.astype(jnp.bfloat16)
    expanded = jnp.dot(
        second_low, expand_weight, preferred_element_type=jnp.float32
    ) + expand_bias.astype(jnp.float32)
    activated, gelu_back = jax.vjp(
        lambda pre_act: jax.nn.gelu(pre_act, approximate=False), expanded
    )
    activated_low = activated.astype(jnp.bfloat16)
    ffn_branch = (
        jnp.dot(activated_low, contract_weight, preferred_element_type=jnp.float32) + bias_rows[6]
    )
    final_norm, final_back = jax.vjp(
        layer_norm, second_low.astype(jnp.float32) + ffn_branch, gain_rows[2], shift_rows[2]
    )
    outputs = final_norm.astype(jnp.bfloat16)
    final_resid, final_gain, final_shift = final_back(cotangent.astype(jnp.float32))
    ffn_branch_grad = final_resid.astype(jnp.bfloat16)
    contract_weight_grad = jnp.dot(
        activated_low.T, ffn_branch_grad, preferred_element_type=jnp.float32
    )
    activated_grad = jnp.dot(ffn_branch_grad, contract_weight.T, preferred_element_type=jnp.float32)
    (expanded_raw,) = gelu_back(activated_grad)
    expanded_grad = expanded_raw.astype(jnp.bfloat16)
    expand_weight_grad = jnp.dot(second_low.T, expanded_grad, preferred_element_type=jnp.float32)
    expand_bias_grad = jnp.sum(expanded_grad.astype(jnp.float32), axis=0)
    second_total = final_resid + jnp.dot(
        expanded_grad, expand_weight.T, preferred_element_type=jnp.float32
    )
    second_resid, second_gain, second_shift = second_back(second_total)
    cross_branch_grad = second_resid.astype(jnp.bfloat16)
    cross_output_grad = jnp.dot(merged_low.T, cross_branch_grad, preferred_element_type=jnp.float32)
    attended_grad = jnp.dot(
        cross_branch_grad, cross_output.T, preferred_element_type=jnp.float32
    ).astype(jnp.bfloat16)
    delta_rows = jnp.sum(
        attended_grad.reshape(tok_count, HEADS, HEAD_DIM).astype(jnp.float32)
        * merged.reshape(tok_count, HEADS, HEAD_DIM),
        axis=-1,
    )
    grad_buffer = place_rows(
        jnp.repeat(attended_grad, TOPB, axis=0),
        slot_ids,
        total_slots,
        store_count,
        local_blocks,
        capacity,
    )
    overall_buffer = place_rows(
        jnp.repeat(overall, TOPB, axis=0),
        slot_ids,
        total_slots,
        store_count,
        local_blocks,
        capacity,
    )
    delta_buffer = place_rows(
        jnp.repeat(delta_rows, TOPB, axis=0),
        slot_ids,
        total_slots,
        store_count,
        local_blocks,
        capacity,
    )
    arrived_grad = lax.all_to_all(grad_buffer, "store", split_axis=0, concat_axis=2, tiled=True)
    arrived_overall, arrived_delta = (
        lax.all_to_all(overall_buffer, "store", split_axis=0, concat_axis=2, tiled=True),
        lax.all_to_all(delta_buffer, "store", split_axis=0, concat_axis=2, tiled=True),
    )
    owner_grad = arrived_grad[0].reshape(local_blocks, rows_in, HEADS, HEAD_DIM)
    overall_heads = jnp.transpose(arrived_overall[0], (0, 2, 1))
    delta_heads = jnp.transpose(arrived_delta[0], (0, 2, 1))
    soft_again = jnp.exp(block_scores(owner_queries) - owner_lse[..., None])
    soft_again_low = soft_again.astype(jnp.bfloat16).astype(jnp.float32)
    weight_mix = jnp.exp(owner_lse - overall_heads)
    value_dots = jnp.einsum(
        "bmhd,bkhd->bhmk", owner_grad, store_values, preferred_element_type=jnp.float32
    )
    exact_sum = jnp.sum(soft_again * value_dots, axis=-1, keepdims=True)
    rounded_sum = jnp.sum(soft_again_low * value_dots, axis=-1, keepdims=True)
    score_grad = (
        weight_mix[..., None]
        * soft_again
        * (value_dots - exact_sum + rounded_sum - delta_heads[..., None])
    ).astype(jnp.bfloat16)
    query_grad = (
        jnp.einsum("bhmk,bkhd->bmhd", score_grad, store_keys, preferred_element_type=jnp.float32)
        .astype(jnp.bfloat16)
        .reshape(local_blocks, rows_in, D)
    )
    key_grad = jnp.einsum(
        "bhmk,bmhd->bkhd", score_grad, owner_queries, preferred_element_type=jnp.float32
    )
    weighted_soft = weight_mix[..., None] * soft_again_low
    value_grad = jnp.einsum(
        "bhmk,bmhd->bkhd",
        weighted_soft,
        owner_grad.astype(jnp.float32),
        precision=lax.Precision.HIGHEST,
    )
    row_count = local_blocks * BLOCK
    memory_grad = jnp.concatenate(
        [key_grad.reshape(row_count, D), value_grad.reshape(row_count, D)], axis=1
    ).astype(jnp.bfloat16)
    cross_memory_grad = jnp.dot(datastore.T, memory_grad, preferred_element_type=jnp.float32)
    value_bias_grad = jnp.sum(memory_grad[:, D:].astype(jnp.float32), axis=0)
    datastore_grad = jnp.dot(memory_grad, cross_memory.T, preferred_element_type=jnp.float32)
    returned_grad = lax.all_to_all(
        query_grad[None], "store", split_axis=2, concat_axis=0, tiled=True
    )
    per_pick = returned_grad.reshape(total_slots, D)[slot_ids].reshape(tok_count, TOPB, D)
    query_sum = jnp.sum(per_pick.astype(jnp.float32), axis=1).astype(jnp.bfloat16)
    cross_pre_grad = (query_sum.astype(jnp.float32) * QUERY_SCALE).astype(jnp.bfloat16)
    cross_query_grad = jnp.dot(first_low.T, cross_pre_grad, preferred_element_type=jnp.float32)
    first_total = second_resid + jnp.dot(
        cross_pre_grad, cross_query.T, preferred_element_type=jnp.float32
    )
    first_resid, first_gain, first_shift = first_back(first_total)
    self_branch_grad = first_resid.astype(jnp.bfloat16)
    self_output_grad = jnp.dot(attended.T, self_branch_grad, preferred_element_type=jnp.float32)
    self_attended_grad = (
        jnp.dot(self_branch_grad, self_output.T, preferred_element_type=jnp.float32)
        .astype(jnp.bfloat16)
        .reshape(tok_count, HEADS, HEAD_DIM)
    )
    soft_self = jnp.exp(self_scores() - self_lse[..., None])
    soft_dots = jnp.einsum(
        "qhd,khd->hqk", self_attended_grad, values_self, preferred_element_type=jnp.float32
    )
    self_score_grad = (
        soft_self * (soft_dots - jnp.sum(soft_self * soft_dots, axis=-1, keepdims=True))
    ).astype(jnp.bfloat16)
    query_self_grad = jnp.einsum(
        "hqk,khd->qhd", self_score_grad, keys_self, preferred_element_type=jnp.float32
    ).reshape(tok_count, D)
    key_self_grad = jnp.einsum(
        "hqk,qhd->khd", self_score_grad, queries, preferred_element_type=jnp.float32
    ).reshape(tok_count, D)
    value_self_grad = jnp.einsum(
        "hqk,qhd->khd", soft_low, self_attended_grad, preferred_element_type=jnp.float32
    ).reshape(tok_count, D)
    heads_grad = jnp.concatenate([query_self_grad, key_self_grad, value_self_grad], axis=1).astype(
        jnp.bfloat16
    )
    project_grad = jnp.concatenate(
        [
            (heads_grad[:, :D].astype(jnp.float32) * QUERY_SCALE).astype(jnp.bfloat16),
            heads_grad[:, D:],
        ],
        axis=1,
    )
    self_project_grad = jnp.dot(inputs.T, project_grad, preferred_element_type=jnp.float32)
    input_grad = first_resid + jnp.dot(
        project_grad, self_project.T, preferred_element_type=jnp.float32
    )
    biases_grad = jnp.stack(
        [
            jnp.sum(project_grad[:, :D].astype(jnp.float32), axis=0),
            jnp.sum(project_grad[:, 2 * D :].astype(jnp.float32), axis=0),
            jnp.sum(self_branch_grad.astype(jnp.float32), axis=0),
            jnp.sum(cross_pre_grad.astype(jnp.float32), axis=0),
            value_bias_grad,
            jnp.sum(cross_branch_grad.astype(jnp.float32), axis=0),
            jnp.sum(ffn_branch_grad.astype(jnp.float32), axis=0),
        ]
    )
    gain_grad = jnp.stack([first_gain, second_gain, final_gain])
    shift_grad = jnp.stack([first_shift, second_shift, final_shift])
    shared = (
        lax.psum_scatter(self_project_grad, "store", scatter_dimension=0, tiled=True),
        lax.psum_scatter(self_output_grad, "store", scatter_dimension=0, tiled=True),
        lax.psum_scatter(cross_query_grad, "store", scatter_dimension=0, tiled=True),
        lax.psum_scatter(cross_memory_grad, "store", scatter_dimension=0, tiled=True),
        lax.psum_scatter(cross_output_grad, "store", scatter_dimension=0, tiled=True),
        lax.psum_scatter(expand_weight_grad, "store", scatter_dimension=0, tiled=True),
        lax.psum_scatter(contract_weight_grad, "store", scatter_dimension=0, tiled=True),
        lax.psum_scatter(biases_grad, "store", scatter_dimension=1, tiled=True),
        lax.psum_scatter(expand_bias_grad, "store", scatter_dimension=0, tiled=True),
        lax.psum_scatter(gain_grad, "store", scatter_dimension=1, tiled=True),
        lax.psum_scatter(shift_grad, "store", scatter_dimension=1, tiled=True),
    )
    reduced = (
        lax.psum(shared[0].astype(jnp.bfloat16), "dp").astype(jnp.float32),
        lax.psum(shared[1].astype(jnp.bfloat16), "dp").astype(jnp.float32),
        lax.psum(shared[2].astype(jnp.bfloat16), "dp").astype(jnp.float32),
        lax.psum(shared[3].astype(jnp.bfloat16), "dp").astype(jnp.float32),
        lax.psum(shared[4].astype(jnp.bfloat16), "dp").astype(jnp.float32),
        lax.psum(shared[5].astype(jnp.bfloat16), "dp").astype(jnp.float32),
        lax.psum(shared[6].astype(jnp.bfloat16), "dp").astype(jnp.float32),
        lax.psum(shared[7].astype(jnp.bfloat16), "dp").astype(jnp.float32),
        lax.psum(shared[8].astype(jnp.bfloat16), "dp").astype(jnp.float32),
        lax.psum(shared[9].astype(jnp.bfloat16), "dp").astype(jnp.float32),
        lax.psum(shared[10].astype(jnp.bfloat16), "dp").astype(jnp.float32),
    )
    return (
        outputs,
        input_grad,
        datastore_grad,
        reduced[0],
        reduced[1],
        reduced[2],
        reduced[3],
        reduced[4],
        reduced[5],
        reduced[6],
        reduced[7],
        reduced[8],
        reduced[9],
        reduced[10],
    )


def solution(mesh):
    placed = (
        P(("dp", "store"), None),
        P(("dp", "store"), None),
        P(("dp", "store"), None),
        P(("dp", "store")),
        P(("dp", "store"), None),
        P(),
        P(),
        P(),
        P(),
        P(),
        P(),
        P(),
        P(),
        P(),
        P(),
        P(),
        P(("dp", "store"), None),
    )
    return jax.shard_map(
        local_tree if mesh.shape["store"] == 16 else local_slots,
        mesh=mesh,
        in_specs=placed,
        out_specs=(
            P(("dp", "store"), None),
            P(("dp", "store"), None),
            P(("dp", "store"), None),
            P("store", None),
            P("store", None),
            P("store", None),
            P("store", None),
            P("store", None),
            P("store", None),
            P("store", None),
            P(None, "store"),
            P("store"),
            P(None, "store"),
            P(None, "store"),
        ),
        check_vma=False,
    )
```

```python
import functools

import jax
import jax.numpy as jnp
from jax import lax
from jax.experimental import pallas as pl
from jax.experimental.pallas import tpu as pltpu
from jax.sharding import PartitionSpec as P

D = 768
HEADS = 12
HEAD_DIM = 64
TOPB = 8
BLOCK = 128
SLAB = 128
PAIRS = D // SLAB
UNIT = 384
LSE_ROWS = 8
SIDE_ROWS = 16
RANK_ROWS = 16

EPSILON = 1e-05
MASKED = -1e30
QUERY_SCALE = 0.125
VMEM_LIMIT = 16 * 1024 * 1024
SMALL_LIMIT = 16 * 1024 * 1024
LONG = 30_000_000_000
UNROLL = 4
MICROSECOND = 50_000_000
LOW = jnp.bfloat16
F32 = jnp.float32

_VMEM = pl.BlockSpec(memory_space=pltpu.VMEM)
_SMEM = pl.BlockSpec(memory_space=pltpu.SMEM)
_ANY = pl.BlockSpec(memory_space=pl.ANY)


def nn(a, b):
    return lax.dot_general(a, b, (((1,), (0,)), ((), ())), preferred_element_type=F32)


def nt(a, b):
    return lax.dot_general(a, b, (((1,), (1,)), ((), ())), preferred_element_type=F32)


def tn(a, b):
    return lax.dot_general(a, b, (((0,), (0,)), ((), ())), preferred_element_type=F32)


def three(v):
    high = v.astype(LOW)
    rest = v - high.astype(F32)
    mid = rest.astype(LOW)
    return high, mid, (rest - mid.astype(F32)).astype(LOW)


def lanes(shape):
    return lax.broadcasted_iota(jnp.int32, shape, len(shape) - 1)


def rows_of(shape):
    return lax.broadcasted_iota(jnp.int32, shape, len(shape) - 2)


def flag(condition):
    return jnp.where(condition, 1.0, 0.0)


def half_masks():
    first = flag(lanes((1, SLAB)) < HEAD_DIM)
    return first.astype(LOW), (1.0 - first).astype(LOW)


def two_heads(slab, first, second):
    return jnp.concatenate([slab * first, slab * second], axis=0)


def join_heads(stacked, count):
    left = lanes((count, SLAB)) < HEAD_DIM
    return jnp.where(left, stacked[:count], stacked[count:])


def norm_forward(residual, gain, shift):
    center = residual - jnp.mean(residual, axis=-1, keepdims=True)
    spread = jnp.mean(center * center, axis=-1, keepdims=True)
    scale = lax.rsqrt(spread + EPSILON)
    unit = center * scale
    return unit * gain + shift, unit, scale


def norm_backward(grad, unit, scale, gain):
    inner = grad * gain
    down = inner - jnp.mean(inner, axis=-1, keepdims=True)
    down = down - unit * jnp.mean(inner * unit, axis=-1, keepdims=True)
    return scale * down


def row_sum(v):
    return jnp.sum(v, axis=0, keepdims=True)


def call(
    kernel,
    outs,
    scratch=(),
    n_smem=0,
    far_in=(),
    far_out=(),
    earlier=(),
    aliases=None,
    flops=0,
    limit=VMEM_LIMIT,
):
    def run(*args):
        count = len(args)

        def body(*refs):
            kernel(*refs[:count], *refs[count + len(earlier) :])

        args = [
            pltpu.with_memory_space_constraint(v, pltpu.HBM) if i in far_in and not aliases else v
            for i, v in enumerate(args)
        ]
        specs = [_ANY if i in far_in else _VMEM for i in range(n_smem, count)]
        return pl.pallas_call(
            body,
            out_shape=[
                pltpu.HBM(s, t) if i in far_out and not aliases else jax.ShapeDtypeStruct(s, t)
                for i, (s, t) in enumerate(outs)
            ],
            in_specs=[_SMEM] * n_smem + specs + [_ANY] * len(earlier),
            out_specs=[_ANY if i in far_out else _VMEM for i in range(len(outs))],
            scratch_shapes=list(scratch),
            input_output_aliases=aliases or {},
            compiler_params=pltpu.CompilerParams(vmem_limit_bytes=limit),
            cost_estimate=pl.CostEstimate(flops=flops, bytes_accessed=0, transcendentals=0),
        )(*args, *earlier)

    return run


def copies(pairs, sems):
    return [pltpu.make_async_copy(a, b, sems.at[i]) for i, (a, b) in enumerate(pairs)]


def after(v, *earlier):
    return call(
        lambda *refs: None,
        [(v.shape, v.dtype)],
        far_in=(0,),
        far_out=(0,),
        earlier=earlier,
        aliases={0: 0},
        limit=1024 * 1024,
    )(v)[0]


def start_all(items):
    for item in items:
        item.start()


def wait_all(items):
    for item in items:
        item.wait()


def plane_ranks(picks_ref, me, k, tokens):
    i = rows_of((RANK_ROWS, tokens))
    group, chip, block = i // 4, (i // 2) % 2, i % 2
    apart = jnp.where(group < 2, 2 * group + chip, 2 * chip + group - 2)
    local = jnp.where(group < 2, block, 2 + block)
    plane = (me // 4) ^ k
    number = plane * 16 + ((me % 4) ^ apart) * 4 + local
    member = jnp.zeros((RANK_ROWS, tokens), F32)
    for j in range(TOPB):
        member = member + flag(picks_ref[j : j + 1, :] == number)
    earlier = flag(rows_of((tokens, tokens)) < lanes((tokens, tokens)))
    rank = nn(member.astype(LOW), earlier.astype(LOW))
    return jnp.where(member > 0.5, rank, -1.0).astype(LOW)


def self_forward_kernel(
    lengths_ref,
    place_ref,
    x_ref,
    picks_ref,
    project_ref,
    output_ref,
    query_ref,
    bias_ref,
    gain_ref,
    shift_ref,
    heads_ref,
    soft_ref,
    attended_ref,
    unit_ref,
    scale_ref,
    first_ref,
    *rest,
):
    payload_refs, (project_scr, output_scr, query_scr, sems) = rest[:4], rest[4:]
    thirds = [slice(i * D, (i + 1) * D) for i in range(3)]
    fetch = copies(
        [(project_ref.at[:, at], project_scr.at[:, at]) for at in thirds]
        + [(output_ref, output_scr), (query_ref, query_scr)],
        sems,
    )
    start_all(fetch)
    tokens = x_ref.shape[0]
    bias = bias_ref[...].astype(F32)
    x = x_ref[...]
    for i, at in enumerate(thirds):
        fetch[i].wait()
        part = nn(x, project_scr[:, at])
        if i == 0:
            part = QUERY_SCALE * (part + bias[0:1])
        if i == 2:
            part = part + bias[1:2]
        heads_ref[:, at] = part.astype(LOW)
    place_row = lax.broadcasted_iota(jnp.int32, (2 * tokens, tokens), 0) % tokens
    place_col = lanes((2 * tokens, tokens))
    segment_row = jnp.zeros((2 * tokens, tokens), jnp.int32)
    segment_col = jnp.zeros((2 * tokens, tokens), jnp.int32)
    bound = 0
    for d in range(lengths_ref.shape[1]):
        bound = bound + lengths_ref[0, d]
        segment_row = segment_row + jnp.where(place_row >= bound, 1, 0)
        segment_col = segment_col + jnp.where(place_col >= bound, 1, 0)
    allowed = (segment_row == segment_col) & (place_row >= place_col)
    first, second = half_masks()
    for p in range(PAIRS):
        at = p * SLAB
        queries = two_heads(heads_ref[:, at : at + SLAB], first, second)
        scores = nt(queries, heads_ref[:, D + at : D + at + SLAB])
        scores = jnp.where(allowed, scores, MASKED)
        top = jnp.max(scores, axis=-1, keepdims=True)
        raised = jnp.exp(scores - top)
        soft = raised / jnp.sum(raised, axis=-1, keepdims=True)
        soft_ref[p] = soft
        mixed = nn(soft.astype(LOW), heads_ref[:, 2 * D + at : 2 * D + at + SLAB])
        attended_ref[:, at : at + SLAB] = join_heads(mixed, tokens).astype(LOW)
    fetch[3].wait()
    residual = x.astype(F32) + nn(attended_ref[...], output_scr[...]) + bias[2:3]
    normed, unit, scale = norm_forward(
        residual, gain_ref[0:1, :].astype(F32), shift_ref[0:1, :].astype(F32)
    )
    unit_ref[...] = unit
    scale_ref[...] = scale
    low = normed.astype(LOW)
    first_ref[...] = low
    fetch[4].wait()
    queries = (QUERY_SCALE * (nn(low, query_scr[...]) + bias[3:4])).astype(LOW)
    for k, out in enumerate(payload_refs):
        out[:tokens] = queries
        out[tokens:, tokens:] = jnp.zeros((RANK_ROWS, D - tokens), LOW)
        out[tokens:, :tokens] = plane_ranks(picks_ref, place_ref[0], k, tokens)


def piece_kernel(rows_ref, kept_ref, a_ref, b_ref):
    for h, out in enumerate((a_ref, b_ref)):
        out[: 2 * BLOCK] = rows_ref[2 * h * BLOCK : 2 * (h + 1) * BLOCK]
        marks = kept_ref[2 * h : 2 * h + 2, :].astype(F32)
        marks = jnp.concatenate([marks, jnp.zeros((RANK_ROWS - 2, BLOCK), F32)], axis=0)
        out[2 * BLOCK :, :BLOCK] = marks.astype(LOW)
        out[2 * BLOCK :, BLOCK:] = jnp.zeros((RANK_ROWS, D - BLOCK), LOW)


def pair_kernel(first_ref, second_ref, out_ref):
    out_ref[0] = first_ref[...]
    out_ref[1] = second_ref[...]


def memory_kernel(*refs):
    far = len(refs) > 12
    if far:
        pieces = [ref.at[j] for ref in refs[:2] for j in range(2)]
        near_pieces, (weight_ref, bias_ref), given = refs[2:6], refs[6:8], refs[8:14]
        outs, rows_ref, sems = refs[14:17], refs[17], refs[18]
        size = 2 * BLOCK
        pairs = []
        for s in range(2):
            for j in range(2):
                at = 8 * s * BLOCK + j * size
                pairs.append((near_pieces[2 * s + j].at[:size], rows_ref.at[at : at + size]))
                at = at + 4 * BLOCK
                pairs.append((pieces[2 * s + j].at[:size], rows_ref.at[at : at + size]))
        keep = copies(pairs, sems)
        start_all(keep)
    else:
        pieces, (weight_ref, bias_ref), outs = refs[:4], refs[4:6], refs[6:]
    bias = bias_ref[4:5, :].astype(F32)
    lane = lanes((RANK_ROWS, SLAB))
    place = lanes((BLOCK, SLAB))
    for s in range(2):
        if far:
            near, here = 8 * s, 8 * s + 4
            memory_ref, hidden_ref, side_ref = outs
            for out, ref in zip(outs, given[3 * s : 3 * s + 3]):
                out[near : near + 4] = ref[...]
        else:
            here = 0
            memory_ref, hidden_ref, side_ref = outs[3 * s : 3 * s + 3]
        for j in range(2):
            piece = pieces[2 * s + j]
            rows = piece[: 2 * BLOCK]
            first = here + 2 * j
            keys = nn(rows, weight_ref[:, :D]).astype(LOW)
            values = (nn(rows, weight_ref[:, D:]) + bias).astype(LOW)
            marks = piece[2 * BLOCK :, :SLAB]
            for l in range(2):
                at = first + l
                memory_ref[at, :, :D] = keys[l * BLOCK : (l + 1) * BLOCK]
                memory_ref[at, :, D:] = values[l * BLOCK : (l + 1) * BLOCK]
                hidden_ref[at] = (1.0 - marks[l : l + 1].astype(F32)) * MASKED
                wanted = flag((rows_of((RANK_ROWS, SLAB)) == l) & (lane == SLAB - 1))
                column = tn(marks, wanted.astype(LOW))
                side = jnp.where(place == SLAB - 1, (1.0 - column) * MASKED, 0.0)
                side_ref[at] = jnp.where(place < 48, -1.0, side).astype(LOW)
    if far:
        wait_all(keep)


def selection(ranks, capacity):
    parts = []
    wanted = rows_of((capacity, ranks.shape[1])).astype(F32)
    for b in range(ranks.shape[0]):
        parts.append(flag(ranks[b : b + 1, :] == wanted).astype(LOW))
    return jnp.concatenate(parts, axis=0)


def fill_slots(sel, rows, out_ref, k, capacity):
    got = nn(sel, rows).astype(LOW)
    for b in range(out_ref.shape[0]):
        out_ref[b, k * capacity : (k + 1) * capacity, :] = got[b * capacity : (b + 1) * capacity]


def around16(v, combine):
    for step in (16, 32, 64):
        v = combine(v, pltpu.roll(v, step, 1))
    return v


def put_side(ref, side, rows):
    tokens = side.shape[0]
    turned = side.astype(F32).T.astype(LOW)
    for q in range(PAIRS):
        ref[tokens:, q * SLAB : (q + 1) * SLAB] = turned[q * rows : (q + 1) * rows]


def get_side(ref, tokens):
    rows = ref.shape[0] - tokens
    parts = [ref[tokens:, q * SLAB : (q + 1) * SLAB].astype(F32) for q in range(PAIRS)]
    parts.append(jnp.zeros((SLAB - PAIRS * rows, SLAB), F32))
    return jnp.concatenate(parts, axis=0).T


def lse_lanes(lse):
    high = lse.astype(LOW).astype(F32)
    rest = lse - high
    mid = rest.astype(LOW).astype(F32)
    low = rest - mid
    lane = lanes(lse.shape)
    packed = jnp.where(
        lane < 16, high, jnp.where(lane < 32, mid, jnp.where(lane < 48, low, 0.0))
    )
    return packed.astype(LOW)


def head_spread(group):
    row = rows_of((SLAB, D))
    row = row % 16 if group else row
    return flag(row == lanes((SLAB, D)) // HEAD_DIM).astype(LOW)


def owner_forward_kernel(capacity, *refs):
    tokens_refs, memory_ref, hidden_ref = refs[0:4], refs[4], refs[5]
    far_slots_ref, out_scr, lse_scr, inv_scr, sel_scr, ranks_scr, slots_ref, sems = refs[6:]
    sources = len(tokens_refs)
    blocks, rows = slots_ref.shape[:2]
    tokens = tokens_refs[0].shape[0] - RANK_ROWS
    first, second = half_masks()
    for k in range(sources):
        ranks_scr[...] = tokens_refs[k][tokens:, :tokens].astype(F32)
        sel = selection(ranks_scr[...], capacity)
        sel_scr[k] = sel
        fill_slots(sel, tokens_refs[k][:tokens], slots_ref, k, capacity)
    keep = copies([(slots_ref, far_slots_ref)], sems)
    start_all(keep)
    ones = jnp.ones((BLOCK, SLAB), LOW)
    lane_of = lanes((rows, SLAB))
    def one_block(i, carry):
        hidden = hidden_ref[i]
        tops = jnp.zeros((rows, SLAB), F32)
        totals = jnp.ones((rows, SLAB), F32)
        base = (i % 8) * 16
        slabs = [slice(p * SLAB, (p + 1) * SLAB) for p in range(PAIRS)]
        scores = [
            nt(two_heads(slots_ref[i, :, at], first, second), memory_ref[i, :, at])
            + hidden
            for at in slabs
        ]
        highest = [jnp.max(v, axis=-1, keepdims=True) for v in scores]
        raised = [jnp.exp(v - top).astype(LOW) for v, top in zip(scores, highest)]
        mixed = [
            nn(v, jnp.concatenate([memory_ref[i, :, D + at.start : D + at.stop], ones], axis=1))
            for v, at in zip(raised, slabs)
        ]
        for p, at in enumerate(slabs):
            out_scr[i, :, at] = join_heads(mixed[p][:, :SLAB], rows)
            for half in range(2):
                here = slice(half * rows, (half + 1) * rows)
                mine = lane_of == base + 2 * p + half
                tops = jnp.where(mine, highest[p][here], tops)
                totals = jnp.where(mine, mixed[p][here, SLAB:], totals)
        own = flag((lane_of >= base) & (lane_of < base + HEADS))
        lse_scr[i] = tops + jnp.log(totals)
        inv_scr[i] = own / totals
        return carry

    lax.fori_loop(0, blocks, one_block, 0, unroll=UNROLL)
    wait_all(keep)


def merge_kernel(capacity, k, value_ref, lse_ref, inv_ref, sel_ref, payload_ref):
    tokens = sel_ref.shape[2]
    group = 8 * capacity
    own_low = flag(
        rows_of((group, SLAB)) // capacity == lanes((group, SLAB)) // 16
    ).astype(LOW)
    spread = head_spread(True)
    here = slice(k * capacity, (k + 1) * capacity)

    def stacked(ref, g, here=here):
        return jnp.concatenate([ref[8 * g + b, here, :] for b in range(8)], axis=0)

    by_token, members, sels = [], [], []
    for g in range(2):
        sel = sel_ref[k, g * group : (g + 1) * group, :]
        turned = sel.T
        found = nn(turned, jnp.concatenate([*three(stacked(lse_ref, g)), own_low], axis=1))
        pieces = [found[:, q * SLAB : (q + 1) * SLAB] for q in range(4)]
        by_token.append(jnp.where(pieces[3] > 0.5, pieces[0] + pieces[1] + pieces[2], MASKED))
        members.append(pieces[3])
        sels.append((sel, turned))
    top = around16(jnp.maximum(*by_token), jnp.maximum)
    weights = [m * jnp.exp(v - top) for m, v in zip(members, by_token)]
    total = around16(weights[0] + weights[1], jnp.add)
    some = total > 0.5
    safe = jnp.where(some, total, 1.0)
    merged_lse = jnp.where(some, top + jnp.log(safe), MASKED)
    put_side(payload_ref, lse_lanes(merged_lse), LSE_ROWS)
    partial = jnp.zeros((tokens, D), F32)
    for g in range(2):
        share = nn(sels[g][0], (weights[g] / safe).astype(LOW)) * stacked(inv_ref, g)
        value = stacked(value_ref, g) * nn(share.astype(LOW), spread)
        partial = partial + nn(sels[g][1], value.astype(LOW))
    payload_ref[:tokens] = partial.astype(LOW)


def owner_backward_kernel(capacity, *refs):
    sel_scr, grad_refs, memory_ref, side_ref, slots_ref = refs[0], refs[1:5], *refs[5:8]
    out, payload_refs, bias_ref = refs[8], refs[9:13], refs[13]
    got_scr, query_scr = refs[14:]
    sources = len(grad_refs)
    blocks, rows = slots_ref.shape[:2]
    tokens = grad_refs[0].shape[0] - SIDE_ROWS
    first, second = half_masks()
    for k in range(sources):
        side = get_side(grad_refs[k], tokens).astype(LOW)
        rows_all = jnp.concatenate([grad_refs[k][:tokens], side], axis=1)
        fill_slots(sel_scr[k], rows_all, got_scr, k, capacity)
    lane = lanes((1, SLAB))
    last = flag(lane == SLAB - 1).astype(LOW)
    value_side = jnp.broadcast_to(
        -flag((lane >= 48) & (lane < 96)).astype(LOW), (BLOCK, SLAB)
    )

    def picked(head, base):
        inside = (lane >= base) & (lane < base + 48)
        return flag(inside & (lane % 16 == head)).astype(LOW)

    def one_block(i, carry):
        side = got_scr[i, :, D:]
        key_side = side_ref[i]
        slabs = [slice(p * SLAB, (p + 1) * SLAB) for p in range(PAIRS)]
        keys = [memory_ref[i, :, at] for at in slabs]
        queries = [two_heads(slots_ref[i, :, at], first, second) for at in slabs]
        grads = [two_heads(got_scr[i, :, at], first, second) for at in slabs]
        scores, dots = [], []
        for p in range(PAIRS):
            lse_side = jnp.concatenate(
                [side * picked(2 * p + h, 0) + last for h in range(2)], axis=0
            )
            scores.append(
                nt(
                    jnp.concatenate([keys[p], key_side], axis=1),
                    jnp.concatenate([queries[p], lse_side], axis=1),
                )
            )
        for p, at in enumerate(slabs):
            delta_side = jnp.concatenate(
                [side * picked(2 * p + h, 48) for h in range(2)], axis=0
            )
            values = memory_ref[i, :, D + at.start : D + at.stop]
            dots.append(
                nt(
                    jnp.concatenate([values, value_side], axis=1),
                    jnp.concatenate([grads[p], delta_side], axis=1),
                )
            )
        softs = [jnp.exp(v) for v in scores]
        score_grads = [(soft * v).astype(LOW) for soft, v in zip(softs, dots)]
        for p, at in enumerate(slabs):
            query_scr[i, :, at] = join_heads(tn(score_grads[p], keys[p]), rows).astype(LOW)
        for p, at in enumerate(slabs):
            out[i, :, at] = nn(score_grads[p], queries[p]).astype(LOW)
        for p, at in enumerate(slabs):
            out[i, :, D + at.start : D + at.stop] = nn(softs[p].astype(LOW), grads[p]).astype(
                LOW
            )
        return carry

    lax.fori_loop(0, blocks, one_block, 0, unroll=UNROLL)
    for k in range(sources):
        here = slice(k * capacity, (k + 1) * capacity)
        value = jnp.concatenate([query_scr[b, here, :] for b in range(blocks)], axis=0)
        payload_refs[k][...] = tn(sel_scr[k], value).astype(LOW)
    total = lax.fori_loop(
        0,
        blocks,
        lambda i, v: v + row_sum(out[i, :, D:].astype(F32)),
        jnp.zeros((1, D), F32),
    )
    bias_ref[...] = jnp.broadcast_to(total, (8, D))


def memory_weight_kernel(count, place_ref, *refs):
    grad_ref, rows_ref, kept_ref, sent_ref, sum_scr = refs
    me, core = place_ref[0], place_ref[1]
    size = 4 * BLOCK
    sum_scr[...] = jnp.zeros(sum_scr.shape, F32)

    def one_set(s, carry):
        at = pl.ds(pl.multiple_of(s * size, size), size)
        rows = rows_ref[at, :].T
        for h in range(2):
            sum_scr[h] = sum_scr[h] + nn(rows, grad_ref[at, h * D : (h + 1) * D])
        return carry

    lax.fori_loop(0, rows_ref.shape[0] // size, one_set, 0)
    block = D // count
    for h in range(2):

        def store(out, h=h):
            total = sum_scr[h].astype(LOW)
            for k in range(count):
                for u in range(D // UNIT):
                    out[me ^ k, u * block : (u + 1) * block, :] = total[
                        k * block : (k + 1) * block, u * UNIT : (u + 1) * UNIT
                    ]

        pl.when(core == h)(functools.partial(store, kept_ref))
        pl.when(core != h)(functools.partial(store, sent_ref))


def datastore_grad_kernel(weight_ref, *refs):
    grad_ref, outs = refs[0], refs[1:7]
    weight = weight_ref[...].T
    near_a0, near_a1, far_a, near_b0, near_b1, far_b = outs
    groups = ((near_a0, near_a1), (far_a,), (near_b0, near_b1), (far_b,))
    for s in range(4):
        value = nn(grad_ref[4 * s * BLOCK : 4 * (s + 1) * BLOCK], weight).astype(LOW)
        size = value.shape[0] // len(groups[s])
        for i, out in enumerate(groups[s]):
            out[...] = value[i * size : (i + 1) * size]


def datastore_step_kernel(*refs):
    ins, sends, keeps = refs[:6], refs[6:8], refs[8:10]
    size = 2 * BLOCK
    for g in range(2):
        stay, go, come = ins[3 * g : 3 * g + 3]
        keeps[g][...] = stay[...].astype(F32) + come[:size].astype(F32)
        sends[g][...] = (go[...].astype(F32) + come[size:].astype(F32)).astype(LOW)


def datastore_sum_kernel(keep_a, come_a, keep_b, come_b, out_ref):
    size = keep_a.shape[0]
    out_ref[:size] = keep_a[...] + come_a[...].astype(F32)
    out_ref[size:] = keep_b[...] + come_b[...].astype(F32)


def middle_kernel(
    p0_ref,
    p1_ref,
    p2_ref,
    p3_ref,
    first_ref,
    cotangent_ref,
    output_ref,
    expand_ref,
    contract_ref,
    bias_ref,
    expand_bias_ref,
    gain_ref,
    shift_ref,
    out_ref,
    merged_ref,
    second_ref,
    active_ref,
    branch_grad_ref,
    expanded_grad_ref,
    cross_grad_ref,
    resid_ref,
    payload_ref,
    small_ref,
    wide_ref,
    expanded_scr,
):
    output_scr, expand_scr, contract_scr = output_ref, expand_ref, contract_ref
    bias = bias_ref[...].astype(F32)
    gain = gain_ref[...].astype(F32)
    shift = shift_ref[...].astype(F32)
    parts = [p0_ref, p1_ref, p2_ref, p3_ref]
    tokens = first_ref.shape[0]
    lses = [around16(get_side(part, tokens), jnp.add) for part in parts]
    top = functools.reduce(jnp.maximum, lses)
    weights = [jnp.exp(lse - top) for lse in lses]
    total = functools.reduce(jnp.add, weights)
    overall = top + jnp.log(total)
    spread = head_spread(False)
    merged = jnp.zeros(first_ref.shape, F32)
    for part, weight in zip(parts, weights):
        share = weight / total
        high = share.astype(LOW)
        rest = (share - high.astype(F32)).astype(LOW)
        merged = merged + (nn(high, spread) + nn(rest, spread)) * part[:tokens].astype(F32)
    merged_low = merged.astype(LOW)
    merged_ref[...] = merged_low
    residual = first_ref[...].astype(F32) + nn(merged_low, output_scr[...]) + bias[5:6]
    second, unit_second, scale_second = norm_forward(residual, gain[1:2], shift[1:2])
    second_low = second.astype(LOW)
    second_ref[...] = second_low
    hidden = contract_scr.shape[0]
    for c in range(hidden // D):
        at = slice(c * D, (c + 1) * D)
        expanded = nn(second_low, expand_scr[:, at]) + expand_bias_ref[:, at].astype(F32)
        bell = 0.5 * (1.0 + lax.erf(expanded * 0.7071067811865476))
        active_ref[:, at] = (expanded * bell).astype(LOW)
        slope = bell + expanded * 0.3989422804014327 * jnp.exp(-0.5 * expanded * expanded)
        expanded_scr[:, at] = slope
    residual = second_low.astype(F32) + nn(active_ref[...], contract_scr[...]) + bias[6:7]
    final, unit_final, scale_final = norm_forward(residual, gain[2:3], shift[2:3])
    out_ref[...] = final.astype(LOW)
    cotangent = cotangent_ref[...].astype(F32)
    final_resid = norm_backward(cotangent, unit_final, scale_final, gain[2:3])
    branch_grad = final_resid.astype(LOW)
    branch_grad_ref[...] = branch_grad
    small_ref[0:1, :] = row_sum(branch_grad.astype(F32))
    small_ref[1:2, :] = row_sum(cotangent * unit_final)
    small_ref[2:3, :] = row_sum(cotangent)
    total_grad = final_resid
    for c in range(hidden // D):
        at = slice(c * D, (c + 1) * D)
        active_grad = nt(branch_grad, contract_scr[at, :])
        expanded_grad = (active_grad * expanded_scr[:, at]).astype(LOW)
        expanded_grad_ref[:, at] = expanded_grad
        wide_ref[:, at] = row_sum(expanded_grad.astype(F32))
        total_grad = total_grad + nt(expanded_grad, expand_scr[:, at])
    small_ref[4:5, :] = row_sum(total_grad * unit_second)
    small_ref[5:6, :] = row_sum(total_grad)
    second_resid = norm_backward(total_grad, unit_second, scale_second, gain[1:2])
    resid_ref[...] = second_resid
    cross_grad = second_resid.astype(LOW)
    cross_grad_ref[...] = cross_grad
    small_ref[3:4, :] = row_sum(cross_grad.astype(F32))
    small_ref[6:8, :] = jnp.zeros((2, D), F32)
    attended_grad = nt(cross_grad, output_scr[...]).astype(LOW)
    payload_ref[:tokens] = attended_grad
    product = attended_grad.astype(F32) * merged
    gather = flag(lanes((D, SLAB)) % 16 == rows_of((D, SLAB)) // HEAD_DIM).astype(LOW)
    high, mid, low = three(product)
    delta = nn(high, gather) + nn(mid, gather) + nn(low, gather)
    lane = lanes(overall.shape)
    packed = jnp.zeros(overall.shape, F32)
    for value, base in ((overall, 0), (delta, 48)):
        for i, piece in enumerate(three(value)):
            inside = (lane >= base + 16 * i) & (lane < base + 16 * i + HEADS)
            packed = jnp.where(inside, piece.astype(F32), packed)
    put_side(payload_ref, packed, SIDE_ROWS)


def self_backward_kernel(
    d0_ref,
    d1_ref,
    d2_ref,
    d3_ref,
    resid_ref,
    unit_ref,
    scale_ref,
    heads_ref,
    soft_ref,
    query_ref,
    output_ref,
    project_ref,
    gain_ref,
    pre_grad_ref,
    branch_grad_ref,
    project_grad_ref,
    input_grad_ref,
    small_ref,
    attended_scr,
):
    query_scr, output_scr, heads_scr = query_ref, output_ref, heads_ref
    soft_scr, project_scr = soft_ref, project_ref
    tokens = resid_ref.shape[0]
    query_sum = functools.reduce(
        jnp.add, [d[...].astype(F32) for d in (d0_ref, d1_ref, d2_ref, d3_ref)]
    ).astype(LOW)
    pre_grad = (query_sum.astype(F32) * QUERY_SCALE).astype(LOW)
    pre_grad_ref[...] = pre_grad
    total = resid_ref[...] + nt(pre_grad, query_scr[...])
    unit = unit_ref[...]
    first_resid = norm_backward(total, unit, scale_ref[...], gain_ref[0:1, :].astype(F32))
    branch_grad = first_resid.astype(LOW)
    branch_grad_ref[...] = branch_grad
    attended_scr[...] = nt(branch_grad, output_scr[...]).astype(LOW)
    first, second = half_masks()
    for p in range(PAIRS):
        at = p * SLAB
        grads = two_heads(attended_scr[:, at : at + SLAB], first, second)
        queries = two_heads(heads_scr[:, at : at + SLAB], first, second)
        keys = heads_scr[:, D + at : D + at + SLAB]
        dots = nt(grads, heads_scr[:, 2 * D + at : 2 * D + at + SLAB])
        soft = soft_scr[p]
        score_grad = (soft * (dots - jnp.sum(soft * dots, axis=-1, keepdims=True))).astype(LOW)
        query_grad = join_heads(nn(score_grad, keys), tokens).astype(LOW)
        project_grad_ref[:, at : at + SLAB] = (query_grad.astype(F32) * QUERY_SCALE).astype(LOW)
        project_grad_ref[:, D + at : D + at + SLAB] = tn(score_grad, queries).astype(LOW)
        project_grad_ref[:, 2 * D + at : 2 * D + at + SLAB] = tn(soft.astype(LOW), grads).astype(
            LOW
        )
    input_grad_ref[...] = first_resid + nt(project_grad_ref[...], project_scr[...])
    small_ref[0:1, :] = row_sum(project_grad_ref[:, :D].astype(F32))
    small_ref[1:2, :] = row_sum(project_grad_ref[:, 2 * D :].astype(F32))
    small_ref[2:3, :] = row_sum(branch_grad.astype(F32))
    small_ref[3:4, :] = row_sum(pre_grad.astype(F32))
    small_ref[4:5, :] = row_sum(total * unit)
    small_ref[5:6, :] = row_sum(total)
    small_ref[6:8, :] = jnp.zeros((2, D), F32)


def weight_grad_kernel(plan, count, packed, held, place_ref, *refs):
    kept_ref, sent_ref = refs[-2:]
    me, core = place_ref[0], place_ref[1]
    at_ref = 0
    for number, rows, columns, at in plan:
        pairs = [refs[at_ref + 2 * i : at_ref + 2 * i + 2] for i in range(number)]
        at_ref += 2 * number
        block = rows // count
        half = columns // 2
        steps = [(c, min(D, half - c)) for c in range(0, half, D)]

        def unit(m, c, wide, block=block, half=half, at=at, pairs=pairs):
            xs = [x_ref[:, pl.ds(pl.multiple_of(m * D, SLAB), D)].T for x_ref, _ in pairs]
            for mine, out in ((core, kept_ref), (1 - core, sent_ref)):
                start = pl.multiple_of(mine * half + c, SLAB)
                part = sum(nn(x, g_ref[:, pl.ds(start, wide)]) for x, (_, g_ref) in zip(xs, pairs))
                part = part.astype(LOW)
                for u in range(wide // UNIT):
                    low = pl.multiple_of(at + (c // UNIT + u) * block, 16)
                    for k in range(D // block):
                        to = me ^ (m * (D // block) + k)
                        out[to, pl.ds(low, block), :] = part[
                            k * block : (k + 1) * block, u * UNIT : (u + 1) * UNIT
                        ]

        if rows > D:
            for c, wide in steps:

                def by_rows(m, carry, c=c, wide=wide, unit=unit):
                    unit(m, c, wide)
                    return carry

                lax.fori_loop(0, rows // D, by_rows, 0)
        elif half % D == 0 and half > D:

            def by_columns(c, carry, unit=unit):
                unit(0, c * D, D)
                return carry

            lax.fori_loop(0, half // D, by_columns, 0)
        else:
            for c, wide in steps:
                unit(0, c, wide)
    if packed is not None:
        pack_small(refs[at_ref : at_ref + 4], kept_ref, sent_ref, packed, me, core, count)
        at_ref += 4
    if held:
        for ref, out in zip(refs[at_ref : at_ref + 2], (kept_ref, sent_ref)):
            out[:, :held, :] = ref[...]


def pack_small(small_refs, kept_ref, sent_ref, low, me, core, count):
    own, middle, value_bias, wide = small_refs
    order = [own[0:4], value_bias[0:1], middle[3:4], middle[0:1], own[4:5], middle[4:5]]
    order += [middle[1:2], own[5:6], middle[5:6], middle[2:3], jnp.zeros((3, D), F32)]
    narrow = jnp.concatenate(order, axis=0)
    share = D // count
    broad = wide.shape[1] // count
    for r in range(count):
        first = narrow[:, r * share : (r + 1) * share]
        first = jnp.concatenate([first, jnp.zeros((RANK_ROWS, UNIT - share), F32)], axis=1)
        second = wide[:, r * broad : (r + 1) * broad]
        second = jnp.concatenate([second, jnp.zeros((1, UNIT - broad), F32)], axis=1)
        second = jnp.broadcast_to(second, (RANK_ROWS, UNIT))
        here = slice(low, low + RANK_ROWS)
        kept_ref[me ^ r, here, :] = jnp.where(core == 0, first, second).astype(LOW)
        sent_ref[me ^ r, here, :] = jnp.where(core == 0, second, first).astype(LOW)


def total_of(*refs):
    return functools.reduce(jnp.add, [ref[...].astype(F32) for ref in refs])


def split_kernel(x, kept_ref, come_ref, *refs):
    far, outs = ((), refs) if x else (refs[:2], refs[2:])
    half = kept_ref.shape[3] // 2
    for z in range(4):
        for g in range(2):
            at = (z, slice(None), x, slice(0, half)) if g == 0 else (z, x, slice(None), slice(half, 2 * half))
            total = kept_ref[at].astype(F32) + come_ref[at].astype(F32)
            if far:
                total = total + far[g][z].astype(F32)
                for i in range(2):
                    outs[2 * g + i][z] = total[i].astype(LOW)
            else:
                outs[g][z] = total.astype(LOW)


def join_kernel(a_keep, a_come, b_keep, b_come, *outs):
    rows = a_keep.shape[1]
    for z, out in enumerate(outs):
        out[:rows] = total_of(a_keep.at[z], a_come.at[z]).astype(LOW)
        out[rows:] = total_of(b_keep.at[z], b_come.at[z]).astype(LOW)


def sum_kernel(*refs):
    refs[-1][...] = total_of(*refs[:-1]).astype(LOW)


def spread_kernel(plan, count, packed, place_ref, own_ref, other_ref, *outs):
    core = place_ref[1]
    for (rows, columns, at), out in zip(plan, outs):
        block = rows // count
        half = columns // 2
        for c in range(half // UNIT):
            low = at + c * block
            for value, mine in ((own_ref, core), (other_ref, 1 - core)):
                start = pl.multiple_of(mine * half + c * UNIT, SLAB)
                out[:, pl.ds(start, UNIT)] = value[low : low + block].astype(F32)
    if packed is not None:
        here = slice(packed, packed + RANK_ROWS)
        own, other = own_ref[here].astype(F32), other_ref[here].astype(F32)
        narrow, wide = jnp.where(core == 0, own, other), jnp.where(core == 0, other, own)
        biases_ref, wide_ref, gain_ref, shift_ref = outs[len(plan) :]
        share = biases_ref.shape[1]
        biases_ref[...] = narrow[0:7, :share]
        gain_ref[...] = narrow[7:10, :share]
        shift_ref[...] = narrow[10:13, :share]
        wide_ref[...] = wide[0:1, : wide_ref.shape[1]]


def swap(v, bits):
    count = lax.axis_size("store")
    return lax.ppermute(v, "store", [(i, i ^ bits) for i in range(count)])


def swap_core(v):
    return lax.ppermute(v, "dp", [(0, 1), (1, 0)])


class WeightSums:
    def __init__(self, place, count, rows):
        self.place, self.count, self.rows = place, count, rows
        self.plan, self.packed, self.at = [], None, 0
        self.buffers = ()

    def add(self, products, small=None, earlier=(), flops=0):
        plan, base, packed = [], self.at, None
        for pairs in products:
            rows, columns = pairs[0][0].shape[1], pairs[0][1].shape[1]
            plan.append((len(pairs), rows, columns, self.at))
            self.plan.append((rows, columns, self.at))
            self.at += rows // self.count * (columns // 2 // UNIT)
        args = [v for pairs in products for pair in pairs for v in pair]
        if small is not None:
            packed = self.packed = self.at
            self.at += RANK_ROWS
            args.extend(small)
        shape = (self.count, self.rows, UNIT)
        self.buffers = call(
            functools.partial(weight_grad_kernel, tuple(plan), self.count, packed, base),
            [(shape, LOW), (shape, LOW)],
            n_smem=1,
            earlier=earlier,
            flops=flops,
        )(self.place, *args, *self.buffers)
        return self.buffers

    def split(self, x, far=(), earlier=()):
        half = (4, 2, self.rows // 2, UNIT)
        outs = [half[:1] + half[2:]] * 4 if far else [half] * 2
        args = [v.reshape(4, 2, 2, self.rows, UNIT) for v in (self.kept, self.come)] + list(far)
        return call(
            functools.partial(split_kernel, x),
            [(shape, LOW) for shape in outs],
            earlier=earlier,
            limit=SMALL_LIMIT,
        )(*args)

    def start(self, earlier=()):
        self.kept, sent = self.buffers
        self.come = swap_core(sent)
        self.sent = self.split(1, earlier=earlier)
        return self.sent

    def first(self, *earlier):
        come = (swap(self.sent[0], 1), swap(self.sent[1], 2))
        a_keep, a_send, b_keep, b_send = self.split(0, come, earlier)
        self.kept, self.sent = (a_keep, b_keep), (a_send, b_send)
        return self.sent

    def second(self, *earlier):
        come = (swap(self.sent[0], 2), swap(self.sent[1], 1))
        self.w = call(
            join_kernel, [((self.rows, UNIT), LOW)] * 4, earlier=earlier, limit=SMALL_LIMIT
        )(self.kept[0], come[0], self.kept[1], come[1])
        return self.w

    def third(self, *earlier):
        come = [swap(self.w[k], 4 * k) for k in (1, 2, 3)]
        (self.own,) = call(
            sum_kernel, [(come[0].shape, LOW)], earlier=earlier, limit=SMALL_LIMIT
        )(self.w[0], *come)
        return self.own

    def finish(self, small=()):
        other = swap_core(self.own)
        shapes = [((rows // self.count, columns), F32) for rows, columns, _ in self.plan]
        shapes += [(shape, F32) for shape in small]
        return call(
            functools.partial(spread_kernel, tuple(self.plan), self.count, self.packed),
            shapes,
            n_smem=1,
            limit=SMALL_LIMIT,
        )(self.place, self.own, other)


def local_tree(
    inputs,
    doc_lengths,
    datastore,
    kept_mask,
    retrieved,
    self_project,
    self_output,
    cross_query,
    cross_memory,
    cross_output,
    expand_weight,
    contract_weight,
    biases,
    expand_bias,
    norm_gain,
    norm_shift,
    cotangent,
):
    tokens = inputs.shape[0]
    count = lax.axis_size("store")
    local_blocks = datastore.shape[0] // BLOCK
    all_blocks = local_blocks * count
    capacity = 2 * tokens * TOPB // all_blocks
    plane_blocks = 4 * local_blocks
    rows_in = 4 * capacity
    hidden = expand_weight.shape[1]
    me = lax.axis_index("store").astype(jnp.int32)
    core = lax.axis_index("dp").astype(jnp.int32)
    place = jnp.stack([me, core])

    piece = ((2 * BLOCK + RANK_ROWS, D), LOW)
    a0, b0 = call(piece_kernel, [piece] * 2)(datastore, kept_mask.reshape(local_blocks, BLOCK))
    a1, b1 = swap(a0, 1), swap(b0, 2)
    heads_all, soft_self, attended, unit_first, scale_first, first_low, *queries = call(
        self_forward_kernel,
        [
            ((tokens, 3 * D), LOW),
            ((PAIRS, 2 * tokens, tokens), F32),
            ((tokens, D), LOW),
            ((tokens, D), F32),
            ((tokens, 1), F32),
            ((tokens, D), LOW),
        ]
        + [((tokens + RANK_ROWS, D), LOW)] * 4,
        scratch=[
            pltpu.VMEM((D, 3 * D), LOW),
            pltpu.VMEM((D, D), LOW),
            pltpu.VMEM((D, D), LOW),
            pltpu.SemaphoreType.DMA((5,)),
        ],
        n_smem=2,
        far_in=(4, 5, 6),
        flops=8 * MICROSECOND,
    )(
        doc_lengths,
        place,
        inputs,
        retrieved.T,
        self_project,
        self_output,
        cross_query,
        biases,
        norm_gain,
        norm_shift,
    )
    pair = call(pair_kernel, [((2, *piece[0]), LOW)], earlier=(first_low,))
    ay, bx = swap(pair(a0, a1)[0], 2), swap(pair(b0, b1)[0], 1)
    queries = [queries[0]] + [swap(queries[k], 4 * k) for k in (1, 2, 3)]

    def of_blocks(blocks):
        return [
            ((blocks, BLOCK, 2 * D), LOW),
            ((blocks, 1, BLOCK), F32),
            ((blocks, BLOCK, SLAB), LOW),
        ]

    near = call(memory_kernel, of_blocks(4) * 2)(a0, a1, b0, b1, cross_memory, biases)
    memory, hidden_rows, key_side, stored = call(
        memory_kernel,
        of_blocks(plane_blocks) + [((plane_blocks * BLOCK, D), LOW)],
        scratch=[pltpu.SemaphoreType.DMA((8,))],
        far_out=(3,),
    )(ay, bx, a0, a1, b0, b1, cross_memory, biases, *near)

    slots, values, lses, inverses, sel = call(
        functools.partial(owner_forward_kernel, capacity),
        [
            ((plane_blocks, rows_in, D), LOW),
            ((plane_blocks, rows_in, D), F32),
            ((plane_blocks, rows_in, SLAB), F32),
            ((plane_blocks, rows_in, SLAB), F32),
            ((4, plane_blocks * capacity, tokens), LOW),
        ],
        scratch=[
            pltpu.VMEM((RANK_ROWS, tokens), F32),
            pltpu.VMEM((plane_blocks, rows_in, D), LOW),
            pltpu.SemaphoreType.DMA((1,)),
        ],
        far_out=(0,),
        flops=20 * MICROSECOND,
    )(*queries, memory, hidden_rows)
    payloads = [None] * 4
    done = ()
    for k in (3, 2, 1, 0):
        payloads[k] = call(
            functools.partial(merge_kernel, capacity, k),
            [((tokens + LSE_ROWS, D), LOW)],
            earlier=done,
        )(values, lses, inverses, sel)[0]
        done = (payloads[k],)
    parts = [payloads[0]] + [swap(payloads[k], 4 * k) for k in (1, 2, 3)]

    (
        outputs,
        merged_low,
        second_low,
        active_low,
        branch_grad,
        expanded_grad,
        cross_grad,
        second_resid,
        payload,
        small_middle,
        wide_bias,
    ) = call(
        middle_kernel,
        [
            ((tokens, D), LOW),
            ((tokens, D), LOW),
            ((tokens, D), LOW),
            ((tokens, hidden), LOW),
            ((tokens, D), LOW),
            ((tokens, hidden), LOW),
            ((tokens, D), LOW),
            ((tokens, D), F32),
            ((tokens + SIDE_ROWS, D), LOW),
            ((8, D), F32),
            ((1, hidden), F32),
        ],
        scratch=[
            pltpu.VMEM((tokens, hidden), F32),
        ],
        flops=12 * MICROSECOND,
    )(
        *parts,
        first_low,
        cotangent,
        cross_output,
        expand_weight,
        contract_weight,
        biases,
        expand_bias.reshape(1, hidden),
        norm_gain,
        norm_shift,
    )
    grads = [payload] + [swap(payload, 4 * k) for k in (1, 2, 3)]

    early = WeightSums(place, count, 432)
    early.add(
        [[(active_low, branch_grad)], [(merged_low, cross_grad)], [(second_low, expanded_grad)]],
        flops=8 * MICROSECOND,
    )
    early_start = early.start()

    out = call(
        functools.partial(owner_backward_kernel, capacity),
        [((plane_blocks, BLOCK, 2 * D), LOW)] + [((tokens, D), LOW)] * 4 + [((8, D), F32)],
        scratch=[
            pltpu.VMEM((plane_blocks, rows_in, D + SLAB), LOW),
            pltpu.VMEM((plane_blocks, rows_in, D), LOW),
        ],
        earlier=early_start,
        flops=LONG,
    )(sel, *grads, memory, key_side, slots)
    memory_grad, query_grads, value_bias_grad = out[0], out[1:5], out[5]
    parts = [query_grads[0]] + [swap(query_grads[k], 4 * k) for k in (1, 2, 3)]

    early_first = early.first(memory_grad)
    late = WeightSums(place, count, 352)
    flat_grad = memory_grad.reshape(plane_blocks * BLOCK, 2 * D)
    late.buffers = call(
        functools.partial(memory_weight_kernel, count),
        [((count, 2 * D // count, UNIT), LOW)] * 2,
        scratch=[pltpu.VMEM((2, D, D), F32)],
        n_smem=1,
        earlier=early_first,
        flops=MICROSECOND // 10,
    )(place, flat_grad, stored)
    late.plan, late.at = [(D, 2 * D, 0)], 2 * D // count

    pre_grad, self_branch_grad, project_grad, input_grad, small_self = call(
        self_backward_kernel,
        [
            ((tokens, D), LOW),
            ((tokens, D), LOW),
            ((tokens, 3 * D), LOW),
            ((tokens, D), F32),
            ((8, D), F32),
        ],
        scratch=[
            pltpu.VMEM((tokens, D), LOW),
        ],
        earlier=(late.buffers[0],),
        flops=LONG // 3,
    )(
        *parts,
        second_resid,
        unit_first,
        scale_first,
        heads_all,
        soft_self,
        cross_query,
        self_output,
        self_project,
        norm_gain,
    )
    early_second = early.second()
    late.add(
        [[(attended, self_branch_grad)], [(first_low, pre_grad)], [(inputs, project_grad)]],
        (small_self, small_middle, value_bias_grad, wide_bias),
        earlier=(early_second[0],),
        flops=MICROSECOND // 10,
    )
    near_a0, near_a1, far_a, near_b0, near_b1, far_b = call(
        datastore_grad_kernel,
        [((2 * BLOCK, D), LOW), ((2 * BLOCK, D), LOW), ((4 * BLOCK, D), LOW)] * 2,
        earlier=(late.buffers[0],),
        flops=MICROSECOND // 10,
    )(cross_memory, flat_grad)
    late.start(earlier=(far_a,))
    late_first = late.first()
    early.third(late_first[0])
    contract_weight_grad, cross_output_grad, expand_weight_grad = early.finish()
    late.second(contract_weight_grad)
    far_a, far_b = (after(v, late.w[0]) for v in (far_a, far_b))
    come_a, come_b = swap(far_a, 2), swap(far_b, 1)
    quarter = (2 * BLOCK, D)
    send_a, send_b, keep_a, keep_b = call(
        datastore_step_kernel, [(quarter, LOW)] * 2 + [(quarter, F32)] * 2, limit=SMALL_LIMIT
    )(near_a0, near_a1, come_a, near_b0, near_b1, come_b)
    (datastore_grad,) = call(
        datastore_sum_kernel, [((4 * BLOCK, D), F32)], limit=SMALL_LIMIT
    )(keep_a, swap(send_a, 1), keep_b, swap(send_b, 2))
    late.third(send_a)
    share = D // count
    (
        cross_memory_grad,
        self_output_grad,
        cross_query_grad,
        self_project_grad,
        biases_grad,
        wide_grad,
        gain_grad,
        shift_grad,
    ) = late.finish([(7, share), (1, hidden // count), (3, share), (3, share)])
    return (
        outputs,
        input_grad,
        datastore_grad,
        self_project_grad,
        self_output_grad,
        cross_query_grad,
        cross_memory_grad,
        cross_output_grad,
        expand_weight_grad,
        contract_weight_grad,
        biases_grad,
        wide_grad.reshape(hidden // count),
        gain_grad,
        shift_grad,
    )


def layer_norm(residual, gain_row, shift_row):
    center = residual - jnp.mean(residual, axis=-1, keepdims=True)
    spread = jnp.mean(center * center, axis=-1, keepdims=True)
    return center * lax.rsqrt(spread + EPSILON) * gain_row + shift_row


def doc_mask(lengths, seq_tokens):
    upto = jnp.tri(lengths.shape[-1], dtype=jnp.int32)
    bounds = jnp.sum(lengths[..., None, :] * upto, axis=-1)
    places = jnp.arange(seq_tokens, dtype=jnp.int32)
    segment = jnp.sum((places[:, None] >= bounds[..., None, :]).astype(jnp.int32), axis=-1)
    causal = places[:, None] >= places[None, :]
    return (segment[..., :, None] == segment[..., None, :]) & causal


def slot_numbers(picks, capacity):
    flat_ids = picks.reshape(-1)
    sorter = jnp.argsort(flat_ids, stable=True)
    sorted_ids = flat_ids[sorter]
    first_seen = jnp.searchsorted(sorted_ids, sorted_ids, side="left")
    rank_sorted = jnp.arange(flat_ids.shape[0], dtype=jnp.int32) - first_seen
    ranks = jnp.zeros_like(flat_ids).at[sorter].set(rank_sorted)
    return flat_ids * capacity + ranks


def place_rows(rows, slot_ids, total_slots, store_count, local_blocks, capacity):
    placed = jnp.zeros((total_slots, rows.shape[1]), rows.dtype).at[slot_ids].set(rows)
    return placed.reshape(store_count, local_blocks, capacity, rows.shape[1])


def local_slots(
    inputs,
    doc_lengths,
    datastore,
    kept_mask,
    retrieved,
    self_project,
    self_output,
    cross_query,
    cross_memory,
    cross_output,
    expand_weight,
    contract_weight,
    biases,
    expand_bias,
    norm_gain,
    norm_shift,
    cotangent,
):
    tok_count = inputs.shape[0]
    store_count = lax.axis_size("store")
    local_blocks = datastore.shape[0] // BLOCK
    all_blocks = local_blocks * store_count
    capacity = 2 * tok_count * TOPB // all_blocks
    rows_in = store_count * capacity
    total_slots = all_blocks * capacity
    gain_rows = norm_gain.astype(jnp.float32)
    shift_rows = norm_shift.astype(jnp.float32)
    bias_rows = biases.astype(jnp.float32)
    projected = jnp.dot(inputs, self_project, preferred_element_type=jnp.float32)
    heads_all = jnp.concatenate(
        [
            QUERY_SCALE * (projected[:, :D] + bias_rows[0]),
            projected[:, D : 2 * D],
            projected[:, 2 * D :] + bias_rows[1],
        ],
        axis=1,
    ).astype(jnp.bfloat16)
    queries = heads_all[:, :D].reshape(tok_count, HEADS, HEAD_DIM)
    keys_self = heads_all[:, D : 2 * D].reshape(tok_count, HEADS, HEAD_DIM)
    values_self = heads_all[:, 2 * D :].reshape(tok_count, HEADS, HEAD_DIM)
    allowed = doc_mask(doc_lengths[0], tok_count)

    def self_scores():
        raw_scores = jnp.einsum(
            "qhd,khd->hqk", queries, keys_self, preferred_element_type=jnp.float32
        )
        return jnp.where(allowed[None], raw_scores, MASKED)

    scores = self_scores()
    self_lse = jax.nn.logsumexp(scores, axis=-1)
    soft_low = jnp.exp(scores - self_lse[..., None]).astype(jnp.bfloat16)
    attended = (
        jnp.einsum("hqk,khd->qhd", soft_low, values_self, preferred_element_type=jnp.float32)
        .reshape(tok_count, D)
        .astype(jnp.bfloat16)
    )
    self_branch = jnp.dot(attended, self_output, preferred_element_type=jnp.float32) + bias_rows[2]
    first_norm, first_back = jax.vjp(
        layer_norm, inputs.astype(jnp.float32) + self_branch, gain_rows[0], shift_rows[0]
    )
    first_low = first_norm.astype(jnp.bfloat16)
    cross_queries = (
        QUERY_SCALE
        * (jnp.dot(first_low, cross_query, preferred_element_type=jnp.float32) + bias_rows[3])
    ).astype(jnp.bfloat16)
    slot_ids = slot_numbers(retrieved, capacity)
    send_buffer = place_rows(
        jnp.repeat(cross_queries, TOPB, axis=0),
        slot_ids,
        total_slots,
        store_count,
        local_blocks,
        capacity,
    )
    arrived = lax.all_to_all(send_buffer, "store", split_axis=0, concat_axis=2, tiled=True)
    owner_queries = arrived[0].reshape(local_blocks, rows_in, HEADS, HEAD_DIM)
    memory_bias = jnp.concatenate([jnp.zeros((D,), jnp.float32), bias_rows[4]])
    memory_low = (
        jnp.dot(datastore, cross_memory, preferred_element_type=jnp.float32) + memory_bias
    ).astype(jnp.bfloat16)
    memory_blocks = memory_low.reshape(local_blocks, BLOCK, 2 * D)
    store_keys = memory_blocks[:, :, :D].reshape(local_blocks, BLOCK, HEADS, HEAD_DIM)
    store_values = memory_blocks[:, :, D:].reshape(local_blocks, BLOCK, HEADS, HEAD_DIM)
    kept_rows = kept_mask.reshape(local_blocks, BLOCK) > 0

    def block_scores(query_blocks):
        raw_scores = jnp.einsum(
            "bmhd,bkhd->bhmk", query_blocks, store_keys, preferred_element_type=jnp.float32
        )
        return jnp.where(kept_rows[:, None, None, :], raw_scores, MASKED)

    owner_scores = block_scores(owner_queries)
    owner_lse = jax.nn.logsumexp(owner_scores, axis=-1)
    owner_soft = jnp.exp(owner_scores - owner_lse[..., None]).astype(jnp.bfloat16)
    partial_value = jnp.einsum(
        "bhmk,bkhd->bmhd", owner_soft, store_values, preferred_element_type=jnp.float32
    ).reshape(local_blocks, rows_in, D)
    partial_lse = jnp.transpose(owner_lse, (0, 2, 1))
    returned, returned_lse = (
        lax.all_to_all(partial_value[None], "store", split_axis=2, concat_axis=0, tiled=True),
        lax.all_to_all(partial_lse[None], "store", split_axis=2, concat_axis=0, tiled=True),
    )
    picked = returned.reshape(total_slots, D)[slot_ids].reshape(tok_count, TOPB, HEADS, HEAD_DIM)
    picked_lse = returned_lse.reshape(total_slots, HEADS)[slot_ids].reshape(tok_count, TOPB, HEADS)
    overall = jax.nn.logsumexp(picked_lse, axis=1)
    mix_weights = jnp.exp(picked_lse - overall[:, None, :])
    merged = jnp.einsum(
        "tjh,tjhd->thd", mix_weights, picked, precision=lax.Precision.HIGHEST
    ).reshape(tok_count, D)
    merged_low = merged.astype(jnp.bfloat16)
    cross_branch = (
        jnp.dot(merged_low, cross_output, preferred_element_type=jnp.float32) + bias_rows[5]
    )
    second_norm, second_back = jax.vjp(
        layer_norm, first_low.astype(jnp.float32) + cross_branch, gain_rows[1], shift_rows[1]
    )
    second_low = second_norm.astype(jnp.bfloat16)
    expanded = jnp.dot(
        second_low, expand_weight, preferred_element_type=jnp.float32
    ) + expand_bias.astype(jnp.float32)
    activated, gelu_back = jax.vjp(
        lambda pre_act: jax.nn.gelu(pre_act, approximate=False), expanded
    )
    activated_low = activated.astype(jnp.bfloat16)
    ffn_branch = (
        jnp.dot(activated_low, contract_weight, preferred_element_type=jnp.float32) + bias_rows[6]
    )
    final_norm, final_back = jax.vjp(
        layer_norm, second_low.astype(jnp.float32) + ffn_branch, gain_rows[2], shift_rows[2]
    )
    outputs = final_norm.astype(jnp.bfloat16)
    final_resid, final_gain, final_shift = final_back(cotangent.astype(jnp.float32))
    ffn_branch_grad = final_resid.astype(jnp.bfloat16)
    contract_weight_grad = jnp.dot(
        activated_low.T, ffn_branch_grad, preferred_element_type=jnp.float32
    )
    activated_grad = jnp.dot(ffn_branch_grad, contract_weight.T, preferred_element_type=jnp.float32)
    (expanded_raw,) = gelu_back(activated_grad)
    expanded_grad = expanded_raw.astype(jnp.bfloat16)
    expand_weight_grad = jnp.dot(second_low.T, expanded_grad, preferred_element_type=jnp.float32)
    expand_bias_grad = jnp.sum(expanded_grad.astype(jnp.float32), axis=0)
    second_total = final_resid + jnp.dot(
        expanded_grad, expand_weight.T, preferred_element_type=jnp.float32
    )
    second_resid, second_gain, second_shift = second_back(second_total)
    cross_branch_grad = second_resid.astype(jnp.bfloat16)
    cross_output_grad = jnp.dot(merged_low.T, cross_branch_grad, preferred_element_type=jnp.float32)
    attended_grad = jnp.dot(
        cross_branch_grad, cross_output.T, preferred_element_type=jnp.float32
    ).astype(jnp.bfloat16)
    delta_rows = jnp.sum(
        attended_grad.reshape(tok_count, HEADS, HEAD_DIM).astype(jnp.float32)
        * merged.reshape(tok_count, HEADS, HEAD_DIM),
        axis=-1,
    )
    grad_buffer = place_rows(
        jnp.repeat(attended_grad, TOPB, axis=0),
        slot_ids,
        total_slots,
        store_count,
        local_blocks,
        capacity,
    )
    overall_buffer = place_rows(
        jnp.repeat(overall, TOPB, axis=0),
        slot_ids,
        total_slots,
        store_count,
        local_blocks,
        capacity,
    )
    delta_buffer = place_rows(
        jnp.repeat(delta_rows, TOPB, axis=0),
        slot_ids,
        total_slots,
        store_count,
        local_blocks,
        capacity,
    )
    arrived_grad = lax.all_to_all(grad_buffer, "store", split_axis=0, concat_axis=2, tiled=True)
    arrived_overall, arrived_delta = (
        lax.all_to_all(overall_buffer, "store", split_axis=0, concat_axis=2, tiled=True),
        lax.all_to_all(delta_buffer, "store", split_axis=0, concat_axis=2, tiled=True),
    )
    owner_grad = arrived_grad[0].reshape(local_blocks, rows_in, HEADS, HEAD_DIM)
    overall_heads = jnp.transpose(arrived_overall[0], (0, 2, 1))
    delta_heads = jnp.transpose(arrived_delta[0], (0, 2, 1))
    soft_again = jnp.exp(block_scores(owner_queries) - owner_lse[..., None])
    soft_again_low = soft_again.astype(jnp.bfloat16).astype(jnp.float32)
    weight_mix = jnp.exp(owner_lse - overall_heads)
    value_dots = jnp.einsum(
        "bmhd,bkhd->bhmk", owner_grad, store_values, preferred_element_type=jnp.float32
    )
    exact_sum = jnp.sum(soft_again * value_dots, axis=-1, keepdims=True)
    rounded_sum = jnp.sum(soft_again_low * value_dots, axis=-1, keepdims=True)
    score_grad = (
        weight_mix[..., None]
        * soft_again
        * (value_dots - exact_sum + rounded_sum - delta_heads[..., None])
    ).astype(jnp.bfloat16)
    query_grad = (
        jnp.einsum("bhmk,bkhd->bmhd", score_grad, store_keys, preferred_element_type=jnp.float32)
        .astype(jnp.bfloat16)
        .reshape(local_blocks, rows_in, D)
    )
    key_grad = jnp.einsum(
        "bhmk,bmhd->bkhd", score_grad, owner_queries, preferred_element_type=jnp.float32
    )
    weighted_soft = weight_mix[..., None] * soft_again_low
    value_grad = jnp.einsum(
        "bhmk,bmhd->bkhd",
        weighted_soft,
        owner_grad.astype(jnp.float32),
        precision=lax.Precision.HIGHEST,
    )
    row_count = local_blocks * BLOCK
    memory_grad = jnp.concatenate(
        [key_grad.reshape(row_count, D), value_grad.reshape(row_count, D)], axis=1
    ).astype(jnp.bfloat16)
    cross_memory_grad = jnp.dot(datastore.T, memory_grad, preferred_element_type=jnp.float32)
    value_bias_grad = jnp.sum(memory_grad[:, D:].astype(jnp.float32), axis=0)
    datastore_grad = jnp.dot(memory_grad, cross_memory.T, preferred_element_type=jnp.float32)
    returned_grad = lax.all_to_all(
        query_grad[None], "store", split_axis=2, concat_axis=0, tiled=True
    )
    per_pick = returned_grad.reshape(total_slots, D)[slot_ids].reshape(tok_count, TOPB, D)
    query_sum = jnp.sum(per_pick.astype(jnp.float32), axis=1).astype(jnp.bfloat16)
    cross_pre_grad = (query_sum.astype(jnp.float32) * QUERY_SCALE).astype(jnp.bfloat16)
    cross_query_grad = jnp.dot(first_low.T, cross_pre_grad, preferred_element_type=jnp.float32)
    first_total = second_resid + jnp.dot(
        cross_pre_grad, cross_query.T, preferred_element_type=jnp.float32
    )
    first_resid, first_gain, first_shift = first_back(first_total)
    self_branch_grad = first_resid.astype(jnp.bfloat16)
    self_output_grad = jnp.dot(attended.T, self_branch_grad, preferred_element_type=jnp.float32)
    self_attended_grad = (
        jnp.dot(self_branch_grad, self_output.T, preferred_element_type=jnp.float32)
        .astype(jnp.bfloat16)
        .reshape(tok_count, HEADS, HEAD_DIM)
    )
    soft_self = jnp.exp(self_scores() - self_lse[..., None])
    soft_dots = jnp.einsum(
        "qhd,khd->hqk", self_attended_grad, values_self, preferred_element_type=jnp.float32
    )
    self_score_grad = (
        soft_self * (soft_dots - jnp.sum(soft_self * soft_dots, axis=-1, keepdims=True))
    ).astype(jnp.bfloat16)
    query_self_grad = jnp.einsum(
        "hqk,khd->qhd", self_score_grad, keys_self, preferred_element_type=jnp.float32
    ).reshape(tok_count, D)
    key_self_grad = jnp.einsum(
        "hqk,qhd->khd", self_score_grad, queries, preferred_element_type=jnp.float32
    ).reshape(tok_count, D)
    value_self_grad = jnp.einsum(
        "hqk,qhd->khd", soft_low, self_attended_grad, preferred_element_type=jnp.float32
    ).reshape(tok_count, D)
    heads_grad = jnp.concatenate([query_self_grad, key_self_grad, value_self_grad], axis=1).astype(
        jnp.bfloat16
    )
    project_grad = jnp.concatenate(
        [
            (heads_grad[:, :D].astype(jnp.float32) * QUERY_SCALE).astype(jnp.bfloat16),
            heads_grad[:, D:],
        ],
        axis=1,
    )
    self_project_grad = jnp.dot(inputs.T, project_grad, preferred_element_type=jnp.float32)
    input_grad = first_resid + jnp.dot(
        project_grad, self_project.T, preferred_element_type=jnp.float32
    )
    biases_grad = jnp.stack(
        [
            jnp.sum(project_grad[:, :D].astype(jnp.float32), axis=0),
            jnp.sum(project_grad[:, 2 * D :].astype(jnp.float32), axis=0),
            jnp.sum(self_branch_grad.astype(jnp.float32), axis=0),
            jnp.sum(cross_pre_grad.astype(jnp.float32), axis=0),
            value_bias_grad,
            jnp.sum(cross_branch_grad.astype(jnp.float32), axis=0),
            jnp.sum(ffn_branch_grad.astype(jnp.float32), axis=0),
        ]
    )
    gain_grad = jnp.stack([first_gain, second_gain, final_gain])
    shift_grad = jnp.stack([first_shift, second_shift, final_shift])
    shared = (
        lax.psum_scatter(self_project_grad, "store", scatter_dimension=0, tiled=True),
        lax.psum_scatter(self_output_grad, "store", scatter_dimension=0, tiled=True),
        lax.psum_scatter(cross_query_grad, "store", scatter_dimension=0, tiled=True),
        lax.psum_scatter(cross_memory_grad, "store", scatter_dimension=0, tiled=True),
        lax.psum_scatter(cross_output_grad, "store", scatter_dimension=0, tiled=True),
        lax.psum_scatter(expand_weight_grad, "store", scatter_dimension=0, tiled=True),
        lax.psum_scatter(contract_weight_grad, "store", scatter_dimension=0, tiled=True),
        lax.psum_scatter(biases_grad, "store", scatter_dimension=1, tiled=True),
        lax.psum_scatter(expand_bias_grad, "store", scatter_dimension=0, tiled=True),
        lax.psum_scatter(gain_grad, "store", scatter_dimension=1, tiled=True),
        lax.psum_scatter(shift_grad, "store", scatter_dimension=1, tiled=True),
    )
    reduced = (
        lax.psum(shared[0].astype(jnp.bfloat16), "dp").astype(jnp.float32),
        lax.psum(shared[1].astype(jnp.bfloat16), "dp").astype(jnp.float32),
        lax.psum(shared[2].astype(jnp.bfloat16), "dp").astype(jnp.float32),
        lax.psum(shared[3].astype(jnp.bfloat16), "dp").astype(jnp.float32),
        lax.psum(shared[4].astype(jnp.bfloat16), "dp").astype(jnp.float32),
        lax.psum(shared[5].astype(jnp.bfloat16), "dp").astype(jnp.float32),
        lax.psum(shared[6].astype(jnp.bfloat16), "dp").astype(jnp.float32),
        lax.psum(shared[7].astype(jnp.bfloat16), "dp").astype(jnp.float32),
        lax.psum(shared[8].astype(jnp.bfloat16), "dp").astype(jnp.float32),
        lax.psum(shared[9].astype(jnp.bfloat16), "dp").astype(jnp.float32),
        lax.psum(shared[10].astype(jnp.bfloat16), "dp").astype(jnp.float32),
    )
    return (
        outputs,
        input_grad,
        datastore_grad,
        reduced[0],
        reduced[1],
        reduced[2],
        reduced[3],
        reduced[4],
        reduced[5],
        reduced[6],
        reduced[7],
        reduced[8],
        reduced[9],
        reduced[10],
    )


def solution(mesh):
    placed = (
        P(("dp", "store"), None),
        P(("dp", "store"), None),
        P(("dp", "store"), None),
        P(("dp", "store")),
        P(("dp", "store"), None),
        P(),
        P(),
        P(),
        P(),
        P(),
        P(),
        P(),
        P(),
        P(),
        P(),
        P(),
        P(("dp", "store"), None),
    )
    return jax.shard_map(
        local_tree if mesh.shape["store"] == 16 else local_slots,
        mesh=mesh,
        in_specs=placed,
        out_specs=(
            P(("dp", "store"), None),
            P(("dp", "store"), None),
            P(("dp", "store"), None),
            P("store", None),
            P("store", None),
            P("store", None),
            P("store", None),
            P("store", None),
            P("store", None),
            P("store", None),
            P(None, "store"),
            P("store"),
            P(None, "store"),
            P(None, "store"),
        ),
        check_vma=False,
    )
```

```python
import functools

import jax
import jax.numpy as jnp
from jax import lax
from jax.experimental import pallas as pl
from jax.experimental.pallas import tpu as pltpu
from jax.sharding import PartitionSpec as P

D = 768
HEADS = 12
HEAD_DIM = 64
TOPB = 8
BLOCK = 128
SLAB = 128
PAIRS = D // SLAB
UNIT = 384
LSE_ROWS = 8
SIDE_ROWS = 16
RANK_ROWS = 16

EPSILON = 1e-05
MASKED = -1e30
QUERY_SCALE = 0.125
VMEM_LIMIT = 16 * 1024 * 1024
SMALL_LIMIT = 16 * 1024 * 1024
LONG = 30_000_000_000
UNROLL = 4
MICROSECOND = 50_000_000
LOW = jnp.bfloat16
F32 = jnp.float32

_VMEM = pl.BlockSpec(memory_space=pltpu.VMEM)
_SMEM = pl.BlockSpec(memory_space=pltpu.SMEM)
_ANY = pl.BlockSpec(memory_space=pl.ANY)


def nn(a, b):
    return lax.dot_general(a, b, (((1,), (0,)), ((), ())), preferred_element_type=F32)


def nt(a, b):
    return lax.dot_general(a, b, (((1,), (1,)), ((), ())), preferred_element_type=F32)


def tn(a, b):
    return lax.dot_general(a, b, (((0,), (0,)), ((), ())), preferred_element_type=F32)


def three(v):
    high = v.astype(LOW)
    rest = v - high.astype(F32)
    mid = rest.astype(LOW)
    return high, mid, (rest - mid.astype(F32)).astype(LOW)


def lanes(shape):
    return lax.broadcasted_iota(jnp.int32, shape, len(shape) - 1)


def rows_of(shape):
    return lax.broadcasted_iota(jnp.int32, shape, len(shape) - 2)


def flag(condition):
    return jnp.where(condition, 1.0, 0.0)


def half_masks():
    first = flag(lanes((1, SLAB)) < HEAD_DIM)
    return first.astype(LOW), (1.0 - first).astype(LOW)


def two_heads(slab, first, second):
    return jnp.concatenate([slab * first, slab * second], axis=0)


def join_heads(stacked, count):
    left = lanes((count, SLAB)) < HEAD_DIM
    return jnp.where(left, stacked[:count], stacked[count:])


def norm_forward(residual, gain, shift):
    center = residual - jnp.mean(residual, axis=-1, keepdims=True)
    spread = jnp.mean(center * center, axis=-1, keepdims=True)
    scale = lax.rsqrt(spread + EPSILON)
    unit = center * scale
    return unit * gain + shift, unit, scale


def norm_backward(grad, unit, scale, gain):
    inner = grad * gain
    down = inner - jnp.mean(inner, axis=-1, keepdims=True)
    down = down - unit * jnp.mean(inner * unit, axis=-1, keepdims=True)
    return scale * down


def row_sum(v):
    return jnp.sum(v, axis=0, keepdims=True)


def call(
    kernel,
    outs,
    scratch=(),
    n_smem=0,
    far_in=(),
    far_out=(),
    earlier=(),
    aliases=None,
    flops=0,
    limit=VMEM_LIMIT,
):
    def run(*args):
        count = len(args)

        def body(*refs):
            kernel(*refs[:count], *refs[count + len(earlier) :])

        args = [
            pltpu.with_memory_space_constraint(v, pltpu.HBM) if i in far_in and not aliases else v
            for i, v in enumerate(args)
        ]
        specs = [_ANY if i in far_in else _VMEM for i in range(n_smem, count)]
        return pl.pallas_call(
            body,
            out_shape=[
                pltpu.HBM(s, t) if i in far_out and not aliases else jax.ShapeDtypeStruct(s, t)
                for i, (s, t) in enumerate(outs)
            ],
            in_specs=[_SMEM] * n_smem + specs + [_ANY] * len(earlier),
            out_specs=[_ANY if i in far_out else _VMEM for i in range(len(outs))],
            scratch_shapes=list(scratch),
            input_output_aliases=aliases or {},
            compiler_params=pltpu.CompilerParams(vmem_limit_bytes=limit),
            cost_estimate=pl.CostEstimate(flops=flops, bytes_accessed=0, transcendentals=0),
        )(*args, *earlier)

    return run


def copies(pairs, sems):
    return [pltpu.make_async_copy(a, b, sems.at[i]) for i, (a, b) in enumerate(pairs)]


def after(v, *earlier):
    return call(
        lambda *refs: None,
        [(v.shape, v.dtype)],
        far_in=(0,),
        far_out=(0,),
        earlier=earlier,
        aliases={0: 0},
        limit=1024 * 1024,
    )(v)[0]


def start_all(items):
    for item in items:
        item.start()


def wait_all(items):
    for item in items:
        item.wait()


def plane_ranks(picks_ref, me, k, tokens):
    i = rows_of((RANK_ROWS, tokens))
    group, chip, block = i // 4, (i // 2) % 2, i % 2
    apart = jnp.where(group < 2, 2 * group + chip, 2 * chip + group - 2)
    local = jnp.where(group < 2, block, 2 + block)
    plane = (me // 4) ^ k
    number = plane * 16 + ((me % 4) ^ apart) * 4 + local
    member = jnp.zeros((RANK_ROWS, tokens), F32)
    for j in range(TOPB):
        member = member + flag(picks_ref[j : j + 1, :] == number)
    earlier = flag(rows_of((tokens, tokens)) < lanes((tokens, tokens)))
    rank = nn(member.astype(LOW), earlier.astype(LOW))
    return jnp.where(member > 0.5, rank, -1.0).astype(LOW)


def self_forward_kernel(
    lengths_ref,
    place_ref,
    x_ref,
    picks_ref,
    project_ref,
    output_ref,
    query_ref,
    bias_ref,
    gain_ref,
    shift_ref,
    heads_ref,
    soft_ref,
    attended_ref,
    unit_ref,
    scale_ref,
    first_ref,
    *rest,
):
    payload_refs, (project_scr, output_scr, query_scr, sems) = rest[:4], rest[4:]
    thirds = [slice(i * D, (i + 1) * D) for i in range(3)]
    fetch = copies(
        [(project_ref.at[:, at], project_scr.at[:, at]) for at in thirds]
        + [(output_ref, output_scr), (query_ref, query_scr)],
        sems,
    )
    start_all(fetch)
    tokens = x_ref.shape[0]
    bias = bias_ref[...].astype(F32)
    x = x_ref[...]
    for i, at in enumerate(thirds):
        fetch[i].wait()
        part = nn(x, project_scr[:, at])
        if i == 0:
            part = QUERY_SCALE * (part + bias[0:1])
        if i == 2:
            part = part + bias[1:2]
        heads_ref[:, at] = part.astype(LOW)
    place_row = lax.broadcasted_iota(jnp.int32, (2 * tokens, tokens), 0) % tokens
    place_col = lanes((2 * tokens, tokens))
    segment_row = jnp.zeros((2 * tokens, tokens), jnp.int32)
    segment_col = jnp.zeros((2 * tokens, tokens), jnp.int32)
    bound = 0
    for d in range(lengths_ref.shape[1]):
        bound = bound + lengths_ref[0, d]
        segment_row = segment_row + jnp.where(place_row >= bound, 1, 0)
        segment_col = segment_col + jnp.where(place_col >= bound, 1, 0)
    allowed = (segment_row == segment_col) & (place_row >= place_col)
    first, second = half_masks()
    for p in range(PAIRS):
        at = p * SLAB
        queries = two_heads(heads_ref[:, at : at + SLAB], first, second)
        scores = nt(queries, heads_ref[:, D + at : D + at + SLAB])
        scores = jnp.where(allowed, scores, MASKED)
        top = jnp.max(scores, axis=-1, keepdims=True)
        raised = jnp.exp(scores - top)
        soft = raised / jnp.sum(raised, axis=-1, keepdims=True)
        soft_ref[p] = soft
        mixed = nn(soft.astype(LOW), heads_ref[:, 2 * D + at : 2 * D + at + SLAB])
        attended_ref[:, at : at + SLAB] = join_heads(mixed, tokens).astype(LOW)
    fetch[3].wait()
    residual = x.astype(F32) + nn(attended_ref[...], output_scr[...]) + bias[2:3]
    normed, unit, scale = norm_forward(
        residual, gain_ref[0:1, :].astype(F32), shift_ref[0:1, :].astype(F32)
    )
    unit_ref[...] = unit
    scale_ref[...] = scale
    low = normed.astype(LOW)
    first_ref[...] = low
    fetch[4].wait()
    queries = (QUERY_SCALE * (nn(low, query_scr[...]) + bias[3:4])).astype(LOW)
    for k, out in enumerate(payload_refs):
        out[:tokens] = queries
        out[tokens:, tokens:] = jnp.zeros((RANK_ROWS, D - tokens), LOW)
        out[tokens:, :tokens] = plane_ranks(picks_ref, place_ref[0], k, tokens)


def piece_kernel(rows_ref, kept_ref, a_ref, b_ref):
    for h, out in enumerate((a_ref, b_ref)):
        out[: 2 * BLOCK] = rows_ref[2 * h * BLOCK : 2 * (h + 1) * BLOCK]
        marks = kept_ref[2 * h : 2 * h + 2, :].astype(F32)
        marks = jnp.concatenate([marks, jnp.zeros((RANK_ROWS - 2, BLOCK), F32)], axis=0)
        out[2 * BLOCK :, :BLOCK] = marks.astype(LOW)
        out[2 * BLOCK :, BLOCK:] = jnp.zeros((RANK_ROWS, D - BLOCK), LOW)


def pair_kernel(first_ref, second_ref, out_ref):
    out_ref[0] = first_ref[...]
    out_ref[1] = second_ref[...]


def memory_kernel(*refs):
    far = len(refs) > 12
    if far:
        pieces = [ref.at[j] for ref in refs[:2] for j in range(2)]
        near_pieces, (weight_ref, bias_ref), given = refs[2:6], refs[6:8], refs[8:14]
        outs, rows_ref, sems = refs[14:17], refs[17], refs[18]
        size = 2 * BLOCK
        pairs = []
        for s in range(2):
            for j in range(2):
                at = 8 * s * BLOCK + j * size
                pairs.append((near_pieces[2 * s + j].at[:size], rows_ref.at[at : at + size]))
                at = at + 4 * BLOCK
                pairs.append((pieces[2 * s + j].at[:size], rows_ref.at[at : at + size]))
        keep = copies(pairs, sems)
        start_all(keep)
    else:
        pieces, (weight_ref, bias_ref), outs = refs[:4], refs[4:6], refs[6:]
    bias = bias_ref[4:5, :].astype(F32)
    lane = lanes((RANK_ROWS, SLAB))
    place = lanes((BLOCK, SLAB))
    for s in range(2):
        if far:
            near, here = 8 * s, 8 * s + 4
            memory_ref, hidden_ref, side_ref = outs
            for out, ref in zip(outs, given[3 * s : 3 * s + 3]):
                out[near : near + 4] = ref[...]
        else:
            here = 0
            memory_ref, hidden_ref, side_ref = outs[3 * s : 3 * s + 3]
        for j in range(2):
            piece = pieces[2 * s + j]
            rows = piece[: 2 * BLOCK]
            first = here + 2 * j
            keys = nn(rows, weight_ref[:, :D]).astype(LOW)
            values = (nn(rows, weight_ref[:, D:]) + bias).astype(LOW)
            marks = piece[2 * BLOCK :, :SLAB]
            for l in range(2):
                at = first + l
                memory_ref[at, :, :D] = keys[l * BLOCK : (l + 1) * BLOCK]
                memory_ref[at, :, D:] = values[l * BLOCK : (l + 1) * BLOCK]
                hidden_ref[at] = (1.0 - marks[l : l + 1].astype(F32)) * MASKED
                wanted = flag((rows_of((RANK_ROWS, SLAB)) == l) & (lane == SLAB - 1))
                column = tn(marks, wanted.astype(LOW))
                side = jnp.where(place == SLAB - 1, (1.0 - column) * MASKED, 0.0)
                side_ref[at] = jnp.where(place < 48, -1.0, side).astype(LOW)
    if far:
        wait_all(keep)


def selection(ranks, capacity):
    parts = []
    wanted = rows_of((capacity, ranks.shape[1])).astype(F32)
    for b in range(ranks.shape[0]):
        parts.append(flag(ranks[b : b + 1, :] == wanted).astype(LOW))
    return jnp.concatenate(parts, axis=0)


def fill_slots(sel, rows, out_ref, k, capacity):
    got = nn(sel, rows).astype(LOW)
    for b in range(out_ref.shape[0]):
        out_ref[b, k * capacity : (k + 1) * capacity, :] = got[b * capacity : (b + 1) * capacity]


def around16(v, combine):
    for step in (16, 32, 64):
        v = combine(v, pltpu.roll(v, step, 1))
    return v


def put_side(ref, side, rows):
    tokens = side.shape[0]
    turned = side.astype(F32).T.astype(LOW)
    for q in range(PAIRS):
        ref[tokens:, q * SLAB : (q + 1) * SLAB] = turned[q * rows : (q + 1) * rows]


def get_side(ref, tokens):
    rows = ref.shape[0] - tokens
    parts = [ref[tokens:, q * SLAB : (q + 1) * SLAB].astype(F32) for q in range(PAIRS)]
    parts.append(jnp.zeros((SLAB - PAIRS * rows, SLAB), F32))
    return jnp.concatenate(parts, axis=0).T


def lse_lanes(lse):
    high = lse.astype(LOW).astype(F32)
    rest = lse - high
    mid = rest.astype(LOW).astype(F32)
    low = rest - mid
    lane = lanes(lse.shape)
    packed = jnp.where(
        lane < 16, high, jnp.where(lane < 32, mid, jnp.where(lane < 48, low, 0.0))
    )
    return packed.astype(LOW)


def head_spread(group):
    row = rows_of((SLAB, D))
    row = row % 16 if group else row
    return flag(row == lanes((SLAB, D)) // HEAD_DIM).astype(LOW)


def owner_forward_kernel(capacity, *refs):
    tokens_refs, memory_ref, hidden_ref = refs[0:4], refs[4], refs[5]
    far_slots_ref, out_scr, lse_scr, inv_scr, sel_scr, ranks_scr, slots_ref, sems = refs[6:]
    sources = len(tokens_refs)
    blocks, rows = slots_ref.shape[:2]
    tokens = tokens_refs[0].shape[0] - RANK_ROWS
    first, second = half_masks()
    for k in range(sources):
        ranks_scr[...] = tokens_refs[k][tokens:, :tokens].astype(F32)
        sel = selection(ranks_scr[...], capacity)
        sel_scr[k] = sel
        fill_slots(sel, tokens_refs[k][:tokens], slots_ref, k, capacity)
    keep = copies([(slots_ref, far_slots_ref)], sems)
    start_all(keep)
    ones = jnp.ones((BLOCK, SLAB), LOW)
    lane_of = lanes((rows, SLAB))
    def one_block(i, carry):
        hidden = hidden_ref[i]
        tops = jnp.zeros((rows, SLAB), F32)
        totals = jnp.ones((rows, SLAB), F32)
        base = (i % 8) * 16
        slabs = [slice(p * SLAB, (p + 1) * SLAB) for p in range(PAIRS)]
        scores = [
            nt(two_heads(slots_ref[i, :, at], first, second), memory_ref[i, :, at])
            + hidden
            for at in slabs
        ]
        highest = [jnp.max(v, axis=-1, keepdims=True) for v in scores]
        raised = [jnp.exp(v - top).astype(LOW) for v, top in zip(scores, highest)]
        mixed = [
            nn(v, jnp.concatenate([memory_ref[i, :, D + at.start : D + at.stop], ones], axis=1))
            for v, at in zip(raised, slabs)
        ]
        for p, at in enumerate(slabs):
            out_scr[i, :, at] = join_heads(mixed[p][:, :SLAB], rows)
            for half in range(2):
                here = slice(half * rows, (half + 1) * rows)
                mine = lane_of == base + 2 * p + half
                tops = jnp.where(mine, highest[p][here], tops)
                totals = jnp.where(mine, mixed[p][here, SLAB:], totals)
        own = flag((lane_of >= base) & (lane_of < base + HEADS))
        lse_scr[i] = tops + jnp.log(totals)
        inv_scr[i] = own / totals
        return carry

    lax.fori_loop(0, blocks, one_block, 0, unroll=UNROLL)
    wait_all(keep)


def merge_kernel(capacity, ks, value_ref, lse_ref, inv_ref, sel_ref, *payload_refs):
    tokens = sel_ref.shape[2]
    group = 8 * capacity
    own_low = flag(
        rows_of((group, SLAB)) // capacity == lanes((group, SLAB)) // 16
    ).astype(LOW)
    spread = head_spread(True)
    each = [(n, g) for n in range(len(ks)) for g in range(2)]

    def stacked(ref, n, g):
        here = slice(ks[n] * capacity, (ks[n] + 1) * capacity)
        return jnp.concatenate([ref[8 * g + b, here, :] for b in range(8)], axis=0)

    sels = {(n, g): sel_ref[ks[n], g * group : (g + 1) * group, :] for n, g in each}
    turned = {at: sels[at].T for at in each}
    found = {
        at: nn(turned[at], jnp.concatenate([*three(stacked(lse_ref, *at)), own_low], axis=1))
        for at in each
    }
    members = {at: found[at][:, 3 * SLAB :] for at in each}
    by_token = {
        at: jnp.where(
            members[at] > 0.5,
            found[at][:, :SLAB] + found[at][:, SLAB : 2 * SLAB] + found[at][:, 2 * SLAB : 3 * SLAB],
            MASKED,
        )
        for at in each
    }
    tops = [
        around16(jnp.maximum(by_token[n, 0], by_token[n, 1]), jnp.maximum) for n in range(len(ks))
    ]
    weights = {at: members[at] * jnp.exp(by_token[at] - tops[at[0]]) for at in each}
    totals = [around16(weights[n, 0] + weights[n, 1], jnp.add) for n in range(len(ks))]
    safes = [jnp.where(total > 0.5, total, 1.0) for total in totals]
    shares = {
        at: nn(sels[at], (weights[at] / safes[at[0]]).astype(LOW)) * stacked(inv_ref, *at)
        for at in each
    }
    wide = {at: nn(shares[at].astype(LOW), spread) for at in each}
    for n, out in enumerate(payload_refs):
        partial = sum(
            nn(turned[n, g], (stacked(value_ref, n, g) * wide[n, g]).astype(LOW)) for g in range(2)
        )
        out[:tokens] = partial.astype(LOW)
        lse = jnp.where(totals[n] > 0.5, tops[n] + jnp.log(safes[n]), MASKED)
        put_side(out, lse_lanes(lse), LSE_ROWS)


def select_grads_kernel(capacity, *refs):
    sel_ref, grad_refs, got_ref = refs[0], refs[1:5], refs[5]
    tokens = grad_refs[0].shape[0] - SIDE_ROWS
    for k, ref in enumerate(grad_refs):
        side = get_side(ref, tokens).astype(LOW)
        rows_all = jnp.concatenate([ref[:tokens], side], axis=1)
        fill_slots(sel_ref[k], rows_all, got_ref, k, capacity)


def owner_backward_kernel(capacity, *refs):
    sel_scr, got_scr, memory_ref, side_ref, slots_ref = refs[:5]
    out, payload_refs, query_scr = refs[5], refs[6:10], refs[10]
    sources = len(payload_refs)
    blocks, rows = slots_ref.shape[:2]
    first, second = half_masks()
    lane = lanes((1, SLAB))
    last = flag(lane == SLAB - 1).astype(LOW)
    value_side = jnp.broadcast_to(
        -flag((lane >= 48) & (lane < 96)).astype(LOW), (BLOCK, SLAB)
    )

    def picked(head, base):
        inside = (lane >= base) & (lane < base + 48)
        return flag(inside & (lane % 16 == head)).astype(LOW)

    def one_block(i, carry):
        side = got_scr[i, :, D:]
        key_side = side_ref[i]
        slabs = [slice(p * SLAB, (p + 1) * SLAB) for p in range(PAIRS)]
        keys = [memory_ref[i, :, at] for at in slabs]
        queries = [two_heads(slots_ref[i, :, at], first, second) for at in slabs]
        grads = [two_heads(got_scr[i, :, at], first, second) for at in slabs]
        scores, dots = [], []
        for p in range(PAIRS):
            lse_side = jnp.concatenate(
                [side * picked(2 * p + h, 0) + last for h in range(2)], axis=0
            )
            scores.append(
                nt(
                    jnp.concatenate([keys[p], key_side], axis=1),
                    jnp.concatenate([queries[p], lse_side], axis=1),
                )
            )
        for p, at in enumerate(slabs):
            delta_side = jnp.concatenate(
                [side * picked(2 * p + h, 48) for h in range(2)], axis=0
            )
            values = memory_ref[i, :, D + at.start : D + at.stop]
            dots.append(
                nt(
                    jnp.concatenate([values, value_side], axis=1),
                    jnp.concatenate([grads[p], delta_side], axis=1),
                )
            )
        softs = [jnp.exp(v) for v in scores]
        score_grads = [(soft * v).astype(LOW) for soft, v in zip(softs, dots)]
        for p, at in enumerate(slabs):
            query_scr[i, :, at] = join_heads(tn(score_grads[p], keys[p]), rows).astype(LOW)
        for p, at in enumerate(slabs):
            out[i, :, at] = nn(score_grads[p], queries[p]).astype(LOW)
        for p, at in enumerate(slabs):
            out[i, :, D + at.start : D + at.stop] = nn(softs[p].astype(LOW), grads[p]).astype(
                LOW
            )
        return carry

    lax.fori_loop(0, blocks, one_block, 0, unroll=UNROLL)
    for k in range(sources):
        here = slice(k * capacity, (k + 1) * capacity)
        value = jnp.concatenate([query_scr[b, here, :] for b in range(blocks)], axis=0)
        payload_refs[k][...] = tn(sel_scr[k], value).astype(LOW)


def memory_weight_kernel(count, place_ref, *refs):
    grad_ref, rows_ref, kept_ref, sent_ref, bias_ref, sum_scr = refs
    me, core = place_ref[0], place_ref[1]
    size = 4 * BLOCK
    sum_scr[...] = jnp.zeros(sum_scr.shape, F32)
    bias_ref[...] = jnp.zeros(bias_ref.shape, F32)

    def one_set(s, carry):
        at = pl.ds(pl.multiple_of(s * size, size), size)
        rows = rows_ref[at, :].T
        for h in range(2):
            sum_scr[h] = sum_scr[h] + nn(rows, grad_ref[at, h * D : (h + 1) * D])
        bias_ref[0:1] = bias_ref[0:1] + row_sum(grad_ref[at, D:].astype(F32))
        return carry

    lax.fori_loop(0, rows_ref.shape[0] // size, one_set, 0)
    block = D // count
    for h in range(2):

        def store(out, h=h):
            total = sum_scr[h].astype(LOW)
            for k in range(count):
                for u in range(D // UNIT):
                    out[me ^ k, u * block : (u + 1) * block, :] = total[
                        k * block : (k + 1) * block, u * UNIT : (u + 1) * UNIT
                    ]

        pl.when(core == h)(functools.partial(store, kept_ref))
        pl.when(core != h)(functools.partial(store, sent_ref))


def datastore_grad_kernel(weight_ref, *refs):
    grad_ref, outs = refs[0], refs[1:7]
    weight = weight_ref[...].T
    near_a0, near_a1, far_a, near_b0, near_b1, far_b = outs
    groups = ((near_a0, near_a1), (far_a,), (near_b0, near_b1), (far_b,))
    for s in range(4):
        value = nn(grad_ref[4 * s * BLOCK : 4 * (s + 1) * BLOCK], weight).astype(LOW)
        size = value.shape[0] // len(groups[s])
        for i, out in enumerate(groups[s]):
            out[...] = value[i * size : (i + 1) * size]


def datastore_step_kernel(*refs):
    ins, sends, keeps = refs[:6], refs[6:8], refs[8:10]
    size = 2 * BLOCK
    for g in range(2):
        stay, go, come = ins[3 * g : 3 * g + 3]
        keeps[g][...] = stay[...].astype(F32) + come[:size].astype(F32)
        sends[g][...] = (go[...].astype(F32) + come[size:].astype(F32)).astype(LOW)


def datastore_sum_kernel(keep_a, come_a, keep_b, come_b, out_ref):
    size = keep_a.shape[0]
    out_ref[:size] = keep_a[...] + come_a[...].astype(F32)
    out_ref[size:] = keep_b[...] + come_b[...].astype(F32)


def middle_kernel(
    p0_ref,
    p1_ref,
    p2_ref,
    p3_ref,
    first_ref,
    cotangent_ref,
    output_ref,
    expand_ref,
    contract_ref,
    bias_ref,
    expand_bias_ref,
    gain_ref,
    shift_ref,
    out_ref,
    merged_ref,
    second_ref,
    active_ref,
    branch_grad_ref,
    expanded_grad_ref,
    cross_grad_ref,
    resid_ref,
    payload_ref,
    small_ref,
    wide_ref,
    expanded_scr,
):
    output_scr, expand_scr, contract_scr = output_ref, expand_ref, contract_ref
    bias = bias_ref[...].astype(F32)
    gain = gain_ref[...].astype(F32)
    shift = shift_ref[...].astype(F32)
    parts = [p0_ref, p1_ref, p2_ref, p3_ref]
    tokens = first_ref.shape[0]
    lses = [around16(get_side(part, tokens), jnp.add) for part in parts]
    top = functools.reduce(jnp.maximum, lses)
    weights = [jnp.exp(lse - top) for lse in lses]
    total = functools.reduce(jnp.add, weights)
    overall = top + jnp.log(total)
    spread = head_spread(False)
    merged = jnp.zeros(first_ref.shape, F32)
    for part, weight in zip(parts, weights):
        share = weight / total
        high = share.astype(LOW)
        rest = (share - high.astype(F32)).astype(LOW)
        merged = merged + (nn(high, spread) + nn(rest, spread)) * part[:tokens].astype(F32)
    merged_low = merged.astype(LOW)
    merged_ref[...] = merged_low
    residual = first_ref[...].astype(F32) + nn(merged_low, output_scr[...]) + bias[5:6]
    second, unit_second, scale_second = norm_forward(residual, gain[1:2], shift[1:2])
    second_low = second.astype(LOW)
    second_ref[...] = second_low
    hidden = contract_scr.shape[0]
    for c in range(hidden // D):
        at = slice(c * D, (c + 1) * D)
        expanded = nn(second_low, expand_scr[:, at]) + expand_bias_ref[:, at].astype(F32)
        bell = 0.5 * (1.0 + lax.erf(expanded * 0.7071067811865476))
        active_ref[:, at] = (expanded * bell).astype(LOW)
        slope = bell + expanded * 0.3989422804014327 * jnp.exp(-0.5 * expanded * expanded)
        expanded_scr[:, at] = slope
    residual = second_low.astype(F32) + nn(active_ref[...], contract_scr[...]) + bias[6:7]
    final, unit_final, scale_final = norm_forward(residual, gain[2:3], shift[2:3])
    out_ref[...] = final.astype(LOW)
    cotangent = cotangent_ref[...].astype(F32)
    final_resid = norm_backward(cotangent, unit_final, scale_final, gain[2:3])
    branch_grad = final_resid.astype(LOW)
    branch_grad_ref[...] = branch_grad
    small_ref[0:1, :] = row_sum(branch_grad.astype(F32))
    small_ref[1:2, :] = row_sum(cotangent * unit_final)
    small_ref[2:3, :] = row_sum(cotangent)
    total_grad = final_resid
    for c in range(hidden // D):
        at = slice(c * D, (c + 1) * D)
        active_grad = nt(branch_grad, contract_scr[at, :])
        expanded_grad = (active_grad * expanded_scr[:, at]).astype(LOW)
        expanded_grad_ref[:, at] = expanded_grad
        wide_ref[:, at] = row_sum(expanded_grad.astype(F32))
        total_grad = total_grad + nt(expanded_grad, expand_scr[:, at])
    small_ref[4:5, :] = row_sum(total_grad * unit_second)
    small_ref[5:6, :] = row_sum(total_grad)
    second_resid = norm_backward(total_grad, unit_second, scale_second, gain[1:2])
    resid_ref[...] = second_resid
    cross_grad = second_resid.astype(LOW)
    cross_grad_ref[...] = cross_grad
    small_ref[3:4, :] = row_sum(cross_grad.astype(F32))
    small_ref[6:8, :] = jnp.zeros((2, D), F32)
    attended_grad = nt(cross_grad, output_scr[...]).astype(LOW)
    payload_ref[:tokens] = attended_grad
    product = attended_grad.astype(F32) * merged
    gather = flag(lanes((D, SLAB)) % 16 == rows_of((D, SLAB)) // HEAD_DIM).astype(LOW)
    high, mid, low = three(product)
    delta = nn(high, gather) + nn(mid, gather) + nn(low, gather)
    lane = lanes(overall.shape)
    packed = jnp.zeros(overall.shape, F32)
    for value, base in ((overall, 0), (delta, 48)):
        for i, piece in enumerate(three(value)):
            inside = (lane >= base + 16 * i) & (lane < base + 16 * i + HEADS)
            packed = jnp.where(inside, piece.astype(F32), packed)
    put_side(payload_ref, packed, SIDE_ROWS)


def self_backward_kernel(
    d0_ref,
    d1_ref,
    d2_ref,
    d3_ref,
    resid_ref,
    unit_ref,
    scale_ref,
    heads_ref,
    soft_ref,
    query_ref,
    output_ref,
    project_ref,
    gain_ref,
    pre_grad_ref,
    branch_grad_ref,
    project_grad_ref,
    input_grad_ref,
    small_ref,
    attended_scr,
):
    query_scr, output_scr, heads_scr = query_ref, output_ref, heads_ref
    soft_scr, project_scr = soft_ref, project_ref
    tokens = resid_ref.shape[0]
    query_sum = functools.reduce(
        jnp.add, [d[...].astype(F32) for d in (d0_ref, d1_ref, d2_ref, d3_ref)]
    ).astype(LOW)
    pre_grad = (query_sum.astype(F32) * QUERY_SCALE).astype(LOW)
    pre_grad_ref[...] = pre_grad
    total = resid_ref[...] + nt(pre_grad, query_scr[...])
    unit = unit_ref[...]
    first_resid = norm_backward(total, unit, scale_ref[...], gain_ref[0:1, :].astype(F32))
    branch_grad = first_resid.astype(LOW)
    branch_grad_ref[...] = branch_grad
    attended_scr[...] = nt(branch_grad, output_scr[...]).astype(LOW)
    first, second = half_masks()
    for p in range(PAIRS):
        at = p * SLAB
        grads = two_heads(attended_scr[:, at : at + SLAB], first, second)
        queries = two_heads(heads_scr[:, at : at + SLAB], first, second)
        keys = heads_scr[:, D + at : D + at + SLAB]
        dots = nt(grads, heads_scr[:, 2 * D + at : 2 * D + at + SLAB])
        soft = soft_scr[p]
        score_grad = (soft * (dots - jnp.sum(soft * dots, axis=-1, keepdims=True))).astype(LOW)
        query_grad = join_heads(nn(score_grad, keys), tokens).astype(LOW)
        project_grad_ref[:, at : at + SLAB] = (query_grad.astype(F32) * QUERY_SCALE).astype(LOW)
        project_grad_ref[:, D + at : D + at + SLAB] = tn(score_grad, queries).astype(LOW)
        project_grad_ref[:, 2 * D + at : 2 * D + at + SLAB] = tn(soft.astype(LOW), grads).astype(
            LOW
        )
    input_grad_ref[...] = first_resid + nt(project_grad_ref[...], project_scr[...])
    small_ref[0:1, :] = row_sum(project_grad_ref[:, :D].astype(F32))
    small_ref[1:2, :] = row_sum(project_grad_ref[:, 2 * D :].astype(F32))
    small_ref[2:3, :] = row_sum(branch_grad.astype(F32))
    small_ref[3:4, :] = row_sum(pre_grad.astype(F32))
    small_ref[4:5, :] = row_sum(total * unit)
    small_ref[5:6, :] = row_sum(total)
    small_ref[6:8, :] = jnp.zeros((2, D), F32)


def weight_grad_kernel(plan, count, packed, held, place_ref, *refs):
    kept_ref, sent_ref = refs[-2:]
    me, core = place_ref[0], place_ref[1]
    at_ref = 0
    for number, rows, columns, at in plan:
        pairs = [refs[at_ref + 2 * i : at_ref + 2 * i + 2] for i in range(number)]
        at_ref += 2 * number
        block = rows // count
        half = columns // 2
        steps = [(c, min(D, half - c)) for c in range(0, half, D)]

        def unit(m, c, wide, block=block, half=half, at=at, pairs=pairs):
            xs = [x_ref[:, pl.ds(pl.multiple_of(m * D, SLAB), D)].T for x_ref, _ in pairs]
            for mine, out in ((core, kept_ref), (1 - core, sent_ref)):
                start = pl.multiple_of(mine * half + c, SLAB)
                part = sum(nn(x, g_ref[:, pl.ds(start, wide)]) for x, (_, g_ref) in zip(xs, pairs))
                part = part.astype(LOW)
                for u in range(wide // UNIT):
                    low = pl.multiple_of(at + (c // UNIT + u) * block, 16)
                    for k in range(D // block):
                        to = me ^ (m * (D // block) + k)
                        out[to, pl.ds(low, block), :] = part[
                            k * block : (k + 1) * block, u * UNIT : (u + 1) * UNIT
                        ]

        if rows > D:
            for c, wide in steps:

                def by_rows(m, carry, c=c, wide=wide, unit=unit):
                    unit(m, c, wide)
                    return carry

                lax.fori_loop(0, rows // D, by_rows, 0)
        elif half % D == 0 and half > D:

            def by_columns(c, carry, unit=unit):
                unit(0, c * D, D)
                return carry

            lax.fori_loop(0, half // D, by_columns, 0)
        else:
            for c, wide in steps:
                unit(0, c, wide)
    if packed is not None:
        pack_small(refs[at_ref : at_ref + 4], kept_ref, sent_ref, packed, me, core, count)
        at_ref += 4
    if held:
        for ref, out in zip(refs[at_ref : at_ref + 2], (kept_ref, sent_ref)):
            out[:, :held, :] = ref[...]


def pack_small(small_refs, kept_ref, sent_ref, low, me, core, count):
    own, middle, value_bias, wide = small_refs
    order = [own[0:4], value_bias[0:1], middle[3:4], middle[0:1], own[4:5], middle[4:5]]
    order += [middle[1:2], own[5:6], middle[5:6], middle[2:3], jnp.zeros((3, D), F32)]
    narrow = jnp.concatenate(order, axis=0)
    share = D // count
    broad = wide.shape[1] // count
    for r in range(count):
        first = narrow[:, r * share : (r + 1) * share]
        first = jnp.concatenate([first, jnp.zeros((RANK_ROWS, UNIT - share), F32)], axis=1)
        second = wide[:, r * broad : (r + 1) * broad]
        second = jnp.concatenate([second, jnp.zeros((1, UNIT - broad), F32)], axis=1)
        second = jnp.broadcast_to(second, (RANK_ROWS, UNIT))
        here = slice(low, low + RANK_ROWS)
        kept_ref[me ^ r, here, :] = jnp.where(core == 0, first, second).astype(LOW)
        sent_ref[me ^ r, here, :] = jnp.where(core == 0, second, first).astype(LOW)


def total_of(*refs):
    return functools.reduce(jnp.add, [ref[...].astype(F32) for ref in refs])


def split_kernel(x, kept_ref, come_ref, *refs):
    far, outs = ((), refs) if x else (refs[:2], refs[2:])
    half = kept_ref.shape[3] // 2
    for z in range(4):
        for g in range(2):
            at = (z, slice(None), x, slice(0, half)) if g == 0 else (z, x, slice(None), slice(half, 2 * half))
            total = kept_ref[at].astype(F32) + come_ref[at].astype(F32)
            if far:
                total = total + far[g][z].astype(F32)
                for i in range(2):
                    outs[2 * g + i][z] = total[i].astype(LOW)
            else:
                outs[g][z] = total.astype(LOW)


def join_kernel(a_keep, a_come, b_keep, b_come, *outs):
    rows = a_keep.shape[1]
    for z, out in enumerate(outs):
        out[:rows] = total_of(a_keep.at[z], a_come.at[z]).astype(LOW)
        out[rows:] = total_of(b_keep.at[z], b_come.at[z]).astype(LOW)


def sum_kernel(*refs):
    refs[-1][...] = total_of(*refs[:-1]).astype(LOW)


def spread_kernel(plan, count, packed, place_ref, own_ref, other_ref, *outs):
    core = place_ref[1]
    for (rows, columns, at), out in zip(plan, outs):
        block = rows // count
        half = columns // 2
        for c in range(half // UNIT):
            low = at + c * block
            for value, mine in ((own_ref, core), (other_ref, 1 - core)):
                start = pl.multiple_of(mine * half + c * UNIT, SLAB)
                out[:, pl.ds(start, UNIT)] = value[low : low + block].astype(F32)
    if packed is not None:
        here = slice(packed, packed + RANK_ROWS)
        own, other = own_ref[here].astype(F32), other_ref[here].astype(F32)
        narrow, wide = jnp.where(core == 0, own, other), jnp.where(core == 0, other, own)
        biases_ref, wide_ref, gain_ref, shift_ref = outs[len(plan) :]
        share = biases_ref.shape[1]
        biases_ref[...] = narrow[0:7, :share]
        gain_ref[...] = narrow[7:10, :share]
        shift_ref[...] = narrow[10:13, :share]
        wide_ref[...] = wide[0:1, : wide_ref.shape[1]]


def swap(v, bits):
    count = lax.axis_size("store")
    return lax.ppermute(v, "store", [(i, i ^ bits) for i in range(count)])


def swap_core(v):
    return lax.ppermute(v, "dp", [(0, 1), (1, 0)])


class WeightSums:
    def __init__(self, place, count, rows):
        self.place, self.count, self.rows = place, count, rows
        self.plan, self.packed, self.at = [], None, 0
        self.buffers = ()

    def add(self, products, small=None, earlier=(), flops=0):
        plan, base, packed = [], self.at, None
        for pairs in products:
            rows, columns = pairs[0][0].shape[1], pairs[0][1].shape[1]
            plan.append((len(pairs), rows, columns, self.at))
            self.plan.append((rows, columns, self.at))
            self.at += rows // self.count * (columns // 2 // UNIT)
        args = [v for pairs in products for pair in pairs for v in pair]
        if small is not None:
            packed = self.packed = self.at
            self.at += RANK_ROWS
            args.extend(small)
        shape = (self.count, self.rows, UNIT)
        self.buffers = call(
            functools.partial(weight_grad_kernel, tuple(plan), self.count, packed, base),
            [(shape, LOW), (shape, LOW)],
            n_smem=1,
            earlier=earlier,
            flops=flops,
        )(self.place, *args, *self.buffers)
        return self.buffers

    def split(self, x, far=(), earlier=()):
        half = (4, 2, self.rows // 2, UNIT)
        outs = [half[:1] + half[2:]] * 4 if far else [half] * 2
        args = [v.reshape(4, 2, 2, self.rows, UNIT) for v in (self.kept, self.come)] + list(far)
        return call(
            functools.partial(split_kernel, x),
            [(shape, LOW) for shape in outs],
            earlier=earlier,
            limit=SMALL_LIMIT,
        )(*args)

    def start(self, earlier=()):
        self.kept, sent = self.buffers
        self.come = swap_core(sent)
        self.sent = self.split(1, earlier=earlier)
        return self.sent

    def first(self, *earlier):
        come = (swap(self.sent[0], 1), swap(self.sent[1], 2))
        a_keep, a_send, b_keep, b_send = self.split(0, come, earlier)
        self.kept, self.sent = (a_keep, b_keep), (a_send, b_send)
        return self.sent

    def second(self, *earlier):
        come = (swap(self.sent[0], 2), swap(self.sent[1], 1))
        self.w = call(
            join_kernel, [((self.rows, UNIT), LOW)] * 4, earlier=earlier, limit=SMALL_LIMIT
        )(self.kept[0], come[0], self.kept[1], come[1])
        return self.w

    def third(self, *earlier):
        come = [swap(self.w[k], 4 * k) for k in (1, 2, 3)]
        (self.own,) = call(
            sum_kernel, [(come[0].shape, LOW)], earlier=earlier, limit=SMALL_LIMIT
        )(self.w[0], *come)
        return self.own

    def finish(self, small=()):
        other = swap_core(self.own)
        shapes = [((rows // self.count, columns), F32) for rows, columns, _ in self.plan]
        shapes += [(shape, F32) for shape in small]
        return call(
            functools.partial(spread_kernel, tuple(self.plan), self.count, self.packed),
            shapes,
            n_smem=1,
            limit=SMALL_LIMIT,
        )(self.place, self.own, other)


def local_tree(
    inputs,
    doc_lengths,
    datastore,
    kept_mask,
    retrieved,
    self_project,
    self_output,
    cross_query,
    cross_memory,
    cross_output,
    expand_weight,
    contract_weight,
    biases,
    expand_bias,
    norm_gain,
    norm_shift,
    cotangent,
):
    tokens = inputs.shape[0]
    count = lax.axis_size("store")
    local_blocks = datastore.shape[0] // BLOCK
    all_blocks = local_blocks * count
    capacity = 2 * tokens * TOPB // all_blocks
    plane_blocks = 4 * local_blocks
    rows_in = 4 * capacity
    hidden = expand_weight.shape[1]
    me = lax.axis_index("store").astype(jnp.int32)
    core = lax.axis_index("dp").astype(jnp.int32)
    place = jnp.stack([me, core])

    piece = ((2 * BLOCK + RANK_ROWS, D), LOW)
    a0, b0 = call(piece_kernel, [piece] * 2)(datastore, kept_mask.reshape(local_blocks, BLOCK))
    a1, b1 = swap(a0, 1), swap(b0, 2)
    heads_all, soft_self, attended, unit_first, scale_first, first_low, *queries = call(
        self_forward_kernel,
        [
            ((tokens, 3 * D), LOW),
            ((PAIRS, 2 * tokens, tokens), F32),
            ((tokens, D), LOW),
            ((tokens, D), F32),
            ((tokens, 1), F32),
            ((tokens, D), LOW),
        ]
        + [((tokens + RANK_ROWS, D), LOW)] * 4,
        scratch=[
            pltpu.VMEM((D, 3 * D), LOW),
            pltpu.VMEM((D, D), LOW),
            pltpu.VMEM((D, D), LOW),
            pltpu.SemaphoreType.DMA((5,)),
        ],
        n_smem=2,
        far_in=(4, 5, 6),
        flops=8 * MICROSECOND,
    )(
        doc_lengths,
        place,
        inputs,
        retrieved.T,
        self_project,
        self_output,
        cross_query,
        biases,
        norm_gain,
        norm_shift,
    )
    pair = call(pair_kernel, [((2, *piece[0]), LOW)], earlier=(first_low,))
    ay, bx = swap(pair(a0, a1)[0], 2), swap(pair(b0, b1)[0], 1)
    queries = [queries[0]] + [swap(queries[k], 4 * k) for k in (1, 2, 3)]

    def of_blocks(blocks):
        return [
            ((blocks, BLOCK, 2 * D), LOW),
            ((blocks, 1, BLOCK), F32),
            ((blocks, BLOCK, SLAB), LOW),
        ]

    near = call(memory_kernel, of_blocks(4) * 2)(a0, a1, b0, b1, cross_memory, biases)
    memory, hidden_rows, key_side, stored = call(
        memory_kernel,
        of_blocks(plane_blocks) + [((plane_blocks * BLOCK, D), LOW)],
        scratch=[pltpu.SemaphoreType.DMA((8,))],
        far_out=(3,),
    )(ay, bx, a0, a1, b0, b1, cross_memory, biases, *near)

    slots, values, lses, inverses, sel = call(
        functools.partial(owner_forward_kernel, capacity),
        [
            ((plane_blocks, rows_in, D), LOW),
            ((plane_blocks, rows_in, D), F32),
            ((plane_blocks, rows_in, SLAB), F32),
            ((plane_blocks, rows_in, SLAB), F32),
            ((4, plane_blocks * capacity, tokens), LOW),
        ],
        scratch=[
            pltpu.VMEM((RANK_ROWS, tokens), F32),
            pltpu.VMEM((plane_blocks, rows_in, D), LOW),
            pltpu.SemaphoreType.DMA((1,)),
        ],
        far_out=(0,),
        flops=20 * MICROSECOND,
    )(*queries, memory, hidden_rows)
    payload = ((tokens + LSE_ROWS, D), LOW)
    payloads = call(functools.partial(merge_kernel, capacity, (1, 2, 3)), [payload] * 3)(
        values, lses, inverses, sel
    )
    payloads = (
        call(
            functools.partial(merge_kernel, capacity, (0,)), [payload], earlier=(payloads[0],)
        )(values, lses, inverses, sel)
        + payloads
    )
    parts = [payloads[0]] + [swap(payloads[k], 4 * k) for k in (1, 2, 3)]

    (
        outputs,
        merged_low,
        second_low,
        active_low,
        branch_grad,
        expanded_grad,
        cross_grad,
        second_resid,
        payload,
        small_middle,
        wide_bias,
    ) = call(
        middle_kernel,
        [
            ((tokens, D), LOW),
            ((tokens, D), LOW),
            ((tokens, D), LOW),
            ((tokens, hidden), LOW),
            ((tokens, D), LOW),
            ((tokens, hidden), LOW),
            ((tokens, D), LOW),
            ((tokens, D), F32),
            ((tokens + SIDE_ROWS, D), LOW),
            ((8, D), F32),
            ((1, hidden), F32),
        ],
        scratch=[
            pltpu.VMEM((tokens, hidden), F32),
        ],
        flops=12 * MICROSECOND,
    )(
        *parts,
        first_low,
        cotangent,
        cross_output,
        expand_weight,
        contract_weight,
        biases,
        expand_bias.reshape(1, hidden),
        norm_gain,
        norm_shift,
    )
    grads = [payload] + [swap(payload, 4 * k) for k in (1, 2, 3)]

    early = WeightSums(place, count, 432)
    early.add(
        [[(active_low, branch_grad)], [(merged_low, cross_grad)], [(second_low, expanded_grad)]],
        flops=8 * MICROSECOND,
    )
    early_start = early.start()

    (got,) = call(
        functools.partial(select_grads_kernel, capacity),
        [((plane_blocks, rows_in, D + SLAB), LOW)],
        flops=4 * LONG,
    )(sel, *grads)
    out = call(
        functools.partial(owner_backward_kernel, capacity),
        [((plane_blocks, BLOCK, 2 * D), LOW)] + [((tokens, D), LOW)] * 4,
        scratch=[pltpu.VMEM((plane_blocks, rows_in, D), LOW)],
        earlier=early_start,
        flops=LONG,
    )(sel, got, memory, key_side, slots)
    memory_grad, query_grads = out[0], out[1:5]
    parts = [query_grads[0]] + [swap(query_grads[k], 4 * k) for k in (1, 2, 3)]

    late = WeightSums(place, count, 352)
    flat_grad = memory_grad.reshape(plane_blocks * BLOCK, 2 * D)
    *late.buffers, value_bias_grad = call(
        functools.partial(memory_weight_kernel, count),
        [((count, 2 * D // count, UNIT), LOW)] * 2 + [((8, D), F32)],
        scratch=[pltpu.VMEM((2, D, D), F32)],
        n_smem=1,
        flops=MICROSECOND // 10,
    )(place, flat_grad, stored)
    early_first = early.first(late.buffers[0])
    late.plan, late.at = [(D, 2 * D, 0)], 2 * D // count

    pre_grad, self_branch_grad, project_grad, input_grad, small_self = call(
        self_backward_kernel,
        [
            ((tokens, D), LOW),
            ((tokens, D), LOW),
            ((tokens, 3 * D), LOW),
            ((tokens, D), F32),
            ((8, D), F32),
        ],
        scratch=[
            pltpu.VMEM((tokens, D), LOW),
        ],
        earlier=early_first,
        flops=LONG // 3,
    )(
        *parts,
        second_resid,
        unit_first,
        scale_first,
        heads_all,
        soft_self,
        cross_query,
        self_output,
        self_project,
        norm_gain,
    )
    early_second = early.second()
    late.add(
        [[(attended, self_branch_grad)], [(first_low, pre_grad)], [(inputs, project_grad)]],
        (small_self, small_middle, value_bias_grad, wide_bias),
        flops=MICROSECOND // 10,
    )
    near_a0, near_a1, far_a, near_b0, near_b1, far_b = call(
        datastore_grad_kernel,
        [((2 * BLOCK, D), LOW), ((2 * BLOCK, D), LOW), ((4 * BLOCK, D), LOW)] * 2,
        earlier=(late.buffers[0], early_second[0]),
        flops=4 * LONG,
    )(cross_memory, flat_grad)
    late.start(earlier=(far_a,))
    late_first = late.first()
    early.third(late_first[0])
    contract_weight_grad, cross_output_grad, expand_weight_grad = early.finish()
    late.second(contract_weight_grad)
    far_a, far_b = (after(v, late.w[0]) for v in (far_a, far_b))
    come_a, come_b = swap(far_a, 2), swap(far_b, 1)
    quarter = (2 * BLOCK, D)
    send_a, send_b, keep_a, keep_b = call(
        datastore_step_kernel, [(quarter, LOW)] * 2 + [(quarter, F32)] * 2, limit=SMALL_LIMIT
    )(near_a0, near_a1, come_a, near_b0, near_b1, come_b)
    (datastore_grad,) = call(
        datastore_sum_kernel, [((4 * BLOCK, D), F32)], limit=SMALL_LIMIT
    )(keep_a, swap(send_a, 1), keep_b, swap(send_b, 2))
    late.third(send_a)
    share = D // count
    (
        cross_memory_grad,
        self_output_grad,
        cross_query_grad,
        self_project_grad,
        biases_grad,
        wide_grad,
        gain_grad,
        shift_grad,
    ) = late.finish([(7, share), (1, hidden // count), (3, share), (3, share)])
    return (
        outputs,
        input_grad,
        datastore_grad,
        self_project_grad,
        self_output_grad,
        cross_query_grad,
        cross_memory_grad,
        cross_output_grad,
        expand_weight_grad,
        contract_weight_grad,
        biases_grad,
        wide_grad.reshape(hidden // count),
        gain_grad,
        shift_grad,
    )


def layer_norm(residual, gain_row, shift_row):
    center = residual - jnp.mean(residual, axis=-1, keepdims=True)
    spread = jnp.mean(center * center, axis=-1, keepdims=True)
    return center * lax.rsqrt(spread + EPSILON) * gain_row + shift_row


def doc_mask(lengths, seq_tokens):
    upto = jnp.tri(lengths.shape[-1], dtype=jnp.int32)
    bounds = jnp.sum(lengths[..., None, :] * upto, axis=-1)
    places = jnp.arange(seq_tokens, dtype=jnp.int32)
    segment = jnp.sum((places[:, None] >= bounds[..., None, :]).astype(jnp.int32), axis=-1)
    causal = places[:, None] >= places[None, :]
    return (segment[..., :, None] == segment[..., None, :]) & causal


def slot_numbers(picks, capacity):
    flat_ids = picks.reshape(-1)
    sorter = jnp.argsort(flat_ids, stable=True)
    sorted_ids = flat_ids[sorter]
    first_seen = jnp.searchsorted(sorted_ids, sorted_ids, side="left")
    rank_sorted = jnp.arange(flat_ids.shape[0], dtype=jnp.int32) - first_seen
    ranks = jnp.zeros_like(flat_ids).at[sorter].set(rank_sorted)
    return flat_ids * capacity + ranks


def place_rows(rows, slot_ids, total_slots, store_count, local_blocks, capacity):
    placed = jnp.zeros((total_slots, rows.shape[1]), rows.dtype).at[slot_ids].set(rows)
    return placed.reshape(store_count, local_blocks, capacity, rows.shape[1])


def local_slots(
    inputs,
    doc_lengths,
    datastore,
    kept_mask,
    retrieved,
    self_project,
    self_output,
    cross_query,
    cross_memory,
    cross_output,
    expand_weight,
    contract_weight,
    biases,
    expand_bias,
    norm_gain,
    norm_shift,
    cotangent,
):
    tok_count = inputs.shape[0]
    store_count = lax.axis_size("store")
    local_blocks = datastore.shape[0] // BLOCK
    all_blocks = local_blocks * store_count
    capacity = 2 * tok_count * TOPB // all_blocks
    rows_in = store_count * capacity
    total_slots = all_blocks * capacity
    gain_rows = norm_gain.astype(jnp.float32)
    shift_rows = norm_shift.astype(jnp.float32)
    bias_rows = biases.astype(jnp.float32)
    projected = jnp.dot(inputs, self_project, preferred_element_type=jnp.float32)
    heads_all = jnp.concatenate(
        [
            QUERY_SCALE * (projected[:, :D] + bias_rows[0]),
            projected[:, D : 2 * D],
            projected[:, 2 * D :] + bias_rows[1],
        ],
        axis=1,
    ).astype(jnp.bfloat16)
    queries = heads_all[:, :D].reshape(tok_count, HEADS, HEAD_DIM)
    keys_self = heads_all[:, D : 2 * D].reshape(tok_count, HEADS, HEAD_DIM)
    values_self = heads_all[:, 2 * D :].reshape(tok_count, HEADS, HEAD_DIM)
    allowed = doc_mask(doc_lengths[0], tok_count)

    def self_scores():
        raw_scores = jnp.einsum(
            "qhd,khd->hqk", queries, keys_self, preferred_element_type=jnp.float32
        )
        return jnp.where(allowed[None], raw_scores, MASKED)

    scores = self_scores()
    self_lse = jax.nn.logsumexp(scores, axis=-1)
    soft_low = jnp.exp(scores - self_lse[..., None]).astype(jnp.bfloat16)
    attended = (
        jnp.einsum("hqk,khd->qhd", soft_low, values_self, preferred_element_type=jnp.float32)
        .reshape(tok_count, D)
        .astype(jnp.bfloat16)
    )
    self_branch = jnp.dot(attended, self_output, preferred_element_type=jnp.float32) + bias_rows[2]
    first_norm, first_back = jax.vjp(
        layer_norm, inputs.astype(jnp.float32) + self_branch, gain_rows[0], shift_rows[0]
    )
    first_low = first_norm.astype(jnp.bfloat16)
    cross_queries = (
        QUERY_SCALE
        * (jnp.dot(first_low, cross_query, preferred_element_type=jnp.float32) + bias_rows[3])
    ).astype(jnp.bfloat16)
    slot_ids = slot_numbers(retrieved, capacity)
    send_buffer = place_rows(
        jnp.repeat(cross_queries, TOPB, axis=0),
        slot_ids,
        total_slots,
        store_count,
        local_blocks,
        capacity,
    )
    arrived = lax.all_to_all(send_buffer, "store", split_axis=0, concat_axis=2, tiled=True)
    owner_queries = arrived[0].reshape(local_blocks, rows_in, HEADS, HEAD_DIM)
    memory_bias = jnp.concatenate([jnp.zeros((D,), jnp.float32), bias_rows[4]])
    memory_low = (
        jnp.dot(datastore, cross_memory, preferred_element_type=jnp.float32) + memory_bias
    ).astype(jnp.bfloat16)
    memory_blocks = memory_low.reshape(local_blocks, BLOCK, 2 * D)
    store_keys = memory_blocks[:, :, :D].reshape(local_blocks, BLOCK, HEADS, HEAD_DIM)
    store_values = memory_blocks[:, :, D:].reshape(local_blocks, BLOCK, HEADS, HEAD_DIM)
    kept_rows = kept_mask.reshape(local_blocks, BLOCK) > 0

    def block_scores(query_blocks):
        raw_scores = jnp.einsum(
            "bmhd,bkhd->bhmk", query_blocks, store_keys, preferred_element_type=jnp.float32
        )
        return jnp.where(kept_rows[:, None, None, :], raw_scores, MASKED)

    owner_scores = block_scores(owner_queries)
    owner_lse = jax.nn.logsumexp(owner_scores, axis=-1)
    owner_soft = jnp.exp(owner_scores - owner_lse[..., None]).astype(jnp.bfloat16)
    partial_value = jnp.einsum(
        "bhmk,bkhd->bmhd", owner_soft, store_values, preferred_element_type=jnp.float32
    ).reshape(local_blocks, rows_in, D)
    partial_lse = jnp.transpose(owner_lse, (0, 2, 1))
    returned, returned_lse = (
        lax.all_to_all(partial_value[None], "store", split_axis=2, concat_axis=0, tiled=True),
        lax.all_to_all(partial_lse[None], "store", split_axis=2, concat_axis=0, tiled=True),
    )
    picked = returned.reshape(total_slots, D)[slot_ids].reshape(tok_count, TOPB, HEADS, HEAD_DIM)
    picked_lse = returned_lse.reshape(total_slots, HEADS)[slot_ids].reshape(tok_count, TOPB, HEADS)
    overall = jax.nn.logsumexp(picked_lse, axis=1)
    mix_weights = jnp.exp(picked_lse - overall[:, None, :])
    merged = jnp.einsum(
        "tjh,tjhd->thd", mix_weights, picked, precision=lax.Precision.HIGHEST
    ).reshape(tok_count, D)
    merged_low = merged.astype(jnp.bfloat16)
    cross_branch = (
        jnp.dot(merged_low, cross_output, preferred_element_type=jnp.float32) + bias_rows[5]
    )
    second_norm, second_back = jax.vjp(
        layer_norm, first_low.astype(jnp.float32) + cross_branch, gain_rows[1], shift_rows[1]
    )
    second_low = second_norm.astype(jnp.bfloat16)
    expanded = jnp.dot(
        second_low, expand_weight, preferred_element_type=jnp.float32
    ) + expand_bias.astype(jnp.float32)
    activated, gelu_back = jax.vjp(
        lambda pre_act: jax.nn.gelu(pre_act, approximate=False), expanded
    )
    activated_low = activated.astype(jnp.bfloat16)
    ffn_branch = (
        jnp.dot(activated_low, contract_weight, preferred_element_type=jnp.float32) + bias_rows[6]
    )
    final_norm, final_back = jax.vjp(
        layer_norm, second_low.astype(jnp.float32) + ffn_branch, gain_rows[2], shift_rows[2]
    )
    outputs = final_norm.astype(jnp.bfloat16)
    final_resid, final_gain, final_shift = final_back(cotangent.astype(jnp.float32))
    ffn_branch_grad = final_resid.astype(jnp.bfloat16)
    contract_weight_grad = jnp.dot(
        activated_low.T, ffn_branch_grad, preferred_element_type=jnp.float32
    )
    activated_grad = jnp.dot(ffn_branch_grad, contract_weight.T, preferred_element_type=jnp.float32)
    (expanded_raw,) = gelu_back(activated_grad)
    expanded_grad = expanded_raw.astype(jnp.bfloat16)
    expand_weight_grad = jnp.dot(second_low.T, expanded_grad, preferred_element_type=jnp.float32)
    expand_bias_grad = jnp.sum(expanded_grad.astype(jnp.float32), axis=0)
    second_total = final_resid + jnp.dot(
        expanded_grad, expand_weight.T, preferred_element_type=jnp.float32
    )
    second_resid, second_gain, second_shift = second_back(second_total)
    cross_branch_grad = second_resid.astype(jnp.bfloat16)
    cross_output_grad = jnp.dot(merged_low.T, cross_branch_grad, preferred_element_type=jnp.float32)
    attended_grad = jnp.dot(
        cross_branch_grad, cross_output.T, preferred_element_type=jnp.float32
    ).astype(jnp.bfloat16)
    delta_rows = jnp.sum(
        attended_grad.reshape(tok_count, HEADS, HEAD_DIM).astype(jnp.float32)
        * merged.reshape(tok_count, HEADS, HEAD_DIM),
        axis=-1,
    )
    grad_buffer = place_rows(
        jnp.repeat(attended_grad, TOPB, axis=0),
        slot_ids,
        total_slots,
        store_count,
        local_blocks,
        capacity,
    )
    overall_buffer = place_rows(
        jnp.repeat(overall, TOPB, axis=0),
        slot_ids,
        total_slots,
        store_count,
        local_blocks,
        capacity,
    )
    delta_buffer = place_rows(
        jnp.repeat(delta_rows, TOPB, axis=0),
        slot_ids,
        total_slots,
        store_count,
        local_blocks,
        capacity,
    )
    arrived_grad = lax.all_to_all(grad_buffer, "store", split_axis=0, concat_axis=2, tiled=True)
    arrived_overall, arrived_delta = (
        lax.all_to_all(overall_buffer, "store", split_axis=0, concat_axis=2, tiled=True),
        lax.all_to_all(delta_buffer, "store", split_axis=0, concat_axis=2, tiled=True),
    )
    owner_grad = arrived_grad[0].reshape(local_blocks, rows_in, HEADS, HEAD_DIM)
    overall_heads = jnp.transpose(arrived_overall[0], (0, 2, 1))
    delta_heads = jnp.transpose(arrived_delta[0], (0, 2, 1))
    soft_again = jnp.exp(block_scores(owner_queries) - owner_lse[..., None])
    soft_again_low = soft_again.astype(jnp.bfloat16).astype(jnp.float32)
    weight_mix = jnp.exp(owner_lse - overall_heads)
    value_dots = jnp.einsum(
        "bmhd,bkhd->bhmk", owner_grad, store_values, preferred_element_type=jnp.float32
    )
    exact_sum = jnp.sum(soft_again * value_dots, axis=-1, keepdims=True)
    rounded_sum = jnp.sum(soft_again_low * value_dots, axis=-1, keepdims=True)
    score_grad = (
        weight_mix[..., None]
        * soft_again
        * (value_dots - exact_sum + rounded_sum - delta_heads[..., None])
    ).astype(jnp.bfloat16)
    query_grad = (
        jnp.einsum("bhmk,bkhd->bmhd", score_grad, store_keys, preferred_element_type=jnp.float32)
        .astype(jnp.bfloat16)
        .reshape(local_blocks, rows_in, D)
    )
    key_grad = jnp.einsum(
        "bhmk,bmhd->bkhd", score_grad, owner_queries, preferred_element_type=jnp.float32
    )
    weighted_soft = weight_mix[..., None] * soft_again_low
    value_grad = jnp.einsum(
        "bhmk,bmhd->bkhd",
        weighted_soft,
        owner_grad.astype(jnp.float32),
        precision=lax.Precision.HIGHEST,
    )
    row_count = local_blocks * BLOCK
    memory_grad = jnp.concatenate(
        [key_grad.reshape(row_count, D), value_grad.reshape(row_count, D)], axis=1
    ).astype(jnp.bfloat16)
    cross_memory_grad = jnp.dot(datastore.T, memory_grad, preferred_element_type=jnp.float32)
    value_bias_grad = jnp.sum(memory_grad[:, D:].astype(jnp.float32), axis=0)
    datastore_grad = jnp.dot(memory_grad, cross_memory.T, preferred_element_type=jnp.float32)
    returned_grad = lax.all_to_all(
        query_grad[None], "store", split_axis=2, concat_axis=0, tiled=True
    )
    per_pick = returned_grad.reshape(total_slots, D)[slot_ids].reshape(tok_count, TOPB, D)
    query_sum = jnp.sum(per_pick.astype(jnp.float32), axis=1).astype(jnp.bfloat16)
    cross_pre_grad = (query_sum.astype(jnp.float32) * QUERY_SCALE).astype(jnp.bfloat16)
    cross_query_grad = jnp.dot(first_low.T, cross_pre_grad, preferred_element_type=jnp.float32)
    first_total = second_resid + jnp.dot(
        cross_pre_grad, cross_query.T, preferred_element_type=jnp.float32
    )
    first_resid, first_gain, first_shift = first_back(first_total)
    self_branch_grad = first_resid.astype(jnp.bfloat16)
    self_output_grad = jnp.dot(attended.T, self_branch_grad, preferred_element_type=jnp.float32)
    self_attended_grad = (
        jnp.dot(self_branch_grad, self_output.T, preferred_element_type=jnp.float32)
        .astype(jnp.bfloat16)
        .reshape(tok_count, HEADS, HEAD_DIM)
    )
    soft_self = jnp.exp(self_scores() - self_lse[..., None])
    soft_dots = jnp.einsum(
        "qhd,khd->hqk", self_attended_grad, values_self, preferred_element_type=jnp.float32
    )
    self_score_grad = (
        soft_self * (soft_dots - jnp.sum(soft_self * soft_dots, axis=-1, keepdims=True))
    ).astype(jnp.bfloat16)
    query_self_grad = jnp.einsum(
        "hqk,khd->qhd", self_score_grad, keys_self, preferred_element_type=jnp.float32
    ).reshape(tok_count, D)
    key_self_grad = jnp.einsum(
        "hqk,qhd->khd", self_score_grad, queries, preferred_element_type=jnp.float32
    ).reshape(tok_count, D)
    value_self_grad = jnp.einsum(
        "hqk,qhd->khd", soft_low, self_attended_grad, preferred_element_type=jnp.float32
    ).reshape(tok_count, D)
    heads_grad = jnp.concatenate([query_self_grad, key_self_grad, value_self_grad], axis=1).astype(
        jnp.bfloat16
    )
    project_grad = jnp.concatenate(
        [
            (heads_grad[:, :D].astype(jnp.float32) * QUERY_SCALE).astype(jnp.bfloat16),
            heads_grad[:, D:],
        ],
        axis=1,
    )
    self_project_grad = jnp.dot(inputs.T, project_grad, preferred_element_type=jnp.float32)
    input_grad = first_resid + jnp.dot(
        project_grad, self_project.T, preferred_element_type=jnp.float32
    )
    biases_grad = jnp.stack(
        [
            jnp.sum(project_grad[:, :D].astype(jnp.float32), axis=0),
            jnp.sum(project_grad[:, 2 * D :].astype(jnp.float32), axis=0),
            jnp.sum(self_branch_grad.astype(jnp.float32), axis=0),
            jnp.sum(cross_pre_grad.astype(jnp.float32), axis=0),
            value_bias_grad,
            jnp.sum(cross_branch_grad.astype(jnp.float32), axis=0),
            jnp.sum(ffn_branch_grad.astype(jnp.float32), axis=0),
        ]
    )
    gain_grad = jnp.stack([first_gain, second_gain, final_gain])
    shift_grad = jnp.stack([first_shift, second_shift, final_shift])
    shared = (
        lax.psum_scatter(self_project_grad, "store", scatter_dimension=0, tiled=True),
        lax.psum_scatter(self_output_grad, "store", scatter_dimension=0, tiled=True),
        lax.psum_scatter(cross_query_grad, "store", scatter_dimension=0, tiled=True),
        lax.psum_scatter(cross_memory_grad, "store", scatter_dimension=0, tiled=True),
        lax.psum_scatter(cross_output_grad, "store", scatter_dimension=0, tiled=True),
        lax.psum_scatter(expand_weight_grad, "store", scatter_dimension=0, tiled=True),
        lax.psum_scatter(contract_weight_grad, "store", scatter_dimension=0, tiled=True),
        lax.psum_scatter(biases_grad, "store", scatter_dimension=1, tiled=True),
        lax.psum_scatter(expand_bias_grad, "store", scatter_dimension=0, tiled=True),
        lax.psum_scatter(gain_grad, "store", scatter_dimension=1, tiled=True),
        lax.psum_scatter(shift_grad, "store", scatter_dimension=1, tiled=True),
    )
    reduced = (
        lax.psum(shared[0].astype(jnp.bfloat16), "dp").astype(jnp.float32),
        lax.psum(shared[1].astype(jnp.bfloat16), "dp").astype(jnp.float32),
        lax.psum(shared[2].astype(jnp.bfloat16), "dp").astype(jnp.float32),
        lax.psum(shared[3].astype(jnp.bfloat16), "dp").astype(jnp.float32),
        lax.psum(shared[4].astype(jnp.bfloat16), "dp").astype(jnp.float32),
        lax.psum(shared[5].astype(jnp.bfloat16), "dp").astype(jnp.float32),
        lax.psum(shared[6].astype(jnp.bfloat16), "dp").astype(jnp.float32),
        lax.psum(shared[7].astype(jnp.bfloat16), "dp").astype(jnp.float32),
        lax.psum(shared[8].astype(jnp.bfloat16), "dp").astype(jnp.float32),
        lax.psum(shared[9].astype(jnp.bfloat16), "dp").astype(jnp.float32),
        lax.psum(shared[10].astype(jnp.bfloat16), "dp").astype(jnp.float32),
    )
    return (
        outputs,
        input_grad,
        datastore_grad,
        reduced[0],
        reduced[1],
        reduced[2],
        reduced[3],
        reduced[4],
        reduced[5],
        reduced[6],
        reduced[7],
        reduced[8],
        reduced[9],
        reduced[10],
    )


def solution(mesh):
    placed = (
        P(("dp", "store"), None),
        P(("dp", "store"), None),
        P(("dp", "store"), None),
        P(("dp", "store")),
        P(("dp", "store"), None),
        P(),
        P(),
        P(),
        P(),
        P(),
        P(),
        P(),
        P(),
        P(),
        P(),
        P(),
        P(("dp", "store"), None),
    )
    return jax.shard_map(
        local_tree if mesh.shape["store"] == 16 else local_slots,
        mesh=mesh,
        in_specs=placed,
        out_specs=(
            P(("dp", "store"), None),
            P(("dp", "store"), None),
            P(("dp", "store"), None),
            P("store", None),
            P("store", None),
            P("store", None),
            P("store", None),
            P("store", None),
            P("store", None),
            P("store", None),
            P(None, "store"),
            P("store"),
            P(None, "store"),
            P(None, "store"),
        ),
        check_vma=False,
    )
```

```python
import functools

import jax
import jax.numpy as jnp
from jax import lax
from jax.experimental import pallas as pl
from jax.experimental.pallas import tpu as pltpu
from jax.sharding import PartitionSpec as P

D = 768
HEADS = 12
HEAD_DIM = 64
TOPB = 8
BLOCK = 128
SLAB = 128
PAIRS = D // SLAB
UNIT = 384
LSE_ROWS = 8
SIDE_ROWS = 16
RANK_ROWS = 16

EPSILON = 1e-05
MASKED = -1e30
QUERY_SCALE = 0.125
VMEM_LIMIT = 16 * 1024 * 1024
SMALL_LIMIT = 16 * 1024 * 1024
LONG = 30_000_000_000
UNROLL = 4
MICROSECOND = 50_000_000
LOW = jnp.bfloat16
F32 = jnp.float32

_VMEM = pl.BlockSpec(memory_space=pltpu.VMEM)
_SMEM = pl.BlockSpec(memory_space=pltpu.SMEM)
_ANY = pl.BlockSpec(memory_space=pl.ANY)


def nn(a, b):
    return lax.dot_general(a, b, (((1,), (0,)), ((), ())), preferred_element_type=F32)


def nt(a, b):
    return lax.dot_general(a, b, (((1,), (1,)), ((), ())), preferred_element_type=F32)


def tn(a, b):
    return lax.dot_general(a, b, (((0,), (0,)), ((), ())), preferred_element_type=F32)


def three(v):
    high = v.astype(LOW)
    rest = v - high.astype(F32)
    mid = rest.astype(LOW)
    return high, mid, (rest - mid.astype(F32)).astype(LOW)


def lanes(shape):
    return lax.broadcasted_iota(jnp.int32, shape, len(shape) - 1)


def rows_of(shape):
    return lax.broadcasted_iota(jnp.int32, shape, len(shape) - 2)


def flag(condition):
    return jnp.where(condition, 1.0, 0.0)


def half_masks():
    first = flag(lanes((1, SLAB)) < HEAD_DIM)
    return first.astype(LOW), (1.0 - first).astype(LOW)


def two_heads(slab, first, second):
    return jnp.concatenate([slab * first, slab * second], axis=0)


def join_heads(stacked, count):
    left = lanes((count, SLAB)) < HEAD_DIM
    return jnp.where(left, stacked[:count], stacked[count:])


def norm_forward(residual, gain, shift):
    center = residual - jnp.mean(residual, axis=-1, keepdims=True)
    spread = jnp.mean(center * center, axis=-1, keepdims=True)
    scale = lax.rsqrt(spread + EPSILON)
    unit = center * scale
    return unit * gain + shift, unit, scale


def norm_backward(grad, unit, scale, gain):
    inner = grad * gain
    down = inner - jnp.mean(inner, axis=-1, keepdims=True)
    down = down - unit * jnp.mean(inner * unit, axis=-1, keepdims=True)
    return scale * down


def row_sum(v):
    return jnp.sum(v, axis=0, keepdims=True)


def call(
    kernel,
    outs,
    scratch=(),
    n_smem=0,
    far_in=(),
    far_out=(),
    earlier=(),
    aliases=None,
    flops=0,
    limit=VMEM_LIMIT,
    pinned=(),
):
    def run(*args):
        count = len(args)

        def body(*refs):
            kernel(*refs[:count], *refs[count + len(earlier) :])

        args = [
            pltpu.with_memory_space_constraint(v, pltpu.HBM)
            if (i in far_in and not aliases) or i in pinned
            else v
            for i, v in enumerate(args)
        ]
        specs = [_ANY if i in far_in else _VMEM for i in range(n_smem, count)]
        return pl.pallas_call(
            body,
            out_shape=[
                pltpu.HBM(s, t) if i in far_out and not aliases else jax.ShapeDtypeStruct(s, t)
                for i, (s, t) in enumerate(outs)
            ],
            in_specs=[_SMEM] * n_smem + specs + [_ANY] * len(earlier),
            out_specs=[_ANY if i in far_out else _VMEM for i in range(len(outs))],
            scratch_shapes=list(scratch),
            input_output_aliases=aliases or {},
            compiler_params=pltpu.CompilerParams(vmem_limit_bytes=limit),
            cost_estimate=pl.CostEstimate(flops=flops, bytes_accessed=0, transcendentals=0),
        )(*args, *earlier)

    return run


def copies(pairs, sems):
    return [pltpu.make_async_copy(a, b, sems.at[i]) for i, (a, b) in enumerate(pairs)]


def after(v, *earlier):
    return call(
        lambda *refs: None,
        [(v.shape, v.dtype)],
        far_in=(0,),
        far_out=(0,),
        earlier=earlier,
        aliases={0: 0},
        limit=1024 * 1024,
    )(v)[0]


def start_all(items):
    for item in items:
        item.start()


def wait_all(items):
    for item in items:
        item.wait()


def plane_ranks(picks_ref, me, k, tokens):
    i = rows_of((RANK_ROWS, tokens))
    group, chip, block = i // 4, (i // 2) % 2, i % 2
    apart = jnp.where(group < 2, 2 * group + chip, 2 * chip + group - 2)
    local = jnp.where(group < 2, block, 2 + block)
    plane = (me // 4) ^ k
    number = plane * 16 + ((me % 4) ^ apart) * 4 + local
    member = jnp.zeros((RANK_ROWS, tokens), F32)
    for j in range(TOPB):
        member = member + flag(picks_ref[j : j + 1, :] == number)
    earlier = flag(rows_of((tokens, tokens)) < lanes((tokens, tokens)))
    rank = nn(member.astype(LOW), earlier.astype(LOW))
    return jnp.where(member > 0.5, rank, -1.0).astype(LOW)


def self_forward_kernel(
    lengths_ref,
    place_ref,
    x_ref,
    picks_ref,
    project_ref,
    output_ref,
    query_ref,
    bias_ref,
    gain_ref,
    shift_ref,
    heads_ref,
    soft_ref,
    attended_ref,
    unit_ref,
    scale_ref,
    first_ref,
    *rest,
):
    payload_refs, (project_scr, output_scr, query_scr, sems) = rest[:4], rest[4:]
    thirds = [slice(i * D, (i + 1) * D) for i in range(3)]
    fetch = copies(
        [(project_ref.at[:, at], project_scr.at[:, at]) for at in thirds]
        + [(output_ref, output_scr), (query_ref, query_scr)],
        sems,
    )
    start_all(fetch)
    tokens = x_ref.shape[0]
    bias = bias_ref[...].astype(F32)
    x = x_ref[...]
    for i, at in enumerate(thirds):
        fetch[i].wait()
        part = nn(x, project_scr[:, at])
        if i == 0:
            part = QUERY_SCALE * (part + bias[0:1])
        if i == 2:
            part = part + bias[1:2]
        heads_ref[:, at] = part.astype(LOW)
    place_row = lax.broadcasted_iota(jnp.int32, (2 * tokens, tokens), 0) % tokens
    place_col = lanes((2 * tokens, tokens))
    segment_row = jnp.zeros((2 * tokens, tokens), jnp.int32)
    segment_col = jnp.zeros((2 * tokens, tokens), jnp.int32)
    bound = 0
    for d in range(lengths_ref.shape[1]):
        bound = bound + lengths_ref[0, d]
        segment_row = segment_row + jnp.where(place_row >= bound, 1, 0)
        segment_col = segment_col + jnp.where(place_col >= bound, 1, 0)
    allowed = (segment_row == segment_col) & (place_row >= place_col)
    first, second = half_masks()
    for p in range(PAIRS):
        at = p * SLAB
        queries = two_heads(heads_ref[:, at : at + SLAB], first, second)
        scores = nt(queries, heads_ref[:, D + at : D + at + SLAB])
        scores = jnp.where(allowed, scores, MASKED)
        top = jnp.max(scores, axis=-1, keepdims=True)
        raised = jnp.exp(scores - top)
        soft = raised / jnp.sum(raised, axis=-1, keepdims=True)
        soft_ref[p] = soft
        mixed = nn(soft.astype(LOW), heads_ref[:, 2 * D + at : 2 * D + at + SLAB])
        attended_ref[:, at : at + SLAB] = join_heads(mixed, tokens).astype(LOW)
    fetch[3].wait()
    residual = x.astype(F32) + nn(attended_ref[...], output_scr[...]) + bias[2:3]
    normed, unit, scale = norm_forward(
        residual, gain_ref[0:1, :].astype(F32), shift_ref[0:1, :].astype(F32)
    )
    unit_ref[...] = unit
    scale_ref[...] = scale
    low = normed.astype(LOW)
    first_ref[...] = low
    fetch[4].wait()
    queries = (QUERY_SCALE * (nn(low, query_scr[...]) + bias[3:4])).astype(LOW)
    for k, out in enumerate(payload_refs):
        out[:tokens] = queries
        out[tokens:, tokens:] = jnp.zeros((RANK_ROWS, D - tokens), LOW)
        out[tokens:, :tokens] = plane_ranks(picks_ref, place_ref[0], k, tokens)


def piece_kernel(rows_ref, kept_ref, a_ref, b_ref):
    for h, out in enumerate((a_ref, b_ref)):
        out[: 2 * BLOCK] = rows_ref[2 * h * BLOCK : 2 * (h + 1) * BLOCK]
        marks = kept_ref[2 * h : 2 * h + 2, :].astype(F32)
        marks = jnp.concatenate([marks, jnp.zeros((RANK_ROWS - 2, BLOCK), F32)], axis=0)
        out[2 * BLOCK :, :BLOCK] = marks.astype(LOW)
        out[2 * BLOCK :, BLOCK:] = jnp.zeros((RANK_ROWS, D - BLOCK), LOW)


def pair_kernel(first_ref, second_ref, out_ref):
    out_ref[0] = first_ref[...]
    out_ref[1] = second_ref[...]


def memory_kernel(*refs):
    far = len(refs) > 12
    if far:
        pieces = [ref.at[j] for ref in refs[:2] for j in range(2)]
        near_pieces, (weight_ref, bias_ref), given = refs[2:6], refs[6:8], refs[8:14]
        outs, rows_ref, sems = refs[14:17], refs[17], refs[18]
        size = 2 * BLOCK
        pairs = []
        for s in range(2):
            for j in range(2):
                at = 8 * s * BLOCK + j * size
                pairs.append((near_pieces[2 * s + j].at[:size], rows_ref.at[at : at + size]))
                at = at + 4 * BLOCK
                pairs.append((pieces[2 * s + j].at[:size], rows_ref.at[at : at + size]))
        keep = copies(pairs, sems)
        start_all(keep)
    else:
        pieces, (weight_ref, bias_ref), outs = refs[:4], refs[4:6], refs[6:]
    bias = bias_ref[4:5, :].astype(F32)
    lane = lanes((RANK_ROWS, SLAB))
    place = lanes((BLOCK, SLAB))
    for s in range(2):
        if far:
            near, here = 8 * s, 8 * s + 4
            memory_ref, hidden_ref, side_ref = outs
            for out, ref in zip(outs, given[3 * s : 3 * s + 3]):
                out[near : near + 4] = ref[...]
        else:
            here = 0
            memory_ref, hidden_ref, side_ref = outs[3 * s : 3 * s + 3]
        for j in range(2):
            piece = pieces[2 * s + j]
            rows = piece[: 2 * BLOCK]
            first = here + 2 * j
            keys = nn(rows, weight_ref[:, :D]).astype(LOW)
            values = (nn(rows, weight_ref[:, D:]) + bias).astype(LOW)
            marks = piece[2 * BLOCK :, :SLAB]
            for l in range(2):
                at = first + l
                memory_ref[at, :, :D] = keys[l * BLOCK : (l + 1) * BLOCK]
                memory_ref[at, :, D:] = values[l * BLOCK : (l + 1) * BLOCK]
                hidden_ref[at] = (1.0 - marks[l : l + 1].astype(F32)) * MASKED
                wanted = flag((rows_of((RANK_ROWS, SLAB)) == l) & (lane == SLAB - 1))
                column = tn(marks, wanted.astype(LOW))
                side = jnp.where(place == SLAB - 1, (1.0 - column) * MASKED, 0.0)
                side_ref[at] = jnp.where(place < 48, -1.0, side).astype(LOW)
    if far:
        wait_all(keep)


def selection(ranks, capacity):
    parts = []
    wanted = rows_of((capacity, ranks.shape[1])).astype(F32)
    for b in range(ranks.shape[0]):
        parts.append(flag(ranks[b : b + 1, :] == wanted).astype(LOW))
    return jnp.concatenate(parts, axis=0)


def fill_slots(sel, rows, out_ref, k, capacity):
    got = nn(sel, rows).astype(LOW)
    for b in range(out_ref.shape[0]):
        out_ref[b, k * capacity : (k + 1) * capacity, :] = got[b * capacity : (b + 1) * capacity]


def around16(v, combine):
    for step in (16, 32, 64):
        v = combine(v, pltpu.roll(v, step, 1))
    return v


def put_side(ref, side, rows):
    tokens = side.shape[0]
    turned = side.astype(F32).T.astype(LOW)
    for q in range(PAIRS):
        ref[tokens:, q * SLAB : (q + 1) * SLAB] = turned[q * rows : (q + 1) * rows]


def get_side(ref, tokens):
    rows = ref.shape[0] - tokens
    parts = [ref[tokens:, q * SLAB : (q + 1) * SLAB].astype(F32) for q in range(PAIRS)]
    parts.append(jnp.zeros((SLAB - PAIRS * rows, SLAB), F32))
    return jnp.concatenate(parts, axis=0).T


def lse_lanes(lse):
    high = lse.astype(LOW).astype(F32)
    rest = lse - high
    mid = rest.astype(LOW).astype(F32)
    low = rest - mid
    lane = lanes(lse.shape)
    packed = jnp.where(
        lane < 16, high, jnp.where(lane < 32, mid, jnp.where(lane < 48, low, 0.0))
    )
    return packed.astype(LOW)


def head_spread(group):
    row = rows_of((SLAB, D))
    row = row % 16 if group else row
    return flag(row == lanes((SLAB, D)) // HEAD_DIM).astype(LOW)


def owner_forward_kernel(capacity, *refs):
    tokens_refs, memory_ref, hidden_ref = refs[0:4], refs[4], refs[5]
    far_slots_ref, out_scr, lse_scr, inv_scr, sel_scr, ranks_scr, slots_ref, sems = refs[6:]
    sources = len(tokens_refs)
    blocks, rows = slots_ref.shape[:2]
    tokens = tokens_refs[0].shape[0] - RANK_ROWS
    first, second = half_masks()
    for k in range(sources):
        ranks_scr[...] = tokens_refs[k][tokens:, :tokens].astype(F32)
        sel = selection(ranks_scr[...], capacity)
        sel_scr[k] = sel
        fill_slots(sel, tokens_refs[k][:tokens], slots_ref, k, capacity)
    keep = copies([(slots_ref, far_slots_ref)], sems)
    start_all(keep)
    ones = jnp.ones((BLOCK, SLAB), LOW)
    lane_of = lanes((rows, SLAB))
    def one_block(i, carry):
        hidden = hidden_ref[i]
        tops = jnp.zeros((rows, SLAB), F32)
        totals = jnp.ones((rows, SLAB), F32)
        base = (i % 8) * 16
        slabs = [slice(p * SLAB, (p + 1) * SLAB) for p in range(PAIRS)]
        scores = [
            nt(two_heads(slots_ref[i, :, at], first, second), memory_ref[i, :, at])
            + hidden
            for at in slabs
        ]
        highest = [jnp.max(v, axis=-1, keepdims=True) for v in scores]
        raised = [jnp.exp(v - top).astype(LOW) for v, top in zip(scores, highest)]
        mixed = [
            nn(v, jnp.concatenate([memory_ref[i, :, D + at.start : D + at.stop], ones], axis=1))
            for v, at in zip(raised, slabs)
        ]
        for p, at in enumerate(slabs):
            out_scr[i, :, at] = join_heads(mixed[p][:, :SLAB], rows)
            for half in range(2):
                here = slice(half * rows, (half + 1) * rows)
                mine = lane_of == base + 2 * p + half
                tops = jnp.where(mine, highest[p][here], tops)
                totals = jnp.where(mine, mixed[p][here, SLAB:], totals)
        own = flag((lane_of >= base) & (lane_of < base + HEADS))
        lse_scr[i] = tops + jnp.log(totals)
        inv_scr[i] = own / totals
        return carry

    lax.fori_loop(0, blocks, one_block, 0, unroll=UNROLL)
    wait_all(keep)


def merge_kernel(capacity, ks, value_ref, lse_ref, inv_ref, sel_ref, *payload_refs):
    tokens = sel_ref.shape[2]
    group = 8 * capacity
    own_low = flag(
        rows_of((group, SLAB)) // capacity == lanes((group, SLAB)) // 16
    ).astype(LOW)
    spread = head_spread(True)
    each = [(n, g) for n in range(len(ks)) for g in range(2)]

    def stacked(ref, n, g):
        here = slice(ks[n] * capacity, (ks[n] + 1) * capacity)
        return jnp.concatenate([ref[8 * g + b, here, :] for b in range(8)], axis=0)

    sels = {(n, g): sel_ref[ks[n], g * group : (g + 1) * group, :] for n, g in each}
    turned = {at: sels[at].T for at in each}
    found = {
        at: nn(turned[at], jnp.concatenate([*three(stacked(lse_ref, *at)), own_low], axis=1))
        for at in each
    }
    members = {at: found[at][:, 3 * SLAB :] for at in each}
    by_token = {
        at: jnp.where(
            members[at] > 0.5,
            found[at][:, :SLAB] + found[at][:, SLAB : 2 * SLAB] + found[at][:, 2 * SLAB : 3 * SLAB],
            MASKED,
        )
        for at in each
    }
    tops = [
        around16(jnp.maximum(by_token[n, 0], by_token[n, 1]), jnp.maximum) for n in range(len(ks))
    ]
    weights = {at: members[at] * jnp.exp(by_token[at] - tops[at[0]]) for at in each}
    totals = [around16(weights[n, 0] + weights[n, 1], jnp.add) for n in range(len(ks))]
    safes = [jnp.where(total > 0.5, total, 1.0) for total in totals]
    shares = {
        at: nn(sels[at], (weights[at] / safes[at[0]]).astype(LOW)) * stacked(inv_ref, *at)
        for at in each
    }
    wide = {at: nn(shares[at].astype(LOW), spread) for at in each}
    for n, out in enumerate(payload_refs):
        partial = sum(
            nn(turned[n, g], (stacked(value_ref, n, g) * wide[n, g]).astype(LOW)) for g in range(2)
        )
        out[:tokens] = partial.astype(LOW)
        lse = jnp.where(totals[n] > 0.5, tops[n] + jnp.log(safes[n]), MASKED)
        put_side(out, lse_lanes(lse), LSE_ROWS)


def select_grads_kernel(capacity, *refs):
    sel_ref, grad_refs, got_ref = refs[0], refs[1:5], refs[5]
    tokens = grad_refs[0].shape[0] - SIDE_ROWS
    for k, ref in enumerate(grad_refs):
        side = get_side(ref, tokens).astype(LOW)
        rows_all = jnp.concatenate([ref[:tokens], side], axis=1)
        fill_slots(sel_ref[k], rows_all, got_ref, k, capacity)


def owner_backward_kernel(capacity, *refs):
    sel_scr, got_scr, memory_ref, side_ref, slots_ref = refs[:5]
    out, payload_refs, query_scr = refs[5], refs[6:10], refs[10]
    sources = len(payload_refs)
    blocks, rows = slots_ref.shape[:2]
    first, second = half_masks()
    lane = lanes((1, SLAB))
    last = flag(lane == SLAB - 1).astype(LOW)
    value_side = jnp.broadcast_to(
        -flag((lane >= 48) & (lane < 96)).astype(LOW), (BLOCK, SLAB)
    )

    def picked(head, base):
        inside = (lane >= base) & (lane < base + 48)
        return flag(inside & (lane % 16 == head)).astype(LOW)

    def one_block(i, carry):
        side = got_scr[i, :, D:]
        key_side = side_ref[i]
        slabs = [slice(p * SLAB, (p + 1) * SLAB) for p in range(PAIRS)]
        keys = [memory_ref[i, :, at] for at in slabs]
        queries = [two_heads(slots_ref[i, :, at], first, second) for at in slabs]
        grads = [two_heads(got_scr[i, :, at], first, second) for at in slabs]
        scores, dots = [], []
        for p in range(PAIRS):
            lse_side = jnp.concatenate(
                [side * picked(2 * p + h, 0) + last for h in range(2)], axis=0
            )
            scores.append(
                nt(
                    jnp.concatenate([keys[p], key_side], axis=1),
                    jnp.concatenate([queries[p], lse_side], axis=1),
                )
            )
        for p, at in enumerate(slabs):
            delta_side = jnp.concatenate(
                [side * picked(2 * p + h, 48) for h in range(2)], axis=0
            )
            values = memory_ref[i, :, D + at.start : D + at.stop]
            dots.append(
                nt(
                    jnp.concatenate([values, value_side], axis=1),
                    jnp.concatenate([grads[p], delta_side], axis=1),
                )
            )
        softs = [jnp.exp(v) for v in scores]
        score_grads = [(soft * v).astype(LOW) for soft, v in zip(softs, dots)]
        for p, at in enumerate(slabs):
            query_scr[i, :, at] = join_heads(tn(score_grads[p], keys[p]), rows).astype(LOW)
        for p, at in enumerate(slabs):
            out[i, :, at] = nn(score_grads[p], queries[p]).astype(LOW)
        for p, at in enumerate(slabs):
            out[i, :, D + at.start : D + at.stop] = nn(softs[p].astype(LOW), grads[p]).astype(
                LOW
            )
        return carry

    lax.fori_loop(0, blocks, one_block, 0, unroll=UNROLL)
    for k in range(sources):
        here = slice(k * capacity, (k + 1) * capacity)
        value = jnp.concatenate([query_scr[b, here, :] for b in range(blocks)], axis=0)
        payload_refs[k][...] = tn(sel_scr[k], value).astype(LOW)


def memory_weight_kernel(count, place_ref, *refs):
    grad_ref, rows_ref, kept_ref, sent_ref, bias_ref, sum_scr = refs
    me, core = place_ref[0], place_ref[1]
    size = 4 * BLOCK
    sum_scr[...] = jnp.zeros(sum_scr.shape, F32)
    bias_ref[...] = jnp.zeros(bias_ref.shape, F32)

    def one_set(s, carry):
        at = pl.ds(pl.multiple_of(s * size, size), size)
        rows = rows_ref[at, :].T
        for h in range(2):
            sum_scr[h] = sum_scr[h] + nn(rows, grad_ref[at, h * D : (h + 1) * D])
        bias_ref[0:1] = bias_ref[0:1] + row_sum(grad_ref[at, D:].astype(F32))
        return carry

    lax.fori_loop(0, rows_ref.shape[0] // size, one_set, 0)
    block = D // count
    for h in range(2):

        def store(out, h=h):
            total = sum_scr[h].astype(LOW)
            for k in range(count):
                for u in range(D // UNIT):
                    out[me ^ k, u * block : (u + 1) * block, :] = total[
                        k * block : (k + 1) * block, u * UNIT : (u + 1) * UNIT
                    ]

        pl.when(core == h)(functools.partial(store, kept_ref))
        pl.when(core != h)(functools.partial(store, sent_ref))


def datastore_grad_kernel(weight_ref, *refs):
    grad_ref, outs = refs[0], refs[1:7]
    weight = weight_ref[...].T
    near_a0, near_a1, far_a, near_b0, near_b1, far_b = outs
    groups = ((near_a0, near_a1), (far_a,), (near_b0, near_b1), (far_b,))
    for s in range(4):
        value = nn(grad_ref[4 * s * BLOCK : 4 * (s + 1) * BLOCK], weight).astype(LOW)
        size = value.shape[0] // len(groups[s])
        for i, out in enumerate(groups[s]):
            out[...] = value[i * size : (i + 1) * size]


def datastore_step_kernel(*refs):
    ins, sends, keeps = refs[:6], refs[6:8], refs[8:10]
    size = 2 * BLOCK
    for g in range(2):
        stay, go, come = ins[3 * g : 3 * g + 3]
        keeps[g][...] = stay[...].astype(F32) + come[:size].astype(F32)
        sends[g][...] = (go[...].astype(F32) + come[size:].astype(F32)).astype(LOW)


def datastore_sum_kernel(keep_a, come_a, keep_b, come_b, out_ref):
    size = keep_a.shape[0]
    out_ref[:size] = keep_a[...] + come_a[...].astype(F32)
    out_ref[size:] = keep_b[...] + come_b[...].astype(F32)


def middle_kernel(
    p0_ref,
    p1_ref,
    p2_ref,
    p3_ref,
    first_ref,
    cotangent_ref,
    output_ref,
    expand_ref,
    contract_ref,
    bias_ref,
    expand_bias_ref,
    gain_ref,
    shift_ref,
    out_ref,
    merged_ref,
    second_ref,
    active_ref,
    branch_grad_ref,
    expanded_grad_ref,
    cross_grad_ref,
    resid_ref,
    payload_ref,
    small_ref,
    wide_ref,
    expanded_scr,
):
    output_scr, expand_scr, contract_scr = output_ref, expand_ref, contract_ref
    bias = bias_ref[...].astype(F32)
    gain = gain_ref[...].astype(F32)
    shift = shift_ref[...].astype(F32)
    parts = [p0_ref, p1_ref, p2_ref, p3_ref]
    tokens = first_ref.shape[0]
    lses = [around16(get_side(part, tokens), jnp.add) for part in parts]
    top = functools.reduce(jnp.maximum, lses)
    weights = [jnp.exp(lse - top) for lse in lses]
    total = functools.reduce(jnp.add, weights)
    overall = top + jnp.log(total)
    spread = head_spread(False)
    merged = jnp.zeros(first_ref.shape, F32)
    for part, weight in zip(parts, weights):
        share = weight / total
        high = share.astype(LOW)
        rest = (share - high.astype(F32)).astype(LOW)
        merged = merged + (nn(high, spread) + nn(rest, spread)) * part[:tokens].astype(F32)
    merged_low = merged.astype(LOW)
    merged_ref[...] = merged_low
    residual = first_ref[...].astype(F32) + nn(merged_low, output_scr[...]) + bias[5:6]
    second, unit_second, scale_second = norm_forward(residual, gain[1:2], shift[1:2])
    second_low = second.astype(LOW)
    second_ref[...] = second_low
    hidden = contract_scr.shape[0]
    for c in range(hidden // D):
        at = slice(c * D, (c + 1) * D)
        expanded = nn(second_low, expand_scr[:, at]) + expand_bias_ref[:, at].astype(F32)
        bell = 0.5 * (1.0 + lax.erf(expanded * 0.7071067811865476))
        active_ref[:, at] = (expanded * bell).astype(LOW)
        slope = bell + expanded * 0.3989422804014327 * jnp.exp(-0.5 * expanded * expanded)
        expanded_scr[:, at] = slope
    residual = second_low.astype(F32) + nn(active_ref[...], contract_scr[...]) + bias[6:7]
    final, unit_final, scale_final = norm_forward(residual, gain[2:3], shift[2:3])
    out_ref[...] = final.astype(LOW)
    cotangent = cotangent_ref[...].astype(F32)
    final_resid = norm_backward(cotangent, unit_final, scale_final, gain[2:3])
    branch_grad = final_resid.astype(LOW)
    branch_grad_ref[...] = branch_grad
    small_ref[0:1, :] = row_sum(branch_grad.astype(F32))
    small_ref[1:2, :] = row_sum(cotangent * unit_final)
    small_ref[2:3, :] = row_sum(cotangent)
    total_grad = final_resid
    for c in range(hidden // D):
        at = slice(c * D, (c + 1) * D)
        active_grad = nt(branch_grad, contract_scr[at, :])
        expanded_grad = (active_grad * expanded_scr[:, at]).astype(LOW)
        expanded_grad_ref[:, at] = expanded_grad
        wide_ref[:, at] = row_sum(expanded_grad.astype(F32))
        total_grad = total_grad + nt(expanded_grad, expand_scr[:, at])
    small_ref[4:5, :] = row_sum(total_grad * unit_second)
    small_ref[5:6, :] = row_sum(total_grad)
    second_resid = norm_backward(total_grad, unit_second, scale_second, gain[1:2])
    resid_ref[...] = second_resid
    cross_grad = second_resid.astype(LOW)
    cross_grad_ref[...] = cross_grad
    small_ref[3:4, :] = row_sum(cross_grad.astype(F32))
    small_ref[6:8, :] = jnp.zeros((2, D), F32)
    attended_grad = nt(cross_grad, output_scr[...]).astype(LOW)
    payload_ref[:tokens] = attended_grad
    product = attended_grad.astype(F32) * merged
    gather = flag(lanes((D, SLAB)) % 16 == rows_of((D, SLAB)) // HEAD_DIM).astype(LOW)
    high, mid, low = three(product)
    delta = nn(high, gather) + nn(mid, gather) + nn(low, gather)
    lane = lanes(overall.shape)
    packed = jnp.zeros(overall.shape, F32)
    for value, base in ((overall, 0), (delta, 48)):
        for i, piece in enumerate(three(value)):
            inside = (lane >= base + 16 * i) & (lane < base + 16 * i + HEADS)
            packed = jnp.where(inside, piece.astype(F32), packed)
    put_side(payload_ref, packed, SIDE_ROWS)


def self_backward_kernel(
    d0_ref,
    d1_ref,
    d2_ref,
    d3_ref,
    resid_ref,
    unit_ref,
    scale_ref,
    heads_ref,
    soft_ref,
    query_ref,
    output_ref,
    project_ref,
    gain_ref,
    pre_grad_ref,
    branch_grad_ref,
    project_grad_ref,
    input_grad_ref,
    small_ref,
    attended_scr,
):
    query_scr, output_scr, heads_scr = query_ref, output_ref, heads_ref
    soft_scr, project_scr = soft_ref, project_ref
    tokens = resid_ref.shape[0]
    query_sum = functools.reduce(
        jnp.add, [d[...].astype(F32) for d in (d0_ref, d1_ref, d2_ref, d3_ref)]
    ).astype(LOW)
    pre_grad = (query_sum.astype(F32) * QUERY_SCALE).astype(LOW)
    pre_grad_ref[...] = pre_grad
    total = resid_ref[...] + nt(pre_grad, query_scr[...])
    unit = unit_ref[...]
    first_resid = norm_backward(total, unit, scale_ref[...], gain_ref[0:1, :].astype(F32))
    branch_grad = first_resid.astype(LOW)
    branch_grad_ref[...] = branch_grad
    attended_scr[...] = nt(branch_grad, output_scr[...]).astype(LOW)
    first, second = half_masks()
    for p in range(PAIRS):
        at = p * SLAB
        grads = two_heads(attended_scr[:, at : at + SLAB], first, second)
        queries = two_heads(heads_scr[:, at : at + SLAB], first, second)
        keys = heads_scr[:, D + at : D + at + SLAB]
        dots = nt(grads, heads_scr[:, 2 * D + at : 2 * D + at + SLAB])
        soft = soft_scr[p]
        score_grad = (soft * (dots - jnp.sum(soft * dots, axis=-1, keepdims=True))).astype(LOW)
        query_grad = join_heads(nn(score_grad, keys), tokens).astype(LOW)
        project_grad_ref[:, at : at + SLAB] = (query_grad.astype(F32) * QUERY_SCALE).astype(LOW)
        project_grad_ref[:, D + at : D + at + SLAB] = tn(score_grad, queries).astype(LOW)
        project_grad_ref[:, 2 * D + at : 2 * D + at + SLAB] = tn(soft.astype(LOW), grads).astype(
            LOW
        )
    input_grad_ref[...] = first_resid + nt(project_grad_ref[...], project_scr[...])
    small_ref[0:1, :] = row_sum(project_grad_ref[:, :D].astype(F32))
    small_ref[1:2, :] = row_sum(project_grad_ref[:, 2 * D :].astype(F32))
    small_ref[2:3, :] = row_sum(branch_grad.astype(F32))
    small_ref[3:4, :] = row_sum(pre_grad.astype(F32))
    small_ref[4:5, :] = row_sum(total * unit)
    small_ref[5:6, :] = row_sum(total)
    small_ref[6:8, :] = jnp.zeros((2, D), F32)


def weight_grad_kernel(plan, count, packed, held, place_ref, *refs):
    kept_ref, sent_ref = refs[-2:]
    me, core = place_ref[0], place_ref[1]
    at_ref = 0
    for number, rows, columns, at in plan:
        pairs = [refs[at_ref + 2 * i : at_ref + 2 * i + 2] for i in range(number)]
        at_ref += 2 * number
        block = rows // count
        half = columns // 2
        steps = [(c, min(D, half - c)) for c in range(0, half, D)]

        def unit(m, c, wide, block=block, half=half, at=at, pairs=pairs):
            xs = [x_ref[:, pl.ds(pl.multiple_of(m * D, SLAB), D)].T for x_ref, _ in pairs]
            for mine, out in ((core, kept_ref), (1 - core, sent_ref)):
                start = pl.multiple_of(mine * half + c, SLAB)
                part = sum(nn(x, g_ref[:, pl.ds(start, wide)]) for x, (_, g_ref) in zip(xs, pairs))
                part = part.astype(LOW)
                for u in range(wide // UNIT):
                    low = pl.multiple_of(at + (c // UNIT + u) * block, 16)
                    for k in range(D // block):
                        to = me ^ (m * (D // block) + k)
                        out[to, pl.ds(low, block), :] = part[
                            k * block : (k + 1) * block, u * UNIT : (u + 1) * UNIT
                        ]

        if rows > D:
            for c, wide in steps:

                def by_rows(m, carry, c=c, wide=wide, unit=unit):
                    unit(m, c, wide)
                    return carry

                lax.fori_loop(0, rows // D, by_rows, 0)
        elif half % D == 0 and half > D:

            def by_columns(c, carry, unit=unit):
                unit(0, c * D, D)
                return carry

            lax.fori_loop(0, half // D, by_columns, 0)
        else:
            for c, wide in steps:
                unit(0, c, wide)
    if packed is not None:
        pack_small(refs[at_ref : at_ref + 4], kept_ref, sent_ref, packed, me, core, count)
        at_ref += 4
    if held:
        for ref, out in zip(refs[at_ref : at_ref + 2], (kept_ref, sent_ref)):
            out[:, :held, :] = ref[...]


def pack_small(small_refs, kept_ref, sent_ref, low, me, core, count):
    own, middle, value_bias, wide = small_refs
    order = [own[0:4], value_bias[0:1], middle[3:4], middle[0:1], own[4:5], middle[4:5]]
    order += [middle[1:2], own[5:6], middle[5:6], middle[2:3], jnp.zeros((3, D), F32)]
    narrow = jnp.concatenate(order, axis=0)
    share = D // count
    broad = wide.shape[1] // count
    for r in range(count):
        first = narrow[:, r * share : (r + 1) * share]
        first = jnp.concatenate([first, jnp.zeros((RANK_ROWS, UNIT - share), F32)], axis=1)
        second = wide[:, r * broad : (r + 1) * broad]
        second = jnp.concatenate([second, jnp.zeros((1, UNIT - broad), F32)], axis=1)
        second = jnp.broadcast_to(second, (RANK_ROWS, UNIT))
        here = slice(low, low + RANK_ROWS)
        kept_ref[me ^ r, here, :] = jnp.where(core == 0, first, second).astype(LOW)
        sent_ref[me ^ r, here, :] = jnp.where(core == 0, second, first).astype(LOW)


def total_of(*refs):
    return functools.reduce(jnp.add, [ref[...].astype(F32) for ref in refs])


def split_kernel(x, kept_ref, come_ref, *refs):
    far, outs = ((), refs) if x else (refs[:2], refs[2:])
    half = kept_ref.shape[3] // 2
    for z in range(4):
        for g in range(2):
            at = (z, slice(None), x, slice(0, half)) if g == 0 else (z, x, slice(None), slice(half, 2 * half))
            total = kept_ref[at].astype(F32) + come_ref[at].astype(F32)
            if far:
                total = total + far[g][z].astype(F32)
                for i in range(2):
                    outs[2 * g + i][z] = total[i].astype(LOW)
            else:
                outs[g][z] = total.astype(LOW)


def join_kernel(a_keep, a_come, b_keep, b_come, *outs):
    rows = a_keep.shape[1]
    for z, out in enumerate(outs):
        out[:rows] = total_of(a_keep.at[z], a_come.at[z]).astype(LOW)
        out[rows:] = total_of(b_keep.at[z], b_come.at[z]).astype(LOW)


def sum_kernel(*refs):
    refs[-1][...] = total_of(*refs[:-1]).astype(LOW)


def spread_kernel(plan, count, packed, place_ref, own_ref, other_ref, *outs):
    core = place_ref[1]
    outs[-1][...] = jnp.zeros(outs[-1].shape, F32)
    for (rows, columns, at), out in zip(plan, outs):
        block = rows // count
        half = columns // 2
        for c in range(half // UNIT):
            low = at + c * block
            for value, mine in ((own_ref, core), (other_ref, 1 - core)):
                start = pl.multiple_of(mine * half + c * UNIT, SLAB)
                out[:, pl.ds(start, UNIT)] = value[low : low + block].astype(F32)
    if packed is not None:
        here = slice(packed, packed + RANK_ROWS)
        own, other = own_ref[here].astype(F32), other_ref[here].astype(F32)
        narrow, wide = jnp.where(core == 0, own, other), jnp.where(core == 0, other, own)
        biases_ref, wide_ref, gain_ref, shift_ref = outs[len(plan) : -1]
        share = biases_ref.shape[1]
        biases_ref[...] = narrow[0:7, :share]
        gain_ref[...] = narrow[7:10, :share]
        shift_ref[...] = narrow[10:13, :share]
        wide_ref[...] = wide[0:1, : wide_ref.shape[1]]


def swap(v, bits):
    count = lax.axis_size("store")
    return lax.ppermute(v, "store", [(i, i ^ bits) for i in range(count)])


def swap_core(v):
    return lax.ppermute(v, "dp", [(0, 1), (1, 0)])


class WeightSums:
    def __init__(self, place, count, rows):
        self.place, self.count, self.rows = place, count, rows
        self.plan, self.packed, self.at = [], None, 0
        self.buffers = ()

    def add(self, products, small=None, earlier=(), flops=0):
        plan, base, packed = [], self.at, None
        for pairs in products:
            rows, columns = pairs[0][0].shape[1], pairs[0][1].shape[1]
            plan.append((len(pairs), rows, columns, self.at))
            self.plan.append((rows, columns, self.at))
            self.at += rows // self.count * (columns // 2 // UNIT)
        args = [v for pairs in products for pair in pairs for v in pair]
        if small is not None:
            packed = self.packed = self.at
            self.at += RANK_ROWS
            args.extend(small)
        shape = (self.count, self.rows, UNIT)
        self.buffers = call(
            functools.partial(weight_grad_kernel, tuple(plan), self.count, packed, base),
            [(shape, LOW), (shape, LOW)],
            n_smem=1,
            earlier=earlier,
            flops=flops,
        )(self.place, *args, *self.buffers)
        return self.buffers

    def split(self, x, far=(), earlier=()):
        half = (4, 2, self.rows // 2, UNIT)
        outs = [half[:1] + half[2:]] * 4 if far else [half] * 2
        args = [v.reshape(4, 2, 2, self.rows, UNIT) for v in (self.kept, self.come)] + list(far)
        return call(
            functools.partial(split_kernel, x),
            [(shape, LOW) for shape in outs],
            earlier=earlier,
            limit=SMALL_LIMIT,
        )(*args)

    def start(self, earlier=()):
        self.kept, sent = self.buffers
        self.come = swap_core(sent)
        self.sent = self.split(1, earlier=earlier)
        return self.sent

    def first(self, *earlier):
        come = (swap(self.sent[0], 1), swap(self.sent[1], 2))
        a_keep, a_send, b_keep, b_send = self.split(0, come, earlier)
        self.kept, self.sent = (a_keep, b_keep), (a_send, b_send)
        return self.sent

    def second(self, *earlier):
        come = (swap(self.sent[0], 2), swap(self.sent[1], 1))
        self.w = call(
            join_kernel, [((self.rows, UNIT), LOW)] * 4, earlier=earlier, limit=SMALL_LIMIT
        )(self.kept[0], come[0], self.kept[1], come[1])
        return self.w

    def third(self, *earlier):
        come = [swap(self.w[k], 4 * k) for k in (1, 2, 3)]
        (self.own,) = call(
            sum_kernel, [(come[0].shape, LOW)], earlier=earlier, limit=SMALL_LIMIT
        )(self.w[0], *come)
        return self.own

    def finish(self, small=()):
        other = swap_core(self.own)
        shapes = [((rows // self.count, columns), F32) for rows, columns, _ in self.plan]
        shapes += [(shape, F32) for shape in (*small, (8, SLAB))]
        return call(
            functools.partial(spread_kernel, tuple(self.plan), self.count, self.packed),
            shapes,
            n_smem=1,
            limit=SMALL_LIMIT,
        )(self.place, self.own, other)


def local_tree(
    inputs,
    doc_lengths,
    datastore,
    kept_mask,
    retrieved,
    self_project,
    self_output,
    cross_query,
    cross_memory,
    cross_output,
    expand_weight,
    contract_weight,
    biases,
    expand_bias,
    norm_gain,
    norm_shift,
    cotangent,
):
    tokens = inputs.shape[0]
    count = lax.axis_size("store")
    local_blocks = datastore.shape[0] // BLOCK
    all_blocks = local_blocks * count
    capacity = 2 * tokens * TOPB // all_blocks
    plane_blocks = 4 * local_blocks
    rows_in = 4 * capacity
    hidden = expand_weight.shape[1]
    me = lax.axis_index("store").astype(jnp.int32)
    core = lax.axis_index("dp").astype(jnp.int32)
    place = jnp.stack([me, core])

    piece = ((2 * BLOCK + RANK_ROWS, D), LOW)
    a0, b0 = call(piece_kernel, [piece] * 2, pinned=(0, 1))(datastore, kept_mask.reshape(local_blocks, BLOCK))
    a1, b1 = swap(a0, 1), swap(b0, 2)
    heads_all, soft_self, attended, unit_first, scale_first, first_low, *queries = call(
        self_forward_kernel,
        [
            ((tokens, 3 * D), LOW),
            ((PAIRS, 2 * tokens, tokens), F32),
            ((tokens, D), LOW),
            ((tokens, D), F32),
            ((tokens, 1), F32),
            ((tokens, D), LOW),
        ]
        + [((tokens + RANK_ROWS, D), LOW)] * 4,
        scratch=[
            pltpu.VMEM((D, 3 * D), LOW),
            pltpu.VMEM((D, D), LOW),
            pltpu.VMEM((D, D), LOW),
            pltpu.SemaphoreType.DMA((5,)),
        ],
        n_smem=2,
        far_in=(4, 5, 6),
        pinned=(2, 3, 7, 8, 9),
        flops=8 * MICROSECOND,
    )(
        doc_lengths,
        place,
        inputs,
        retrieved.T,
        self_project,
        self_output,
        cross_query,
        biases,
        norm_gain,
        norm_shift,
    )
    pair = call(pair_kernel, [((2, *piece[0]), LOW)], earlier=(first_low,))
    ay, bx = swap(pair(a0, a1)[0], 2), swap(pair(b0, b1)[0], 1)
    queries = [queries[0]] + [swap(queries[k], 4 * k) for k in (1, 2, 3)]

    def of_blocks(blocks):
        return [
            ((blocks, BLOCK, 2 * D), LOW),
            ((blocks, 1, BLOCK), F32),
            ((blocks, BLOCK, SLAB), LOW),
        ]

    near = call(memory_kernel, of_blocks(4) * 2)(a0, a1, b0, b1, cross_memory, biases)
    memory, hidden_rows, key_side, stored = call(
        memory_kernel,
        of_blocks(plane_blocks) + [((plane_blocks * BLOCK, D), LOW)],
        scratch=[pltpu.SemaphoreType.DMA((8,))],
        far_out=(3,),
    )(ay, bx, a0, a1, b0, b1, cross_memory, biases, *near)

    slots, values, lses, inverses, sel = call(
        functools.partial(owner_forward_kernel, capacity),
        [
            ((plane_blocks, rows_in, D), LOW),
            ((plane_blocks, rows_in, D), F32),
            ((plane_blocks, rows_in, SLAB), F32),
            ((plane_blocks, rows_in, SLAB), F32),
            ((4, plane_blocks * capacity, tokens), LOW),
        ],
        scratch=[
            pltpu.VMEM((RANK_ROWS, tokens), F32),
            pltpu.VMEM((plane_blocks, rows_in, D), LOW),
            pltpu.SemaphoreType.DMA((1,)),
        ],
        far_out=(0,),
        flops=20 * MICROSECOND,
    )(*queries, memory, hidden_rows)
    payload = ((tokens + LSE_ROWS, D), LOW)
    payloads = call(functools.partial(merge_kernel, capacity, (1, 2, 3)), [payload] * 3)(
        values, lses, inverses, sel
    )
    payloads = (
        call(
            functools.partial(merge_kernel, capacity, (0,)), [payload], earlier=(payloads[0],)
        )(values, lses, inverses, sel)
        + payloads
    )
    parts = [payloads[0]] + [swap(payloads[k], 4 * k) for k in (1, 2, 3)]

    (
        outputs,
        merged_low,
        second_low,
        active_low,
        branch_grad,
        expanded_grad,
        cross_grad,
        second_resid,
        payload,
        small_middle,
        wide_bias,
    ) = call(
        middle_kernel,
        [
            ((tokens, D), LOW),
            ((tokens, D), LOW),
            ((tokens, D), LOW),
            ((tokens, hidden), LOW),
            ((tokens, D), LOW),
            ((tokens, hidden), LOW),
            ((tokens, D), LOW),
            ((tokens, D), F32),
            ((tokens + SIDE_ROWS, D), LOW),
            ((8, D), F32),
            ((1, hidden), F32),
        ],
        scratch=[
            pltpu.VMEM((tokens, hidden), F32),
        ],
        flops=12 * MICROSECOND,
    )(
        *parts,
        first_low,
        cotangent,
        cross_output,
        expand_weight,
        contract_weight,
        biases,
        expand_bias.reshape(1, hidden),
        norm_gain,
        norm_shift,
    )
    grads = [payload] + [swap(payload, 4 * k) for k in (1, 2, 3)]

    early = WeightSums(place, count, 432)
    early.add(
        [[(active_low, branch_grad)], [(merged_low, cross_grad)], [(second_low, expanded_grad)]],
        flops=8 * MICROSECOND,
    )
    early_start = early.start()

    (got,) = call(
        functools.partial(select_grads_kernel, capacity),
        [((plane_blocks, rows_in, D + SLAB), LOW)],
        flops=4 * LONG,
    )(sel, *grads)
    out = call(
        functools.partial(owner_backward_kernel, capacity),
        [((plane_blocks, BLOCK, 2 * D), LOW)] + [((tokens, D), LOW)] * 4,
        scratch=[pltpu.VMEM((plane_blocks, rows_in, D), LOW)],
        earlier=early_start,
        flops=LONG,
    )(sel, got, memory, key_side, slots)
    memory_grad, query_grads = out[0], out[1:5]
    parts = [query_grads[0]] + [swap(query_grads[k], 4 * k) for k in (1, 2, 3)]

    late = WeightSums(place, count, 352)
    flat_grad = memory_grad.reshape(plane_blocks * BLOCK, 2 * D)
    *late.buffers, value_bias_grad = call(
        functools.partial(memory_weight_kernel, count),
        [((count, 2 * D // count, UNIT), LOW)] * 2 + [((8, D), F32)],
        scratch=[pltpu.VMEM((2, D, D), F32)],
        n_smem=1,
        flops=MICROSECOND // 10,
    )(place, flat_grad, stored)
    early_first = early.first(late.buffers[0])
    late.plan, late.at = [(D, 2 * D, 0)], 2 * D // count

    pre_grad, self_branch_grad, project_grad, input_grad, small_self = call(
        self_backward_kernel,
        [
            ((tokens, D), LOW),
            ((tokens, D), LOW),
            ((tokens, 3 * D), LOW),
            ((tokens, D), F32),
            ((8, D), F32),
        ],
        scratch=[
            pltpu.VMEM((tokens, D), LOW),
        ],
        earlier=early_first,
        flops=LONG // 3,
    )(
        *parts,
        second_resid,
        unit_first,
        scale_first,
        heads_all,
        soft_self,
        cross_query,
        self_output,
        self_project,
        norm_gain,
    )
    early_second = early.second()
    late.add(
        [[(attended, self_branch_grad)], [(first_low, pre_grad)], [(inputs, project_grad)]],
        (small_self, small_middle, value_bias_grad, wide_bias),
        flops=MICROSECOND // 10,
    )
    near_a0, near_a1, far_a, near_b0, near_b1, far_b = call(
        datastore_grad_kernel,
        [((2 * BLOCK, D), LOW), ((2 * BLOCK, D), LOW), ((4 * BLOCK, D), LOW)] * 2,
        earlier=(late.buffers[0],),
        flops=4 * LONG,
    )(cross_memory, flat_grad)
    late.start(earlier=(far_a, early_second[0]))
    late_first = late.first()
    early.third(late_first[0])
    contract_weight_grad, cross_output_grad, expand_weight_grad, ended = early.finish()
    late.second(ended)
    far_a, far_b = (after(v, late.w[0]) for v in (far_a, far_b))
    come_a, come_b = swap(far_a, 2), swap(far_b, 1)
    quarter = (2 * BLOCK, D)
    send_a, send_b, keep_a, keep_b = call(
        datastore_step_kernel, [(quarter, LOW)] * 2 + [(quarter, F32)] * 2, limit=SMALL_LIMIT
    )(near_a0, near_a1, come_a, near_b0, near_b1, come_b)
    (datastore_grad,) = call(
        datastore_sum_kernel, [((4 * BLOCK, D), F32)], limit=SMALL_LIMIT
    )(keep_a, swap(send_a, 1), keep_b, swap(send_b, 2))
    late.third(send_a)
    share = D // count
    (
        cross_memory_grad,
        self_output_grad,
        cross_query_grad,
        self_project_grad,
        biases_grad,
        wide_grad,
        gain_grad,
        shift_grad,
        _,
    ) = late.finish([(7, share), (1, hidden // count), (3, share), (3, share)])
    return (
        outputs,
        input_grad,
        datastore_grad,
        self_project_grad,
        self_output_grad,
        cross_query_grad,
        cross_memory_grad,
        cross_output_grad,
        expand_weight_grad,
        contract_weight_grad,
        biases_grad,
        wide_grad.reshape(hidden // count),
        gain_grad,
        shift_grad,
    )


def layer_norm(residual, gain_row, shift_row):
    center = residual - jnp.mean(residual, axis=-1, keepdims=True)
    spread = jnp.mean(center * center, axis=-1, keepdims=True)
    return center * lax.rsqrt(spread + EPSILON) * gain_row + shift_row


def doc_mask(lengths, seq_tokens):
    upto = jnp.tri(lengths.shape[-1], dtype=jnp.int32)
    bounds = jnp.sum(lengths[..., None, :] * upto, axis=-1)
    places = jnp.arange(seq_tokens, dtype=jnp.int32)
    segment = jnp.sum((places[:, None] >= bounds[..., None, :]).astype(jnp.int32), axis=-1)
    causal = places[:, None] >= places[None, :]
    return (segment[..., :, None] == segment[..., None, :]) & causal


def slot_numbers(picks, capacity):
    flat_ids = picks.reshape(-1)
    sorter = jnp.argsort(flat_ids, stable=True)
    sorted_ids = flat_ids[sorter]
    first_seen = jnp.searchsorted(sorted_ids, sorted_ids, side="left")
    rank_sorted = jnp.arange(flat_ids.shape[0], dtype=jnp.int32) - first_seen
    ranks = jnp.zeros_like(flat_ids).at[sorter].set(rank_sorted)
    return flat_ids * capacity + ranks


def place_rows(rows, slot_ids, total_slots, store_count, local_blocks, capacity):
    placed = jnp.zeros((total_slots, rows.shape[1]), rows.dtype).at[slot_ids].set(rows)
    return placed.reshape(store_count, local_blocks, capacity, rows.shape[1])


def local_slots(
    inputs,
    doc_lengths,
    datastore,
    kept_mask,
    retrieved,
    self_project,
    self_output,
    cross_query,
    cross_memory,
    cross_output,
    expand_weight,
    contract_weight,
    biases,
    expand_bias,
    norm_gain,
    norm_shift,
    cotangent,
):
    tok_count = inputs.shape[0]
    store_count = lax.axis_size("store")
    local_blocks = datastore.shape[0] // BLOCK
    all_blocks = local_blocks * store_count
    capacity = 2 * tok_count * TOPB // all_blocks
    rows_in = store_count * capacity
    total_slots = all_blocks * capacity
    gain_rows = norm_gain.astype(jnp.float32)
    shift_rows = norm_shift.astype(jnp.float32)
    bias_rows = biases.astype(jnp.float32)
    projected = jnp.dot(inputs, self_project, preferred_element_type=jnp.float32)
    heads_all = jnp.concatenate(
        [
            QUERY_SCALE * (projected[:, :D] + bias_rows[0]),
            projected[:, D : 2 * D],
            projected[:, 2 * D :] + bias_rows[1],
        ],
        axis=1,
    ).astype(jnp.bfloat16)
    queries = heads_all[:, :D].reshape(tok_count, HEADS, HEAD_DIM)
    keys_self = heads_all[:, D : 2 * D].reshape(tok_count, HEADS, HEAD_DIM)
    values_self = heads_all[:, 2 * D :].reshape(tok_count, HEADS, HEAD_DIM)
    allowed = doc_mask(doc_lengths[0], tok_count)

    def self_scores():
        raw_scores = jnp.einsum(
            "qhd,khd->hqk", queries, keys_self, preferred_element_type=jnp.float32
        )
        return jnp.where(allowed[None], raw_scores, MASKED)

    scores = self_scores()
    self_lse = jax.nn.logsumexp(scores, axis=-1)
    soft_low = jnp.exp(scores - self_lse[..., None]).astype(jnp.bfloat16)
    attended = (
        jnp.einsum("hqk,khd->qhd", soft_low, values_self, preferred_element_type=jnp.float32)
        .reshape(tok_count, D)
        .astype(jnp.bfloat16)
    )
    self_branch = jnp.dot(attended, self_output, preferred_element_type=jnp.float32) + bias_rows[2]
    first_norm, first_back = jax.vjp(
        layer_norm, inputs.astype(jnp.float32) + self_branch, gain_rows[0], shift_rows[0]
    )
    first_low = first_norm.astype(jnp.bfloat16)
    cross_queries = (
        QUERY_SCALE
        * (jnp.dot(first_low, cross_query, preferred_element_type=jnp.float32) + bias_rows[3])
    ).astype(jnp.bfloat16)
    slot_ids = slot_numbers(retrieved, capacity)
    send_buffer = place_rows(
        jnp.repeat(cross_queries, TOPB, axis=0),
        slot_ids,
        total_slots,
        store_count,
        local_blocks,
        capacity,
    )
    arrived = lax.all_to_all(send_buffer, "store", split_axis=0, concat_axis=2, tiled=True)
    owner_queries = arrived[0].reshape(local_blocks, rows_in, HEADS, HEAD_DIM)
    memory_bias = jnp.concatenate([jnp.zeros((D,), jnp.float32), bias_rows[4]])
    memory_low = (
        jnp.dot(datastore, cross_memory, preferred_element_type=jnp.float32) + memory_bias
    ).astype(jnp.bfloat16)
    memory_blocks = memory_low.reshape(local_blocks, BLOCK, 2 * D)
    store_keys = memory_blocks[:, :, :D].reshape(local_blocks, BLOCK, HEADS, HEAD_DIM)
    store_values = memory_blocks[:, :, D:].reshape(local_blocks, BLOCK, HEADS, HEAD_DIM)
    kept_rows = kept_mask.reshape(local_blocks, BLOCK) > 0

    def block_scores(query_blocks):
        raw_scores = jnp.einsum(
            "bmhd,bkhd->bhmk", query_blocks, store_keys, preferred_element_type=jnp.float32
        )
        return jnp.where(kept_rows[:, None, None, :], raw_scores, MASKED)

    owner_scores = block_scores(owner_queries)
    owner_lse = jax.nn.logsumexp(owner_scores, axis=-1)
    owner_soft = jnp.exp(owner_scores - owner_lse[..., None]).astype(jnp.bfloat16)
    partial_value = jnp.einsum(
        "bhmk,bkhd->bmhd", owner_soft, store_values, preferred_element_type=jnp.float32
    ).reshape(local_blocks, rows_in, D)
    partial_lse = jnp.transpose(owner_lse, (0, 2, 1))
    returned, returned_lse = (
        lax.all_to_all(partial_value[None], "store", split_axis=2, concat_axis=0, tiled=True),
        lax.all_to_all(partial_lse[None], "store", split_axis=2, concat_axis=0, tiled=True),
    )
    picked = returned.reshape(total_slots, D)[slot_ids].reshape(tok_count, TOPB, HEADS, HEAD_DIM)
    picked_lse = returned_lse.reshape(total_slots, HEADS)[slot_ids].reshape(tok_count, TOPB, HEADS)
    overall = jax.nn.logsumexp(picked_lse, axis=1)
    mix_weights = jnp.exp(picked_lse - overall[:, None, :])
    merged = jnp.einsum(
        "tjh,tjhd->thd", mix_weights, picked, precision=lax.Precision.HIGHEST
    ).reshape(tok_count, D)
    merged_low = merged.astype(jnp.bfloat16)
    cross_branch = (
        jnp.dot(merged_low, cross_output, preferred_element_type=jnp.float32) + bias_rows[5]
    )
    second_norm, second_back = jax.vjp(
        layer_norm, first_low.astype(jnp.float32) + cross_branch, gain_rows[1], shift_rows[1]
    )
    second_low = second_norm.astype(jnp.bfloat16)
    expanded = jnp.dot(
        second_low, expand_weight, preferred_element_type=jnp.float32
    ) + expand_bias.astype(jnp.float32)
    activated, gelu_back = jax.vjp(
        lambda pre_act: jax.nn.gelu(pre_act, approximate=False), expanded
    )
    activated_low = activated.astype(jnp.bfloat16)
    ffn_branch = (
        jnp.dot(activated_low, contract_weight, preferred_element_type=jnp.float32) + bias_rows[6]
    )
    final_norm, final_back = jax.vjp(
        layer_norm, second_low.astype(jnp.float32) + ffn_branch, gain_rows[2], shift_rows[2]
    )
    outputs = final_norm.astype(jnp.bfloat16)
    final_resid, final_gain, final_shift = final_back(cotangent.astype(jnp.float32))
    ffn_branch_grad = final_resid.astype(jnp.bfloat16)
    contract_weight_grad = jnp.dot(
        activated_low.T, ffn_branch_grad, preferred_element_type=jnp.float32
    )
    activated_grad = jnp.dot(ffn_branch_grad, contract_weight.T, preferred_element_type=jnp.float32)
    (expanded_raw,) = gelu_back(activated_grad)
    expanded_grad = expanded_raw.astype(jnp.bfloat16)
    expand_weight_grad = jnp.dot(second_low.T, expanded_grad, preferred_element_type=jnp.float32)
    expand_bias_grad = jnp.sum(expanded_grad.astype(jnp.float32), axis=0)
    second_total = final_resid + jnp.dot(
        expanded_grad, expand_weight.T, preferred_element_type=jnp.float32
    )
    second_resid, second_gain, second_shift = second_back(second_total)
    cross_branch_grad = second_resid.astype(jnp.bfloat16)
    cross_output_grad = jnp.dot(merged_low.T, cross_branch_grad, preferred_element_type=jnp.float32)
    attended_grad = jnp.dot(
        cross_branch_grad, cross_output.T, preferred_element_type=jnp.float32
    ).astype(jnp.bfloat16)
    delta_rows = jnp.sum(
        attended_grad.reshape(tok_count, HEADS, HEAD_DIM).astype(jnp.float32)
        * merged.reshape(tok_count, HEADS, HEAD_DIM),
        axis=-1,
    )
    grad_buffer = place_rows(
        jnp.repeat(attended_grad, TOPB, axis=0),
        slot_ids,
        total_slots,
        store_count,
        local_blocks,
        capacity,
    )
    overall_buffer = place_rows(
        jnp.repeat(overall, TOPB, axis=0),
        slot_ids,
        total_slots,
        store_count,
        local_blocks,
        capacity,
    )
    delta_buffer = place_rows(
        jnp.repeat(delta_rows, TOPB, axis=0),
        slot_ids,
        total_slots,
        store_count,
        local_blocks,
        capacity,
    )
    arrived_grad = lax.all_to_all(grad_buffer, "store", split_axis=0, concat_axis=2, tiled=True)
    arrived_overall, arrived_delta = (
        lax.all_to_all(overall_buffer, "store", split_axis=0, concat_axis=2, tiled=True),
        lax.all_to_all(delta_buffer, "store", split_axis=0, concat_axis=2, tiled=True),
    )
    owner_grad = arrived_grad[0].reshape(local_blocks, rows_in, HEADS, HEAD_DIM)
    overall_heads = jnp.transpose(arrived_overall[0], (0, 2, 1))
    delta_heads = jnp.transpose(arrived_delta[0], (0, 2, 1))
    soft_again = jnp.exp(block_scores(owner_queries) - owner_lse[..., None])
    soft_again_low = soft_again.astype(jnp.bfloat16).astype(jnp.float32)
    weight_mix = jnp.exp(owner_lse - overall_heads)
    value_dots = jnp.einsum(
        "bmhd,bkhd->bhmk", owner_grad, store_values, preferred_element_type=jnp.float32
    )
    exact_sum = jnp.sum(soft_again * value_dots, axis=-1, keepdims=True)
    rounded_sum = jnp.sum(soft_again_low * value_dots, axis=-1, keepdims=True)
    score_grad = (
        weight_mix[..., None]
        * soft_again
        * (value_dots - exact_sum + rounded_sum - delta_heads[..., None])
    ).astype(jnp.bfloat16)
    query_grad = (
        jnp.einsum("bhmk,bkhd->bmhd", score_grad, store_keys, preferred_element_type=jnp.float32)
        .astype(jnp.bfloat16)
        .reshape(local_blocks, rows_in, D)
    )
    key_grad = jnp.einsum(
        "bhmk,bmhd->bkhd", score_grad, owner_queries, preferred_element_type=jnp.float32
    )
    weighted_soft = weight_mix[..., None] * soft_again_low
    value_grad = jnp.einsum(
        "bhmk,bmhd->bkhd",
        weighted_soft,
        owner_grad.astype(jnp.float32),
        precision=lax.Precision.HIGHEST,
    )
    row_count = local_blocks * BLOCK
    memory_grad = jnp.concatenate(
        [key_grad.reshape(row_count, D), value_grad.reshape(row_count, D)], axis=1
    ).astype(jnp.bfloat16)
    cross_memory_grad = jnp.dot(datastore.T, memory_grad, preferred_element_type=jnp.float32)
    value_bias_grad = jnp.sum(memory_grad[:, D:].astype(jnp.float32), axis=0)
    datastore_grad = jnp.dot(memory_grad, cross_memory.T, preferred_element_type=jnp.float32)
    returned_grad = lax.all_to_all(
        query_grad[None], "store", split_axis=2, concat_axis=0, tiled=True
    )
    per_pick = returned_grad.reshape(total_slots, D)[slot_ids].reshape(tok_count, TOPB, D)
    query_sum = jnp.sum(per_pick.astype(jnp.float32), axis=1).astype(jnp.bfloat16)
    cross_pre_grad = (query_sum.astype(jnp.float32) * QUERY_SCALE).astype(jnp.bfloat16)
    cross_query_grad = jnp.dot(first_low.T, cross_pre_grad, preferred_element_type=jnp.float32)
    first_total = second_resid + jnp.dot(
        cross_pre_grad, cross_query.T, preferred_element_type=jnp.float32
    )
    first_resid, first_gain, first_shift = first_back(first_total)
    self_branch_grad = first_resid.astype(jnp.bfloat16)
    self_output_grad = jnp.dot(attended.T, self_branch_grad, preferred_element_type=jnp.float32)
    self_attended_grad = (
        jnp.dot(self_branch_grad, self_output.T, preferred_element_type=jnp.float32)
        .astype(jnp.bfloat16)
        .reshape(tok_count, HEADS, HEAD_DIM)
    )
    soft_self = jnp.exp(self_scores() - self_lse[..., None])
    soft_dots = jnp.einsum(
        "qhd,khd->hqk", self_attended_grad, values_self, preferred_element_type=jnp.float32
    )
    self_score_grad = (
        soft_self * (soft_dots - jnp.sum(soft_self * soft_dots, axis=-1, keepdims=True))
    ).astype(jnp.bfloat16)
    query_self_grad = jnp.einsum(
        "hqk,khd->qhd", self_score_grad, keys_self, preferred_element_type=jnp.float32
    ).reshape(tok_count, D)
    key_self_grad = jnp.einsum(
        "hqk,qhd->khd", self_score_grad, queries, preferred_element_type=jnp.float32
    ).reshape(tok_count, D)
    value_self_grad = jnp.einsum(
        "hqk,qhd->khd", soft_low, self_attended_grad, preferred_element_type=jnp.float32
    ).reshape(tok_count, D)
    heads_grad = jnp.concatenate([query_self_grad, key_self_grad, value_self_grad], axis=1).astype(
        jnp.bfloat16
    )
    project_grad = jnp.concatenate(
        [
            (heads_grad[:, :D].astype(jnp.float32) * QUERY_SCALE).astype(jnp.bfloat16),
            heads_grad[:, D:],
        ],
        axis=1,
    )
    self_project_grad = jnp.dot(inputs.T, project_grad, preferred_element_type=jnp.float32)
    input_grad = first_resid + jnp.dot(
        project_grad, self_project.T, preferred_element_type=jnp.float32
    )
    biases_grad = jnp.stack(
        [
            jnp.sum(project_grad[:, :D].astype(jnp.float32), axis=0),
            jnp.sum(project_grad[:, 2 * D :].astype(jnp.float32), axis=0),
            jnp.sum(self_branch_grad.astype(jnp.float32), axis=0),
            jnp.sum(cross_pre_grad.astype(jnp.float32), axis=0),
            value_bias_grad,
            jnp.sum(cross_branch_grad.astype(jnp.float32), axis=0),
            jnp.sum(ffn_branch_grad.astype(jnp.float32), axis=0),
        ]
    )
    gain_grad = jnp.stack([first_gain, second_gain, final_gain])
    shift_grad = jnp.stack([first_shift, second_shift, final_shift])
    shared = (
        lax.psum_scatter(self_project_grad, "store", scatter_dimension=0, tiled=True),
        lax.psum_scatter(self_output_grad, "store", scatter_dimension=0, tiled=True),
        lax.psum_scatter(cross_query_grad, "store", scatter_dimension=0, tiled=True),
        lax.psum_scatter(cross_memory_grad, "store", scatter_dimension=0, tiled=True),
        lax.psum_scatter(cross_output_grad, "store", scatter_dimension=0, tiled=True),
        lax.psum_scatter(expand_weight_grad, "store", scatter_dimension=0, tiled=True),
        lax.psum_scatter(contract_weight_grad, "store", scatter_dimension=0, tiled=True),
        lax.psum_scatter(biases_grad, "store", scatter_dimension=1, tiled=True),
        lax.psum_scatter(expand_bias_grad, "store", scatter_dimension=0, tiled=True),
        lax.psum_scatter(gain_grad, "store", scatter_dimension=1, tiled=True),
        lax.psum_scatter(shift_grad, "store", scatter_dimension=1, tiled=True),
    )
    reduced = (
        lax.psum(shared[0].astype(jnp.bfloat16), "dp").astype(jnp.float32),
        lax.psum(shared[1].astype(jnp.bfloat16), "dp").astype(jnp.float32),
        lax.psum(shared[2].astype(jnp.bfloat16), "dp").astype(jnp.float32),
        lax.psum(shared[3].astype(jnp.bfloat16), "dp").astype(jnp.float32),
        lax.psum(shared[4].astype(jnp.bfloat16), "dp").astype(jnp.float32),
        lax.psum(shared[5].astype(jnp.bfloat16), "dp").astype(jnp.float32),
        lax.psum(shared[6].astype(jnp.bfloat16), "dp").astype(jnp.float32),
        lax.psum(shared[7].astype(jnp.bfloat16), "dp").astype(jnp.float32),
        lax.psum(shared[8].astype(jnp.bfloat16), "dp").astype(jnp.float32),
        lax.psum(shared[9].astype(jnp.bfloat16), "dp").astype(jnp.float32),
        lax.psum(shared[10].astype(jnp.bfloat16), "dp").astype(jnp.float32),
    )
    return (
        outputs,
        input_grad,
        datastore_grad,
        reduced[0],
        reduced[1],
        reduced[2],
        reduced[3],
        reduced[4],
        reduced[5],
        reduced[6],
        reduced[7],
        reduced[8],
        reduced[9],
        reduced[10],
    )


def solution(mesh):
    placed = (
        P(("dp", "store"), None),
        P(("dp", "store"), None),
        P(("dp", "store"), None),
        P(("dp", "store")),
        P(("dp", "store"), None),
        P(),
        P(),
        P(),
        P(),
        P(),
        P(),
        P(),
        P(),
        P(),
        P(),
        P(),
        P(("dp", "store"), None),
    )
    return jax.shard_map(
        local_tree if mesh.shape["store"] == 16 else local_slots,
        mesh=mesh,
        in_specs=placed,
        out_specs=(
            P(("dp", "store"), None),
            P(("dp", "store"), None),
            P(("dp", "store"), None),
            P("store", None),
            P("store", None),
            P("store", None),
            P("store", None),
            P("store", None),
            P("store", None),
            P("store", None),
            P(None, "store"),
            P("store"),
            P(None, "store"),
            P(None, "store"),
        ),
        check_vma=False,
    )
```

```python
import functools

import jax
import jax.numpy as jnp
from jax import lax
from jax.experimental import pallas as pl
from jax.experimental.pallas import tpu as pltpu
from jax.sharding import PartitionSpec as P

D = 768
HEADS = 12
HEAD_DIM = 64
TOPB = 8
BLOCK = 128
SLAB = 128
PAIRS = D // SLAB
UNIT = 384
LSE_ROWS = 8
SIDE_ROWS = 16
RANK_ROWS = 16
MARK_ROWS = 8

EPSILON = 1e-05
MASKED = -1e30
QUERY_SCALE = 0.125
VMEM_LIMIT = 16 * 1024 * 1024
SMALL_LIMIT = 16 * 1024 * 1024
LONG = 30_000_000_000
UNROLL = 8
MICROSECOND = 50_000_000
LOW = jnp.bfloat16
F32 = jnp.float32

_VMEM = pl.BlockSpec(memory_space=pltpu.VMEM)
_SMEM = pl.BlockSpec(memory_space=pltpu.SMEM)
_ANY = pl.BlockSpec(memory_space=pl.ANY)


def nn(a, b):
    return lax.dot_general(a, b, (((1,), (0,)), ((), ())), preferred_element_type=F32)


def nt(a, b):
    return lax.dot_general(a, b, (((1,), (1,)), ((), ())), preferred_element_type=F32)


def tn(a, b):
    return lax.dot_general(a, b, (((0,), (0,)), ((), ())), preferred_element_type=F32)


def three(v):
    high = v.astype(LOW)
    rest = v - high.astype(F32)
    mid = rest.astype(LOW)
    return high, mid, (rest - mid.astype(F32)).astype(LOW)


def lanes(shape):
    return lax.broadcasted_iota(jnp.int32, shape, len(shape) - 1)


def rows_of(shape):
    return lax.broadcasted_iota(jnp.int32, shape, len(shape) - 2)


def flag(condition):
    return jnp.where(condition, 1.0, 0.0)


def half_masks():
    first = flag(lanes((1, SLAB)) < HEAD_DIM)
    return first.astype(LOW), (1.0 - first).astype(LOW)


def two_heads(slab, first, second):
    return jnp.concatenate([slab * first, slab * second], axis=0)


def join_heads(stacked, count):
    left = lanes((count, SLAB)) < HEAD_DIM
    return jnp.where(left, stacked[:count], stacked[count:])


def norm_forward(residual, gain, shift):
    center = residual - jnp.mean(residual, axis=-1, keepdims=True)
    spread = jnp.mean(center * center, axis=-1, keepdims=True)
    scale = lax.rsqrt(spread + EPSILON)
    unit = center * scale
    return unit * gain + shift, unit, scale


def norm_backward(grad, unit, scale, gain):
    inner = grad * gain
    down = inner - jnp.mean(inner, axis=-1, keepdims=True)
    down = down - unit * jnp.mean(inner * unit, axis=-1, keepdims=True)
    return scale * down


def row_sum(v):
    return jnp.sum(v, axis=0, keepdims=True)


def call(
    kernel,
    outs,
    scratch=(),
    n_smem=0,
    far_in=(),
    far_out=(),
    earlier=(),
    aliases=None,
    flops=0,
    limit=VMEM_LIMIT,
    pinned=(),
):
    def run(*args):
        count = len(args)

        def body(*refs):
            kernel(*refs[:count], *refs[count + len(earlier) :])

        args = [
            pltpu.with_memory_space_constraint(v, pltpu.HBM)
            if (i in far_in and not aliases) or i in pinned
            else v
            for i, v in enumerate(args)
        ]
        specs = [_ANY if i in far_in else _VMEM for i in range(n_smem, count)]
        return pl.pallas_call(
            body,
            out_shape=[
                pltpu.HBM(s, t) if i in far_out and not aliases else jax.ShapeDtypeStruct(s, t)
                for i, (s, t) in enumerate(outs)
            ],
            in_specs=[_SMEM] * n_smem + specs + [_ANY] * len(earlier),
            out_specs=[_ANY if i in far_out else _VMEM for i in range(len(outs))],
            scratch_shapes=list(scratch),
            input_output_aliases=aliases or {},
            compiler_params=pltpu.CompilerParams(vmem_limit_bytes=limit),
            cost_estimate=pl.CostEstimate(flops=flops, bytes_accessed=0, transcendentals=0),
        )(*args, *earlier)

    return run


def copies(pairs, sems):
    return [pltpu.make_async_copy(a, b, sems.at[i]) for i, (a, b) in enumerate(pairs)]


def after(v, *earlier):
    return call(
        lambda *refs: None,
        [(v.shape, v.dtype)],
        far_in=(0,),
        far_out=(0,),
        earlier=earlier,
        aliases={0: 0},
        limit=1024 * 1024,
    )(v)[0]


def start_all(items):
    for item in items:
        item.start()


def wait_all(items):
    for item in items:
        item.wait()


def plane_ranks(picks_ref, me, k, tokens):
    i = rows_of((RANK_ROWS, tokens))
    group, chip, block = i // 4, (i // 2) % 2, i % 2
    apart = jnp.where(group < 2, 2 * group + chip, 2 * chip + group - 2)
    local = jnp.where(group < 2, block, 2 + block)
    plane = (me // 4) ^ k
    number = plane * 16 + ((me % 4) ^ apart) * 4 + local
    member = jnp.zeros((RANK_ROWS, tokens), F32)
    for j in range(TOPB):
        member = member + flag(picks_ref[j : j + 1, :] == number)
    earlier = flag(rows_of((tokens, tokens)) < lanes((tokens, tokens)))
    rank = nn(member.astype(LOW), earlier.astype(LOW))
    return jnp.where(member > 0.5, rank, -1.0).astype(LOW)


def self_forward_kernel(
    lengths_ref,
    place_ref,
    x_ref,
    picks_ref,
    project_ref,
    output_ref,
    query_ref,
    bias_ref,
    gain_ref,
    shift_ref,
    heads_ref,
    soft_ref,
    attended_ref,
    unit_ref,
    scale_ref,
    first_ref,
    *rest,
):
    payload_refs, (project_scr, output_scr, query_scr, sems) = rest[:4], rest[4:]
    thirds = [slice(i * D, (i + 1) * D) for i in range(3)]
    fetch = copies(
        [(project_ref.at[:, at], project_scr.at[:, at]) for at in thirds]
        + [(output_ref, output_scr), (query_ref, query_scr)],
        sems,
    )
    start_all(fetch)
    tokens = x_ref.shape[0]
    bias = bias_ref[...].astype(F32)
    x = x_ref[...]
    for i, at in enumerate(thirds):
        fetch[i].wait()
        part = nn(x, project_scr[:, at])
        if i == 0:
            part = QUERY_SCALE * (part + bias[0:1])
        if i == 2:
            part = part + bias[1:2]
        heads_ref[:, at] = part.astype(LOW)
    place_row = lax.broadcasted_iota(jnp.int32, (2 * tokens, tokens), 0) % tokens
    place_col = lanes((2 * tokens, tokens))
    segment_row = jnp.zeros((2 * tokens, tokens), jnp.int32)
    segment_col = jnp.zeros((2 * tokens, tokens), jnp.int32)
    bound = 0
    for d in range(lengths_ref.shape[1]):
        bound = bound + lengths_ref[0, d]
        segment_row = segment_row + jnp.where(place_row >= bound, 1, 0)
        segment_col = segment_col + jnp.where(place_col >= bound, 1, 0)
    allowed = (segment_row == segment_col) & (place_row >= place_col)
    first, second = half_masks()
    for p in range(PAIRS):
        at = p * SLAB
        queries = two_heads(heads_ref[:, at : at + SLAB], first, second)
        scores = nt(queries, heads_ref[:, D + at : D + at + SLAB])
        scores = jnp.where(allowed, scores, MASKED)
        top = jnp.max(scores, axis=-1, keepdims=True)
        raised = jnp.exp(scores - top)
        soft = raised / jnp.sum(raised, axis=-1, keepdims=True)
        soft_ref[p] = soft
        mixed = nn(soft.astype(LOW), heads_ref[:, 2 * D + at : 2 * D + at + SLAB])
        attended_ref[:, at : at + SLAB] = join_heads(mixed, tokens).astype(LOW)
    fetch[3].wait()
    residual = x.astype(F32) + nn(attended_ref[...], output_scr[...]) + bias[2:3]
    normed, unit, scale = norm_forward(
        residual, gain_ref[0:1, :].astype(F32), shift_ref[0:1, :].astype(F32)
    )
    unit_ref[...] = unit
    scale_ref[...] = scale
    low = normed.astype(LOW)
    first_ref[...] = low
    fetch[4].wait()
    queries = (QUERY_SCALE * (nn(low, query_scr[...]) + bias[3:4])).astype(LOW)
    for k, out in enumerate(payload_refs):
        out[:tokens] = queries
        out[tokens:, tokens:] = jnp.zeros((RANK_ROWS, D - tokens), LOW)
        out[tokens:, :tokens] = plane_ranks(picks_ref, place_ref[0], k, tokens)


def piece_kernel(rows_ref, kept_ref, a_ref, b_ref):
    for h, out in enumerate((a_ref, b_ref)):
        out[: 2 * BLOCK] = rows_ref[2 * h * BLOCK : 2 * (h + 1) * BLOCK]
        marks = kept_ref[2 * h : 2 * h + 2, :].astype(F32)
        marks = jnp.concatenate([marks, jnp.zeros((MARK_ROWS - 2, BLOCK), F32)], axis=0)
        out[2 * BLOCK :, :BLOCK] = marks.astype(LOW)
        out[2 * BLOCK :, BLOCK:] = jnp.zeros((MARK_ROWS, D - BLOCK), LOW)


def pair_kernel(first_ref, second_ref, out_ref):
    out_ref[0] = first_ref[...]
    out_ref[1] = second_ref[...]


def memory_kernel(*refs):
    far = len(refs) > 12
    if far:
        pieces = [ref.at[j] for ref in refs[:2] for j in range(2)]
        near_pieces, (weight_ref, bias_ref), given = refs[2:6], refs[6:8], refs[8:14]
        outs, rows_ref, sems = refs[14:17], refs[17], refs[18]
        size = 2 * BLOCK
        pairs = []
        for s in range(2):
            for j in range(2):
                at = 8 * s * BLOCK + j * size
                pairs.append((near_pieces[2 * s + j].at[:size], rows_ref.at[at : at + size]))
                at = at + 4 * BLOCK
                pairs.append((pieces[2 * s + j].at[:size], rows_ref.at[at : at + size]))
        keep = copies(pairs, sems)
        start_all(keep)
    else:
        pieces, (weight_ref, bias_ref), outs = refs[:4], refs[4:6], refs[6:]
    bias = bias_ref[4:5, :].astype(F32)
    lane = lanes((MARK_ROWS, SLAB))
    place = lanes((BLOCK, SLAB))
    for s in range(2):
        if far:
            near, here = 8 * s, 8 * s + 4
            memory_ref, hidden_ref, side_ref = outs
            for out, ref in zip(outs, given[3 * s : 3 * s + 3]):
                out[near : near + 4] = ref[...]
        else:
            here = 0
            memory_ref, hidden_ref, side_ref = outs[3 * s : 3 * s + 3]
        for j in range(2):
            piece = pieces[2 * s + j]
            rows = piece[: 2 * BLOCK]
            first = here + 2 * j
            keys = nn(rows, weight_ref[:, :D]).astype(LOW)
            values = (nn(rows, weight_ref[:, D:]) + bias).astype(LOW)
            marks = piece[2 * BLOCK :, :SLAB]
            for l in range(2):
                at = first + l
                memory_ref[at, :, :D] = keys[l * BLOCK : (l + 1) * BLOCK]
                memory_ref[at, :, D:] = values[l * BLOCK : (l + 1) * BLOCK]
                hidden_ref[at] = (1.0 - marks[l : l + 1].astype(F32)) * MASKED
                wanted = flag((rows_of((MARK_ROWS, SLAB)) == l) & (lane == SLAB - 1))
                column = tn(marks, wanted.astype(LOW))
                side = jnp.where(place == SLAB - 1, (1.0 - column) * MASKED, 0.0)
                side_ref[at] = jnp.where(place < 48, -1.0, side).astype(LOW)
    if far:
        wait_all(keep)


def selection(ranks, capacity):
    parts = []
    wanted = rows_of((capacity, ranks.shape[1])).astype(F32)
    for b in range(ranks.shape[0]):
        parts.append(flag(ranks[b : b + 1, :] == wanted).astype(LOW))
    return jnp.concatenate(parts, axis=0)


def fill_slots(sel, rows, out_ref, k, capacity):
    got = nn(sel, rows).astype(LOW)
    for b in range(out_ref.shape[0]):
        out_ref[b, k * capacity : (k + 1) * capacity, :] = got[b * capacity : (b + 1) * capacity]


def around16(v, combine):
    for step in (16, 32, 64):
        v = combine(v, pltpu.roll(v, step, 1))
    return v


def put_side(ref, side, rows):
    tokens = side.shape[0]
    turned = side.astype(F32).T.astype(LOW)
    for q in range(PAIRS):
        ref[tokens:, q * SLAB : (q + 1) * SLAB] = turned[q * rows : (q + 1) * rows]


def get_side(ref, tokens):
    rows = ref.shape[0] - tokens
    parts = [ref[tokens:, q * SLAB : (q + 1) * SLAB].astype(F32) for q in range(PAIRS)]
    parts.append(jnp.zeros((SLAB - PAIRS * rows, SLAB), F32))
    return jnp.concatenate(parts, axis=0).T


def lse_lanes(lse):
    high = lse.astype(LOW).astype(F32)
    rest = lse - high
    mid = rest.astype(LOW).astype(F32)
    low = rest - mid
    lane = lanes(lse.shape)
    packed = jnp.where(
        lane < 16, high, jnp.where(lane < 32, mid, jnp.where(lane < 48, low, 0.0))
    )
    return packed.astype(LOW)


def head_spread(group):
    row = rows_of((SLAB, D))
    row = row % 16 if group else row
    return flag(row == lanes((SLAB, D)) // HEAD_DIM).astype(LOW)


def owner_forward_kernel(capacity, *refs):
    tokens_refs, memory_ref, hidden_ref = refs[0:4], refs[4], refs[5]
    far_slots_ref, out_scr, lse_scr, inv_scr, sel_scr, ranks_scr, slots_ref, sems = refs[6:]
    sources = len(tokens_refs)
    blocks, rows = slots_ref.shape[:2]
    tokens = tokens_refs[0].shape[0] - RANK_ROWS
    first, second = half_masks()
    for k in range(sources):
        ranks_scr[...] = tokens_refs[k][tokens:, :tokens].astype(F32)
        sel = selection(ranks_scr[...], capacity)
        sel_scr[k] = sel
        fill_slots(sel, tokens_refs[k][:tokens], slots_ref, k, capacity)
    keep = copies([(slots_ref, far_slots_ref)], sems)
    start_all(keep)
    ones = jnp.ones((BLOCK, SLAB), LOW)
    lane_of = lanes((rows, SLAB))
    def one_block(i, carry):
        hidden = hidden_ref[i]
        tops = jnp.zeros((rows, SLAB), F32)
        totals = jnp.ones((rows, SLAB), F32)
        base = (i % 8) * 16
        slabs = [slice(p * SLAB, (p + 1) * SLAB) for p in range(PAIRS)]
        scores = [
            nt(two_heads(slots_ref[i, :, at], first, second), memory_ref[i, :, at])
            + hidden
            for at in slabs
        ]
        highest = [jnp.max(v, axis=-1, keepdims=True) for v in scores]
        raised = [jnp.exp(v - top).astype(LOW) for v, top in zip(scores, highest)]
        mixed = [
            nn(v, jnp.concatenate([memory_ref[i, :, D + at.start : D + at.stop], ones], axis=1))
            for v, at in zip(raised, slabs)
        ]
        for p, at in enumerate(slabs):
            out_scr[i, :, at] = join_heads(mixed[p][:, :SLAB], rows)
            for half in range(2):
                here = slice(half * rows, (half + 1) * rows)
                mine = lane_of == base + 2 * p + half
                tops = jnp.where(mine, highest[p][here], tops)
                totals = jnp.where(mine, mixed[p][here, SLAB:], totals)
        own = flag((lane_of >= base) & (lane_of < base + HEADS))
        lse_scr[i] = tops + jnp.log(totals)
        inv_scr[i] = own / totals
        return carry

    lax.fori_loop(0, blocks, one_block, 0, unroll=UNROLL)
    wait_all(keep)


def merge_kernel(capacity, ks, value_ref, lse_ref, inv_ref, sel_ref, *payload_refs):
    tokens = sel_ref.shape[2]
    group = 8 * capacity
    own_low = flag(
        rows_of((group, SLAB)) // capacity == lanes((group, SLAB)) // 16
    ).astype(LOW)
    spread = head_spread(True)
    each = [(n, g) for n in range(len(ks)) for g in range(2)]

    def stacked(ref, n, g):
        here = slice(ks[n] * capacity, (ks[n] + 1) * capacity)
        return jnp.concatenate([ref[8 * g + b, here, :] for b in range(8)], axis=0)

    sels = {(n, g): sel_ref[ks[n], g * group : (g + 1) * group, :] for n, g in each}
    turned = {at: sels[at].T for at in each}
    found = {
        at: nn(turned[at], jnp.concatenate([*three(stacked(lse_ref, *at)), own_low], axis=1))
        for at in each
    }
    members = {at: found[at][:, 3 * SLAB :] for at in each}
    by_token = {
        at: jnp.where(
            members[at] > 0.5,
            found[at][:, :SLAB] + found[at][:, SLAB : 2 * SLAB] + found[at][:, 2 * SLAB : 3 * SLAB],
            MASKED,
        )
        for at in each
    }
    tops = [
        around16(jnp.maximum(by_token[n, 0], by_token[n, 1]), jnp.maximum) for n in range(len(ks))
    ]
    weights = {at: members[at] * jnp.exp(by_token[at] - tops[at[0]]) for at in each}
    totals = [around16(weights[n, 0] + weights[n, 1], jnp.add) for n in range(len(ks))]
    safes = [jnp.where(total > 0.5, total, 1.0) for total in totals]
    shares = {
        at: nn(sels[at], (weights[at] / safes[at[0]]).astype(LOW)) * stacked(inv_ref, *at)
        for at in each
    }
    wide = {at: nn(shares[at].astype(LOW), spread) for at in each}
    for n, out in enumerate(payload_refs):
        partial = sum(
            nn(turned[n, g], (stacked(value_ref, n, g) * wide[n, g]).astype(LOW)) for g in range(2)
        )
        out[:tokens] = partial.astype(LOW)
        lse = jnp.where(totals[n] > 0.5, tops[n] + jnp.log(safes[n]), MASKED)
        put_side(out, lse_lanes(lse), LSE_ROWS)


def select_grads_kernel(capacity, *refs):
    sel_ref, grad_refs, got_ref = refs[0], refs[1:5], refs[5]
    tokens = grad_refs[0].shape[0] - SIDE_ROWS
    for k, ref in enumerate(grad_refs):
        side = get_side(ref, tokens).astype(LOW)
        rows_all = jnp.concatenate([ref[:tokens], side], axis=1)
        fill_slots(sel_ref[k], rows_all, got_ref, k, capacity)


def owner_backward_kernel(capacity, *refs):
    sel_scr, got_scr, memory_ref, side_ref, slots_ref = refs[:5]
    out, payload_refs, query_scr = refs[5], refs[6:10], refs[10]
    sources = len(payload_refs)
    blocks, rows = slots_ref.shape[:2]
    first, second = half_masks()
    lane = lanes((1, SLAB))
    last = flag(lane == SLAB - 1).astype(LOW)
    value_side = jnp.broadcast_to(
        -flag((lane >= 48) & (lane < 96)).astype(LOW), (BLOCK, SLAB)
    )

    def picked(head, base):
        inside = (lane >= base) & (lane < base + 48)
        return flag(inside & (lane % 16 == head)).astype(LOW)

    def one_block(i, carry):
        side = got_scr[i, :, D:]
        key_side = side_ref[i]
        slabs = [slice(p * SLAB, (p + 1) * SLAB) for p in range(PAIRS)]
        keys = [memory_ref[i, :, at] for at in slabs]
        queries = [two_heads(slots_ref[i, :, at], first, second) for at in slabs]
        grads = [two_heads(got_scr[i, :, at], first, second) for at in slabs]
        scores, dots = [], []
        for p in range(PAIRS):
            lse_side = jnp.concatenate(
                [side * picked(2 * p + h, 0) + last for h in range(2)], axis=0
            )
            scores.append(
                nt(
                    jnp.concatenate([keys[p], key_side], axis=1),
                    jnp.concatenate([queries[p], lse_side], axis=1),
                )
            )
        for p, at in enumerate(slabs):
            delta_side = jnp.concatenate(
                [side * picked(2 * p + h, 48) for h in range(2)], axis=0
            )
            values = memory_ref[i, :, D + at.start : D + at.stop]
            dots.append(
                nt(
                    jnp.concatenate([values, value_side], axis=1),
                    jnp.concatenate([grads[p], delta_side], axis=1),
                )
            )
        softs = [jnp.exp(v) for v in scores]
        score_grads = [(soft * v).astype(LOW) for soft, v in zip(softs, dots)]
        for p, at in enumerate(slabs):
            query_scr[i, :, at] = join_heads(tn(score_grads[p], keys[p]), rows).astype(LOW)
        for p, at in enumerate(slabs):
            out[i, :, at] = nn(score_grads[p], queries[p]).astype(LOW)
        for p, at in enumerate(slabs):
            out[i, :, D + at.start : D + at.stop] = nn(softs[p].astype(LOW), grads[p]).astype(
                LOW
            )
        return carry

    lax.fori_loop(0, blocks, one_block, 0, unroll=UNROLL)
    for k in range(sources):
        here = slice(k * capacity, (k + 1) * capacity)
        value = jnp.concatenate([query_scr[b, here, :] for b in range(blocks)], axis=0)
        payload_refs[k][...] = tn(sel_scr[k], value).astype(LOW)


def memory_weight_kernel(count, place_ref, *refs):
    grad_ref, rows_ref, kept_ref, sent_ref, bias_ref, sum_scr = refs
    me, core = place_ref[0], place_ref[1]
    size = 4 * BLOCK
    sum_scr[...] = jnp.zeros(sum_scr.shape, F32)
    bias_ref[...] = jnp.zeros(bias_ref.shape, F32)

    def one_set(s, carry):
        at = pl.ds(pl.multiple_of(s * size, size), size)
        rows = rows_ref[at, :].T
        for h in range(2):
            sum_scr[h] = sum_scr[h] + nn(rows, grad_ref[at, h * D : (h + 1) * D])
        bias_ref[0:1] = bias_ref[0:1] + row_sum(grad_ref[at, D:].astype(F32))
        return carry

    lax.fori_loop(0, rows_ref.shape[0] // size, one_set, 0)
    block = D // count
    for h in range(2):

        def store(out, h=h):
            total = sum_scr[h].astype(LOW)
            for k in range(count):
                for u in range(D // UNIT):
                    out[me ^ k, u * block : (u + 1) * block, :] = total[
                        k * block : (k + 1) * block, u * UNIT : (u + 1) * UNIT
                    ]

        pl.when(core == h)(functools.partial(store, kept_ref))
        pl.when(core != h)(functools.partial(store, sent_ref))


def datastore_grad_kernel(weight_ref, *refs):
    grad_ref, outs = refs[0], refs[1:7]
    weight = weight_ref[...].T
    near_a0, near_a1, far_a, near_b0, near_b1, far_b = outs
    groups = ((near_a0, near_a1), (far_a,), (near_b0, near_b1), (far_b,))
    for s in range(4):
        value = nn(grad_ref[4 * s * BLOCK : 4 * (s + 1) * BLOCK], weight).astype(LOW)
        size = value.shape[0] // len(groups[s])
        for i, out in enumerate(groups[s]):
            out[...] = value[i * size : (i + 1) * size]


def datastore_step_kernel(*refs):
    ins, sends, keeps = refs[:6], refs[6:8], refs[8:10]
    size = 2 * BLOCK
    for g in range(2):
        stay, go, come = ins[3 * g : 3 * g + 3]
        keeps[g][...] = stay[...].astype(F32) + come[:size].astype(F32)
        sends[g][...] = (go[...].astype(F32) + come[size:].astype(F32)).astype(LOW)


def datastore_sum_kernel(keep_a, come_a, keep_b, come_b, out_ref):
    size = keep_a.shape[0]
    out_ref[:size] = keep_a[...] + come_a[...].astype(F32)
    out_ref[size:] = keep_b[...] + come_b[...].astype(F32)


def middle_kernel(
    p0_ref,
    p1_ref,
    p2_ref,
    p3_ref,
    first_ref,
    cotangent_ref,
    output_ref,
    expand_ref,
    contract_ref,
    bias_ref,
    expand_bias_ref,
    gain_ref,
    shift_ref,
    out_ref,
    merged_ref,
    second_ref,
    active_ref,
    branch_grad_ref,
    expanded_grad_ref,
    cross_grad_ref,
    resid_ref,
    payload_ref,
    small_ref,
    wide_ref,
    expanded_scr,
):
    output_scr, expand_scr, contract_scr = output_ref, expand_ref, contract_ref
    bias = bias_ref[...].astype(F32)
    gain = gain_ref[...].astype(F32)
    shift = shift_ref[...].astype(F32)
    parts = [p0_ref, p1_ref, p2_ref, p3_ref]
    tokens = first_ref.shape[0]
    lses = [around16(get_side(part, tokens), jnp.add) for part in parts]
    top = functools.reduce(jnp.maximum, lses)
    weights = [jnp.exp(lse - top) for lse in lses]
    total = functools.reduce(jnp.add, weights)
    overall = top + jnp.log(total)
    spread = head_spread(False)
    merged = jnp.zeros(first_ref.shape, F32)
    for part, weight in zip(parts, weights):
        share = weight / total
        high = share.astype(LOW)
        rest = (share - high.astype(F32)).astype(LOW)
        merged = merged + (nn(high, spread) + nn(rest, spread)) * part[:tokens].astype(F32)
    merged_low = merged.astype(LOW)
    merged_ref[...] = merged_low
    residual = first_ref[...].astype(F32) + nn(merged_low, output_scr[...]) + bias[5:6]
    second, unit_second, scale_second = norm_forward(residual, gain[1:2], shift[1:2])
    second_low = second.astype(LOW)
    second_ref[...] = second_low
    hidden = contract_scr.shape[0]
    for c in range(hidden // D):
        at = slice(c * D, (c + 1) * D)
        expanded = nn(second_low, expand_scr[:, at]) + expand_bias_ref[:, at].astype(F32)
        bell = 0.5 * (1.0 + lax.erf(expanded * 0.7071067811865476))
        active_ref[:, at] = (expanded * bell).astype(LOW)
        slope = bell + expanded * 0.3989422804014327 * jnp.exp(-0.5 * expanded * expanded)
        expanded_scr[:, at] = slope
    residual = second_low.astype(F32) + nn(active_ref[...], contract_scr[...]) + bias[6:7]
    final, unit_final, scale_final = norm_forward(residual, gain[2:3], shift[2:3])
    out_ref[...] = final.astype(LOW)
    cotangent = cotangent_ref[...].astype(F32)
    final_resid = norm_backward(cotangent, unit_final, scale_final, gain[2:3])
    branch_grad = final_resid.astype(LOW)
    branch_grad_ref[...] = branch_grad
    small_ref[0:1, :] = row_sum(branch_grad.astype(F32))
    small_ref[1:2, :] = row_sum(cotangent * unit_final)
    small_ref[2:3, :] = row_sum(cotangent)
    total_grad = final_resid
    for c in range(hidden // D):
        at = slice(c * D, (c + 1) * D)
        active_grad = nt(branch_grad, contract_scr[at, :])
        expanded_grad = (active_grad * expanded_scr[:, at]).astype(LOW)
        expanded_grad_ref[:, at] = expanded_grad
        wide_ref[:, at] = row_sum(expanded_grad.astype(F32))
        total_grad = total_grad + nt(expanded_grad, expand_scr[:, at])
    small_ref[4:5, :] = row_sum(total_grad * unit_second)
    small_ref[5:6, :] = row_sum(total_grad)
    second_resid = norm_backward(total_grad, unit_second, scale_second, gain[1:2])
    resid_ref[...] = second_resid
    cross_grad = second_resid.astype(LOW)
    cross_grad_ref[...] = cross_grad
    small_ref[3:4, :] = row_sum(cross_grad.astype(F32))
    small_ref[6:8, :] = jnp.zeros((2, D), F32)
    attended_grad = nt(cross_grad, output_scr[...]).astype(LOW)
    payload_ref[:tokens] = attended_grad
    product = attended_grad.astype(F32) * merged
    gather = flag(lanes((D, SLAB)) % 16 == rows_of((D, SLAB)) // HEAD_DIM).astype(LOW)
    high, mid, low = three(product)
    delta = nn(high, gather) + nn(mid, gather) + nn(low, gather)
    lane = lanes(overall.shape)
    packed = jnp.zeros(overall.shape, F32)
    for value, base in ((overall, 0), (delta, 48)):
        for i, piece in enumerate(three(value)):
            inside = (lane >= base + 16 * i) & (lane < base + 16 * i + HEADS)
            packed = jnp.where(inside, piece.astype(F32), packed)
    put_side(payload_ref, packed, SIDE_ROWS)


def self_backward_kernel(
    d0_ref,
    d1_ref,
    d2_ref,
    d3_ref,
    resid_ref,
    unit_ref,
    scale_ref,
    heads_ref,
    soft_ref,
    query_ref,
    output_ref,
    project_ref,
    gain_ref,
    pre_grad_ref,
    branch_grad_ref,
    project_grad_ref,
    input_grad_ref,
    small_ref,
    attended_scr,
):
    query_scr, output_scr, heads_scr = query_ref, output_ref, heads_ref
    soft_scr, project_scr = soft_ref, project_ref
    tokens = resid_ref.shape[0]
    query_sum = functools.reduce(
        jnp.add, [d[...].astype(F32) for d in (d0_ref, d1_ref, d2_ref, d3_ref)]
    ).astype(LOW)
    pre_grad = (query_sum.astype(F32) * QUERY_SCALE).astype(LOW)
    pre_grad_ref[...] = pre_grad
    total = resid_ref[...] + nt(pre_grad, query_scr[...])
    unit = unit_ref[...]
    first_resid = norm_backward(total, unit, scale_ref[...], gain_ref[0:1, :].astype(F32))
    branch_grad = first_resid.astype(LOW)
    branch_grad_ref[...] = branch_grad
    attended_scr[...] = nt(branch_grad, output_scr[...]).astype(LOW)
    first, second = half_masks()
    for p in range(PAIRS):
        at = p * SLAB
        grads = two_heads(attended_scr[:, at : at + SLAB], first, second)
        queries = two_heads(heads_scr[:, at : at + SLAB], first, second)
        keys = heads_scr[:, D + at : D + at + SLAB]
        dots = nt(grads, heads_scr[:, 2 * D + at : 2 * D + at + SLAB])
        soft = soft_scr[p]
        score_grad = (soft * (dots - jnp.sum(soft * dots, axis=-1, keepdims=True))).astype(LOW)
        query_grad = join_heads(nn(score_grad, keys), tokens).astype(LOW)
        project_grad_ref[:, at : at + SLAB] = (query_grad.astype(F32) * QUERY_SCALE).astype(LOW)
        project_grad_ref[:, D + at : D + at + SLAB] = tn(score_grad, queries).astype(LOW)
        project_grad_ref[:, 2 * D + at : 2 * D + at + SLAB] = tn(soft.astype(LOW), grads).astype(
            LOW
        )
    input_grad_ref[...] = first_resid + nt(project_grad_ref[...], project_scr[...])
    small_ref[0:1, :] = row_sum(project_grad_ref[:, :D].astype(F32))
    small_ref[1:2, :] = row_sum(project_grad_ref[:, 2 * D :].astype(F32))
    small_ref[2:3, :] = row_sum(branch_grad.astype(F32))
    small_ref[3:4, :] = row_sum(pre_grad.astype(F32))
    small_ref[4:5, :] = row_sum(total * unit)
    small_ref[5:6, :] = row_sum(total)
    small_ref[6:8, :] = jnp.zeros((2, D), F32)


def weight_grad_kernel(plan, count, packed, held, place_ref, *refs):
    kept_ref, sent_ref = refs[-2:]
    me, core = place_ref[0], place_ref[1]
    at_ref = 0
    for number, rows, columns, at in plan:
        pairs = [refs[at_ref + 2 * i : at_ref + 2 * i + 2] for i in range(number)]
        at_ref += 2 * number
        block = rows // count
        half = columns // 2
        steps = [(c, min(D, half - c)) for c in range(0, half, D)]

        def unit(m, c, wide, block=block, half=half, at=at, pairs=pairs):
            xs = [x_ref[:, pl.ds(pl.multiple_of(m * D, SLAB), D)].T for x_ref, _ in pairs]
            for mine, out in ((core, kept_ref), (1 - core, sent_ref)):
                start = pl.multiple_of(mine * half + c, SLAB)
                part = sum(nn(x, g_ref[:, pl.ds(start, wide)]) for x, (_, g_ref) in zip(xs, pairs))
                part = part.astype(LOW)
                for u in range(wide // UNIT):
                    low = pl.multiple_of(at + (c // UNIT + u) * block, 16)
                    for k in range(D // block):
                        to = me ^ (m * (D // block) + k)
                        out[to, pl.ds(low, block), :] = part[
                            k * block : (k + 1) * block, u * UNIT : (u + 1) * UNIT
                        ]

        if rows > D:
            for c, wide in steps:

                def by_rows(m, carry, c=c, wide=wide, unit=unit):
                    unit(m, c, wide)
                    return carry

                lax.fori_loop(0, rows // D, by_rows, 0)
        elif half % D == 0 and half > D:

            def by_columns(c, carry, unit=unit):
                unit(0, c * D, D)
                return carry

            lax.fori_loop(0, half // D, by_columns, 0)
        else:
            for c, wide in steps:
                unit(0, c, wide)
    if packed is not None:
        pack_small(refs[at_ref : at_ref + 4], kept_ref, sent_ref, packed, me, core, count)
        at_ref += 4
    if held:
        for ref, out in zip(refs[at_ref : at_ref + 2], (kept_ref, sent_ref)):
            out[:, :held, :] = ref[...]


def pack_small(small_refs, kept_ref, sent_ref, low, me, core, count):
    own, middle, value_bias, wide = small_refs
    order = [own[0:4], value_bias[0:1], middle[3:4], middle[0:1], own[4:5], middle[4:5]]
    order += [middle[1:2], own[5:6], middle[5:6], middle[2:3], jnp.zeros((3, D), F32)]
    narrow = jnp.concatenate(order, axis=0)
    share = D // count
    broad = wide.shape[1] // count
    for r in range(count):
        first = narrow[:, r * share : (r + 1) * share]
        first = jnp.concatenate([first, jnp.zeros((RANK_ROWS, UNIT - share), F32)], axis=1)
        second = wide[:, r * broad : (r + 1) * broad]
        second = jnp.concatenate([second, jnp.zeros((1, UNIT - broad), F32)], axis=1)
        second = jnp.broadcast_to(second, (RANK_ROWS, UNIT))
        here = slice(low, low + RANK_ROWS)
        kept_ref[me ^ r, here, :] = jnp.where(core == 0, first, second).astype(LOW)
        sent_ref[me ^ r, here, :] = jnp.where(core == 0, second, first).astype(LOW)


def total_of(*refs):
    return functools.reduce(jnp.add, [ref[...].astype(F32) for ref in refs])


def split_kernel(x, kept_ref, come_ref, *refs):
    far, outs = ((), refs) if x else (refs[:2], refs[2:])
    half = kept_ref.shape[3] // 2
    for z in range(4):
        for g in range(2):
            at = (z, slice(None), x, slice(0, half)) if g == 0 else (z, x, slice(None), slice(half, 2 * half))
            total = kept_ref[at].astype(F32) + come_ref[at].astype(F32)
            if far:
                total = total + far[g][z].astype(F32)
                for i in range(2):
                    outs[2 * g + i][z] = total[i].astype(LOW)
            else:
                outs[g][z] = total.astype(LOW)


def join_kernel(a_keep, a_come, b_keep, b_come, *outs):
    rows = a_keep.shape[1]
    for z, out in enumerate(outs):
        out[:rows] = total_of(a_keep.at[z], a_come.at[z]).astype(LOW)
        out[rows:] = total_of(b_keep.at[z], b_come.at[z]).astype(LOW)


def sum_kernel(*refs):
    refs[-1][...] = total_of(*refs[:-1]).astype(LOW)


def spread_kernel(plan, count, packed, place_ref, own_ref, other_ref, *outs):
    core = place_ref[1]
    outs[-1][...] = jnp.zeros(outs[-1].shape, F32)
    for (rows, columns, at), out in zip(plan, outs):
        block = rows // count
        half = columns // 2
        for c in range(half // UNIT):
            low = at + c * block
            for value, mine in ((own_ref, core), (other_ref, 1 - core)):
                start = pl.multiple_of(mine * half + c * UNIT, SLAB)
                out[:, pl.ds(start, UNIT)] = value[low : low + block].astype(F32)
    if packed is not None:
        here = slice(packed, packed + RANK_ROWS)
        own, other = own_ref[here].astype(F32), other_ref[here].astype(F32)
        narrow, wide = jnp.where(core == 0, own, other), jnp.where(core == 0, other, own)
        biases_ref, wide_ref, gain_ref, shift_ref = outs[len(plan) : -1]
        share = biases_ref.shape[1]
        biases_ref[...] = narrow[0:7, :share]
        gain_ref[...] = narrow[7:10, :share]
        shift_ref[...] = narrow[10:13, :share]
        wide_ref[...] = wide[0:1, : wide_ref.shape[1]]


def swap(v, bits):
    count = lax.axis_size("store")
    return lax.ppermute(v, "store", [(i, i ^ bits) for i in range(count)])


def swap_core(v):
    return lax.ppermute(v, "dp", [(0, 1), (1, 0)])


class WeightSums:
    def __init__(self, place, count, rows):
        self.place, self.count, self.rows = place, count, rows
        self.plan, self.packed, self.at = [], None, 0
        self.buffers = ()

    def add(self, products, small=None, earlier=(), flops=0):
        plan, base, packed = [], self.at, None
        for pairs in products:
            rows, columns = pairs[0][0].shape[1], pairs[0][1].shape[1]
            plan.append((len(pairs), rows, columns, self.at))
            self.plan.append((rows, columns, self.at))
            self.at += rows // self.count * (columns // 2 // UNIT)
        args = [v for pairs in products for pair in pairs for v in pair]
        if small is not None:
            packed = self.packed = self.at
            self.at += RANK_ROWS
            args.extend(small)
        shape = (self.count, self.rows, UNIT)
        self.buffers = call(
            functools.partial(weight_grad_kernel, tuple(plan), self.count, packed, base),
            [(shape, LOW), (shape, LOW)],
            n_smem=1,
            earlier=earlier,
            flops=flops,
        )(self.place, *args, *self.buffers)
        return self.buffers

    def split(self, x, far=(), earlier=()):
        half = (4, 2, self.rows // 2, UNIT)
        outs = [half[:1] + half[2:]] * 4 if far else [half] * 2
        args = [v.reshape(4, 2, 2, self.rows, UNIT) for v in (self.kept, self.come)] + list(far)
        return call(
            functools.partial(split_kernel, x),
            [(shape, LOW) for shape in outs],
            earlier=earlier,
            limit=SMALL_LIMIT,
        )(*args)

    def start(self, earlier=()):
        self.kept, sent = self.buffers
        self.come = swap_core(sent)
        self.sent = self.split(1, earlier=earlier)
        return self.sent

    def first(self, *earlier):
        come = (swap(self.sent[0], 1), swap(self.sent[1], 2))
        a_keep, a_send, b_keep, b_send = self.split(0, come, earlier)
        self.kept, self.sent = (a_keep, b_keep), (a_send, b_send)
        return self.sent

    def second(self, *earlier):
        come = (swap(self.sent[0], 2), swap(self.sent[1], 1))
        self.w = call(
            join_kernel, [((self.rows, UNIT), LOW)] * 4, earlier=earlier, limit=SMALL_LIMIT
        )(self.kept[0], come[0], self.kept[1], come[1])
        return self.w

    def third(self, *earlier):
        come = [swap(self.w[k], 4 * k) for k in (1, 2, 3)]
        (self.own,) = call(
            sum_kernel, [(come[0].shape, LOW)], earlier=earlier, limit=SMALL_LIMIT
        )(self.w[0], *come)
        return self.own

    def finish(self, small=()):
        other = swap_core(self.own)
        shapes = [((rows // self.count, columns), F32) for rows, columns, _ in self.plan]
        shapes += [(shape, F32) for shape in (*small, (8, SLAB))]
        return call(
            functools.partial(spread_kernel, tuple(self.plan), self.count, self.packed),
            shapes,
            n_smem=1,
            limit=SMALL_LIMIT,
        )(self.place, self.own, other)


def local_tree(
    inputs,
    doc_lengths,
    datastore,
    kept_mask,
    retrieved,
    self_project,
    self_output,
    cross_query,
    cross_memory,
    cross_output,
    expand_weight,
    contract_weight,
    biases,
    expand_bias,
    norm_gain,
    norm_shift,
    cotangent,
):
    tokens = inputs.shape[0]
    count = lax.axis_size("store")
    local_blocks = datastore.shape[0] // BLOCK
    all_blocks = local_blocks * count
    capacity = 2 * tokens * TOPB // all_blocks
    plane_blocks = 4 * local_blocks
    rows_in = 4 * capacity
    hidden = expand_weight.shape[1]
    me = lax.axis_index("store").astype(jnp.int32)
    core = lax.axis_index("dp").astype(jnp.int32)
    place = jnp.stack([me, core])

    piece = ((2 * BLOCK + MARK_ROWS, D), LOW)
    a0, b0 = call(piece_kernel, [piece] * 2, pinned=(0, 1))(datastore, kept_mask.reshape(local_blocks, BLOCK))
    a1, b1 = swap(a0, 1), swap(b0, 2)
    heads_all, soft_self, attended, unit_first, scale_first, first_low, *queries = call(
        self_forward_kernel,
        [
            ((tokens, 3 * D), LOW),
            ((PAIRS, 2 * tokens, tokens), F32),
            ((tokens, D), LOW),
            ((tokens, D), F32),
            ((tokens, 1), F32),
            ((tokens, D), LOW),
        ]
        + [((tokens + RANK_ROWS, D), LOW)] * 4,
        scratch=[
            pltpu.VMEM((D, 3 * D), LOW),
            pltpu.VMEM((D, D), LOW),
            pltpu.VMEM((D, D), LOW),
            pltpu.SemaphoreType.DMA((5,)),
        ],
        n_smem=2,
        far_in=(4, 5, 6),
        pinned=(2, 3, 7, 8, 9),
        flops=8 * MICROSECOND,
    )(
        doc_lengths,
        place,
        inputs,
        retrieved.T,
        self_project,
        self_output,
        cross_query,
        biases,
        norm_gain,
        norm_shift,
    )
    pair = call(pair_kernel, [((2, *piece[0]), LOW)], earlier=(first_low,))
    ay, bx = swap(pair(a0, a1)[0], 2), swap(pair(b0, b1)[0], 1)
    queries = [queries[0]] + [swap(queries[k], 4 * k) for k in (1, 2, 3)]

    def of_blocks(blocks):
        return [
            ((blocks, BLOCK, 2 * D), LOW),
            ((blocks, 1, BLOCK), F32),
            ((blocks, BLOCK, SLAB), LOW),
        ]

    near = call(memory_kernel, of_blocks(4) * 2)(a0, a1, b0, b1, cross_memory, biases)
    memory, hidden_rows, key_side, stored = call(
        memory_kernel,
        of_blocks(plane_blocks) + [((plane_blocks * BLOCK, D), LOW)],
        scratch=[pltpu.SemaphoreType.DMA((8,))],
        far_out=(3,),
    )(ay, bx, a0, a1, b0, b1, cross_memory, biases, *near)

    slots, values, lses, inverses, sel = call(
        functools.partial(owner_forward_kernel, capacity),
        [
            ((plane_blocks, rows_in, D), LOW),
            ((plane_blocks, rows_in, D), F32),
            ((plane_blocks, rows_in, SLAB), F32),
            ((plane_blocks, rows_in, SLAB), F32),
            ((4, plane_blocks * capacity, tokens), LOW),
        ],
        scratch=[
            pltpu.VMEM((RANK_ROWS, tokens), F32),
            pltpu.VMEM((plane_blocks, rows_in, D), LOW),
            pltpu.SemaphoreType.DMA((1,)),
        ],
        far_out=(0,),
        flops=20 * MICROSECOND,
    )(*queries, memory, hidden_rows)
    payload = ((tokens + LSE_ROWS, D), LOW)
    payloads = call(functools.partial(merge_kernel, capacity, (1, 2, 3)), [payload] * 3)(
        values, lses, inverses, sel
    )
    payloads = (
        call(
            functools.partial(merge_kernel, capacity, (0,)), [payload], earlier=(payloads[0],)
        )(values, lses, inverses, sel)
        + payloads
    )
    parts = [payloads[0]] + [swap(payloads[k], 4 * k) for k in (1, 2, 3)]

    (
        outputs,
        merged_low,
        second_low,
        active_low,
        branch_grad,
        expanded_grad,
        cross_grad,
        second_resid,
        payload,
        small_middle,
        wide_bias,
    ) = call(
        middle_kernel,
        [
            ((tokens, D), LOW),
            ((tokens, D), LOW),
            ((tokens, D), LOW),
            ((tokens, hidden), LOW),
            ((tokens, D), LOW),
            ((tokens, hidden), LOW),
            ((tokens, D), LOW),
            ((tokens, D), F32),
            ((tokens + SIDE_ROWS, D), LOW),
            ((8, D), F32),
            ((1, hidden), F32),
        ],
        scratch=[
            pltpu.VMEM((tokens, hidden), F32),
        ],
        flops=12 * MICROSECOND,
    )(
        *parts,
        first_low,
        cotangent,
        cross_output,
        expand_weight,
        contract_weight,
        biases,
        expand_bias.reshape(1, hidden),
        norm_gain,
        norm_shift,
    )
    grads = [payload] + [swap(payload, 4 * k) for k in (1, 2, 3)]

    early = WeightSums(place, count, 432)
    early.add(
        [[(active_low, branch_grad)], [(merged_low, cross_grad)], [(second_low, expanded_grad)]],
        flops=8 * MICROSECOND,
    )
    early_start = early.start()

    (got,) = call(
        functools.partial(select_grads_kernel, capacity),
        [((plane_blocks, rows_in, D + SLAB), LOW)],
        flops=4 * LONG,
    )(sel, *grads)
    out = call(
        functools.partial(owner_backward_kernel, capacity),
        [((plane_blocks, BLOCK, 2 * D), LOW)] + [((tokens, D), LOW)] * 4,
        scratch=[pltpu.VMEM((plane_blocks, rows_in, D), LOW)],
        earlier=early_start,
        flops=LONG,
    )(sel, got, memory, key_side, slots)
    memory_grad, query_grads = out[0], out[1:5]
    parts = [query_grads[0]] + [swap(query_grads[k], 4 * k) for k in (1, 2, 3)]

    late = WeightSums(place, count, 352)
    flat_grad = memory_grad.reshape(plane_blocks * BLOCK, 2 * D)
    *late.buffers, value_bias_grad = call(
        functools.partial(memory_weight_kernel, count),
        [((count, 2 * D // count, UNIT), LOW)] * 2 + [((8, D), F32)],
        scratch=[pltpu.VMEM((2, D, D), F32)],
        n_smem=1,
        flops=MICROSECOND // 10,
    )(place, flat_grad, stored)
    early_first = early.first(late.buffers[0])
    late.plan, late.at = [(D, 2 * D, 0)], 2 * D // count

    pre_grad, self_branch_grad, project_grad, input_grad, small_self = call(
        self_backward_kernel,
        [
            ((tokens, D), LOW),
            ((tokens, D), LOW),
            ((tokens, 3 * D), LOW),
            ((tokens, D), F32),
            ((8, D), F32),
        ],
        scratch=[
            pltpu.VMEM((tokens, D), LOW),
        ],
        earlier=early_first,
        flops=LONG // 3,
    )(
        *parts,
        second_resid,
        unit_first,
        scale_first,
        heads_all,
        soft_self,
        cross_query,
        self_output,
        self_project,
        norm_gain,
    )
    early_second = early.second()
    late.add(
        [[(attended, self_branch_grad)], [(first_low, pre_grad)], [(inputs, project_grad)]],
        (small_self, small_middle, value_bias_grad, wide_bias),
        flops=MICROSECOND // 10,
    )
    near_a0, near_a1, far_a, near_b0, near_b1, far_b = call(
        datastore_grad_kernel,
        [((2 * BLOCK, D), LOW), ((2 * BLOCK, D), LOW), ((4 * BLOCK, D), LOW)] * 2,
        earlier=(late.buffers[0],),
        flops=4 * LONG,
    )(cross_memory, flat_grad)
    late.start(earlier=(far_a, early_second[0]))
    late_first = late.first()
    early.third(late_first[0])
    contract_weight_grad, cross_output_grad, expand_weight_grad, ended = early.finish()
    late.second(ended)
    far_a, far_b = (after(v, late.w[0]) for v in (far_a, far_b))
    come_a, come_b = swap(far_a, 2), swap(far_b, 1)
    quarter = (2 * BLOCK, D)
    send_a, send_b, keep_a, keep_b = call(
        datastore_step_kernel, [(quarter, LOW)] * 2 + [(quarter, F32)] * 2, limit=SMALL_LIMIT
    )(near_a0, near_a1, come_a, near_b0, near_b1, come_b)
    (datastore_grad,) = call(
        datastore_sum_kernel, [((4 * BLOCK, D), F32)], limit=SMALL_LIMIT
    )(keep_a, swap(send_a, 1), keep_b, swap(send_b, 2))
    late.third(send_a)
    share = D // count
    (
        cross_memory_grad,
        self_output_grad,
        cross_query_grad,
        self_project_grad,
        biases_grad,
        wide_grad,
        gain_grad,
        shift_grad,
        _,
    ) = late.finish([(7, share), (1, hidden // count), (3, share), (3, share)])
    return (
        outputs,
        input_grad,
        datastore_grad,
        self_project_grad,
        self_output_grad,
        cross_query_grad,
        cross_memory_grad,
        cross_output_grad,
        expand_weight_grad,
        contract_weight_grad,
        biases_grad,
        wide_grad.reshape(hidden // count),
        gain_grad,
        shift_grad,
    )


def layer_norm(residual, gain_row, shift_row):
    center = residual - jnp.mean(residual, axis=-1, keepdims=True)
    spread = jnp.mean(center * center, axis=-1, keepdims=True)
    return center * lax.rsqrt(spread + EPSILON) * gain_row + shift_row


def doc_mask(lengths, seq_tokens):
    upto = jnp.tri(lengths.shape[-1], dtype=jnp.int32)
    bounds = jnp.sum(lengths[..., None, :] * upto, axis=-1)
    places = jnp.arange(seq_tokens, dtype=jnp.int32)
    segment = jnp.sum((places[:, None] >= bounds[..., None, :]).astype(jnp.int32), axis=-1)
    causal = places[:, None] >= places[None, :]
    return (segment[..., :, None] == segment[..., None, :]) & causal


def slot_numbers(picks, capacity):
    flat_ids = picks.reshape(-1)
    sorter = jnp.argsort(flat_ids, stable=True)
    sorted_ids = flat_ids[sorter]
    first_seen = jnp.searchsorted(sorted_ids, sorted_ids, side="left")
    rank_sorted = jnp.arange(flat_ids.shape[0], dtype=jnp.int32) - first_seen
    ranks = jnp.zeros_like(flat_ids).at[sorter].set(rank_sorted)
    return flat_ids * capacity + ranks


def place_rows(rows, slot_ids, total_slots, store_count, local_blocks, capacity):
    placed = jnp.zeros((total_slots, rows.shape[1]), rows.dtype).at[slot_ids].set(rows)
    return placed.reshape(store_count, local_blocks, capacity, rows.shape[1])


def local_slots(
    inputs,
    doc_lengths,
    datastore,
    kept_mask,
    retrieved,
    self_project,
    self_output,
    cross_query,
    cross_memory,
    cross_output,
    expand_weight,
    contract_weight,
    biases,
    expand_bias,
    norm_gain,
    norm_shift,
    cotangent,
):
    tok_count = inputs.shape[0]
    store_count = lax.axis_size("store")
    local_blocks = datastore.shape[0] // BLOCK
    all_blocks = local_blocks * store_count
    capacity = 2 * tok_count * TOPB // all_blocks
    rows_in = store_count * capacity
    total_slots = all_blocks * capacity
    gain_rows = norm_gain.astype(jnp.float32)
    shift_rows = norm_shift.astype(jnp.float32)
    bias_rows = biases.astype(jnp.float32)
    projected = jnp.dot(inputs, self_project, preferred_element_type=jnp.float32)
    heads_all = jnp.concatenate(
        [
            QUERY_SCALE * (projected[:, :D] + bias_rows[0]),
            projected[:, D : 2 * D],
            projected[:, 2 * D :] + bias_rows[1],
        ],
        axis=1,
    ).astype(jnp.bfloat16)
    queries = heads_all[:, :D].reshape(tok_count, HEADS, HEAD_DIM)
    keys_self = heads_all[:, D : 2 * D].reshape(tok_count, HEADS, HEAD_DIM)
    values_self = heads_all[:, 2 * D :].reshape(tok_count, HEADS, HEAD_DIM)
    allowed = doc_mask(doc_lengths[0], tok_count)

    def self_scores():
        raw_scores = jnp.einsum(
            "qhd,khd->hqk", queries, keys_self, preferred_element_type=jnp.float32
        )
        return jnp.where(allowed[None], raw_scores, MASKED)

    scores = self_scores()
    self_lse = jax.nn.logsumexp(scores, axis=-1)
    soft_low = jnp.exp(scores - self_lse[..., None]).astype(jnp.bfloat16)
    attended = (
        jnp.einsum("hqk,khd->qhd", soft_low, values_self, preferred_element_type=jnp.float32)
        .reshape(tok_count, D)
        .astype(jnp.bfloat16)
    )
    self_branch = jnp.dot(attended, self_output, preferred_element_type=jnp.float32) + bias_rows[2]
    first_norm, first_back = jax.vjp(
        layer_norm, inputs.astype(jnp.float32) + self_branch, gain_rows[0], shift_rows[0]
    )
    first_low = first_norm.astype(jnp.bfloat16)
    cross_queries = (
        QUERY_SCALE
        * (jnp.dot(first_low, cross_query, preferred_element_type=jnp.float32) + bias_rows[3])
    ).astype(jnp.bfloat16)
    slot_ids = slot_numbers(retrieved, capacity)
    send_buffer = place_rows(
        jnp.repeat(cross_queries, TOPB, axis=0),
        slot_ids,
        total_slots,
        store_count,
        local_blocks,
        capacity,
    )
    arrived = lax.all_to_all(send_buffer, "store", split_axis=0, concat_axis=2, tiled=True)
    owner_queries = arrived[0].reshape(local_blocks, rows_in, HEADS, HEAD_DIM)
    memory_bias = jnp.concatenate([jnp.zeros((D,), jnp.float32), bias_rows[4]])
    memory_low = (
        jnp.dot(datastore, cross_memory, preferred_element_type=jnp.float32) + memory_bias
    ).astype(jnp.bfloat16)
    memory_blocks = memory_low.reshape(local_blocks, BLOCK, 2 * D)
    store_keys = memory_blocks[:, :, :D].reshape(local_blocks, BLOCK, HEADS, HEAD_DIM)
    store_values = memory_blocks[:, :, D:].reshape(local_blocks, BLOCK, HEADS, HEAD_DIM)
    kept_rows = kept_mask.reshape(local_blocks, BLOCK) > 0

    def block_scores(query_blocks):
        raw_scores = jnp.einsum(
            "bmhd,bkhd->bhmk", query_blocks, store_keys, preferred_element_type=jnp.float32
        )
        return jnp.where(kept_rows[:, None, None, :], raw_scores, MASKED)

    owner_scores = block_scores(owner_queries)
    owner_lse = jax.nn.logsumexp(owner_scores, axis=-1)
    owner_soft = jnp.exp(owner_scores - owner_lse[..., None]).astype(jnp.bfloat16)
    partial_value = jnp.einsum(
        "bhmk,bkhd->bmhd", owner_soft, store_values, preferred_element_type=jnp.float32
    ).reshape(local_blocks, rows_in, D)
    partial_lse = jnp.transpose(owner_lse, (0, 2, 1))
    returned, returned_lse = (
        lax.all_to_all(partial_value[None], "store", split_axis=2, concat_axis=0, tiled=True),
        lax.all_to_all(partial_lse[None], "store", split_axis=2, concat_axis=0, tiled=True),
    )
    picked = returned.reshape(total_slots, D)[slot_ids].reshape(tok_count, TOPB, HEADS, HEAD_DIM)
    picked_lse = returned_lse.reshape(total_slots, HEADS)[slot_ids].reshape(tok_count, TOPB, HEADS)
    overall = jax.nn.logsumexp(picked_lse, axis=1)
    mix_weights = jnp.exp(picked_lse - overall[:, None, :])
    merged = jnp.einsum(
        "tjh,tjhd->thd", mix_weights, picked, precision=lax.Precision.HIGHEST
    ).reshape(tok_count, D)
    merged_low = merged.astype(jnp.bfloat16)
    cross_branch = (
        jnp.dot(merged_low, cross_output, preferred_element_type=jnp.float32) + bias_rows[5]
    )
    second_norm, second_back = jax.vjp(
        layer_norm, first_low.astype(jnp.float32) + cross_branch, gain_rows[1], shift_rows[1]
    )
    second_low = second_norm.astype(jnp.bfloat16)
    expanded = jnp.dot(
        second_low, expand_weight, preferred_element_type=jnp.float32
    ) + expand_bias.astype(jnp.float32)
    activated, gelu_back = jax.vjp(
        lambda pre_act: jax.nn.gelu(pre_act, approximate=False), expanded
    )
    activated_low = activated.astype(jnp.bfloat16)
    ffn_branch = (
        jnp.dot(activated_low, contract_weight, preferred_element_type=jnp.float32) + bias_rows[6]
    )
    final_norm, final_back = jax.vjp(
        layer_norm, second_low.astype(jnp.float32) + ffn_branch, gain_rows[2], shift_rows[2]
    )
    outputs = final_norm.astype(jnp.bfloat16)
    final_resid, final_gain, final_shift = final_back(cotangent.astype(jnp.float32))
    ffn_branch_grad = final_resid.astype(jnp.bfloat16)
    contract_weight_grad = jnp.dot(
        activated_low.T, ffn_branch_grad, preferred_element_type=jnp.float32
    )
    activated_grad = jnp.dot(ffn_branch_grad, contract_weight.T, preferred_element_type=jnp.float32)
    (expanded_raw,) = gelu_back(activated_grad)
    expanded_grad = expanded_raw.astype(jnp.bfloat16)
    expand_weight_grad = jnp.dot(second_low.T, expanded_grad, preferred_element_type=jnp.float32)
    expand_bias_grad = jnp.sum(expanded_grad.astype(jnp.float32), axis=0)
    second_total = final_resid + jnp.dot(
        expanded_grad, expand_weight.T, preferred_element_type=jnp.float32
    )
    second_resid, second_gain, second_shift = second_back(second_total)
    cross_branch_grad = second_resid.astype(jnp.bfloat16)
    cross_output_grad = jnp.dot(merged_low.T, cross_branch_grad, preferred_element_type=jnp.float32)
    attended_grad = jnp.dot(
        cross_branch_grad, cross_output.T, preferred_element_type=jnp.float32
    ).astype(jnp.bfloat16)
    delta_rows = jnp.sum(
        attended_grad.reshape(tok_count, HEADS, HEAD_DIM).astype(jnp.float32)
        * merged.reshape(tok_count, HEADS, HEAD_DIM),
        axis=-1,
    )
    grad_buffer = place_rows(
        jnp.repeat(attended_grad, TOPB, axis=0),
        slot_ids,
        total_slots,
        store_count,
        local_blocks,
        capacity,
    )
    overall_buffer = place_rows(
        jnp.repeat(overall, TOPB, axis=0),
        slot_ids,
        total_slots,
        store_count,
        local_blocks,
        capacity,
    )
    delta_buffer = place_rows(
        jnp.repeat(delta_rows, TOPB, axis=0),
        slot_ids,
        total_slots,
        store_count,
        local_blocks,
        capacity,
    )
    arrived_grad = lax.all_to_all(grad_buffer, "store", split_axis=0, concat_axis=2, tiled=True)
    arrived_overall, arrived_delta = (
        lax.all_to_all(overall_buffer, "store", split_axis=0, concat_axis=2, tiled=True),
        lax.all_to_all(delta_buffer, "store", split_axis=0, concat_axis=2, tiled=True),
    )
    owner_grad = arrived_grad[0].reshape(local_blocks, rows_in, HEADS, HEAD_DIM)
    overall_heads = jnp.transpose(arrived_overall[0], (0, 2, 1))
    delta_heads = jnp.transpose(arrived_delta[0], (0, 2, 1))
    soft_again = jnp.exp(block_scores(owner_queries) - owner_lse[..., None])
    soft_again_low = soft_again.astype(jnp.bfloat16).astype(jnp.float32)
    weight_mix = jnp.exp(owner_lse - overall_heads)
    value_dots = jnp.einsum(
        "bmhd,bkhd->bhmk", owner_grad, store_values, preferred_element_type=jnp.float32
    )
    exact_sum = jnp.sum(soft_again * value_dots, axis=-1, keepdims=True)
    rounded_sum = jnp.sum(soft_again_low * value_dots, axis=-1, keepdims=True)
    score_grad = (
        weight_mix[..., None]
        * soft_again
        * (value_dots - exact_sum + rounded_sum - delta_heads[..., None])
    ).astype(jnp.bfloat16)
    query_grad = (
        jnp.einsum("bhmk,bkhd->bmhd", score_grad, store_keys, preferred_element_type=jnp.float32)
        .astype(jnp.bfloat16)
        .reshape(local_blocks, rows_in, D)
    )
    key_grad = jnp.einsum(
        "bhmk,bmhd->bkhd", score_grad, owner_queries, preferred_element_type=jnp.float32
    )
    weighted_soft = weight_mix[..., None] * soft_again_low
    value_grad = jnp.einsum(
        "bhmk,bmhd->bkhd",
        weighted_soft,
        owner_grad.astype(jnp.float32),
        precision=lax.Precision.HIGHEST,
    )
    row_count = local_blocks * BLOCK
    memory_grad = jnp.concatenate(
        [key_grad.reshape(row_count, D), value_grad.reshape(row_count, D)], axis=1
    ).astype(jnp.bfloat16)
    cross_memory_grad = jnp.dot(datastore.T, memory_grad, preferred_element_type=jnp.float32)
    value_bias_grad = jnp.sum(memory_grad[:, D:].astype(jnp.float32), axis=0)
    datastore_grad = jnp.dot(memory_grad, cross_memory.T, preferred_element_type=jnp.float32)
    returned_grad = lax.all_to_all(
        query_grad[None], "store", split_axis=2, concat_axis=0, tiled=True
    )
    per_pick = returned_grad.reshape(total_slots, D)[slot_ids].reshape(tok_count, TOPB, D)
    query_sum = jnp.sum(per_pick.astype(jnp.float32), axis=1).astype(jnp.bfloat16)
    cross_pre_grad = (query_sum.astype(jnp.float32) * QUERY_SCALE).astype(jnp.bfloat16)
    cross_query_grad = jnp.dot(first_low.T, cross_pre_grad, preferred_element_type=jnp.float32)
    first_total = second_resid + jnp.dot(
        cross_pre_grad, cross_query.T, preferred_element_type=jnp.float32
    )
    first_resid, first_gain, first_shift = first_back(first_total)
    self_branch_grad = first_resid.astype(jnp.bfloat16)
    self_output_grad = jnp.dot(attended.T, self_branch_grad, preferred_element_type=jnp.float32)
    self_attended_grad = (
        jnp.dot(self_branch_grad, self_output.T, preferred_element_type=jnp.float32)
        .astype(jnp.bfloat16)
        .reshape(tok_count, HEADS, HEAD_DIM)
    )
    soft_self = jnp.exp(self_scores() - self_lse[..., None])
    soft_dots = jnp.einsum(
        "qhd,khd->hqk", self_attended_grad, values_self, preferred_element_type=jnp.float32
    )
    self_score_grad = (
        soft_self * (soft_dots - jnp.sum(soft_self * soft_dots, axis=-1, keepdims=True))
    ).astype(jnp.bfloat16)
    query_self_grad = jnp.einsum(
        "hqk,khd->qhd", self_score_grad, keys_self, preferred_element_type=jnp.float32
    ).reshape(tok_count, D)
    key_self_grad = jnp.einsum(
        "hqk,qhd->khd", self_score_grad, queries, preferred_element_type=jnp.float32
    ).reshape(tok_count, D)
    value_self_grad = jnp.einsum(
        "hqk,qhd->khd", soft_low, self_attended_grad, preferred_element_type=jnp.float32
    ).reshape(tok_count, D)
    heads_grad = jnp.concatenate([query_self_grad, key_self_grad, value_self_grad], axis=1).astype(
        jnp.bfloat16
    )
    project_grad = jnp.concatenate(
        [
            (heads_grad[:, :D].astype(jnp.float32) * QUERY_SCALE).astype(jnp.bfloat16),
            heads_grad[:, D:],
        ],
        axis=1,
    )
    self_project_grad = jnp.dot(inputs.T, project_grad, preferred_element_type=jnp.float32)
    input_grad = first_resid + jnp.dot(
        project_grad, self_project.T, preferred_element_type=jnp.float32
    )
    biases_grad = jnp.stack(
        [
            jnp.sum(project_grad[:, :D].astype(jnp.float32), axis=0),
            jnp.sum(project_grad[:, 2 * D :].astype(jnp.float32), axis=0),
            jnp.sum(self_branch_grad.astype(jnp.float32), axis=0),
            jnp.sum(cross_pre_grad.astype(jnp.float32), axis=0),
            value_bias_grad,
            jnp.sum(cross_branch_grad.astype(jnp.float32), axis=0),
            jnp.sum(ffn_branch_grad.astype(jnp.float32), axis=0),
        ]
    )
    gain_grad = jnp.stack([first_gain, second_gain, final_gain])
    shift_grad = jnp.stack([first_shift, second_shift, final_shift])
    shared = (
        lax.psum_scatter(self_project_grad, "store", scatter_dimension=0, tiled=True),
        lax.psum_scatter(self_output_grad, "store", scatter_dimension=0, tiled=True),
        lax.psum_scatter(cross_query_grad, "store", scatter_dimension=0, tiled=True),
        lax.psum_scatter(cross_memory_grad, "store", scatter_dimension=0, tiled=True),
        lax.psum_scatter(cross_output_grad, "store", scatter_dimension=0, tiled=True),
        lax.psum_scatter(expand_weight_grad, "store", scatter_dimension=0, tiled=True),
        lax.psum_scatter(contract_weight_grad, "store", scatter_dimension=0, tiled=True),
        lax.psum_scatter(biases_grad, "store", scatter_dimension=1, tiled=True),
        lax.psum_scatter(expand_bias_grad, "store", scatter_dimension=0, tiled=True),
        lax.psum_scatter(gain_grad, "store", scatter_dimension=1, tiled=True),
        lax.psum_scatter(shift_grad, "store", scatter_dimension=1, tiled=True),
    )
    reduced = (
        lax.psum(shared[0].astype(jnp.bfloat16), "dp").astype(jnp.float32),
        lax.psum(shared[1].astype(jnp.bfloat16), "dp").astype(jnp.float32),
        lax.psum(shared[2].astype(jnp.bfloat16), "dp").astype(jnp.float32),
        lax.psum(shared[3].astype(jnp.bfloat16), "dp").astype(jnp.float32),
        lax.psum(shared[4].astype(jnp.bfloat16), "dp").astype(jnp.float32),
        lax.psum(shared[5].astype(jnp.bfloat16), "dp").astype(jnp.float32),
        lax.psum(shared[6].astype(jnp.bfloat16), "dp").astype(jnp.float32),
        lax.psum(shared[7].astype(jnp.bfloat16), "dp").astype(jnp.float32),
        lax.psum(shared[8].astype(jnp.bfloat16), "dp").astype(jnp.float32),
        lax.psum(shared[9].astype(jnp.bfloat16), "dp").astype(jnp.float32),
        lax.psum(shared[10].astype(jnp.bfloat16), "dp").astype(jnp.float32),
    )
    return (
        outputs,
        input_grad,
        datastore_grad,
        reduced[0],
        reduced[1],
        reduced[2],
        reduced[3],
        reduced[4],
        reduced[5],
        reduced[6],
        reduced[7],
        reduced[8],
        reduced[9],
        reduced[10],
    )


def solution(mesh):
    placed = (
        P(("dp", "store"), None),
        P(("dp", "store"), None),
        P(("dp", "store"), None),
        P(("dp", "store")),
        P(("dp", "store"), None),
        P(),
        P(),
        P(),
        P(),
        P(),
        P(),
        P(),
        P(),
        P(),
        P(),
        P(),
        P(("dp", "store"), None),
    )
    return jax.shard_map(
        local_tree if mesh.shape["store"] == 16 else local_slots,
        mesh=mesh,
        in_specs=placed,
        out_specs=(
            P(("dp", "store"), None),
            P(("dp", "store"), None),
            P(("dp", "store"), None),
            P("store", None),
            P("store", None),
            P("store", None),
            P("store", None),
            P("store", None),
            P("store", None),
            P("store", None),
            P(None, "store"),
            P("store"),
            P(None, "store"),
            P(None, "store"),
        ),
        check_vma=False,
    )
```

```python
import functools

import jax
import jax.numpy as jnp
from jax import lax
from jax.experimental import pallas as pl
from jax.experimental.pallas import tpu as pltpu
from jax.sharding import PartitionSpec as P

D = 768
HEADS = 12
HEAD_DIM = 64
TOPB = 8
BLOCK = 128
SLAB = 128
PAIRS = D // SLAB
UNIT = 384
LSE_ROWS = 8
SIDE_ROWS = 16
RANK_ROWS = 16
MARK_ROWS = 8

EPSILON = 1e-05
MASKED = -1e30
QUERY_SCALE = 0.125
VMEM_LIMIT = 16 * 1024 * 1024
SMALL_LIMIT = 16 * 1024 * 1024
LONG = 30_000_000_000
UNROLL = 4
MICROSECOND = 50_000_000
LOW = jnp.bfloat16
F32 = jnp.float32

_VMEM = pl.BlockSpec(memory_space=pltpu.VMEM)
_SMEM = pl.BlockSpec(memory_space=pltpu.SMEM)
_ANY = pl.BlockSpec(memory_space=pl.ANY)


def nn(a, b):
    return lax.dot_general(a, b, (((1,), (0,)), ((), ())), preferred_element_type=F32)


def nt(a, b):
    return lax.dot_general(a, b, (((1,), (1,)), ((), ())), preferred_element_type=F32)


def tn(a, b):
    return lax.dot_general(a, b, (((0,), (0,)), ((), ())), preferred_element_type=F32)


def three(v):
    high = v.astype(LOW)
    rest = v - high.astype(F32)
    mid = rest.astype(LOW)
    return high, mid, (rest - mid.astype(F32)).astype(LOW)


def lanes(shape):
    return lax.broadcasted_iota(jnp.int32, shape, len(shape) - 1)


def rows_of(shape):
    return lax.broadcasted_iota(jnp.int32, shape, len(shape) - 2)


def flag(condition):
    return jnp.where(condition, 1.0, 0.0)


def half_masks():
    first = flag(lanes((1, SLAB)) < HEAD_DIM)
    return first.astype(LOW), (1.0 - first).astype(LOW)


def two_heads(slab, first, second):
    return jnp.concatenate([slab * first, slab * second], axis=0)


def join_heads(stacked, count):
    left = lanes((count, SLAB)) < HEAD_DIM
    return jnp.where(left, stacked[:count], stacked[count:])


def norm_forward(residual, gain, shift):
    center = residual - jnp.mean(residual, axis=-1, keepdims=True)
    spread = jnp.mean(center * center, axis=-1, keepdims=True)
    scale = lax.rsqrt(spread + EPSILON)
    unit = center * scale
    return unit * gain + shift, unit, scale


def norm_backward(grad, unit, scale, gain):
    inner = grad * gain
    down = inner - jnp.mean(inner, axis=-1, keepdims=True)
    down = down - unit * jnp.mean(inner * unit, axis=-1, keepdims=True)
    return scale * down


def row_sum(v):
    return jnp.sum(v, axis=0, keepdims=True)


def call(
    kernel,
    outs,
    scratch=(),
    n_smem=0,
    far_in=(),
    far_out=(),
    earlier=(),
    aliases=None,
    flops=0,
    limit=VMEM_LIMIT,
    pinned=(),
):
    def run(*args):
        count = len(args)

        def body(*refs):
            kernel(*refs[:count], *refs[count + len(earlier) :])

        args = [
            pltpu.with_memory_space_constraint(v, pltpu.HBM)
            if (i in far_in and not aliases) or i in pinned
            else v
            for i, v in enumerate(args)
        ]
        specs = [_ANY if i in far_in else _VMEM for i in range(n_smem, count)]
        return pl.pallas_call(
            body,
            out_shape=[
                pltpu.HBM(s, t) if i in far_out and not aliases else jax.ShapeDtypeStruct(s, t)
                for i, (s, t) in enumerate(outs)
            ],
            in_specs=[_SMEM] * n_smem + specs + [_ANY] * len(earlier),
            out_specs=[_ANY if i in far_out else _VMEM for i in range(len(outs))],
            scratch_shapes=list(scratch),
            input_output_aliases=aliases or {},
            compiler_params=pltpu.CompilerParams(vmem_limit_bytes=limit),
            cost_estimate=pl.CostEstimate(flops=flops, bytes_accessed=0, transcendentals=0),
        )(*args, *earlier)

    return run


def copies(pairs, sems):
    return [pltpu.make_async_copy(a, b, sems.at[i]) for i, (a, b) in enumerate(pairs)]


def after(v, *earlier):
    return call(
        lambda *refs: None,
        [(v.shape, v.dtype)],
        far_in=(0,),
        far_out=(0,),
        earlier=earlier,
        aliases={0: 0},
        limit=1024 * 1024,
    )(v)[0]


def start_all(items):
    for item in items:
        item.start()


def wait_all(items):
    for item in items:
        item.wait()


def plane_ranks(picks_ref, me, k, tokens):
    i = rows_of((RANK_ROWS, tokens))
    group, chip, block = i // 4, (i // 2) % 2, i % 2
    apart = jnp.where(group < 2, 2 * group + chip, 2 * chip + group - 2)
    local = jnp.where(group < 2, block, 2 + block)
    plane = (me // 4) ^ k
    number = plane * 16 + ((me % 4) ^ apart) * 4 + local
    member = jnp.zeros((RANK_ROWS, tokens), F32)
    for j in range(TOPB):
        member = member + flag(picks_ref[j : j + 1, :] == number)
    earlier = flag(rows_of((tokens, tokens)) < lanes((tokens, tokens)))
    rank = nn(member.astype(LOW), earlier.astype(LOW))
    return jnp.where(member > 0.5, rank, -1.0).astype(LOW)


def self_forward_kernel(
    lengths_ref,
    place_ref,
    x_ref,
    picks_ref,
    project_ref,
    output_ref,
    query_ref,
    bias_ref,
    gain_ref,
    shift_ref,
    heads_ref,
    soft_ref,
    attended_ref,
    unit_ref,
    scale_ref,
    first_ref,
    *rest,
):
    payload_refs, (project_scr, output_scr, query_scr, sems) = rest[:4], rest[4:]
    thirds = [slice(i * D, (i + 1) * D) for i in range(3)]
    fetch = copies(
        [(project_ref.at[:, at], project_scr.at[:, at]) for at in thirds]
        + [(output_ref, output_scr), (query_ref, query_scr)],
        sems,
    )
    start_all(fetch)
    tokens = x_ref.shape[0]
    bias = bias_ref[...].astype(F32)
    x = x_ref[...]
    for i, at in enumerate(thirds):
        fetch[i].wait()
        part = nn(x, project_scr[:, at])
        if i == 0:
            part = QUERY_SCALE * (part + bias[0:1])
        if i == 2:
            part = part + bias[1:2]
        heads_ref[:, at] = part.astype(LOW)
    place_row = lax.broadcasted_iota(jnp.int32, (2 * tokens, tokens), 0) % tokens
    place_col = lanes((2 * tokens, tokens))
    segment_row = jnp.zeros((2 * tokens, tokens), jnp.int32)
    segment_col = jnp.zeros((2 * tokens, tokens), jnp.int32)
    bound = 0
    for d in range(lengths_ref.shape[1]):
        bound = bound + lengths_ref[0, d]
        segment_row = segment_row + jnp.where(place_row >= bound, 1, 0)
        segment_col = segment_col + jnp.where(place_col >= bound, 1, 0)
    allowed = (segment_row == segment_col) & (place_row >= place_col)
    first, second = half_masks()
    for p in range(PAIRS):
        at = p * SLAB
        queries = two_heads(heads_ref[:, at : at + SLAB], first, second)
        scores = nt(queries, heads_ref[:, D + at : D + at + SLAB])
        scores = jnp.where(allowed, scores, MASKED)
        top = jnp.max(scores, axis=-1, keepdims=True)
        raised = jnp.exp(scores - top)
        soft = raised / jnp.sum(raised, axis=-1, keepdims=True)
        soft_ref[p] = soft
        mixed = nn(soft.astype(LOW), heads_ref[:, 2 * D + at : 2 * D + at + SLAB])
        attended_ref[:, at : at + SLAB] = join_heads(mixed, tokens).astype(LOW)
    fetch[3].wait()
    residual = x.astype(F32) + nn(attended_ref[...], output_scr[...]) + bias[2:3]
    normed, unit, scale = norm_forward(
        residual, gain_ref[0:1, :].astype(F32), shift_ref[0:1, :].astype(F32)
    )
    unit_ref[...] = unit
    scale_ref[...] = scale
    low = normed.astype(LOW)
    first_ref[...] = low
    fetch[4].wait()
    queries = (QUERY_SCALE * (nn(low, query_scr[...]) + bias[3:4])).astype(LOW)
    for k, out in enumerate(payload_refs):
        out[:tokens] = queries
        out[tokens:, tokens:] = jnp.zeros((RANK_ROWS, D - tokens), LOW)
        out[tokens:, :tokens] = plane_ranks(picks_ref, place_ref[0], k, tokens)


def piece_kernel(rows_ref, kept_ref, a_ref, b_ref):
    for h, out in enumerate((a_ref, b_ref)):
        out[: 2 * BLOCK] = rows_ref[2 * h * BLOCK : 2 * (h + 1) * BLOCK]
        marks = kept_ref[2 * h : 2 * h + 2, :].astype(F32)
        marks = jnp.concatenate([marks, jnp.zeros((MARK_ROWS - 2, BLOCK), F32)], axis=0)
        out[2 * BLOCK :, :BLOCK] = marks.astype(LOW)
        out[2 * BLOCK :, BLOCK:] = jnp.zeros((MARK_ROWS, D - BLOCK), LOW)


def pair_kernel(first_ref, second_ref, out_ref):
    out_ref[0] = first_ref[...]
    out_ref[1] = second_ref[...]


def memory_kernel(*refs):
    far = len(refs) > 12
    if far:
        pieces = [ref.at[j] for ref in refs[:2] for j in range(2)]
        near_pieces, (weight_ref, bias_ref), given = refs[2:6], refs[6:8], refs[8:14]
        outs, rows_ref, sems = refs[14:17], refs[17], refs[18]
        size = 2 * BLOCK
        pairs = []
        for s in range(2):
            for j in range(2):
                at = 8 * s * BLOCK + j * size
                pairs.append((near_pieces[2 * s + j].at[:size], rows_ref.at[at : at + size]))
                at = at + 4 * BLOCK
                pairs.append((pieces[2 * s + j].at[:size], rows_ref.at[at : at + size]))
        keep = copies(pairs, sems)
        start_all(keep)
    else:
        pieces, (weight_ref, bias_ref), outs = refs[:4], refs[4:6], refs[6:]
    bias = bias_ref[4:5, :].astype(F32)
    lane = lanes((MARK_ROWS, SLAB))
    place = lanes((BLOCK, SLAB))
    for s in range(2):
        if far:
            near, here = 8 * s, 8 * s + 4
            memory_ref, hidden_ref, side_ref = outs
            for out, ref in zip(outs, given[3 * s : 3 * s + 3]):
                out[near : near + 4] = ref[...]
        else:
            here = 0
            memory_ref, hidden_ref, side_ref = outs[3 * s : 3 * s + 3]
        for j in range(2):
            piece = pieces[2 * s + j]
            rows = piece[: 2 * BLOCK]
            first = here + 2 * j
            keys = nn(rows, weight_ref[:, :D]).astype(LOW)
            values = (nn(rows, weight_ref[:, D:]) + bias).astype(LOW)
            marks = piece[2 * BLOCK :, :SLAB]
            for l in range(2):
                at = first + l
                memory_ref[at, :, :D] = keys[l * BLOCK : (l + 1) * BLOCK]
                memory_ref[at, :, D:] = values[l * BLOCK : (l + 1) * BLOCK]
                hidden_ref[at] = (1.0 - marks[l : l + 1].astype(F32)) * MASKED
                wanted = flag((rows_of((MARK_ROWS, SLAB)) == l) & (lane == SLAB - 1))
                column = tn(marks, wanted.astype(LOW))
                side = jnp.where(place == SLAB - 1, (1.0 - column) * MASKED, 0.0)
                side_ref[at] = jnp.where(place < 48, -1.0, side).astype(LOW)
    if far:
        wait_all(keep)


def selection(ranks, capacity):
    parts = []
    wanted = rows_of((capacity, ranks.shape[1])).astype(F32)
    for b in range(ranks.shape[0]):
        parts.append(flag(ranks[b : b + 1, :] == wanted).astype(LOW))
    return jnp.concatenate(parts, axis=0)


def fill_slots(sel, rows, out_ref, k, capacity):
    got = nn(sel, rows).astype(LOW)
    for b in range(out_ref.shape[0]):
        out_ref[b, k * capacity : (k + 1) * capacity, :] = got[b * capacity : (b + 1) * capacity]


def around16(v, combine):
    for step in (16, 32, 64):
        v = combine(v, pltpu.roll(v, step, 1))
    return v


def put_side(ref, side, rows):
    tokens = side.shape[0]
    turned = side.astype(F32).T.astype(LOW)
    for q in range(PAIRS):
        ref[tokens:, q * SLAB : (q + 1) * SLAB] = turned[q * rows : (q + 1) * rows]


def get_side(ref, tokens):
    rows = ref.shape[0] - tokens
    parts = [ref[tokens:, q * SLAB : (q + 1) * SLAB].astype(F32) for q in range(PAIRS)]
    parts.append(jnp.zeros((SLAB - PAIRS * rows, SLAB), F32))
    return jnp.concatenate(parts, axis=0).T


def lse_lanes(lse):
    high = lse.astype(LOW).astype(F32)
    rest = lse - high
    mid = rest.astype(LOW).astype(F32)
    low = rest - mid
    lane = lanes(lse.shape)
    packed = jnp.where(
        lane < 16, high, jnp.where(lane < 32, mid, jnp.where(lane < 48, low, 0.0))
    )
    return packed.astype(LOW)


def head_spread(group):
    row = rows_of((SLAB, D))
    row = row % 16 if group else row
    return flag(row == lanes((SLAB, D)) // HEAD_DIM).astype(LOW)


def owner_forward_kernel(capacity, *refs):
    tokens_refs, memory_ref, hidden_ref = refs[0:4], refs[4], refs[5]
    far_slots_ref, out_scr, lse_scr, inv_scr, sel_scr, ranks_scr, slots_ref, sems = refs[6:]
    sources = len(tokens_refs)
    blocks, rows = slots_ref.shape[:2]
    tokens = tokens_refs[0].shape[0] - RANK_ROWS
    first, second = half_masks()
    for k in range(sources):
        ranks_scr[...] = tokens_refs[k][tokens:, :tokens].astype(F32)
        sel = selection(ranks_scr[...], capacity)
        sel_scr[k] = sel
        fill_slots(sel, tokens_refs[k][:tokens], slots_ref, k, capacity)
    keep = copies([(slots_ref, far_slots_ref)], sems)
    start_all(keep)
    ones = jnp.ones((BLOCK, SLAB), LOW)
    lane_of = lanes((rows, SLAB))
    def one_block(i, carry):
        hidden = hidden_ref[i]
        tops = jnp.zeros((rows, SLAB), F32)
        totals = jnp.ones((rows, SLAB), F32)
        base = (i % 8) * 16
        slabs = [slice(p * SLAB, (p + 1) * SLAB) for p in range(PAIRS)]
        scores = [
            nt(two_heads(slots_ref[i, :, at], first, second), memory_ref[i, :, at])
            + hidden
            for at in slabs
        ]
        highest = [jnp.max(v, axis=-1, keepdims=True) for v in scores]
        raised = [jnp.exp(v - top).astype(LOW) for v, top in zip(scores, highest)]
        mixed = [
            nn(v, jnp.concatenate([memory_ref[i, :, D + at.start : D + at.stop], ones], axis=1))
            for v, at in zip(raised, slabs)
        ]
        for p, at in enumerate(slabs):
            out_scr[i, :, at] = join_heads(mixed[p][:, :SLAB], rows)
            for half in range(2):
                here = slice(half * rows, (half + 1) * rows)
                mine = lane_of == base + 2 * p + half
                tops = jnp.where(mine, highest[p][here], tops)
                totals = jnp.where(mine, mixed[p][here, SLAB:], totals)
        own = flag((lane_of >= base) & (lane_of < base + HEADS))
        lse_scr[i] = tops + jnp.log(totals)
        inv_scr[i] = own / totals
        return carry

    lax.fori_loop(0, blocks, one_block, 0, unroll=UNROLL)
    wait_all(keep)


def merge_kernel(capacity, ks, value_ref, lse_ref, inv_ref, sel_ref, *payload_refs):
    tokens = sel_ref.shape[2]
    group = 8 * capacity
    own_low = flag(
        rows_of((group, SLAB)) // capacity == lanes((group, SLAB)) // 16
    ).astype(LOW)
    spread = head_spread(True)
    each = [(n, g) for n in range(len(ks)) for g in range(2)]

    def stacked(ref, n, g):
        here = slice(ks[n] * capacity, (ks[n] + 1) * capacity)
        return jnp.concatenate([ref[8 * g + b, here, :] for b in range(8)], axis=0)

    sels = {(n, g): sel_ref[ks[n], g * group : (g + 1) * group, :] for n, g in each}
    turned = {at: sels[at].T for at in each}
    found = {
        at: nn(turned[at], jnp.concatenate([*three(stacked(lse_ref, *at)), own_low], axis=1))
        for at in each
    }
    members = {at: found[at][:, 3 * SLAB :] for at in each}
    by_token = {
        at: jnp.where(
            members[at] > 0.5,
            found[at][:, :SLAB] + found[at][:, SLAB : 2 * SLAB] + found[at][:, 2 * SLAB : 3 * SLAB],
            MASKED,
        )
        for at in each
    }
    tops = [
        around16(jnp.maximum(by_token[n, 0], by_token[n, 1]), jnp.maximum) for n in range(len(ks))
    ]
    weights = {at: members[at] * jnp.exp(by_token[at] - tops[at[0]]) for at in each}
    totals = [around16(weights[n, 0] + weights[n, 1], jnp.add) for n in range(len(ks))]
    safes = [jnp.where(total > 0.5, total, 1.0) for total in totals]
    shares = {
        at: nn(sels[at], (weights[at] / safes[at[0]]).astype(LOW)) * stacked(inv_ref, *at)
        for at in each
    }
    wide = {at: nn(shares[at].astype(LOW), spread) for at in each}
    for n, out in enumerate(payload_refs):
        partial = sum(
            nn(turned[n, g], (stacked(value_ref, n, g) * wide[n, g]).astype(LOW)) for g in range(2)
        )
        out[:tokens] = partial.astype(LOW)
        lse = jnp.where(totals[n] > 0.5, tops[n] + jnp.log(safes[n]), MASKED)
        put_side(out, lse_lanes(lse), LSE_ROWS)


def select_grads_kernel(capacity, *refs):
    sel_ref, grad_refs, got_ref = refs[0], refs[1:5], refs[5]
    tokens = grad_refs[0].shape[0] - SIDE_ROWS
    for k, ref in enumerate(grad_refs):
        side = get_side(ref, tokens).astype(LOW)
        rows_all = jnp.concatenate([ref[:tokens], side], axis=1)
        fill_slots(sel_ref[k], rows_all, got_ref, k, capacity)


def owner_backward_kernel(capacity, *refs):
    sel_scr, got_scr, memory_ref, side_ref, slots_ref = refs[:5]
    out, payload_refs, query_scr = refs[5], refs[6:10], refs[10]
    sources = len(payload_refs)
    blocks, rows = slots_ref.shape[:2]
    first, second = half_masks()
    lane = lanes((1, SLAB))
    last = flag(lane == SLAB - 1).astype(LOW)
    value_side = jnp.broadcast_to(
        -flag((lane >= 48) & (lane < 96)).astype(LOW), (BLOCK, SLAB)
    )

    def picked(head, base):
        inside = (lane >= base) & (lane < base + 48)
        return flag(inside & (lane % 16 == head)).astype(LOW)

    def one_block(i, carry):
        side = got_scr[i, :, D:]
        key_side = side_ref[i]
        slabs = [slice(p * SLAB, (p + 1) * SLAB) for p in range(PAIRS)]
        keys = [memory_ref[i, :, at] for at in slabs]
        queries = [two_heads(slots_ref[i, :, at], first, second) for at in slabs]
        grads = [two_heads(got_scr[i, :, at], first, second) for at in slabs]
        scores, dots = [], []
        for p in range(PAIRS):
            lse_side = jnp.concatenate(
                [side * picked(2 * p + h, 0) + last for h in range(2)], axis=0
            )
            scores.append(
                nt(
                    jnp.concatenate([keys[p], key_side], axis=1),
                    jnp.concatenate([queries[p], lse_side], axis=1),
                )
            )
        for p, at in enumerate(slabs):
            delta_side = jnp.concatenate(
                [side * picked(2 * p + h, 48) for h in range(2)], axis=0
            )
            values = memory_ref[i, :, D + at.start : D + at.stop]
            dots.append(
                nt(
                    jnp.concatenate([values, value_side], axis=1),
                    jnp.concatenate([grads[p], delta_side], axis=1),
                )
            )
        softs = [jnp.exp(v) for v in scores]
        score_grads = [(soft * v).astype(LOW) for soft, v in zip(softs, dots)]
        for p, at in enumerate(slabs):
            query_scr[i, :, at] = join_heads(tn(score_grads[p], keys[p]), rows).astype(LOW)
        for p, at in enumerate(slabs):
            out[i, :, at] = nn(score_grads[p], queries[p]).astype(LOW)
        for p, at in enumerate(slabs):
            out[i, :, D + at.start : D + at.stop] = nn(softs[p].astype(LOW), grads[p]).astype(
                LOW
            )
        return carry

    lax.fori_loop(0, blocks, one_block, 0, unroll=UNROLL)
    for k in range(sources):
        here = slice(k * capacity, (k + 1) * capacity)
        value = jnp.concatenate([query_scr[b, here, :] for b in range(blocks)], axis=0)
        payload_refs[k][...] = tn(sel_scr[k], value).astype(LOW)


def memory_weight_kernel(count, place_ref, *refs):
    grad_ref, rows_ref, kept_ref, sent_ref, bias_ref, sum_scr = refs
    me, core = place_ref[0], place_ref[1]
    size = 4 * BLOCK
    sum_scr[...] = jnp.zeros(sum_scr.shape, F32)
    bias_ref[...] = jnp.zeros(bias_ref.shape, F32)

    def one_set(s, carry):
        at = pl.ds(pl.multiple_of(s * size, size), size)
        rows = rows_ref[at, :].T
        for h in range(2):
            sum_scr[h] = sum_scr[h] + nn(rows, grad_ref[at, h * D : (h + 1) * D])
        bias_ref[0:1] = bias_ref[0:1] + row_sum(grad_ref[at, D:].astype(F32))
        return carry

    lax.fori_loop(0, rows_ref.shape[0] // size, one_set, 0)
    block = D // count
    for h in range(2):

        def store(out, h=h):
            total = sum_scr[h].astype(LOW)
            for k in range(count):
                for u in range(D // UNIT):
                    out[me ^ k, u * block : (u + 1) * block, :] = total[
                        k * block : (k + 1) * block, u * UNIT : (u + 1) * UNIT
                    ]

        pl.when(core == h)(functools.partial(store, kept_ref))
        pl.when(core != h)(functools.partial(store, sent_ref))


def datastore_grad_kernel(weight_ref, *refs):
    grad_ref, outs = refs[0], refs[1:7]
    weight = weight_ref[...].T
    near_a0, near_a1, far_a, near_b0, near_b1, far_b = outs
    groups = ((near_a0, near_a1), (far_a,), (near_b0, near_b1), (far_b,))
    for s in range(4):
        value = nn(grad_ref[4 * s * BLOCK : 4 * (s + 1) * BLOCK], weight).astype(LOW)
        size = value.shape[0] // len(groups[s])
        for i, out in enumerate(groups[s]):
            out[...] = value[i * size : (i + 1) * size]


def datastore_step_kernel(*refs):
    ins, sends, keeps = refs[:6], refs[6:8], refs[8:10]
    size = 2 * BLOCK
    for g in range(2):
        stay, go, come = ins[3 * g : 3 * g + 3]
        keeps[g][...] = stay[...].astype(F32) + come[:size].astype(F32)
        sends[g][...] = (go[...].astype(F32) + come[size:].astype(F32)).astype(LOW)


def datastore_sum_kernel(keep_a, come_a, keep_b, come_b, out_ref):
    size = keep_a.shape[0]
    out_ref[:size] = keep_a[...] + come_a[...].astype(F32)
    out_ref[size:] = keep_b[...] + come_b[...].astype(F32)


def middle_kernel(
    p0_ref,
    p1_ref,
    p2_ref,
    p3_ref,
    first_ref,
    cotangent_ref,
    output_ref,
    expand_ref,
    contract_ref,
    bias_ref,
    expand_bias_ref,
    gain_ref,
    shift_ref,
    out_ref,
    merged_ref,
    second_ref,
    active_ref,
    branch_grad_ref,
    expanded_grad_ref,
    cross_grad_ref,
    resid_ref,
    payload_ref,
    small_ref,
    wide_ref,
    expanded_scr,
):
    output_scr, expand_scr, contract_scr = output_ref, expand_ref, contract_ref
    bias = bias_ref[...].astype(F32)
    gain = gain_ref[...].astype(F32)
    shift = shift_ref[...].astype(F32)
    parts = [p0_ref, p1_ref, p2_ref, p3_ref]
    tokens = first_ref.shape[0]
    lses = [around16(get_side(part, tokens), jnp.add) for part in parts]
    top = functools.reduce(jnp.maximum, lses)
    weights = [jnp.exp(lse - top) for lse in lses]
    total = functools.reduce(jnp.add, weights)
    overall = top + jnp.log(total)
    spread = head_spread(False)
    merged = jnp.zeros(first_ref.shape, F32)
    for part, weight in zip(parts, weights):
        share = weight / total
        high = share.astype(LOW)
        rest = (share - high.astype(F32)).astype(LOW)
        merged = merged + (nn(high, spread) + nn(rest, spread)) * part[:tokens].astype(F32)
    merged_low = merged.astype(LOW)
    merged_ref[...] = merged_low
    residual = first_ref[...].astype(F32) + nn(merged_low, output_scr[...]) + bias[5:6]
    second, unit_second, scale_second = norm_forward(residual, gain[1:2], shift[1:2])
    second_low = second.astype(LOW)
    second_ref[...] = second_low
    hidden = contract_scr.shape[0]
    for c in range(hidden // D):
        at = slice(c * D, (c + 1) * D)
        expanded = nn(second_low, expand_scr[:, at]) + expand_bias_ref[:, at].astype(F32)
        bell = 0.5 * (1.0 + lax.erf(expanded * 0.7071067811865476))
        active_ref[:, at] = (expanded * bell).astype(LOW)
        slope = bell + expanded * 0.3989422804014327 * jnp.exp(-0.5 * expanded * expanded)
        expanded_scr[:, at] = slope
    residual = second_low.astype(F32) + nn(active_ref[...], contract_scr[...]) + bias[6:7]
    final, unit_final, scale_final = norm_forward(residual, gain[2:3], shift[2:3])
    out_ref[...] = final.astype(LOW)
    cotangent = cotangent_ref[...].astype(F32)
    final_resid = norm_backward(cotangent, unit_final, scale_final, gain[2:3])
    branch_grad = final_resid.astype(LOW)
    branch_grad_ref[...] = branch_grad
    small_ref[0:1, :] = row_sum(branch_grad.astype(F32))
    small_ref[1:2, :] = row_sum(cotangent * unit_final)
    small_ref[2:3, :] = row_sum(cotangent)
    total_grad = final_resid
    for c in range(hidden // D):
        at = slice(c * D, (c + 1) * D)
        active_grad = nt(branch_grad, contract_scr[at, :])
        expanded_grad = (active_grad * expanded_scr[:, at]).astype(LOW)
        expanded_grad_ref[:, at] = expanded_grad
        wide_ref[:, at] = row_sum(expanded_grad.astype(F32))
        total_grad = total_grad + nt(expanded_grad, expand_scr[:, at])
    small_ref[4:5, :] = row_sum(total_grad * unit_second)
    small_ref[5:6, :] = row_sum(total_grad)
    second_resid = norm_backward(total_grad, unit_second, scale_second, gain[1:2])
    resid_ref[...] = second_resid
    cross_grad = second_resid.astype(LOW)
    cross_grad_ref[...] = cross_grad
    small_ref[3:4, :] = row_sum(cross_grad.astype(F32))
    small_ref[6:8, :] = jnp.zeros((2, D), F32)
    attended_grad = nt(cross_grad, output_scr[...]).astype(LOW)
    payload_ref[:tokens] = attended_grad
    product = attended_grad.astype(F32) * merged
    gather = flag(lanes((D, SLAB)) % 16 == rows_of((D, SLAB)) // HEAD_DIM).astype(LOW)
    high, mid, low = three(product)
    delta = nn(high, gather) + nn(mid, gather) + nn(low, gather)
    lane = lanes(overall.shape)
    packed = jnp.zeros(overall.shape, F32)
    for value, base in ((overall, 0), (delta, 48)):
        for i, piece in enumerate(three(value)):
            inside = (lane >= base + 16 * i) & (lane < base + 16 * i + HEADS)
            packed = jnp.where(inside, piece.astype(F32), packed)
    put_side(payload_ref, packed, SIDE_ROWS)


def self_backward_kernel(
    d0_ref,
    d1_ref,
    d2_ref,
    d3_ref,
    resid_ref,
    unit_ref,
    scale_ref,
    heads_ref,
    soft_ref,
    query_ref,
    output_ref,
    project_ref,
    gain_ref,
    pre_grad_ref,
    branch_grad_ref,
    project_grad_ref,
    input_grad_ref,
    small_ref,
    attended_scr,
):
    query_scr, output_scr, heads_scr = query_ref, output_ref, heads_ref
    soft_scr, project_scr = soft_ref, project_ref
    tokens = resid_ref.shape[0]
    query_sum = functools.reduce(
        jnp.add, [d[...].astype(F32) for d in (d0_ref, d1_ref, d2_ref, d3_ref)]
    ).astype(LOW)
    pre_grad = (query_sum.astype(F32) * QUERY_SCALE).astype(LOW)
    pre_grad_ref[...] = pre_grad
    total = resid_ref[...] + nt(pre_grad, query_scr[...])
    unit = unit_ref[...]
    first_resid = norm_backward(total, unit, scale_ref[...], gain_ref[0:1, :].astype(F32))
    branch_grad = first_resid.astype(LOW)
    branch_grad_ref[...] = branch_grad
    attended_scr[...] = nt(branch_grad, output_scr[...]).astype(LOW)
    first, second = half_masks()
    for p in range(PAIRS):
        at = p * SLAB
        grads = two_heads(attended_scr[:, at : at + SLAB], first, second)
        queries = two_heads(heads_scr[:, at : at + SLAB], first, second)
        keys = heads_scr[:, D + at : D + at + SLAB]
        dots = nt(grads, heads_scr[:, 2 * D + at : 2 * D + at + SLAB])
        soft = soft_scr[p]
        score_grad = (soft * (dots - jnp.sum(soft * dots, axis=-1, keepdims=True))).astype(LOW)
        query_grad = join_heads(nn(score_grad, keys), tokens).astype(LOW)
        project_grad_ref[:, at : at + SLAB] = (query_grad.astype(F32) * QUERY_SCALE).astype(LOW)
        project_grad_ref[:, D + at : D + at + SLAB] = tn(score_grad, queries).astype(LOW)
        project_grad_ref[:, 2 * D + at : 2 * D + at + SLAB] = tn(soft.astype(LOW), grads).astype(
            LOW
        )
    input_grad_ref[...] = first_resid + nt(project_grad_ref[...], project_scr[...])
    small_ref[0:1, :] = row_sum(project_grad_ref[:, :D].astype(F32))
    small_ref[1:2, :] = row_sum(project_grad_ref[:, 2 * D :].astype(F32))
    small_ref[2:3, :] = row_sum(branch_grad.astype(F32))
    small_ref[3:4, :] = row_sum(pre_grad.astype(F32))
    small_ref[4:5, :] = row_sum(total * unit)
    small_ref[5:6, :] = row_sum(total)
    small_ref[6:8, :] = jnp.zeros((2, D), F32)


def weight_grad_kernel(plan, count, packed, held, place_ref, *refs):
    kept_ref, sent_ref = refs[-2:]
    me, core = place_ref[0], place_ref[1]
    at_ref = 0
    for number, rows, columns, at in plan:
        pairs = [refs[at_ref + 2 * i : at_ref + 2 * i + 2] for i in range(number)]
        at_ref += 2 * number
        block = rows // count
        half = columns // 2
        steps = [(c, min(D, half - c)) for c in range(0, half, D)]

        def unit(m, c, wide, block=block, half=half, at=at, pairs=pairs):
            xs = [x_ref[:, pl.ds(pl.multiple_of(m * D, SLAB), D)].T for x_ref, _ in pairs]
            for mine, out in ((core, kept_ref), (1 - core, sent_ref)):
                start = pl.multiple_of(mine * half + c, SLAB)
                part = sum(nn(x, g_ref[:, pl.ds(start, wide)]) for x, (_, g_ref) in zip(xs, pairs))
                part = part.astype(LOW)
                for u in range(wide // UNIT):
                    low = pl.multiple_of(at + (c // UNIT + u) * block, 16)
                    for k in range(D // block):
                        to = me ^ (m * (D // block) + k)
                        out[to, pl.ds(low, block), :] = part[
                            k * block : (k + 1) * block, u * UNIT : (u + 1) * UNIT
                        ]

        if rows > D:
            for c, wide in steps:

                def by_rows(m, carry, c=c, wide=wide, unit=unit):
                    unit(m, c, wide)
                    return carry

                lax.fori_loop(0, rows // D, by_rows, 0)
        elif half % D == 0 and half > D:

            def by_columns(c, carry, unit=unit):
                unit(0, c * D, D)
                return carry

            lax.fori_loop(0, half // D, by_columns, 0)
        else:
            for c, wide in steps:
                unit(0, c, wide)
    if packed is not None:
        pack_small(refs[at_ref : at_ref + 4], kept_ref, sent_ref, packed, me, core, count)
        at_ref += 4
    if held:
        for ref, out in zip(refs[at_ref : at_ref + 2], (kept_ref, sent_ref)):
            out[:, :held, :] = ref[...]


def pack_small(small_refs, kept_ref, sent_ref, low, me, core, count):
    own, middle, value_bias, wide = small_refs
    order = [own[0:4], value_bias[0:1], middle[3:4], middle[0:1], own[4:5], middle[4:5]]
    order += [middle[1:2], own[5:6], middle[5:6], middle[2:3], jnp.zeros((3, D), F32)]
    narrow = jnp.concatenate(order, axis=0)
    share = D // count
    broad = wide.shape[1] // count
    for r in range(count):
        first = narrow[:, r * share : (r + 1) * share]
        first = jnp.concatenate([first, jnp.zeros((RANK_ROWS, UNIT - share), F32)], axis=1)
        second = wide[:, r * broad : (r + 1) * broad]
        second = jnp.concatenate([second, jnp.zeros((1, UNIT - broad), F32)], axis=1)
        second = jnp.broadcast_to(second, (RANK_ROWS, UNIT))
        here = slice(low, low + RANK_ROWS)
        kept_ref[me ^ r, here, :] = jnp.where(core == 0, first, second).astype(LOW)
        sent_ref[me ^ r, here, :] = jnp.where(core == 0, second, first).astype(LOW)


def total_of(*refs):
    return functools.reduce(jnp.add, [ref[...].astype(F32) for ref in refs])


def split_kernel(x, kept_ref, come_ref, *refs):
    far, outs = ((), refs) if x else (refs[:2], refs[2:])
    half = kept_ref.shape[3] // 2
    for z in range(4):
        for g in range(2):
            at = (z, slice(None), x, slice(0, half)) if g == 0 else (z, x, slice(None), slice(half, 2 * half))
            total = kept_ref[at].astype(F32) + come_ref[at].astype(F32)
            if far:
                total = total + far[g][z].astype(F32)
                for i in range(2):
                    outs[2 * g + i][z] = total[i].astype(LOW)
            else:
                outs[g][z] = total.astype(LOW)


def join_kernel(a_keep, a_come, b_keep, b_come, *outs):
    rows = a_keep.shape[1]
    for z, out in enumerate(outs):
        out[:rows] = total_of(a_keep.at[z], a_come.at[z]).astype(LOW)
        out[rows:] = total_of(b_keep.at[z], b_come.at[z]).astype(LOW)


def sum_kernel(*refs):
    refs[-1][...] = total_of(*refs[:-1]).astype(LOW)


def spread_kernel(plan, count, packed, place_ref, own_ref, other_ref, *outs):
    core = place_ref[1]
    outs[-1][...] = jnp.zeros(outs[-1].shape, F32)
    for (rows, columns, at), out in zip(plan, outs):
        block = rows // count
        half = columns // 2
        for c in range(half // UNIT):
            low = at + c * block
            for value, mine in ((own_ref, core), (other_ref, 1 - core)):
                start = pl.multiple_of(mine * half + c * UNIT, SLAB)
                out[:, pl.ds(start, UNIT)] = value[low : low + block].astype(F32)
    if packed is not None:
        here = slice(packed, packed + RANK_ROWS)
        own, other = own_ref[here].astype(F32), other_ref[here].astype(F32)
        narrow, wide = jnp.where(core == 0, own, other), jnp.where(core == 0, other, own)
        biases_ref, wide_ref, gain_ref, shift_ref = outs[len(plan) : -1]
        share = biases_ref.shape[1]
        biases_ref[...] = narrow[0:7, :share]
        gain_ref[...] = narrow[7:10, :share]
        shift_ref[...] = narrow[10:13, :share]
        wide_ref[...] = wide[0:1, : wide_ref.shape[1]]


def swap(v, bits):
    count = lax.axis_size("store")
    return lax.ppermute(v, "store", [(i, i ^ bits) for i in range(count)])


def swap_core(v):
    return lax.ppermute(v, "dp", [(0, 1), (1, 0)])


class WeightSums:
    def __init__(self, place, count, rows):
        self.place, self.count, self.rows = place, count, rows
        self.plan, self.packed, self.at = [], None, 0
        self.buffers = ()

    def add(self, products, small=None, earlier=(), flops=0):
        plan, base, packed = [], self.at, None
        for pairs in products:
            rows, columns = pairs[0][0].shape[1], pairs[0][1].shape[1]
            plan.append((len(pairs), rows, columns, self.at))
            self.plan.append((rows, columns, self.at))
            self.at += rows // self.count * (columns // 2 // UNIT)
        args = [v for pairs in products for pair in pairs for v in pair]
        if small is not None:
            packed = self.packed = self.at
            self.at += RANK_ROWS
            args.extend(small)
        shape = (self.count, self.rows, UNIT)
        self.buffers = call(
            functools.partial(weight_grad_kernel, tuple(plan), self.count, packed, base),
            [(shape, LOW), (shape, LOW)],
            n_smem=1,
            earlier=earlier,
            flops=flops,
        )(self.place, *args, *self.buffers)
        return self.buffers

    def split(self, x, far=(), earlier=()):
        half = (4, 2, self.rows // 2, UNIT)
        outs = [half[:1] + half[2:]] * 4 if far else [half] * 2
        args = [v.reshape(4, 2, 2, self.rows, UNIT) for v in (self.kept, self.come)] + list(far)
        return call(
            functools.partial(split_kernel, x),
            [(shape, LOW) for shape in outs],
            earlier=earlier,
            limit=SMALL_LIMIT,
        )(*args)

    def start(self, earlier=()):
        self.kept, sent = self.buffers
        self.come = swap_core(sent)
        self.sent = self.split(1, earlier=earlier)
        return self.sent

    def first(self, *earlier):
        come = (swap(self.sent[0], 1), swap(self.sent[1], 2))
        a_keep, a_send, b_keep, b_send = self.split(0, come, earlier)
        self.kept, self.sent = (a_keep, b_keep), (a_send, b_send)
        return self.sent

    def second(self, *earlier):
        come = (swap(self.sent[0], 2), swap(self.sent[1], 1))
        self.w = call(
            join_kernel, [((self.rows, UNIT), LOW)] * 4, earlier=earlier, limit=SMALL_LIMIT
        )(self.kept[0], come[0], self.kept[1], come[1])
        return self.w

    def third(self, *earlier):
        come = [swap(self.w[k], 4 * k) for k in (1, 2, 3)]
        (self.own,) = call(
            sum_kernel, [(come[0].shape, LOW)], earlier=earlier, limit=SMALL_LIMIT
        )(self.w[0], *come)
        return self.own

    def finish(self, small=()):
        other = swap_core(self.own)
        shapes = [((rows // self.count, columns), F32) for rows, columns, _ in self.plan]
        shapes += [(shape, F32) for shape in (*small, (8, SLAB))]
        return call(
            functools.partial(spread_kernel, tuple(self.plan), self.count, self.packed),
            shapes,
            n_smem=1,
            limit=SMALL_LIMIT,
        )(self.place, self.own, other)


def local_tree(
    inputs,
    doc_lengths,
    datastore,
    kept_mask,
    retrieved,
    self_project,
    self_output,
    cross_query,
    cross_memory,
    cross_output,
    expand_weight,
    contract_weight,
    biases,
    expand_bias,
    norm_gain,
    norm_shift,
    cotangent,
):
    tokens = inputs.shape[0]
    count = lax.axis_size("store")
    local_blocks = datastore.shape[0] // BLOCK
    all_blocks = local_blocks * count
    capacity = 2 * tokens * TOPB // all_blocks
    plane_blocks = 4 * local_blocks
    rows_in = 4 * capacity
    hidden = expand_weight.shape[1]
    me = lax.axis_index("store").astype(jnp.int32)
    core = lax.axis_index("dp").astype(jnp.int32)
    place = jnp.stack([me, core])

    piece = ((2 * BLOCK + MARK_ROWS, D), LOW)
    a0, b0 = call(piece_kernel, [piece] * 2, pinned=(0, 1))(datastore, kept_mask.reshape(local_blocks, BLOCK))
    a1, b1 = swap(a0, 1), swap(b0, 2)
    heads_all, soft_self, attended, unit_first, scale_first, first_low, *queries = call(
        self_forward_kernel,
        [
            ((tokens, 3 * D), LOW),
            ((PAIRS, 2 * tokens, tokens), F32),
            ((tokens, D), LOW),
            ((tokens, D), F32),
            ((tokens, 1), F32),
            ((tokens, D), LOW),
        ]
        + [((tokens + RANK_ROWS, D), LOW)] * 4,
        scratch=[
            pltpu.VMEM((D, 3 * D), LOW),
            pltpu.VMEM((D, D), LOW),
            pltpu.VMEM((D, D), LOW),
            pltpu.SemaphoreType.DMA((5,)),
        ],
        n_smem=2,
        far_in=(4, 5, 6),
        pinned=(2, 3, 7, 8, 9),
        flops=8 * MICROSECOND,
    )(
        doc_lengths,
        place,
        inputs,
        retrieved.T,
        self_project,
        self_output,
        cross_query,
        biases,
        norm_gain,
        norm_shift,
    )
    pair = call(pair_kernel, [((2, *piece[0]), LOW)], earlier=(first_low,))
    ay, bx = swap(pair(a0, a1)[0], 2), swap(pair(b0, b1)[0], 1)
    queries = [queries[0]] + [swap(queries[k], 4 * k) for k in (1, 2, 3)]

    def of_blocks(blocks):
        return [
            ((blocks, BLOCK, 2 * D), LOW),
            ((blocks, 1, BLOCK), F32),
            ((blocks, BLOCK, SLAB), LOW),
        ]

    near = call(memory_kernel, of_blocks(4) * 2)(a0, a1, b0, b1, cross_memory, biases)
    memory, hidden_rows, key_side, stored = call(
        memory_kernel,
        of_blocks(plane_blocks) + [((plane_blocks * BLOCK, D), LOW)],
        scratch=[pltpu.SemaphoreType.DMA((8,))],
        far_out=(3,),
    )(ay, bx, a0, a1, b0, b1, cross_memory, biases, *near)

    slots, values, lses, inverses, sel = call(
        functools.partial(owner_forward_kernel, capacity),
        [
            ((plane_blocks, rows_in, D), LOW),
            ((plane_blocks, rows_in, D), F32),
            ((plane_blocks, rows_in, SLAB), F32),
            ((plane_blocks, rows_in, SLAB), F32),
            ((4, plane_blocks * capacity, tokens), LOW),
        ],
        scratch=[
            pltpu.VMEM((RANK_ROWS, tokens), F32),
            pltpu.VMEM((plane_blocks, rows_in, D), LOW),
            pltpu.SemaphoreType.DMA((1,)),
        ],
        far_out=(0,),
        flops=20 * MICROSECOND,
    )(*queries, memory, hidden_rows)
    payload = ((tokens + LSE_ROWS, D), LOW)
    payloads = call(functools.partial(merge_kernel, capacity, (1, 2, 3)), [payload] * 3)(
        values, lses, inverses, sel
    )
    payloads = (
        call(
            functools.partial(merge_kernel, capacity, (0,)), [payload], earlier=(payloads[0],)
        )(values, lses, inverses, sel)
        + payloads
    )
    parts = [payloads[0]] + [swap(payloads[k], 4 * k) for k in (1, 2, 3)]

    (
        outputs,
        merged_low,
        second_low,
        active_low,
        branch_grad,
        expanded_grad,
        cross_grad,
        second_resid,
        payload,
        small_middle,
        wide_bias,
    ) = call(
        middle_kernel,
        [
            ((tokens, D), LOW),
            ((tokens, D), LOW),
            ((tokens, D), LOW),
            ((tokens, hidden), LOW),
            ((tokens, D), LOW),
            ((tokens, hidden), LOW),
            ((tokens, D), LOW),
            ((tokens, D), F32),
            ((tokens + SIDE_ROWS, D), LOW),
            ((8, D), F32),
            ((1, hidden), F32),
        ],
        scratch=[
            pltpu.VMEM((tokens, hidden), F32),
        ],
        flops=12 * MICROSECOND,
    )(
        *parts,
        first_low,
        cotangent,
        cross_output,
        expand_weight,
        contract_weight,
        biases,
        expand_bias.reshape(1, hidden),
        norm_gain,
        norm_shift,
    )
    grads = [payload] + [swap(payload, 4 * k) for k in (1, 2, 3)]

    early = WeightSums(place, count, 432)
    early.add(
        [[(active_low, branch_grad)], [(merged_low, cross_grad)], [(second_low, expanded_grad)]],
        flops=8 * MICROSECOND,
    )
    early_start = early.start()

    (got,) = call(
        functools.partial(select_grads_kernel, capacity),
        [((plane_blocks, rows_in, D + SLAB), LOW)],
        flops=4 * LONG,
    )(sel, *grads)
    out = call(
        functools.partial(owner_backward_kernel, capacity),
        [((plane_blocks, BLOCK, 2 * D), LOW)] + [((tokens, D), LOW)] * 4,
        scratch=[pltpu.VMEM((plane_blocks, rows_in, D), LOW)],
        earlier=early_start,
        flops=LONG,
    )(sel, got, memory, key_side, slots)
    memory_grad, query_grads = out[0], out[1:5]
    parts = [query_grads[0]] + [swap(query_grads[k], 4 * k) for k in (1, 2, 3)]

    late = WeightSums(place, count, 352)
    flat_grad = memory_grad.reshape(plane_blocks * BLOCK, 2 * D)
    *late.buffers, value_bias_grad = call(
        functools.partial(memory_weight_kernel, count),
        [((count, 2 * D // count, UNIT), LOW)] * 2 + [((8, D), F32)],
        scratch=[pltpu.VMEM((2, D, D), F32)],
        n_smem=1,
        flops=MICROSECOND // 10,
    )(place, flat_grad, stored)
    early_first = early.first(late.buffers[0])
    late.plan, late.at = [(D, 2 * D, 0)], 2 * D // count

    pre_grad, self_branch_grad, project_grad, input_grad, small_self = call(
        self_backward_kernel,
        [
            ((tokens, D), LOW),
            ((tokens, D), LOW),
            ((tokens, 3 * D), LOW),
            ((tokens, D), F32),
            ((8, D), F32),
        ],
        scratch=[
            pltpu.VMEM((tokens, D), LOW),
        ],
        earlier=early_first,
        flops=LONG // 3,
    )(
        *parts,
        second_resid,
        unit_first,
        scale_first,
        heads_all,
        soft_self,
        cross_query,
        self_output,
        self_project,
        norm_gain,
    )
    early_second = early.second()
    late.add(
        [[(attended, self_branch_grad)], [(first_low, pre_grad)], [(inputs, project_grad)]],
        (small_self, small_middle, value_bias_grad, wide_bias),
        flops=MICROSECOND // 10,
    )
    near_a0, near_a1, far_a, near_b0, near_b1, far_b = call(
        datastore_grad_kernel,
        [((2 * BLOCK, D), LOW), ((2 * BLOCK, D), LOW), ((4 * BLOCK, D), LOW)] * 2,
        earlier=(late.buffers[0],),
        flops=4 * LONG,
    )(cross_memory, flat_grad)
    late.start(earlier=(far_a, early_second[0]))
    late_first = late.first()
    early.third(late_first[0])
    contract_weight_grad, cross_output_grad, expand_weight_grad, ended = early.finish()
    late.second(ended)
    far_a, far_b = (after(v, late.w[0]) for v in (far_a, far_b))
    come_a, come_b = swap(far_a, 2), swap(far_b, 1)
    quarter = (2 * BLOCK, D)
    send_a, send_b, keep_a, keep_b = call(
        datastore_step_kernel, [(quarter, LOW)] * 2 + [(quarter, F32)] * 2, limit=SMALL_LIMIT
    )(near_a0, near_a1, come_a, near_b0, near_b1, come_b)
    (datastore_grad,) = call(
        datastore_sum_kernel, [((4 * BLOCK, D), F32)], limit=SMALL_LIMIT
    )(keep_a, swap(send_a, 1), keep_b, swap(send_b, 2))
    late.third(send_a)
    share = D // count
    (
        cross_memory_grad,
        self_output_grad,
        cross_query_grad,
        self_project_grad,
        biases_grad,
        wide_grad,
        gain_grad,
        shift_grad,
        _,
    ) = late.finish([(7, share), (1, hidden // count), (3, share), (3, share)])
    return (
        outputs,
        input_grad,
        datastore_grad,
        self_project_grad,
        self_output_grad,
        cross_query_grad,
        cross_memory_grad,
        cross_output_grad,
        expand_weight_grad,
        contract_weight_grad,
        biases_grad,
        wide_grad.reshape(hidden // count),
        gain_grad,
        shift_grad,
    )


def layer_norm(residual, gain_row, shift_row):
    center = residual - jnp.mean(residual, axis=-1, keepdims=True)
    spread = jnp.mean(center * center, axis=-1, keepdims=True)
    return center * lax.rsqrt(spread + EPSILON) * gain_row + shift_row


def doc_mask(lengths, seq_tokens):
    upto = jnp.tri(lengths.shape[-1], dtype=jnp.int32)
    bounds = jnp.sum(lengths[..., None, :] * upto, axis=-1)
    places = jnp.arange(seq_tokens, dtype=jnp.int32)
    segment = jnp.sum((places[:, None] >= bounds[..., None, :]).astype(jnp.int32), axis=-1)
    causal = places[:, None] >= places[None, :]
    return (segment[..., :, None] == segment[..., None, :]) & causal


def slot_numbers(picks, capacity):
    flat_ids = picks.reshape(-1)
    sorter = jnp.argsort(flat_ids, stable=True)
    sorted_ids = flat_ids[sorter]
    first_seen = jnp.searchsorted(sorted_ids, sorted_ids, side="left")
    rank_sorted = jnp.arange(flat_ids.shape[0], dtype=jnp.int32) - first_seen
    ranks = jnp.zeros_like(flat_ids).at[sorter].set(rank_sorted)
    return flat_ids * capacity + ranks


def place_rows(rows, slot_ids, total_slots, store_count, local_blocks, capacity):
    placed = jnp.zeros((total_slots, rows.shape[1]), rows.dtype).at[slot_ids].set(rows)
    return placed.reshape(store_count, local_blocks, capacity, rows.shape[1])


def local_slots(
    inputs,
    doc_lengths,
    datastore,
    kept_mask,
    retrieved,
    self_project,
    self_output,
    cross_query,
    cross_memory,
    cross_output,
    expand_weight,
    contract_weight,
    biases,
    expand_bias,
    norm_gain,
    norm_shift,
    cotangent,
):
    tok_count = inputs.shape[0]
    store_count = lax.axis_size("store")
    local_blocks = datastore.shape[0] // BLOCK
    all_blocks = local_blocks * store_count
    capacity = 2 * tok_count * TOPB // all_blocks
    rows_in = store_count * capacity
    total_slots = all_blocks * capacity
    gain_rows = norm_gain.astype(jnp.float32)
    shift_rows = norm_shift.astype(jnp.float32)
    bias_rows = biases.astype(jnp.float32)
    projected = jnp.dot(inputs, self_project, preferred_element_type=jnp.float32)
    heads_all = jnp.concatenate(
        [
            QUERY_SCALE * (projected[:, :D] + bias_rows[0]),
            projected[:, D : 2 * D],
            projected[:, 2 * D :] + bias_rows[1],
        ],
        axis=1,
    ).astype(jnp.bfloat16)
    queries = heads_all[:, :D].reshape(tok_count, HEADS, HEAD_DIM)
    keys_self = heads_all[:, D : 2 * D].reshape(tok_count, HEADS, HEAD_DIM)
    values_self = heads_all[:, 2 * D :].reshape(tok_count, HEADS, HEAD_DIM)
    allowed = doc_mask(doc_lengths[0], tok_count)

    def self_scores():
        raw_scores = jnp.einsum(
            "qhd,khd->hqk", queries, keys_self, preferred_element_type=jnp.float32
        )
        return jnp.where(allowed[None], raw_scores, MASKED)

    scores = self_scores()
    self_lse = jax.nn.logsumexp(scores, axis=-1)
    soft_low = jnp.exp(scores - self_lse[..., None]).astype(jnp.bfloat16)
    attended = (
        jnp.einsum("hqk,khd->qhd", soft_low, values_self, preferred_element_type=jnp.float32)
        .reshape(tok_count, D)
        .astype(jnp.bfloat16)
    )
    self_branch = jnp.dot(attended, self_output, preferred_element_type=jnp.float32) + bias_rows[2]
    first_norm, first_back = jax.vjp(
        layer_norm, inputs.astype(jnp.float32) + self_branch, gain_rows[0], shift_rows[0]
    )
    first_low = first_norm.astype(jnp.bfloat16)
    cross_queries = (
        QUERY_SCALE
        * (jnp.dot(first_low, cross_query, preferred_element_type=jnp.float32) + bias_rows[3])
    ).astype(jnp.bfloat16)
    slot_ids = slot_numbers(retrieved, capacity)
    send_buffer = place_rows(
        jnp.repeat(cross_queries, TOPB, axis=0),
        slot_ids,
        total_slots,
        store_count,
        local_blocks,
        capacity,
    )
    arrived = lax.all_to_all(send_buffer, "store", split_axis=0, concat_axis=2, tiled=True)
    owner_queries = arrived[0].reshape(local_blocks, rows_in, HEADS, HEAD_DIM)
    memory_bias = jnp.concatenate([jnp.zeros((D,), jnp.float32), bias_rows[4]])
    memory_low = (
        jnp.dot(datastore, cross_memory, preferred_element_type=jnp.float32) + memory_bias
    ).astype(jnp.bfloat16)
    memory_blocks = memory_low.reshape(local_blocks, BLOCK, 2 * D)
    store_keys = memory_blocks[:, :, :D].reshape(local_blocks, BLOCK, HEADS, HEAD_DIM)
    store_values = memory_blocks[:, :, D:].reshape(local_blocks, BLOCK, HEADS, HEAD_DIM)
    kept_rows = kept_mask.reshape(local_blocks, BLOCK) > 0

    def block_scores(query_blocks):
        raw_scores = jnp.einsum(
            "bmhd,bkhd->bhmk", query_blocks, store_keys, preferred_element_type=jnp.float32
        )
        return jnp.where(kept_rows[:, None, None, :], raw_scores, MASKED)

    owner_scores = block_scores(owner_queries)
    owner_lse = jax.nn.logsumexp(owner_scores, axis=-1)
    owner_soft = jnp.exp(owner_scores - owner_lse[..., None]).astype(jnp.bfloat16)
    partial_value = jnp.einsum(
        "bhmk,bkhd->bmhd", owner_soft, store_values, preferred_element_type=jnp.float32
    ).reshape(local_blocks, rows_in, D)
    partial_lse = jnp.transpose(owner_lse, (0, 2, 1))
    returned, returned_lse = (
        lax.all_to_all(partial_value[None], "store", split_axis=2, concat_axis=0, tiled=True),
        lax.all_to_all(partial_lse[None], "store", split_axis=2, concat_axis=0, tiled=True),
    )
    picked = returned.reshape(total_slots, D)[slot_ids].reshape(tok_count, TOPB, HEADS, HEAD_DIM)
    picked_lse = returned_lse.reshape(total_slots, HEADS)[slot_ids].reshape(tok_count, TOPB, HEADS)
    overall = jax.nn.logsumexp(picked_lse, axis=1)
    mix_weights = jnp.exp(picked_lse - overall[:, None, :])
    merged = jnp.einsum(
        "tjh,tjhd->thd", mix_weights, picked, precision=lax.Precision.HIGHEST
    ).reshape(tok_count, D)
    merged_low = merged.astype(jnp.bfloat16)
    cross_branch = (
        jnp.dot(merged_low, cross_output, preferred_element_type=jnp.float32) + bias_rows[5]
    )
    second_norm, second_back = jax.vjp(
        layer_norm, first_low.astype(jnp.float32) + cross_branch, gain_rows[1], shift_rows[1]
    )
    second_low = second_norm.astype(jnp.bfloat16)
    expanded = jnp.dot(
        second_low, expand_weight, preferred_element_type=jnp.float32
    ) + expand_bias.astype(jnp.float32)
    activated, gelu_back = jax.vjp(
        lambda pre_act: jax.nn.gelu(pre_act, approximate=False), expanded
    )
    activated_low = activated.astype(jnp.bfloat16)
    ffn_branch = (
        jnp.dot(activated_low, contract_weight, preferred_element_type=jnp.float32) + bias_rows[6]
    )
    final_norm, final_back = jax.vjp(
        layer_norm, second_low.astype(jnp.float32) + ffn_branch, gain_rows[2], shift_rows[2]
    )
    outputs = final_norm.astype(jnp.bfloat16)
    final_resid, final_gain, final_shift = final_back(cotangent.astype(jnp.float32))
    ffn_branch_grad = final_resid.astype(jnp.bfloat16)
    contract_weight_grad = jnp.dot(
        activated_low.T, ffn_branch_grad, preferred_element_type=jnp.float32
    )
    activated_grad = jnp.dot(ffn_branch_grad, contract_weight.T, preferred_element_type=jnp.float32)
    (expanded_raw,) = gelu_back(activated_grad)
    expanded_grad = expanded_raw.astype(jnp.bfloat16)
    expand_weight_grad = jnp.dot(second_low.T, expanded_grad, preferred_element_type=jnp.float32)
    expand_bias_grad = jnp.sum(expanded_grad.astype(jnp.float32), axis=0)
    second_total = final_resid + jnp.dot(
        expanded_grad, expand_weight.T, preferred_element_type=jnp.float32
    )
    second_resid, second_gain, second_shift = second_back(second_total)
    cross_branch_grad = second_resid.astype(jnp.bfloat16)
    cross_output_grad = jnp.dot(merged_low.T, cross_branch_grad, preferred_element_type=jnp.float32)
    attended_grad = jnp.dot(
        cross_branch_grad, cross_output.T, preferred_element_type=jnp.float32
    ).astype(jnp.bfloat16)
    delta_rows = jnp.sum(
        attended_grad.reshape(tok_count, HEADS, HEAD_DIM).astype(jnp.float32)
        * merged.reshape(tok_count, HEADS, HEAD_DIM),
        axis=-1,
    )
    grad_buffer = place_rows(
        jnp.repeat(attended_grad, TOPB, axis=0),
        slot_ids,
        total_slots,
        store_count,
        local_blocks,
        capacity,
    )
    overall_buffer = place_rows(
        jnp.repeat(overall, TOPB, axis=0),
        slot_ids,
        total_slots,
        store_count,
        local_blocks,
        capacity,
    )
    delta_buffer = place_rows(
        jnp.repeat(delta_rows, TOPB, axis=0),
        slot_ids,
        total_slots,
        store_count,
        local_blocks,
        capacity,
    )
    arrived_grad = lax.all_to_all(grad_buffer, "store", split_axis=0, concat_axis=2, tiled=True)
    arrived_overall, arrived_delta = (
        lax.all_to_all(overall_buffer, "store", split_axis=0, concat_axis=2, tiled=True),
        lax.all_to_all(delta_buffer, "store", split_axis=0, concat_axis=2, tiled=True),
    )
    owner_grad = arrived_grad[0].reshape(local_blocks, rows_in, HEADS, HEAD_DIM)
    overall_heads = jnp.transpose(arrived_overall[0], (0, 2, 1))
    delta_heads = jnp.transpose(arrived_delta[0], (0, 2, 1))
    soft_again = jnp.exp(block_scores(owner_queries) - owner_lse[..., None])
    soft_again_low = soft_again.astype(jnp.bfloat16).astype(jnp.float32)
    weight_mix = jnp.exp(owner_lse - overall_heads)
    value_dots = jnp.einsum(
        "bmhd,bkhd->bhmk", owner_grad, store_values, preferred_element_type=jnp.float32
    )
    exact_sum = jnp.sum(soft_again * value_dots, axis=-1, keepdims=True)
    rounded_sum = jnp.sum(soft_again_low * value_dots, axis=-1, keepdims=True)
    score_grad = (
        weight_mix[..., None]
        * soft_again
        * (value_dots - exact_sum + rounded_sum - delta_heads[..., None])
    ).astype(jnp.bfloat16)
    query_grad = (
        jnp.einsum("bhmk,bkhd->bmhd", score_grad, store_keys, preferred_element_type=jnp.float32)
        .astype(jnp.bfloat16)
        .reshape(local_blocks, rows_in, D)
    )
    key_grad = jnp.einsum(
        "bhmk,bmhd->bkhd", score_grad, owner_queries, preferred_element_type=jnp.float32
    )
    weighted_soft = weight_mix[..., None] * soft_again_low
    value_grad = jnp.einsum(
        "bhmk,bmhd->bkhd",
        weighted_soft,
        owner_grad.astype(jnp.float32),
        precision=lax.Precision.HIGHEST,
    )
    row_count = local_blocks * BLOCK
    memory_grad = jnp.concatenate(
        [key_grad.reshape(row_count, D), value_grad.reshape(row_count, D)], axis=1
    ).astype(jnp.bfloat16)
    cross_memory_grad = jnp.dot(datastore.T, memory_grad, preferred_element_type=jnp.float32)
    value_bias_grad = jnp.sum(memory_grad[:, D:].astype(jnp.float32), axis=0)
    datastore_grad = jnp.dot(memory_grad, cross_memory.T, preferred_element_type=jnp.float32)
    returned_grad = lax.all_to_all(
        query_grad[None], "store", split_axis=2, concat_axis=0, tiled=True
    )
    per_pick = returned_grad.reshape(total_slots, D)[slot_ids].reshape(tok_count, TOPB, D)
    query_sum = jnp.sum(per_pick.astype(jnp.float32), axis=1).astype(jnp.bfloat16)
    cross_pre_grad = (query_sum.astype(jnp.float32) * QUERY_SCALE).astype(jnp.bfloat16)
    cross_query_grad = jnp.dot(first_low.T, cross_pre_grad, preferred_element_type=jnp.float32)
    first_total = second_resid + jnp.dot(
        cross_pre_grad, cross_query.T, preferred_element_type=jnp.float32
    )
    first_resid, first_gain, first_shift = first_back(first_total)
    self_branch_grad = first_resid.astype(jnp.bfloat16)
    self_output_grad = jnp.dot(attended.T, self_branch_grad, preferred_element_type=jnp.float32)
    self_attended_grad = (
        jnp.dot(self_branch_grad, self_output.T, preferred_element_type=jnp.float32)
        .astype(jnp.bfloat16)
        .reshape(tok_count, HEADS, HEAD_DIM)
    )
    soft_self = jnp.exp(self_scores() - self_lse[..., None])
    soft_dots = jnp.einsum(
        "qhd,khd->hqk", self_attended_grad, values_self, preferred_element_type=jnp.float32
    )
    self_score_grad = (
        soft_self * (soft_dots - jnp.sum(soft_self * soft_dots, axis=-1, keepdims=True))
    ).astype(jnp.bfloat16)
    query_self_grad = jnp.einsum(
        "hqk,khd->qhd", self_score_grad, keys_self, preferred_element_type=jnp.float32
    ).reshape(tok_count, D)
    key_self_grad = jnp.einsum(
        "hqk,qhd->khd", self_score_grad, queries, preferred_element_type=jnp.float32
    ).reshape(tok_count, D)
    value_self_grad = jnp.einsum(
        "hqk,qhd->khd", soft_low, self_attended_grad, preferred_element_type=jnp.float32
    ).reshape(tok_count, D)
    heads_grad = jnp.concatenate([query_self_grad, key_self_grad, value_self_grad], axis=1).astype(
        jnp.bfloat16
    )
    project_grad = jnp.concatenate(
        [
            (heads_grad[:, :D].astype(jnp.float32) * QUERY_SCALE).astype(jnp.bfloat16),
            heads_grad[:, D:],
        ],
        axis=1,
    )
    self_project_grad = jnp.dot(inputs.T, project_grad, preferred_element_type=jnp.float32)
    input_grad = first_resid + jnp.dot(
        project_grad, self_project.T, preferred_element_type=jnp.float32
    )
    biases_grad = jnp.stack(
        [
            jnp.sum(project_grad[:, :D].astype(jnp.float32), axis=0),
            jnp.sum(project_grad[:, 2 * D :].astype(jnp.float32), axis=0),
            jnp.sum(self_branch_grad.astype(jnp.float32), axis=0),
            jnp.sum(cross_pre_grad.astype(jnp.float32), axis=0),
            value_bias_grad,
            jnp.sum(cross_branch_grad.astype(jnp.float32), axis=0),
            jnp.sum(ffn_branch_grad.astype(jnp.float32), axis=0),
        ]
    )
    gain_grad = jnp.stack([first_gain, second_gain, final_gain])
    shift_grad = jnp.stack([first_shift, second_shift, final_shift])
    shared = (
        lax.psum_scatter(self_project_grad, "store", scatter_dimension=0, tiled=True),
        lax.psum_scatter(self_output_grad, "store", scatter_dimension=0, tiled=True),
        lax.psum_scatter(cross_query_grad, "store", scatter_dimension=0, tiled=True),
        lax.psum_scatter(cross_memory_grad, "store", scatter_dimension=0, tiled=True),
        lax.psum_scatter(cross_output_grad, "store", scatter_dimension=0, tiled=True),
        lax.psum_scatter(expand_weight_grad, "store", scatter_dimension=0, tiled=True),
        lax.psum_scatter(contract_weight_grad, "store", scatter_dimension=0, tiled=True),
        lax.psum_scatter(biases_grad, "store", scatter_dimension=1, tiled=True),
        lax.psum_scatter(expand_bias_grad, "store", scatter_dimension=0, tiled=True),
        lax.psum_scatter(gain_grad, "store", scatter_dimension=1, tiled=True),
        lax.psum_scatter(shift_grad, "store", scatter_dimension=1, tiled=True),
    )
    reduced = (
        lax.psum(shared[0].astype(jnp.bfloat16), "dp").astype(jnp.float32),
        lax.psum(shared[1].astype(jnp.bfloat16), "dp").astype(jnp.float32),
        lax.psum(shared[2].astype(jnp.bfloat16), "dp").astype(jnp.float32),
        lax.psum(shared[3].astype(jnp.bfloat16), "dp").astype(jnp.float32),
        lax.psum(shared[4].astype(jnp.bfloat16), "dp").astype(jnp.float32),
        lax.psum(shared[5].astype(jnp.bfloat16), "dp").astype(jnp.float32),
        lax.psum(shared[6].astype(jnp.bfloat16), "dp").astype(jnp.float32),
        lax.psum(shared[7].astype(jnp.bfloat16), "dp").astype(jnp.float32),
        lax.psum(shared[8].astype(jnp.bfloat16), "dp").astype(jnp.float32),
        lax.psum(shared[9].astype(jnp.bfloat16), "dp").astype(jnp.float32),
        lax.psum(shared[10].astype(jnp.bfloat16), "dp").astype(jnp.float32),
    )
    return (
        outputs,
        input_grad,
        datastore_grad,
        reduced[0],
        reduced[1],
        reduced[2],
        reduced[3],
        reduced[4],
        reduced[5],
        reduced[6],
        reduced[7],
        reduced[8],
        reduced[9],
        reduced[10],
    )


def solution(mesh):
    placed = (
        P(("dp", "store"), None),
        P(("dp", "store"), None),
        P(("dp", "store"), None),
        P(("dp", "store")),
        P(("dp", "store"), None),
        P(),
        P(),
        P(),
        P(),
        P(),
        P(),
        P(),
        P(),
        P(),
        P(),
        P(),
        P(("dp", "store"), None),
    )
    return jax.shard_map(
        local_tree if mesh.shape["store"] == 16 else local_slots,
        mesh=mesh,
        in_specs=placed,
        out_specs=(
            P(("dp", "store"), None),
            P(("dp", "store"), None),
            P(("dp", "store"), None),
            P("store", None),
            P("store", None),
            P("store", None),
            P("store", None),
            P("store", None),
            P("store", None),
            P("store", None),
            P(None, "store"),
            P("store"),
            P(None, "store"),
            P(None, "store"),
        ),
        check_vma=False,
    )
```
